32 devices in a mesh: dp: 16 (over z, y, core), own: 2 (over x).
Axes of the slice: x: 2, y: 2, z: 4, core: 2. Of those that a mesh axis runs over, the one named last changes fastest.
Arguments:
- wide_rows: bfloat16 [8, 24576, 256], P(None, ('dp', 'own'))
- narrow_rows: bfloat16 [8, 24576, 128], P(None, ('dp', 'own'))
- owner_map: int32 [8], replicated, may hold values from 0 to 1, as said below
Outputs:
- kept_inverse: float32 [10, 256, 256], P('own', None, 'dp')
- update: float32 [8, 128, 256], P(None, 'own', 'dp')
The draws below stay inside these ranges and needn't reach their ends.
Inputs may be any that keep to these rules, and one draw needn't show every extreme that they name: owner_map[l] names the owner of layer l; no owner has more than 5 layers, and one owner has exactly 5.
All inputs are finite; a program needn't handle non-finite values.
Results may differ from the reference program's by a relative error of at most 0.0003.
Values sent between devices are 32-bit elements; how exact they have to be, the bound alone decides.
No kernel may reach another device: no remote copies, remote signals or barrier semaphores. Data moves between devices by JAX's collectives and lax.ppermute only.
A program may use at most 64 MiB of HBM per device.

```python
import jax
import jax.numpy as jnp
from jax import lax

WIDE = 256
NARROW = 128
LAYERS = 8
ROWS_DEV = 768
CAP = 5
ROWS = 24576
SLOTS = 10
N_OWN = 2


def base_noise(key, shape):
    return jax.random.normal(key, shape, jnp.float32)


def shaped_rows(key, raw, width):
    row_ids = jnp.arange(ROWS, dtype=jnp.int32)
    frac = row_ids.astype(jnp.float32) / ROWS
    scale = jnp.exp(jnp.log(3.0) * (frac - 0.5))
    mixed = raw + 0.7 * jnp.roll(raw, 1, axis=2) - 0.5 * jnp.roll(raw, 7, axis=2)
    device = row_ids // ROWS_DEV
    column = jnp.arange(width, dtype=jnp.int32)
    boost = 1.0 + 2.0 * (column[None, :] == (device % width)[:, None]).astype(jnp.float32)
    column_draw = jax.random.uniform(jax.random.fold_in(key, 37), (LAYERS, 1, width), jnp.float32, 0.0, 1.0)
    column_scale = 4.0 * jnp.exp(jnp.log(10.0) * (column_draw - 0.5))
    return mixed * scale[None, :, None] * boost[None, :, :] * column_scale


def draw_wide_rows(key, part):
    raw = base_noise(jax.random.fold_in(key, 11), (LAYERS, ROWS, WIDE))
    return shaped_rows(jax.random.fold_in(key, 13), raw, WIDE).astype(jnp.bfloat16)


def draw_narrow_rows(key, part):
    shared = base_noise(jax.random.fold_in(key, 11), (LAYERS, ROWS, WIDE))
    own_part = base_noise(jax.random.fold_in(key, 12), (LAYERS, ROWS, NARROW))
    raw = own_part + 0.8 * shared[:, :, :NARROW]
    return shaped_rows(jax.random.fold_in(key, 14), raw, NARROW).astype(jnp.bfloat16)


def draw_owner_map(key, part):
    first = jax.random.randint(jax.random.fold_in(key, 21), (), 0, N_OWN)
    layer_order = jax.random.permutation(jax.random.fold_in(key, 22), LAYERS)
    other_slots = jax.random.permutation(jax.random.fold_in(key, 23), (N_OWN - 1) * CAP)
    ranks = jnp.arange(LAYERS, dtype=jnp.int32)
    picked = other_slots[jnp.clip(ranks - CAP, 0, (N_OWN - 1) * CAP - 1)]
    others = (first + 1 + picked // CAP) % N_OWN
    owners = jnp.where(ranks < CAP, first, others).astype(jnp.int32)
    result = jnp.zeros((LAYERS,), jnp.int32).at[layer_order].set(owners)
    return result


def setup_inputs(seed: int = 0) -> dict:
    keys = jax.random.split(jax.random.key(seed), 4)
    wide_rows = draw_wide_rows(jax.random.fold_in(keys[3], 71), 0)
    narrow_rows = draw_narrow_rows(jax.random.fold_in(keys[3], 71), 0)
    owner_map = draw_owner_map(jax.random.fold_in(keys[3], 71), 0)
    return {"wide_rows": wide_rows, "narrow_rows": narrow_rows, "owner_map": owner_map}


DAMP = 0.5

def layer_stats(pair):
    wide, narrow = pair
    wcov = jnp.dot(wide.T.astype(jnp.float32), wide.astype(jnp.float32), preferred_element_type=jnp.float32)
    ncov = jnp.dot(narrow.T.astype(jnp.float32), narrow.astype(jnp.float32), preferred_element_type=jnp.float32)
    mixed = jnp.dot(narrow.T.astype(jnp.float32), wide.astype(jnp.float32), preferred_element_type=jnp.float32)
    return (wcov, ncov, mixed)

def solve_with(factor, rhs):
    return jax.scipy.linalg.cho_solve((factor, True), rhs)

def reference(wide_rows, narrow_rows, owner_map):
    wcov, ncov, mixed = lax.map(layer_stats, (wide_rows, narrow_rows))
    wcov = wcov / ROWS
    ncov = ncov / ROWS
    mixed = mixed / ROWS
    wide_eye = jnp.eye(WIDE, dtype=jnp.float32)
    narrow_eye = jnp.eye(NARROW, dtype=jnp.float32)
    wchol = jax.vmap(jnp.linalg.cholesky)(wcov + DAMP * wide_eye)
    nchol = jax.vmap(jnp.linalg.cholesky)(ncov + DAMP * narrow_eye)
    winv = jax.vmap(lambda c: solve_with(c, wide_eye))(wchol)
    inner = jnp.einsum('lnw,lwk->lnk', mixed, winv, precision=lax.Precision.HIGHEST)
    update = jax.vmap(solve_with)(nchol, inner)
    same = owner_map[:, None] == owner_map[None, :]
    order = jnp.arange(LAYERS, dtype=jnp.int32)
    earlier = order[None, :] < order[:, None]
    rank = jnp.sum((same & earlier).astype(jnp.int32), axis=1)
    slot = (owner_map * CAP + rank).astype(jnp.int32)
    kept = jnp.broadcast_to(wide_eye / DAMP, (SLOTS, WIDE, WIDE))
    kept = kept.at[slot].set(winv)
    return (kept, update)
```

```python
import functools

import jax
import jax.numpy as jnp
import numpy as np
from jax import lax
from jax.experimental import pallas as pl
from jax.experimental.pallas import tpu as pltpu
from jax.sharding import PartitionSpec as P

DAMP = 0.5
LANES = 128
PANEL = 8
VMEM_LIMIT = 48 * 1024 * 1024
HIGHEST = lax.Precision.HIGHEST


def transposed_dot(a, b, precision=None):
    return lax.dot_general(
        a, b, (((0,), (0,)), ((), ())), precision=precision, preferred_element_type=jnp.float32
    )


def gram_kernel(place, wide_ref, narrow_ref, *refs):
    outs, blocks, mixed_blocks = refs[:8], refs[8], refs[9]
    a_keep, a_send, b_keep, b_send, ma_keep, ma_send, mb_keep, mb_send = outs
    wide = wide_ref[0]
    narrow = narrow_ref[0]
    wcov = transposed_dot(wide, wide)
    mixed = transposed_dot(narrow, wide)
    half = wcov.shape[0] // 2
    low = mixed.shape[0] // 2
    blocks[0] = wcov[:half, :half]
    blocks[1] = wcov[:half, half:]
    blocks[2] = wcov[half:, half:]
    blocks[3] = transposed_dot(narrow, narrow)
    mixed_blocks[0] = mixed[:low, :half]
    mixed_blocks[1] = mixed[low:, :half]
    mixed_blocks[2] = mixed[:low, half:]
    mixed_blocks[3] = mixed[low:, half:]
    core, near = place[1], place[2]
    for q in range(2):
        kept = core * 2 + (q ^ near)
        sent = (1 - core) * 2 + (q ^ near)
        rows = half // 2
        a_keep[0, 0, 0, q] = blocks[kept, :rows]
        b_keep[0, 0, 0, q] = blocks[kept, rows:]
        a_send[0, 0, 0, q] = blocks[sent, :rows]
        b_send[0, 0, 0, q] = blocks[sent, rows:]
        rows = low // 2
        ma_keep[0, 0, 0, q] = mixed_blocks[kept, :rows]
        mb_keep[0, 0, 0, q] = mixed_blocks[kept, rows:]
        ma_send[0, 0, 0, q] = mixed_blocks[sent, :rows]
        mb_send[0, 0, 0, q] = mixed_blocks[sent, rows:]


def gram(place, wide_rows, narrow_rows):
    layers, rows, wide = wide_rows.shape
    narrow = narrow_rows.shape[2]

    def layer_block(i, place):
        return (jnp.bitwise_xor(i, place[0]), 0, 0)

    def order_a(i, place):
        return (i % 2, (i // 2) % 2, i // 4, 0, 0, 0)

    def order_b(i, place):
        return ((i // 2) % 2, i % 2, i // 4, 0, 0, 0)

    specs, shapes = [], []
    for height in (wide // 4, narrow // 4):
        for order in (order_a, order_a, order_b, order_b):
            specs.append(pl.BlockSpec((1, 1, 1, 2, height, LANES), order))
            shapes.append(jax.ShapeDtypeStruct((2, 2, 2, 2, height, LANES), jnp.float32))
    return pl.pallas_call(
        gram_kernel,
        grid_spec=pltpu.PrefetchScalarGridSpec(
            num_scalar_prefetch=1,
            grid=(layers,),
            in_specs=[
                pl.BlockSpec((1, rows, wide), layer_block),
                pl.BlockSpec((1, rows, narrow), layer_block),
            ],
            out_specs=specs,
            scratch_shapes=[
                pltpu.VMEM((4, wide // 2, LANES), jnp.float32),
                pltpu.VMEM((4, narrow // 2, LANES), jnp.float32),
            ],
        ),
        out_shape=shapes,
        compiler_params=pltpu.CompilerParams(vmem_limit_bytes=VMEM_LIMIT),
        name="gram",
    )(place, wide_rows, narrow_rows)


def lane_gather(x, index):
    return jnp.take_along_axis(x, index, axis=1, mode="promise_in_bounds")


def trailing_update(a_ref, left_ref, right_ref, base):
    size = a_ref.shape[1]
    a_ref[pl.ds(pl.multiple_of(base, PANEL), PANEL), :] = jnp.zeros((PANEL, size), jnp.float32)
    lane = lax.broadcasted_iota(jnp.int32, (1, size), 1)
    swept = (lane >= base - PANEL) & (lane < base)
    update = transposed_dot(left_ref[...], right_ref[...])
    a_ref[PANEL : PANEL + size, :] = (
        jnp.where(swept, 0.0, a_ref[PANEL : PANEL + size, :]) - update
    )


def sweep_panel(a_ref, left_ref, right_ref, tile, step, panel):
    size = a_ref.shape[1]
    tiles = size // LANES
    first = step * PANEL
    base = tile * LANES + first
    trailing_update(a_ref, left_ref, right_ref, base)

    shape = (PANEL, LANES)
    sub = lax.broadcasted_iota(jnp.int32, shape, 0)
    lane = lax.broadcasted_iota(jnp.int32, shape, 1)
    parts = [panel[:, LANES * t : LANES * (t + 1)] for t in range(tiles)]
    rows = [
        [jnp.broadcast_to(part[k : k + 1, :], shape) for part in parts] for k in range(PANEL)
    ]
    index = [jnp.full(shape, 0, jnp.int32) + (first + i) for i in range(PANEL)]
    d = [[None] * PANEL for _ in range(PANEL)]
    for j in range(PANEL):
        for i in range(j, PANEL):
            d[i][j] = lane_gather(rows[j][tile], index[i])
    own = (lane >= first) & (lane < first + PANEL)
    q = [[None] * tiles for _ in range(PANEL)]
    factor = [[None] * PANEL for _ in range(PANEL)]
    for k in range(PANEL):
        scale = lax.rsqrt(d[k][k])
        for i in range(k + 1, PANEL):
            factor[i][k] = d[i][k] * scale
        for i in range(k + 1, PANEL):
            for j in range(k + 1, i + 1):
                d[i][j] = d[i][j] - factor[i][k] * factor[j][k]
        for t in range(tiles):
            value = rows[k][t]
            if t == tile:
                value = jnp.where(own, jnp.where(lane == first + k, -1.0, 0.0), value)
            for j in range(k):
                value = value - factor[k][j] * q[j][t]
            q[k][t] = value * scale

    packed = []
    for t in range(tiles):
        value = q[0][t]
        for k in range(1, PANEL):
            value = jnp.where(sub == k, q[k][t], value)
        packed.append(value)
    whole = jnp.concatenate(packed, axis=1) if tiles > 1 else packed[0]
    high = whole.astype(jnp.bfloat16).astype(jnp.float32)
    rest = whole - high
    middle = rest.astype(jnp.bfloat16).astype(jnp.float32)
    low = rest - middle
    left = jnp.concatenate([high, high, middle, middle, high, low], axis=0)
    right = jnp.concatenate([high, middle, high, middle, low, high], axis=0)
    left_ref[...] = left.astype(jnp.bfloat16)
    right_ref[...] = right.astype(jnp.bfloat16)

    after = pl.multiple_of(base + 2 * PANEL, PANEL)
    following = a_ref[pl.ds(after, PANEL), :]
    last = first == LANES - PANEL
    next_lane = jnp.where(last, 0, first + PANEL) + sub
    weights = []
    for k in range(PANEL):
        source = q[k][tile]
        if tile + 1 < tiles:
            source = jnp.where(last, q[k][tile + 1], source)
        weights.append(lane_gather(source, next_lane))
    result = []
    for t in range(tiles):
        value = following[:, LANES * t : LANES * (t + 1)]
        if t == tile:
            value = jnp.where(own, 0.0, value)
        terms = [weights[k] * q[k][t] for k in range(PANEL)]
        while len(terms) > 1:
            terms = [terms[i] + terms[i + 1] for i in range(0, len(terms), 2)]
        result.append(value - terms[0])
    return jnp.concatenate(result, axis=1) if tiles > 1 else result[0]


def inverse_kernel(total, place, *refs):
    pieces, refs = refs[:4], refs[4:]
    winv_ref, ninv_ref, blocks, wa, na, wl, wr, nl, nr = refs
    mine = place[1] * 2 + place[2]
    for r in range(4):
        blocks[jnp.bitwise_xor(mine, r)] = pieces[r][...]
    half = blocks.shape[1]

    def eye(size):
        return jnp.where(
            lax.broadcasted_iota(jnp.int32, (size, size), 0)
            == lax.broadcasted_iota(jnp.int32, (size, size), 1),
            DAMP,
            0.0,
        )

    wide, narrow = wa.shape[1], na.shape[1]
    wa[...] = jnp.zeros(wa.shape, jnp.float32)
    na[...] = jnp.zeros(na.shape, jnp.float32)
    corner = blocks[1] / total
    damp = eye(half)
    wa[PANEL : PANEL + half, :half] = blocks[0] / total + damp
    wa[PANEL : PANEL + half, half:] = corner
    wa[PANEL + half : PANEL + wide, :half] = corner.T
    wa[PANEL + half : PANEL + wide, half:] = blocks[2] / total + damp
    na[PANEL : PANEL + narrow, :] = blocks[3] / total + damp
    for ref in (wl, wr, nl, nr):
        ref[...] = jnp.zeros(ref.shape, ref.dtype)

    def both(step, carry):
        wp, np_ = carry
        wp = sweep_panel(wa, wl, wr, 0, step, wp)
        np_ = sweep_panel(na, nl, nr, 0, step, np_)
        return (wp, np_)

    steps = LANES // PANEL
    start = (wa[PANEL : 2 * PANEL, :], na[PANEL : 2 * PANEL, :])
    panel, _ = lax.fori_loop(0, steps, both, start)
    trailing_update(na, nl, nr, narrow)
    ninv_ref[...] = -na[PANEL : PANEL + narrow, :]

    def only(step, panel):
        return sweep_panel(wa, wl, wr, 1, step, panel)

    lax.fori_loop(0, steps, only, panel)
    trailing_update(wa, wl, wr, wide)
    winv_ref[...] = -wa[PANEL : PANEL + wide, :]


def inverses(place, pieces, wide, narrow, total):
    vmem = pl.BlockSpec(memory_space=pltpu.VMEM)
    splits = 6 * PANEL
    return pl.pallas_call(
        functools.partial(inverse_kernel, total),
        in_specs=[pl.BlockSpec(memory_space=pltpu.SMEM)] + [vmem] * 4,
        out_specs=[vmem] * 2,
        out_shape=[
            jax.ShapeDtypeStruct((wide, wide), jnp.float32),
            jax.ShapeDtypeStruct((narrow, narrow), jnp.float32),
        ],
        scratch_shapes=[
            pltpu.VMEM((4, wide // 2, LANES), jnp.float32),
            pltpu.VMEM((wide + 2 * PANEL, wide), jnp.float32),
            pltpu.VMEM((narrow + 2 * PANEL, narrow), jnp.float32),
            pltpu.VMEM((splits, wide), jnp.bfloat16),
            pltpu.VMEM((splits, wide), jnp.bfloat16),
            pltpu.VMEM((splits, narrow), jnp.bfloat16),
            pltpu.VMEM((splits, narrow), jnp.bfloat16),
        ],
        compiler_params=pltpu.CompilerParams(vmem_limit_bytes=VMEM_LIMIT),
        name="inverses",
    )(place, *pieces)


def aligned_rows(ref, index, count):
    if count % PANEL == 0:
        return ref[pl.ds(pl.multiple_of(index * count, count), count), :]
    per_slab = PANEL // count
    slab = ref[pl.ds(pl.multiple_of(index // per_slab * PANEL, PANEL), PANEL), :]
    value = slab[:count]
    for i in range(1, per_slab):
        value = jnp.where(index % per_slab == i, slab[i * count : (i + 1) * count], value)
    return value


def product_kernel(total, far_stride, place, winv_ref, ninv_ref, *refs):
    pieces, (out_ref, blocks) = refs[:4], refs[4:]
    mine = place[1] * 2 + place[2]
    for r in range(4):
        blocks[jnp.bitwise_xor(mine, r)] = pieces[r][...]
    low = blocks.shape[1]
    ninv = ninv_ref[...]
    parts = []
    for h in range(2):
        mixed = blocks[2 * h : 2 * h + 2].reshape(2 * low, LANES) / total
        parts.append(transposed_dot(mixed, ninv, HIGHEST))
    inner = jnp.concatenate(parts, axis=0)
    cols = out_ref.shape[1]
    wide = winv_ref.shape[1]
    for j in range(4):
        index = place[3] + (j // 2) * far_stride + (j % 2) * 2
        picked = aligned_rows(winv_ref, index, cols)
        update = lax.dot_general(
            picked,
            inner,
            (((1,), (0,)), ((), ())),
            precision=HIGHEST,
            preferred_element_type=jnp.float32,
        )
        for x in range(2):
            out_ref[2 * j + x, :, :wide] = picked
            out_ref[2 * j + x, :, wide:] = update


def products(place, winv, ninv, pieces, cols, far_stride, total):
    vmem = pl.BlockSpec(memory_space=pltpu.VMEM)
    wide, narrow = winv.shape[0], ninv.shape[0]
    return pl.pallas_call(
        functools.partial(product_kernel, total, far_stride),
        in_specs=[pl.BlockSpec(memory_space=pltpu.SMEM)] + [vmem] * 6,
        out_specs=vmem,
        out_shape=jax.ShapeDtypeStruct((8, cols, wide + narrow), jnp.float32),
        scratch_shapes=[pltpu.VMEM((4, narrow // 2, LANES), jnp.float32)],
        compiler_params=pltpu.CompilerParams(vmem_limit_bytes=VMEM_LIMIT),
        name="products",
    )(place, winv, ninv, *pieces)


def placing_kernel(place, owner_map, got_ref, kept_ref, update_ref, turned):
    layers, cols, _ = got_ref.shape
    wide = kept_ref.shape[1]
    rows = update_ref.shape[1]
    own, dp = place[4], place[5]
    sub = lax.broadcasted_iota(jnp.int32, (cols, wide), 0)
    lane = lax.broadcasted_iota(jnp.int32, (cols, wide), 1)
    empty = jnp.where(lane == sub + dp * cols, 1.0 / DAMP, 0.0)
    owners = [owner_map[l] for l in range(layers)]
    ranks = []
    for l in range(layers):
        rank = jnp.int32(0)
        for j in range(l):
            rank = rank + (owners[j] == owners[l]).astype(jnp.int32)
        ranks.append(rank)
    for c in range(kept_ref.shape[0]):
        value = empty
        for l in range(layers):
            taken = (owners[l] == own) & (ranks[l] == c)
            value = jnp.where(taken, got_ref[l, :, :wide], value)
        kept_ref[c] = value.T
    for l in range(layers):
        turned[...] = got_ref[l, :, wide:].T
        update_ref[l] = turned[pl.ds(pl.multiple_of(own * rows, rows), rows), :]


def placing(place, owner_map, got, wide, narrow, slots, rows):
    vmem = pl.BlockSpec(memory_space=pltpu.VMEM)
    smem = pl.BlockSpec(memory_space=pltpu.SMEM)
    layers, cols, _ = got.shape
    return pl.pallas_call(
        placing_kernel,
        in_specs=[smem, smem, vmem],
        out_specs=[vmem, vmem],
        out_shape=[
            jax.ShapeDtypeStruct((slots, wide, cols), jnp.float32),
            jax.ShapeDtypeStruct((layers, rows, cols), jnp.float32),
        ],
        scratch_shapes=[pltpu.VMEM((narrow, cols), jnp.float32)],
        compiler_params=pltpu.CompilerParams(vmem_limit_bytes=VMEM_LIMIT),
        name="placing",
    )(place, owner_map, got)


def swap(value, axis):
    return lax.ppermute(value, axis, [(0, 1), (1, 0)])


def swap_both(value, axes):
    return lax.ppermute(value, axes, [(0, 3), (1, 2), (2, 1), (3, 0)])


def fold(value, axis):
    return value[0] + swap(value[1], axis)


def reduce_pieces(a_keep, a_send, b_keep, b_send, names):
    core, near, far, first, second, extra = names
    a = a_keep + swap(a_send, core)
    b = b_keep + swap(b_send, core)
    a = fold(a, first)
    b = fold(b, second)
    a = fold(a, second)
    b = fold(b, first)
    both = jnp.concatenate([a, b], axis=2)
    both = jnp.moveaxis(both, 1, 0)
    both = fold(both, near)
    both = fold(both, far)
    if extra:
        both = lax.psum(both, extra)
    return [both, swap(both, near), swap(both, core), swap_both(both, (near, core))]


def on_device(dp_names, own_names, wide_rows, narrow_rows, owner_map):
    layers, rows, wide = wide_rows.shape
    narrow = narrow_rows.shape[2]
    n_dp, n_own = 2 ** len(dp_names), 2 ** len(own_names)
    total = float(rows * n_dp * n_own)
    core, second, near, far = dp_names[-1], dp_names[-2], dp_names[1], dp_names[0]
    first = own_names[-1]
    extra = tuple(
        n for n in dp_names + own_names if n not in (core, near, far, first, second)
    )
    names = (core, near, far, first, second, extra)
    index = {name: lax.axis_index(name) for name in dp_names + own_names}

    def combine(axes):
        value = jnp.int32(0)
        for name in axes:
            value = value * 2 + index[name]
        return value

    dp_index = combine(dp_names)
    far_stride = n_dp // 2
    place = jnp.stack(
        [
            index[far] * 4 + index[second] * 2 + index[first],
            index[core],
            index[near],
            dp_index - index[far] * far_stride - index[second] * 2,
            combine(own_names),
            dp_index,
        ]
    ).astype(jnp.int32)

    outs = gram(place, wide_rows, narrow_rows)
    squares = reduce_pieces(*outs[:4], names)
    mixed = reduce_pieces(*outs[4:], names)
    winv, ninv = inverses(place, squares, wide, narrow, total)
    cols = wide // n_dp
    sent = products(place, winv, ninv, mixed, cols, far_stride, total)
    got = lax.all_to_all(sent, (far, second, first), 0, 0)
    kept, update = placing(
        place, owner_map, got, wide, narrow, layers // n_own + 1, narrow // n_own
    )
    return (kept, update)


def solution(mesh):
    n_dp, n_own = mesh.shape["dp"], mesh.shape["own"]
    dp_names = tuple(f"dp{i}" for i in range(int(np.log2(n_dp))))
    own_names = tuple(f"own{i}" for i in range(int(np.log2(n_own))))
    names = dp_names + own_names
    bits = jax.sharding.Mesh(mesh.devices.reshape((2,) * len(names)), names)
    in_specs = (P(None, names, None), P(None, names, None), P())
    out_specs = (P(own_names, None, dp_names), P(None, own_names, dp_names))
    return jax.shard_map(
        functools.partial(on_device, dp_names, own_names),
        mesh=bits,
        in_specs=in_specs,
        out_specs=out_specs,
        check_vma=False,
    )
```

```python
import functools

import jax
import jax.numpy as jnp
import numpy as np
from jax import lax
from jax.experimental import pallas as pl
from jax.experimental.pallas import tpu as pltpu
from jax.sharding import PartitionSpec as P

DAMP = 0.5
LANES = 128
PANEL = 8
VMEM_LIMIT = 48 * 1024 * 1024
HIGHEST = lax.Precision.HIGHEST
VMEM = pl.BlockSpec(memory_space=pltpu.VMEM)
SMEM = pl.BlockSpec(memory_space=pltpu.SMEM)
HBM = pl.BlockSpec(memory_space=pltpu.HBM)
PARAMS = pltpu.CompilerParams(vmem_limit_bytes=VMEM_LIMIT)


class Place:
    def __init__(self, dp_names, own_names):
        self.dp, self.own = dp_names, own_names
        self.core, self.second, self.near, self.far = (
            dp_names[-1],
            dp_names[-2],
            dp_names[1],
            dp_names[0],
        )
        self.first = own_names[-1]
        used = (self.core, self.second, self.near, self.far, self.first)
        self.extra = tuple(n for n in dp_names + own_names if n not in used)

    def index(self, names):
        value = jnp.int32(0)
        for name in names:
            value = value * 2 + lax.axis_index(name)
        return value

    def layer(self):
        return self.index((self.far, self.second, self.first))

    def quarter(self):
        return self.index((self.core, self.near))


def transposed_dot(a, b, precision=None):
    return lax.dot_general(
        a, b, (((0,), (0,)), ((), ())), precision=precision, preferred_element_type=jnp.float32
    )


def read_layers(place, sources, buffers, sems):
    layer = place.layer()
    copies = []
    for i in range(buffers[0].shape[0]):
        group = [
            pltpu.make_async_copy(
                source.at[jnp.bitwise_xor(layer, i)], buffer.at[i], sems.at[i, s]
            )
            for s, (source, buffer) in enumerate(zip(sources, buffers))
        ]
        for copy in group:
            copy.start()
        copies.append(group)
    return copies


def write_quarters(place, i, flat, keep_ref, send_ref):
    rows = keep_ref.shape[3]
    quarter = place.quarter()
    for q in range(2):
        kept = pl.multiple_of(jnp.bitwise_xor(quarter, q) * rows, PANEL)
        sent = pl.multiple_of(jnp.bitwise_xor(quarter, 2 + q) * rows, PANEL)
        keep_ref[i % 4, i // 4, q] = flat[i, pl.ds(kept, rows), :]
        send_ref[i % 4, i // 4, q] = flat[i, pl.ds(sent, rows), :]


def iotas(shape):
    return (
        lax.broadcasted_iota(jnp.int32, shape, 0),
        lax.broadcasted_iota(jnp.int32, shape, 1),
    )


def pack_squares(flat, i, first, corner, second, narrow):
    n = LANES
    row, col = iotas((n, n))
    flat[i, :n] = jnp.where(row >= col, first, second)
    flat[i, n : 2 * n] = corner
    h = n // 2
    row_h, col_h = iotas((h, n))
    lower = pltpu.roll(narrow[h:], h, 1)
    flat[i, 2 * n : 2 * n + h] = jnp.where(
        (col_h >= h) | (row_h >= col_h), narrow[:h], lower
    )
    diagonal = row == col
    pair = [
        jnp.sum(jnp.where(diagonal, block, 0.0), axis=0, keepdims=True)
        for block in (second, narrow)
    ]
    row_p, _ = iotas((PANEL, n))
    shape = (PANEL, n)
    base = 2 * n + h
    flat[i, base : base + PANEL] = jnp.where(
        row_p == 0,
        jnp.broadcast_to(pair[0], shape),
        jnp.where(row_p == 1, jnp.broadcast_to(pair[1], shape), 0.0),
    )
    pad = flat.shape[1] - base - PANEL
    flat[i, base + PANEL :] = jnp.zeros((pad, n), jnp.float32)


def unpack_squares(flat):
    n = LANES
    h = n // 2
    row, col = iotas((n, n))
    packed = flat[:n]
    turned = packed.T
    corner = flat[n : 2 * n]
    folded = jnp.concatenate([flat[2 * n : 2 * n + h], jnp.zeros((h, n), jnp.float32)], axis=0)
    slab = flat[2 * n + h : 2 * n + h + PANEL]
    second_diagonal = jnp.broadcast_to(slab[0:1], (n, n))
    narrow_diagonal = jnp.broadcast_to(slab[1:2], (n, n))
    first = jnp.where(row >= col, packed, turned)
    second = jnp.where(col > row, packed, turned)
    second = jnp.where(row == col, second_diagonal, second)
    folded_t = folded.T
    top = jnp.where((col >= h) | (col <= row), folded, folded_t)
    moved = pltpu.roll(pltpu.roll(folded, h, 0), h, 1)
    moved_t = pltpu.roll(pltpu.roll(folded_t, h, 0), h, 1)
    corner_n = jnp.where(col > row, moved, moved_t)
    corner_n = jnp.where(row == col, narrow_diagonal, corner_n)
    bottom = jnp.where(col < h, folded_t, corner_n)
    return (first, corner, second, jnp.where(row < h, top, bottom))


def squares_kernel(place, wide_hbm, narrow_hbm, keep_ref, send_ref, wides, narrows, flat, sems):
    copies = read_layers(place, (wide_hbm, narrow_hbm), (wides, narrows), sems)
    for i, group in enumerate(copies):
        for copy in group:
            copy.wait()
        wide = wides[i]
        narrow = narrows[i]
        wcov = transposed_dot(wide, wide)
        ncov = transposed_dot(narrow, narrow)
        n = LANES
        pack_squares(flat, i, wcov[:n, :n], wcov[:n, n:], wcov[n:, n:], ncov)
        write_quarters(place, i, flat, keep_ref, send_ref)


def mixed_kernel(place, wide_hbm, narrow_hbm, keep_ref, send_ref, wides, narrows, flat, sems):
    copies = read_layers(place, (wide_hbm, narrow_hbm), (wides, narrows), sems)
    for i, group in enumerate(copies):
        for copy in group:
            copy.wait()
        mixed = transposed_dot(narrows[i], wides[i])
        flat[i, :LANES] = mixed[:, :LANES]
        flat[i, LANES:] = mixed[:, LANES:]
        write_quarters(place, i, flat, keep_ref, send_ref)


def gram(kernel, name, place, quarter_rows, wide_rows, narrow_rows):
    layers = wide_rows.shape[0]
    shape = jax.ShapeDtypeStruct((4, 2, 2, quarter_rows, LANES), jnp.float32)
    macs = wide_rows.shape[1] * wide_rows.shape[2] * 256
    return pl.pallas_call(
        functools.partial(kernel, place),
        in_specs=[HBM, HBM],
        out_specs=[VMEM, VMEM],
        out_shape=[shape, shape],
        scratch_shapes=[
            pltpu.VMEM(wide_rows.shape, wide_rows.dtype),
            pltpu.VMEM(narrow_rows.shape, narrow_rows.dtype),
            pltpu.VMEM((layers, 4 * quarter_rows, LANES), jnp.float32),
            pltpu.SemaphoreType.DMA((layers, 2)),
        ],
        cost_estimate=pl.CostEstimate(
            flops=2 * layers * macs, bytes_accessed=2 * wide_rows.size * 2, transcendentals=0
        ),
        compiler_params=PARAMS,
        name=name,
    )(wide_rows, narrow_rows)


def lane_gather(x, index):
    return jnp.take_along_axis(x, index, axis=1, mode="promise_in_bounds")


def trailing_update(a_ref, left_ref, right_ref, base):
    size = a_ref.shape[1]
    a_ref[pl.ds(pl.multiple_of(base, PANEL), PANEL), :] = jnp.zeros((PANEL, size), jnp.float32)
    lane = lax.broadcasted_iota(jnp.int32, (1, size), 1)
    swept = (lane >= base - PANEL) & (lane < base)
    update = transposed_dot(left_ref[...], right_ref[...])
    a_ref[PANEL : PANEL + size, :] = (
        jnp.where(swept, 0.0, a_ref[PANEL : PANEL + size, :]) - update
    )


def sweep_panel(a_ref, left_ref, right_ref, tile, step, panel):
    size = a_ref.shape[1]
    tiles = size // LANES
    first = step * PANEL
    base = tile * LANES + first
    trailing_update(a_ref, left_ref, right_ref, base)

    shape = (PANEL, LANES)
    sub = lax.broadcasted_iota(jnp.int32, shape, 0)
    lane = lax.broadcasted_iota(jnp.int32, shape, 1)
    parts = [panel[:, LANES * t : LANES * (t + 1)] for t in range(tiles)]
    rows = [
        [jnp.broadcast_to(part[k : k + 1, :], shape) for part in parts] for k in range(PANEL)
    ]
    index = [jnp.full(shape, 0, jnp.int32) + (first + i) for i in range(PANEL)]
    d = [[None] * PANEL for _ in range(PANEL)]
    for j in range(PANEL):
        for i in range(j, PANEL):
            d[i][j] = lane_gather(rows[j][tile], index[i])
    own = (lane >= first) & (lane < first + PANEL)
    q = [[None] * tiles for _ in range(PANEL)]
    factor = [[None] * PANEL for _ in range(PANEL)]
    for k in range(PANEL):
        scale = lax.rsqrt(d[k][k])
        for i in range(k + 1, PANEL):
            factor[i][k] = d[i][k] * scale
        for i in range(k + 1, PANEL):
            for j in range(k + 1, i + 1):
                d[i][j] = d[i][j] - factor[i][k] * factor[j][k]
        for t in range(tiles):
            value = rows[k][t]
            if t == tile:
                value = jnp.where(own, jnp.where(lane == first + k, -1.0, 0.0), value)
            for j in range(k):
                value = value - factor[k][j] * q[j][t]
            q[k][t] = value * scale

    packed = []
    for t in range(tiles):
        value = q[0][t]
        for k in range(1, PANEL):
            value = jnp.where(sub == k, q[k][t], value)
        packed.append(value)
    whole = jnp.concatenate(packed, axis=1) if tiles > 1 else packed[0]
    high = whole.astype(jnp.bfloat16).astype(jnp.float32)
    rest = whole - high
    middle = rest.astype(jnp.bfloat16).astype(jnp.float32)
    low = rest - middle
    left = jnp.concatenate([high, high, middle, middle, high, low], axis=0)
    right = jnp.concatenate([high, middle, high, middle, low, high], axis=0)
    left_ref[...] = left.astype(jnp.bfloat16)
    right_ref[...] = right.astype(jnp.bfloat16)

    after = pl.multiple_of(base + 2 * PANEL, PANEL)
    following = a_ref[pl.ds(after, PANEL), :]
    last = first == LANES - PANEL
    next_lane = jnp.where(last, 0, first + PANEL) + sub
    weights = []
    for k in range(PANEL):
        source = q[k][tile]
        if tile + 1 < tiles:
            source = jnp.where(last, q[k][tile + 1], source)
        weights.append(lane_gather(source, next_lane))
    result = []
    for t in range(tiles):
        value = following[:, LANES * t : LANES * (t + 1)]
        if t == tile:
            value = jnp.where(own, 0.0, value)
        terms = [weights[k] * q[k][t] for k in range(PANEL)]
        while len(terms) > 1:
            terms = [terms[i] + terms[i + 1] for i in range(0, len(terms), 2)]
        result.append(value - terms[0])
    return jnp.concatenate(result, axis=1) if tiles > 1 else result[0]


def place_pieces(place, flat, pieces):
    quarter = place.quarter()
    rows = pieces[0].shape[0]
    for r, piece in enumerate(pieces):
        start = pl.multiple_of(jnp.bitwise_xor(quarter, r) * rows, PANEL)
        flat[pl.ds(start, rows), :] = piece[...]


def first_half_kernel(place, total, *refs):
    pieces, refs = refs[:4], refs[4:]
    ninv_ref, wa, wl, wr, panel_ref, flat, na, nl, nr = refs
    place_pieces(place, flat, pieces)
    wide, narrow = wa.shape[1], na.shape[1]
    half = LANES
    first, corner, second, square = unpack_squares(flat)
    row, col = iotas((half, half))
    damp = jnp.where(row == col, DAMP, 0.0)
    wa[:PANEL] = jnp.zeros((PANEL, wide), jnp.float32)
    wa[PANEL + wide :] = jnp.zeros((PANEL, wide), jnp.float32)
    na[:PANEL] = jnp.zeros((PANEL, narrow), jnp.float32)
    na[PANEL + narrow :] = jnp.zeros((PANEL, narrow), jnp.float32)
    corner = corner / total
    wa[PANEL : PANEL + half, :half] = first / total + damp
    wa[PANEL : PANEL + half, half:] = corner
    wa[PANEL + half : PANEL + wide, :half] = corner.T
    wa[PANEL + half : PANEL + wide, half:] = second / total + damp
    na[PANEL : PANEL + narrow, :] = square / total + damp
    for ref in (wl, wr, nl, nr):
        ref[...] = jnp.zeros(ref.shape, ref.dtype)

    def both(step, carry):
        wide_panel, narrow_panel = carry
        wide_panel = sweep_panel(wa, wl, wr, 0, step, wide_panel)
        narrow_panel = sweep_panel(na, nl, nr, 0, step, narrow_panel)
        return (wide_panel, narrow_panel)

    start = (wa[PANEL : 2 * PANEL, :], na[PANEL : 2 * PANEL, :])
    panel, _ = lax.fori_loop(0, LANES // PANEL, both, start)
    panel_ref[...] = panel
    trailing_update(na, nl, nr, narrow)
    ninv_ref[...] = -na[PANEL : PANEL + narrow, :]


def second_half_kernel(wa_in, wl_in, wr_in, panel_ref, winv_ref, wa, wl, wr):
    wide = wa.shape[1]
    wa[...] = wa_in[...]
    wl[...] = wl_in[...]
    wr[...] = wr_in[...]

    def only(step, panel):
        return sweep_panel(wa, wl, wr, 1, step, panel)

    lax.fori_loop(0, LANES // PANEL, only, panel_ref[...])
    trailing_update(wa, wl, wr, wide)
    winv_ref[...] = -wa[PANEL : PANEL + wide, :]


def sweep_cost(wide):
    return pl.CostEstimate(
        flops=64 * wide * wide * wide, bytes_accessed=16 * wide * wide, transcendentals=0
    )


def first_half(place, pieces, wide, narrow, total):
    splits = 6 * PANEL
    rows = pieces[0].shape[0]
    matrix = (wide + 2 * PANEL, wide)
    return pl.pallas_call(
        functools.partial(first_half_kernel, place, total),
        in_specs=[VMEM] * 4,
        out_specs=[VMEM] * 5,
        out_shape=[
            jax.ShapeDtypeStruct((narrow, narrow), jnp.float32),
            jax.ShapeDtypeStruct(matrix, jnp.float32),
            jax.ShapeDtypeStruct((splits, wide), jnp.bfloat16),
            jax.ShapeDtypeStruct((splits, wide), jnp.bfloat16),
            jax.ShapeDtypeStruct((PANEL, wide), jnp.float32),
        ],
        scratch_shapes=[
            pltpu.VMEM((4 * rows, LANES), jnp.float32),
            pltpu.VMEM((narrow + 2 * PANEL, narrow), jnp.float32),
            pltpu.VMEM((splits, narrow), jnp.bfloat16),
            pltpu.VMEM((splits, narrow), jnp.bfloat16),
        ],
        cost_estimate=sweep_cost(wide),
        compiler_params=PARAMS,
        name="first_half",
    )(*pieces)


def second_half(wa, wl, wr, panel):
    wide = wa.shape[1]
    return pl.pallas_call(
        second_half_kernel,
        in_specs=[VMEM] * 4,
        out_specs=VMEM,
        out_shape=jax.ShapeDtypeStruct((wide, wide), jnp.float32),
        scratch_shapes=[
            pltpu.VMEM(wa.shape, wa.dtype),
            pltpu.VMEM(wl.shape, wl.dtype),
            pltpu.VMEM(wr.shape, wr.dtype),
        ],
        cost_estimate=sweep_cost(wide),
        compiler_params=PARAMS,
        name="second_half",
    )(wa, wl, wr, panel)


def aligned_rows(ref, index, count):
    if count % PANEL == 0:
        return ref[pl.ds(pl.multiple_of(index * count, count), count), :]
    per_slab = PANEL // count
    slab = ref[pl.ds(pl.multiple_of(index // per_slab * PANEL, PANEL), PANEL), :]
    value = slab[:count]
    for i in range(1, per_slab):
        value = jnp.where(index % per_slab == i, slab[i * count : (i + 1) * count], value)
    return value


def product_kernel(place, total, winv_ref, ninv_ref, *refs):
    pieces, outs, flat = refs[:4], refs[4:12], refs[12]
    place_pieces(place, flat, pieces)
    ninv = ninv_ref[...]
    half = flat.shape[0] // 2
    inner = jnp.concatenate(
        [
            transposed_dot(flat[h * half : (h + 1) * half] / total, ninv, HIGHEST)
            for h in range(2)
        ],
        axis=0,
    )
    cols, _ = outs[0].shape
    wide = winv_ref.shape[1]
    far, second = lax.axis_index(place.far), lax.axis_index(place.second)
    far_stride = 2 ** (len(place.dp) - 1)
    base = place.index(place.dp) - far * far_stride - second * 2
    for j in range(4):
        index = base + (far ^ (j // 2)) * far_stride + (second ^ (j % 2)) * 2
        picked = aligned_rows(winv_ref, index, cols)
        update = lax.dot_general(
            picked,
            inner,
            (((1,), (0,)), ((), ())),
            precision=HIGHEST,
            preferred_element_type=jnp.float32,
        )
        for x in range(2):
            outs[2 * j + x][:, :wide] = picked
            outs[2 * j + x][:, wide:] = update


def products(place, winv, ninv, pieces, cols, total):
    wide, narrow = winv.shape[0], ninv.shape[0]
    shape = jax.ShapeDtypeStruct((cols, wide + narrow), jnp.float32)
    return pl.pallas_call(
        functools.partial(product_kernel, place, total),
        in_specs=[VMEM] * 6,
        out_specs=[VMEM] * 8,
        out_shape=[shape] * 8,
        scratch_shapes=[pltpu.VMEM((2 * narrow, LANES), jnp.float32)],
        compiler_params=PARAMS,
        name="products",
    )(winv, ninv, *pieces)


def placing_kernel(place, owner_map, *refs):
    got, (kept_ref, update_ref, slot_of) = refs[:8], refs[8:]
    slots, cols, wide = kept_ref.shape
    rows = update_ref.shape[2]
    own, dp = place.index(place.own), place.index(place.dp)
    row, col = iotas((cols, wide))
    empty = jnp.where(col == row + dp * cols, 1.0 / DAMP, 0.0)
    count = jnp.int32(0)
    for l in range(len(got)):
        mine = owner_map[l] == own
        slot_of[l] = jnp.where(mine, count, -1)
        count = count + mine.astype(jnp.int32)
    layer = place.layer()
    slot = [slot_of[jnp.bitwise_xor(layer, r)] for r in range(len(got))]
    for c in range(slots):
        value = empty
        for r, ref in enumerate(got):
            value = jnp.where(slot[r] == c, ref[:, :wide], value)
        kept_ref[c] = value
    parts = (got[0].shape[1] - wide) // rows
    for r, ref in enumerate(got):
        value = ref[:, wide : wide + rows]
        for p in range(1, parts):
            value = jnp.where(own == p, ref[:, wide + p * rows : wide + (p + 1) * rows], value)
        update_ref[jnp.bitwise_xor(layer, r)] = value


def placing(place, owner_map, got, wide, slots, rows):
    cols = got[0].shape[0]
    return pl.pallas_call(
        functools.partial(placing_kernel, place),
        in_specs=[SMEM] + [VMEM] * 8,
        out_specs=[VMEM, VMEM],
        out_shape=[
            jax.ShapeDtypeStruct((slots, cols, wide), jnp.float32),
            jax.ShapeDtypeStruct((len(got), cols, rows), jnp.float32),
        ],
        scratch_shapes=[pltpu.SMEM((len(got),), jnp.int32)],
        compiler_params=PARAMS,
        name="placing",
    )(owner_map, *got)


def swap(value, *axes):
    count = 2 ** len(axes)
    name = axes if len(axes) > 1 else axes[0]
    return lax.ppermute(value, name, [(i, count - 1 - i) for i in range(count)])


def swap_parts(parts, high, low):
    return [swap(parts[1], low), swap(parts[2], high), swap(parts[3], high, low)]


def add_parts(part, got):
    return (part + got[0]) + (got[1] + got[2])


def after(value, *others):
    return lax.optimization_barrier((value,) + others)[0]


def on_device(place, wide_rows, narrow_rows, owner_map):
    layers, rows, wide = wide_rows.shape
    narrow = narrow_rows.shape[2]
    n_dp, n_own = 2 ** len(place.dp), 2 ** len(place.own)
    total = float(rows * n_dp * n_own)

    s_keep, s_send = gram(squares_kernel, "squares", place, 88, wide_rows, narrow_rows)
    s_got = swap(s_send, place.core)
    m_keep, m_send = gram(mixed_kernel, "mixed", place, 64, after(wide_rows, s_send), narrow_rows)

    s = s_keep + s_got
    s_got = swap_parts(s, place.second, place.first)
    m_got = swap(after(m_send, s), place.core)

    s = add_parts(s[0], s_got).reshape((4,) + s.shape[3:])
    s_got = swap_parts(s, place.far, place.near)
    m = after(m_keep, s) + m_got
    m_got = swap_parts(m, place.second, place.first)

    s = add_parts(s[0], s_got)
    if place.extra:
        s = lax.psum(s, place.extra)
    pieces = [
        s,
        swap(s, place.near),
        swap(s, place.core),
        swap(s, place.near, place.core),
    ]
    m = add_parts(after(m[0], s), m_got).reshape((4,) + m.shape[3:])
    m_got = swap_parts(m, place.far, place.near)

    ninv, wa, wl, wr, panel = first_half(place, pieces, wide, narrow, total)
    m = add_parts(after(m[0], panel), m_got)
    if place.extra:
        m = lax.psum(m, place.extra)
    mixed = [
        m,
        swap(m, place.near),
        swap(m, place.core),
        swap(m, place.near, place.core),
    ]
    winv = second_half(wa, wl, wr, panel)
    cols = wide // n_dp
    sent = products(place, winv, ninv, mixed, cols, total)
    got = [sent[0]]
    axes = (place.far, place.second, place.first)
    for r in range(1, layers):
        used = tuple(a for b, a in enumerate(axes) if r >> (2 - b) & 1)
        got.append(swap(sent[r], *used))
    kept, update = placing(
        place, owner_map, got, wide, layers // n_own + 1, narrow // n_own
    )
    return (jnp.swapaxes(kept, 1, 2), jnp.swapaxes(update, 1, 2))


def solution(mesh):
    n_dp, n_own = mesh.shape["dp"], mesh.shape["own"]
    dp_names = tuple(f"dp{i}" for i in range(int(np.log2(n_dp))))
    own_names = tuple(f"own{i}" for i in range(int(np.log2(n_own))))
    names = dp_names + own_names
    bits = jax.sharding.Mesh(mesh.devices.reshape((2,) * len(names)), names)
    in_specs = (P(None, names, None), P(None, names, None), P())
    out_specs = (P(own_names, None, dp_names), P(None, own_names, dp_names))
    return jax.shard_map(
        functools.partial(on_device, Place(dp_names, own_names)),
        mesh=bits,
        in_specs=in_specs,
        out_specs=out_specs,
        check_vma=False,
    )
```

```python
import functools

import jax
import jax.numpy as jnp
import numpy as np
from jax import lax
from jax.experimental import pallas as pl
from jax.experimental.pallas import tpu as pltpu
from jax.sharding import PartitionSpec as P

DAMP = 0.5
LANES = 128
PANEL = 8
VMEM_LIMIT = 48 * 1024 * 1024
HIGHEST = lax.Precision.HIGHEST
VMEM = pl.BlockSpec(memory_space=pltpu.VMEM)
SMEM = pl.BlockSpec(memory_space=pltpu.SMEM)
HBM = pl.BlockSpec(memory_space=pltpu.HBM)
PARAMS = pltpu.CompilerParams(vmem_limit_bytes=VMEM_LIMIT)


class Place:
    def __init__(self, dp_names, own_names):
        self.dp, self.own = dp_names, own_names
        self.core, self.second, self.near, self.far = (
            dp_names[-1],
            dp_names[-2],
            dp_names[1],
            dp_names[0],
        )
        self.first = own_names[-1]
        used = (self.core, self.second, self.near, self.far, self.first)
        self.extra = tuple(n for n in dp_names + own_names if n not in used)

    def index(self, names):
        value = jnp.int32(0)
        for name in names:
            value = value * 2 + lax.axis_index(name)
        return value

    def layer(self):
        return self.index((self.far, self.second, self.first))

    def quarter(self):
        return self.index((self.core, self.near))


def transposed_dot(a, b, precision=None):
    return lax.dot_general(
        a, b, (((0,), (0,)), ((), ())), precision=precision, preferred_element_type=jnp.float32
    )


def read_layers(place, sources, buffers, sems):
    layer = place.layer()
    copies = []
    for i in range(buffers[0].shape[0]):
        group = [
            pltpu.make_async_copy(
                source.at[jnp.bitwise_xor(layer, i)], buffer.at[i], sems.at[i, s]
            )
            for s, (source, buffer) in enumerate(zip(sources, buffers))
        ]
        for copy in group:
            copy.start()
        copies.append(group)
    return copies


def write_quarters(place, i, flat, keep_ref, send_ref):
    rows = keep_ref.shape[3]
    quarter = place.quarter()
    for q in range(2):
        kept = pl.multiple_of(jnp.bitwise_xor(quarter, q) * rows, PANEL)
        sent = pl.multiple_of(jnp.bitwise_xor(quarter, 2 + q) * rows, PANEL)
        keep_ref[i % 4, i // 4, q] = flat[i, pl.ds(kept, rows), :]
        send_ref[i % 4, i // 4, q] = flat[i, pl.ds(sent, rows), :]


def iotas(shape):
    return (
        lax.broadcasted_iota(jnp.int32, shape, 0),
        lax.broadcasted_iota(jnp.int32, shape, 1),
    )


def pack_squares(flat, i, first, corner, second, narrow):
    n = LANES
    row, col = iotas((n, n))
    flat[i, :n] = jnp.where(row >= col, first, second)
    flat[i, n : 2 * n] = corner
    h = n // 2
    row_h, col_h = iotas((h, n))
    lower = pltpu.roll(narrow[h:], h, 1)
    flat[i, 2 * n : 2 * n + h] = jnp.where(
        (col_h >= h) | (row_h >= col_h), narrow[:h], lower
    )
    diagonal = row == col
    pair = [
        jnp.sum(jnp.where(diagonal, block, 0.0), axis=0, keepdims=True)
        for block in (second, narrow)
    ]
    row_p, _ = iotas((PANEL, n))
    shape = (PANEL, n)
    base = 2 * n + h
    flat[i, base : base + PANEL] = jnp.where(
        row_p == 0,
        jnp.broadcast_to(pair[0], shape),
        jnp.where(row_p == 1, jnp.broadcast_to(pair[1], shape), 0.0),
    )
    pad = flat.shape[1] - base - PANEL
    flat[i, base + PANEL :] = jnp.zeros((pad, n), jnp.float32)


def unpack_squares(flat):
    n = LANES
    h = n // 2
    row, col = iotas((n, n))
    packed = flat[:n]
    turned = packed.T
    corner = flat[n : 2 * n]
    folded = jnp.concatenate([flat[2 * n : 2 * n + h], jnp.zeros((h, n), jnp.float32)], axis=0)
    slab = flat[2 * n + h : 2 * n + h + PANEL]
    second_diagonal = jnp.broadcast_to(slab[0:1], (n, n))
    narrow_diagonal = jnp.broadcast_to(slab[1:2], (n, n))
    first = jnp.where(row >= col, packed, turned)
    second = jnp.where(col > row, packed, turned)
    second = jnp.where(row == col, second_diagonal, second)
    folded_t = folded.T
    top = jnp.where((col >= h) | (col <= row), folded, folded_t)
    moved = pltpu.roll(pltpu.roll(folded, h, 0), h, 1)
    moved_t = pltpu.roll(pltpu.roll(folded_t, h, 0), h, 1)
    corner_n = jnp.where(col > row, moved, moved_t)
    corner_n = jnp.where(row == col, narrow_diagonal, corner_n)
    bottom = jnp.where(col < h, folded_t, corner_n)
    return (first, corner, second, jnp.where(row < h, top, bottom))


def squares_kernel(place, wide_hbm, narrow_hbm, keep_ref, send_ref, wides, narrows, flat, sems):
    copies = read_layers(place, (wide_hbm, narrow_hbm), (wides, narrows), sems)
    for i, group in enumerate(copies):
        for copy in group:
            copy.wait()
        wide = wides[i]
        narrow = narrows[i]
        wcov = transposed_dot(wide, wide)
        ncov = transposed_dot(narrow, narrow)
        n = LANES
        pack_squares(flat, i, wcov[:n, :n], wcov[:n, n:], wcov[n:, n:], ncov)
        write_quarters(place, i, flat, keep_ref, send_ref)


def mixed_kernel(place, wide_hbm, narrow_hbm, out_ref, wides, narrows, sems):
    copies = read_layers(place, (wide_hbm, narrow_hbm), (wides, narrows), sems)
    rows = out_ref.shape[5]
    layer = place.layer()
    for i, group in enumerate(copies):
        for copy in group:
            copy.wait()
        mixed = transposed_dot(narrows[i], wides[i])
        here = jnp.bitwise_xor(layer, i)
        for q in range(4):
            core, near = q // 2, q % 2
            part = mixed[near * rows : (near + 1) * rows, core * LANES : (core + 1) * LANES]
            out_ref[here // 4, near, (here // 2) % 2, core, here % 2] = part


def gram(kernel, name, place, out_shapes, extra_scratch, wide_rows, narrow_rows):
    layers = wide_rows.shape[0]
    macs = wide_rows.shape[1] * wide_rows.shape[2] * 256
    return pl.pallas_call(
        functools.partial(kernel, place),
        in_specs=[HBM, HBM],
        out_specs=[VMEM] * len(out_shapes),
        out_shape=[jax.ShapeDtypeStruct(shape, jnp.float32) for shape in out_shapes],
        scratch_shapes=[
            pltpu.VMEM(wide_rows.shape, wide_rows.dtype),
            pltpu.VMEM(narrow_rows.shape, narrow_rows.dtype),
            *extra_scratch,
            pltpu.SemaphoreType.DMA((layers, 2)),
        ],
        cost_estimate=pl.CostEstimate(
            flops=2 * layers * macs, bytes_accessed=2 * wide_rows.size * 2, transcendentals=0
        ),
        compiler_params=PARAMS,
        name=name,
    )(
        pltpu.with_memory_space_constraint(wide_rows, pltpu.HBM),
        pltpu.with_memory_space_constraint(narrow_rows, pltpu.HBM),
    )


def lane_gather(x, index):
    return jnp.take_along_axis(x, index, axis=1, mode="promise_in_bounds")


def trailing_update(a_ref, left_ref, right_ref, base):
    size = a_ref.shape[1]
    a_ref[pl.ds(pl.multiple_of(base, PANEL), PANEL), :] = jnp.zeros((PANEL, size), jnp.float32)
    lane = lax.broadcasted_iota(jnp.int32, (1, size), 1)
    swept = (lane >= base - PANEL) & (lane < base)
    update = transposed_dot(left_ref[...], right_ref[...])
    a_ref[PANEL : PANEL + size, :] = (
        jnp.where(swept, 0.0, a_ref[PANEL : PANEL + size, :]) - update
    )


def sweep_panel(a_ref, left_ref, right_ref, tile, step, panel):
    size = a_ref.shape[1]
    tiles = size // LANES
    first = step * PANEL
    base = tile * LANES + first
    trailing_update(a_ref, left_ref, right_ref, base)

    shape = (PANEL, LANES)
    sub = lax.broadcasted_iota(jnp.int32, shape, 0)
    lane = lax.broadcasted_iota(jnp.int32, shape, 1)
    parts = [panel[:, LANES * t : LANES * (t + 1)] for t in range(tiles)]
    rows = [
        [jnp.broadcast_to(part[k : k + 1, :], shape) for part in parts] for k in range(PANEL)
    ]
    index = [jnp.full(shape, 0, jnp.int32) + (first + i) for i in range(PANEL)]
    d = [[None] * PANEL for _ in range(PANEL)]
    for j in range(PANEL):
        for i in range(j, PANEL):
            d[i][j] = lane_gather(rows[j][tile], index[i])
    own = (lane >= first) & (lane < first + PANEL)
    q = [[None] * tiles for _ in range(PANEL)]
    factor = [[None] * PANEL for _ in range(PANEL)]
    for k in range(PANEL):
        scale = lax.rsqrt(d[k][k])
        for i in range(k + 1, PANEL):
            factor[i][k] = d[i][k] * scale
        for i in range(k + 1, PANEL):
            for j in range(k + 1, i + 1):
                d[i][j] = d[i][j] - factor[i][k] * factor[j][k]
        for t in range(tiles):
            value = rows[k][t]
            if t == tile:
                value = jnp.where(own, jnp.where(lane == first + k, -1.0, 0.0), value)
            for j in range(k):
                value = value - factor[k][j] * q[j][t]
            q[k][t] = value * scale

    packed = []
    for t in range(tiles):
        value = q[0][t]
        for k in range(1, PANEL):
            value = jnp.where(sub == k, q[k][t], value)
        packed.append(value)
    whole = jnp.concatenate(packed, axis=1) if tiles > 1 else packed[0]
    high = whole.astype(jnp.bfloat16).astype(jnp.float32)
    rest = whole - high
    middle = rest.astype(jnp.bfloat16).astype(jnp.float32)
    low = rest - middle
    left = jnp.concatenate([high, high, middle, middle, high, low], axis=0)
    right = jnp.concatenate([high, middle, high, middle, low, high], axis=0)
    left_ref[...] = left.astype(jnp.bfloat16)
    right_ref[...] = right.astype(jnp.bfloat16)

    after = pl.multiple_of(base + 2 * PANEL, PANEL)
    following = a_ref[pl.ds(after, PANEL), :]
    last = first == LANES - PANEL
    next_lane = jnp.where(last, 0, first + PANEL) + sub
    weights = []
    for k in range(PANEL):
        source = q[k][tile]
        if tile + 1 < tiles:
            source = jnp.where(last, q[k][tile + 1], source)
        weights.append(lane_gather(source, next_lane))
    result = []
    for t in range(tiles):
        value = following[:, LANES * t : LANES * (t + 1)]
        if t == tile:
            value = jnp.where(own, 0.0, value)
        terms = [weights[k] * q[k][t] for k in range(PANEL)]
        while len(terms) > 1:
            terms = [terms[i] + terms[i + 1] for i in range(0, len(terms), 2)]
        result.append(value - terms[0])
    return jnp.concatenate(result, axis=1) if tiles > 1 else result[0]


def place_pieces(place, flat, pieces):
    quarter = place.quarter()
    rows = pieces[0].shape[0]
    for r, piece in enumerate(pieces):
        start = pl.multiple_of(jnp.bitwise_xor(quarter, r) * rows, PANEL)
        flat[pl.ds(start, rows), :] = piece[...]


def first_half_kernel(place, total, *refs):
    pieces, refs = refs[:4], refs[4:]
    ninv_ref, wa, wl, wr, panel_ref, flat, na, nl, nr = refs
    place_pieces(place, flat, pieces)
    wide, narrow = wa.shape[1], na.shape[1]
    half = LANES
    first, corner, second, square = unpack_squares(flat)
    row, col = iotas((half, half))
    damp = jnp.where(row == col, DAMP, 0.0)
    wa[:PANEL] = jnp.zeros((PANEL, wide), jnp.float32)
    wa[PANEL + wide :] = jnp.zeros((PANEL, wide), jnp.float32)
    na[:PANEL] = jnp.zeros((PANEL, narrow), jnp.float32)
    na[PANEL + narrow :] = jnp.zeros((PANEL, narrow), jnp.float32)
    corner = corner / total
    wa[PANEL : PANEL + half, :half] = first / total + damp
    wa[PANEL : PANEL + half, half:] = corner
    wa[PANEL + half : PANEL + wide, :half] = corner.T
    wa[PANEL + half : PANEL + wide, half:] = second / total + damp
    na[PANEL : PANEL + narrow, :] = square / total + damp
    for ref in (wl, wr, nl, nr):
        ref[...] = jnp.zeros(ref.shape, ref.dtype)

    def both(step, carry):
        wide_panel, narrow_panel = carry
        wide_panel = sweep_panel(wa, wl, wr, 0, step, wide_panel)
        narrow_panel = sweep_panel(na, nl, nr, 0, step, narrow_panel)
        return (wide_panel, narrow_panel)

    start = (wa[PANEL : 2 * PANEL, :], na[PANEL : 2 * PANEL, :])
    panel, _ = lax.fori_loop(0, LANES // PANEL, both, start)
    panel_ref[...] = panel
    trailing_update(na, nl, nr, narrow)
    ninv_ref[...] = -na[PANEL : PANEL + narrow, :]


def second_half_kernel(wa_in, wl_in, wr_in, panel_ref, winv_ref, wa, wl, wr):
    wide = wa.shape[1]
    wa[...] = wa_in[...]
    wl[...] = wl_in[...]
    wr[...] = wr_in[...]

    def only(step, panel):
        return sweep_panel(wa, wl, wr, 1, step, panel)

    lax.fori_loop(0, LANES // PANEL, only, panel_ref[...])
    trailing_update(wa, wl, wr, wide)
    winv_ref[...] = -wa[PANEL : PANEL + wide, :]


def sweep_cost(wide):
    return pl.CostEstimate(
        flops=64 * wide * wide * wide, bytes_accessed=16 * wide * wide, transcendentals=0
    )


def first_half(place, pieces, wide, narrow, total):
    splits = 6 * PANEL
    rows = pieces[0].shape[0]
    matrix = (wide + 2 * PANEL, wide)
    return pl.pallas_call(
        functools.partial(first_half_kernel, place, total),
        in_specs=[VMEM] * 4,
        out_specs=[VMEM] * 5,
        out_shape=[
            jax.ShapeDtypeStruct((narrow, narrow), jnp.float32),
            jax.ShapeDtypeStruct(matrix, jnp.float32),
            jax.ShapeDtypeStruct((splits, wide), jnp.bfloat16),
            jax.ShapeDtypeStruct((splits, wide), jnp.bfloat16),
            jax.ShapeDtypeStruct((PANEL, wide), jnp.float32),
        ],
        scratch_shapes=[
            pltpu.VMEM((4 * rows, LANES), jnp.float32),
            pltpu.VMEM((narrow + 2 * PANEL, narrow), jnp.float32),
            pltpu.VMEM((splits, narrow), jnp.bfloat16),
            pltpu.VMEM((splits, narrow), jnp.bfloat16),
        ],
        cost_estimate=sweep_cost(wide),
        compiler_params=PARAMS,
        name="first_half",
    )(*pieces)


def second_half(wa, wl, wr, panel):
    wide = wa.shape[1]
    return pl.pallas_call(
        second_half_kernel,
        in_specs=[VMEM] * 4,
        out_specs=VMEM,
        out_shape=jax.ShapeDtypeStruct((wide, wide), jnp.float32),
        scratch_shapes=[
            pltpu.VMEM(wa.shape, wa.dtype),
            pltpu.VMEM(wl.shape, wl.dtype),
            pltpu.VMEM(wr.shape, wr.dtype),
        ],
        cost_estimate=sweep_cost(wide),
        compiler_params=PARAMS,
        name="second_half",
    )(wa, wl, wr, panel)


def aligned_rows(ref, index, count):
    if count % PANEL == 0:
        return ref[pl.ds(pl.multiple_of(index * count, count), count), :]
    per_slab = PANEL // count
    slab = ref[pl.ds(pl.multiple_of(index // per_slab * PANEL, PANEL), PANEL), :]
    value = slab[:count]
    for i in range(1, per_slab):
        value = jnp.where(index % per_slab == i, slab[i * count : (i + 1) * count], value)
    return value


def packs(cols, rows):
    return cols == 2 * PANEL and 2 * rows == LANES


def product_kernel(place, total, rows, winv_ref, ninv_ref, mixed_ref, out_ref):
    ninv = ninv_ref[...]
    half = mixed_ref.shape[0]
    inner = jnp.concatenate(
        [
            transposed_dot(
                jnp.concatenate([mixed_ref[n, c] for n in range(half)], axis=0) / total,
                ninv,
                HIGHEST,
            )
            for c in range(2)
        ],
        axis=0,
    )
    wide = winv_ref.shape[1]
    cols = wide // 2 ** len(place.dp)
    far, second = lax.axis_index(place.far), lax.axis_index(place.second)
    far_stride = 2 ** (len(place.dp) - 1)
    base = place.index(place.dp) - far * far_stride - second * 2
    _, lane = iotas((PANEL, LANES))
    for j in range(4):
        index = base + (j // 2) * far_stride + (j % 2) * 2
        picked = aligned_rows(winv_ref, index, cols)
        update = lax.dot_general(
            picked,
            inner,
            (((1,), (0,)), ((), ())),
            precision=HIGHEST,
            preferred_element_type=jnp.float32,
        )
        for x in range(2):
            block = 2 * j + x
            out_ref[block, :cols] = picked[:, :LANES]
            out_ref[block, cols : 2 * cols] = picked[:, LANES:]
            if packs(cols, rows):
                upper, lower = update[:PANEL], update[PANEL:]
                if x == 0:
                    lower = pltpu.roll(lower, rows, 1)
                else:
                    upper = pltpu.roll(upper, rows, 1)
                out_ref[block, 2 * cols :] = jnp.where(lane < rows, upper, lower)
            else:
                out_ref[block, 2 * cols :] = update


def products(place, winv, ninv, mixed, cols, rows, total):
    height = 2 * cols + (PANEL if packs(cols, rows) else cols)
    return pl.pallas_call(
        functools.partial(product_kernel, place, total, rows),
        in_specs=[VMEM] * 3,
        out_specs=VMEM,
        out_shape=jax.ShapeDtypeStruct((8, height, LANES), jnp.float32),
        compiler_params=PARAMS,
        name="products",
    )(winv, ninv, mixed)


def placing_kernel(place, owner_map, got_ref, kept_ref, update_ref):
    layers = got_ref.shape[0]
    slots, cols, wide = kept_ref.shape
    rows = update_ref.shape[2]
    own, dp = place.index(place.own), place.index(place.dp)
    row, col = iotas((cols, wide))
    empty = jnp.where(col == row + dp * cols, 1.0 / DAMP, 0.0)
    count = jnp.int32(0)
    slot = []
    for l in range(layers):
        mine = owner_map[l] == own
        slot.append(jnp.where(mine, count, -1))
        count = count + mine.astype(jnp.int32)
    for h in range(2):
        lanes = slice(h * LANES, (h + 1) * LANES)
        for c in range(slots):
            value = empty[:, lanes]
            for l in range(layers):
                value = jnp.where(slot[l] == c, got_ref[l, h * cols : (h + 1) * cols], value)
            kept_ref[c, :, lanes] = value
    for l in range(layers):
        value = got_ref[l, 2 * cols :]
        if packs(cols, rows):
            update_ref[l, :PANEL] = value[:, :rows]
            update_ref[l, PANEL:] = value[:, rows:]
        else:
            part = value[:, :rows]
            for p in range(1, LANES // rows):
                part = jnp.where(own == p, value[:, p * rows : (p + 1) * rows], part)
            update_ref[l] = part


def placing(place, owner_map, got, wide, cols, slots, rows):
    layers = got.shape[0]
    return pl.pallas_call(
        functools.partial(placing_kernel, place),
        in_specs=[SMEM, VMEM],
        out_specs=[VMEM, VMEM],
        out_shape=[
            jax.ShapeDtypeStruct((slots, cols, wide), jnp.float32),
            jax.ShapeDtypeStruct((layers, cols, rows), jnp.float32),
        ],
        compiler_params=PARAMS,
        name="placing",
    )(owner_map, got)


def swap(value, *axes):
    count = 2 ** len(axes)
    name = axes if len(axes) > 1 else axes[0]
    return lax.ppermute(value, name, [(i, count - 1 - i) for i in range(count)])


def swap_parts(parts, high, low):
    return [swap(parts[1], low), swap(parts[2], high), swap(parts[3], high, low)]


def add_parts(part, got):
    return (part + got[0]) + (got[1] + got[2])


def after(value, *others):
    return lax.optimization_barrier((value,) + others)[0]


def on_device(place, wide_rows, narrow_rows, owner_map):
    layers, rows, wide = wide_rows.shape
    narrow = narrow_rows.shape[2]
    n_dp, n_own = 2 ** len(place.dp), 2 ** len(place.own)
    total = float(rows * n_dp * n_own)

    quarter = 88
    split = (4, 2, 2, quarter, LANES)
    s_keep, s_send = gram(
        squares_kernel,
        "squares",
        place,
        [split, split],
        [pltpu.VMEM((layers, 4 * quarter, LANES), jnp.float32)],
        wide_rows,
        narrow_rows,
    )
    s_got = swap(s_send, place.core)
    group = (place.far, place.near, place.second, place.core, place.first)
    (m,) = gram(
        mixed_kernel,
        "mixed",
        place,
        [(2, 2, 2, 2, 2, narrow // 2, LANES)],
        [],
        after(wide_rows, s_send),
        narrow_rows,
    )
    s_keep, m = lax.optimization_barrier((s_keep, m))
    m = m.reshape((-1,) + m.shape[5:])
    m = lax.psum_scatter(m, group, scatter_dimension=0, tiled=True)
    if place.extra:
        m = lax.psum(m, place.extra)
    m = lax.all_gather(m[0], (place.near, place.core))
    m = m.reshape((2, 2) + m.shape[1:])

    s = s_keep + s_got
    s_got = swap_parts(s, place.second, place.first)
    s = add_parts(s[0], s_got).reshape((4,) + s.shape[3:])
    s_got = swap_parts(s, place.far, place.near)
    s = add_parts(s[0], s_got)
    if place.extra:
        s = lax.psum(s, place.extra)
    pieces = [
        s,
        swap(s, place.near),
        swap(s, place.core),
        swap(s, place.near, place.core),
    ]
    ninv, wa, wl, wr, panel = first_half(place, pieces, wide, narrow, total)
    winv = second_half(wa, wl, wr, panel)
    cols, own_rows = wide // n_dp, narrow // n_own
    sent = products(place, winv, ninv, m, cols, own_rows, total)
    got = lax.all_to_all(sent, (place.far, place.second, place.first), 0, 0)
    kept, update = placing(
        place, owner_map, got, wide, cols, layers // n_own + 1, own_rows
    )
    return (jnp.swapaxes(kept, 1, 2), jnp.swapaxes(update, 1, 2))


def solution(mesh):
    n_dp, n_own = mesh.shape["dp"], mesh.shape["own"]
    dp_names = tuple(f"dp{i}" for i in range(int(np.log2(n_dp))))
    own_names = tuple(f"own{i}" for i in range(int(np.log2(n_own))))
    names = dp_names + own_names
    bits = jax.sharding.Mesh(mesh.devices.reshape((2,) * len(names)), names)
    in_specs = (P(None, names, None), P(None, names, None), P())
    out_specs = (P(own_names, None, dp_names), P(None, own_names, dp_names))
    return jax.shard_map(
        functools.partial(on_device, Place(dp_names, own_names)),
        mesh=bits,
        in_specs=in_specs,
        out_specs=out_specs,
        check_vma=False,
    )
```

```python
import functools

import jax
import jax.numpy as jnp
import numpy as np
from jax import lax
from jax.experimental import pallas as pl
from jax.experimental.pallas import tpu as pltpu
from jax.sharding import PartitionSpec as P

DAMP = 0.5
LANES = 128
PANEL = 8
VMEM_LIMIT = 48 * 1024 * 1024
HIGHEST = lax.Precision.HIGHEST
VMEM = pl.BlockSpec(memory_space=pltpu.VMEM)
SMEM = pl.BlockSpec(memory_space=pltpu.SMEM)
HBM = pl.BlockSpec(memory_space=pltpu.HBM)
PARAMS = pltpu.CompilerParams(vmem_limit_bytes=VMEM_LIMIT)


class Place:
    def __init__(self, dp_names, own_names):
        self.dp, self.own = dp_names, own_names
        self.core, self.second, self.near, self.far = (
            dp_names[-1],
            dp_names[-2],
            dp_names[1],
            dp_names[0],
        )
        self.first = own_names[-1]
        used = (self.core, self.second, self.near, self.far, self.first)
        self.extra = tuple(n for n in dp_names + own_names if n not in used)

    def index(self, names):
        value = jnp.int32(0)
        for name in names:
            value = value * 2 + lax.axis_index(name)
        return value

    def layer(self):
        return self.index((self.far, self.second, self.first))

    def quarter(self):
        return self.index((self.core, self.near))


def transposed_dot(a, b, precision=None):
    return lax.dot_general(
        a, b, (((0,), (0,)), ((), ())), precision=precision, preferred_element_type=jnp.float32
    )


def read_layers(place, sources, buffers, sems):
    layer = place.layer()
    copies = []
    for i in range(buffers[0].shape[0]):
        group = [
            pltpu.make_async_copy(
                source.at[jnp.bitwise_xor(layer, i)], buffer.at[i], sems.at[i, s]
            )
            for s, (source, buffer) in enumerate(zip(sources, buffers))
        ]
        for copy in group:
            copy.start()
        copies.append(group)
    return copies


def write_halves(place, i, flat, keep_ref, send_ref):
    rows = keep_ref.shape[2]
    core = lax.axis_index(place.core)
    z, y, x = i // 4, (i // 2) % 2, i % 2
    mine = jnp.where(core == 0, x * 2 + y, y * 2 + x)
    other = jnp.where(core == 0, y * 2 + x, x * 2 + y)
    kept = pl.multiple_of(core * rows, PANEL)
    sent = pl.multiple_of((1 - core) * rows, PANEL)
    keep_ref[mine, z] = flat[i, pl.ds(kept, rows), :]
    send_ref[other, z] = flat[i, pl.ds(sent, rows), :]


def iotas(shape):
    return (
        lax.broadcasted_iota(jnp.int32, shape, 0),
        lax.broadcasted_iota(jnp.int32, shape, 1),
    )


def pack_squares(flat, i, first, corner, second, narrow):
    n = LANES
    row, col = iotas((n, n))
    flat[i, :n] = jnp.where(row >= col, first, second)
    flat[i, n : 2 * n] = corner
    h = n // 2
    row_h, col_h = iotas((h, n))
    lower = pltpu.roll(narrow[h:], h, 1)
    flat[i, 2 * n : 2 * n + h] = jnp.where(
        (col_h >= h) | (row_h >= col_h), narrow[:h], lower
    )
    diagonal = row == col
    pair = [
        jnp.sum(jnp.where(diagonal, block, 0.0), axis=0, keepdims=True)
        for block in (second, narrow)
    ]
    row_p, _ = iotas((PANEL, n))
    shape = (PANEL, n)
    base = 2 * n + h
    flat[i, base : base + PANEL] = jnp.where(
        row_p == 0,
        jnp.broadcast_to(pair[0], shape),
        jnp.where(row_p == 1, jnp.broadcast_to(pair[1], shape), 0.0),
    )
    pad = flat.shape[1] - base - PANEL
    flat[i, base + PANEL :] = jnp.zeros((pad, n), jnp.float32)


def unpack_squares(flat):
    n = LANES
    h = n // 2
    row, col = iotas((n, n))
    packed = flat[:n]
    turned = packed.T
    corner = flat[n : 2 * n]
    folded = jnp.concatenate([flat[2 * n : 2 * n + h], jnp.zeros((h, n), jnp.float32)], axis=0)
    slab = flat[2 * n + h : 2 * n + h + PANEL]
    second_diagonal = jnp.broadcast_to(slab[0:1], (n, n))
    narrow_diagonal = jnp.broadcast_to(slab[1:2], (n, n))
    first = jnp.where(row >= col, packed, turned)
    second = jnp.where(col > row, packed, turned)
    second = jnp.where(row == col, second_diagonal, second)
    folded_t = folded.T
    top = jnp.where((col >= h) | (col <= row), folded, folded_t)
    moved = pltpu.roll(pltpu.roll(folded, h, 0), h, 1)
    moved_t = pltpu.roll(pltpu.roll(folded_t, h, 0), h, 1)
    corner_n = jnp.where(col > row, moved, moved_t)
    corner_n = jnp.where(row == col, narrow_diagonal, corner_n)
    bottom = jnp.where(col < h, folded_t, corner_n)
    return (first, corner, second, jnp.where(row < h, top, bottom))


def squares_kernel(place, wide_hbm, narrow_hbm, keep_ref, send_ref, wides, narrows, flat, sems):
    copies = read_layers(place, (wide_hbm, narrow_hbm), (wides, narrows), sems)
    n = LANES
    for i, group in enumerate(copies):
        for copy in group:
            copy.wait()
        wide = wides[i]
        narrow = narrows[i]
        wcov = transposed_dot(wide, wide)
        ncov = transposed_dot(narrow, narrow)
        pack_squares(flat, i, wcov[:n, :n], wcov[:n, n:], wcov[n:, n:], ncov)
        write_halves(place, i, flat, keep_ref, send_ref)


def mixed_kernel(place, wides, narrows, keep_ref, send_ref, flat):
    for i in range(wides.shape[0]):
        mixed = transposed_dot(narrows[i], wides[i])
        flat[i, :LANES] = mixed[:, :LANES]
        flat[i, LANES:] = mixed[:, LANES:]
        write_halves(place, i, flat, keep_ref, send_ref)


def gram_cost(wide_rows, columns):
    return pl.CostEstimate(
        flops=2 * wide_rows.size * columns, bytes_accessed=2 * wide_rows.size, transcendentals=0
    )


def squares(place, wide_rows, narrow_rows):
    layers = wide_rows.shape[0]
    half = 176
    shape = jax.ShapeDtypeStruct((4, 2, half, LANES), jnp.float32)
    return pl.pallas_call(
        functools.partial(squares_kernel, place),
        in_specs=[HBM, HBM],
        out_specs=[VMEM] * 4,
        out_shape=[
            shape,
            shape,
            jax.ShapeDtypeStruct(wide_rows.shape, wide_rows.dtype),
            jax.ShapeDtypeStruct(narrow_rows.shape, narrow_rows.dtype),
        ],
        scratch_shapes=[
            pltpu.VMEM((layers, 2 * half, LANES), jnp.float32),
            pltpu.SemaphoreType.DMA((layers, 2)),
        ],
        cost_estimate=gram_cost(wide_rows, 320),
        compiler_params=PARAMS,
        name="squares",
    )(
        pltpu.with_memory_space_constraint(wide_rows, pltpu.HBM),
        pltpu.with_memory_space_constraint(narrow_rows, pltpu.HBM),
    )


def mixed_sums(place, wides, narrows):
    layers, _, narrow = narrows.shape
    shape = jax.ShapeDtypeStruct((4, 2, narrow, LANES), jnp.float32)
    return pl.pallas_call(
        functools.partial(mixed_kernel, place),
        in_specs=[VMEM, VMEM],
        out_specs=[VMEM, VMEM],
        out_shape=[shape, shape],
        scratch_shapes=[pltpu.VMEM((layers, 2 * narrow, LANES), jnp.float32)],
        cost_estimate=gram_cost(wides, 128),
        compiler_params=PARAMS,
        name="mixed",
    )(wides, narrows)


def lane_gather(x, index):
    return jnp.take_along_axis(x, index, axis=1, mode="promise_in_bounds")


def trailing_update(a_ref, left_ref, right_ref, base):
    size = a_ref.shape[1]
    a_ref[pl.ds(pl.multiple_of(base, PANEL), PANEL), :] = jnp.zeros((PANEL, size), jnp.float32)
    lane = lax.broadcasted_iota(jnp.int32, (1, size), 1)
    swept = (lane >= base - PANEL) & (lane < base)
    update = transposed_dot(left_ref[...], right_ref[...])
    a_ref[PANEL : PANEL + size, :] = (
        jnp.where(swept, 0.0, a_ref[PANEL : PANEL + size, :]) - update
    )


def sweep_panel(a_ref, left_ref, right_ref, tile, step, panel):
    size = a_ref.shape[1]
    tiles = size // LANES
    first = step * PANEL
    base = tile * LANES + first
    trailing_update(a_ref, left_ref, right_ref, base)

    shape = (PANEL, LANES)
    sub = lax.broadcasted_iota(jnp.int32, shape, 0)
    lane = lax.broadcasted_iota(jnp.int32, shape, 1)
    parts = [panel[:, LANES * t : LANES * (t + 1)] for t in range(tiles)]
    rows = [
        [jnp.broadcast_to(part[k : k + 1, :], shape) for part in parts] for k in range(PANEL)
    ]
    index = [jnp.full(shape, 0, jnp.int32) + (first + i) for i in range(PANEL)]
    d = [[None] * PANEL for _ in range(PANEL)]
    for j in range(PANEL):
        for i in range(j, PANEL):
            d[i][j] = lane_gather(rows[j][tile], index[i])
    own = (lane >= first) & (lane < first + PANEL)
    q = [[None] * tiles for _ in range(PANEL)]
    factor = [[None] * PANEL for _ in range(PANEL)]
    for k in range(PANEL):
        scale = lax.rsqrt(d[k][k])
        for i in range(k + 1, PANEL):
            factor[i][k] = d[i][k] * scale
        for i in range(k + 1, PANEL):
            for j in range(k + 1, i + 1):
                d[i][j] = d[i][j] - factor[i][k] * factor[j][k]
        for t in range(tiles):
            value = rows[k][t]
            if t == tile:
                value = jnp.where(own, jnp.where(lane == first + k, -1.0, 0.0), value)
            for j in range(k):
                value = value - factor[k][j] * q[j][t]
            q[k][t] = value * scale

    packed = []
    for t in range(tiles):
        value = q[0][t]
        for k in range(1, PANEL):
            value = jnp.where(sub == k, q[k][t], value)
        packed.append(value)
    whole = jnp.concatenate(packed, axis=1) if tiles > 1 else packed[0]
    high = whole.astype(jnp.bfloat16).astype(jnp.float32)
    rest = whole - high
    middle = rest.astype(jnp.bfloat16).astype(jnp.float32)
    low = rest - middle
    left = jnp.concatenate([high, high, middle, middle, high, low], axis=0)
    right = jnp.concatenate([high, middle, high, middle, low, high], axis=0)
    left_ref[...] = left.astype(jnp.bfloat16)
    right_ref[...] = right.astype(jnp.bfloat16)

    after = pl.multiple_of(base + 2 * PANEL, PANEL)
    following = a_ref[pl.ds(after, PANEL), :]
    last = first == LANES - PANEL
    next_lane = jnp.where(last, 0, first + PANEL) + sub
    weights = []
    for k in range(PANEL):
        source = q[k][tile]
        if tile + 1 < tiles:
            source = jnp.where(last, q[k][tile + 1], source)
        weights.append(lane_gather(source, next_lane))
    result = []
    for t in range(tiles):
        value = following[:, LANES * t : LANES * (t + 1)]
        if t == tile:
            value = jnp.where(own, 0.0, value)
        terms = [weights[k] * q[k][t] for k in range(PANEL)]
        while len(terms) > 1:
            terms = [terms[i] + terms[i + 1] for i in range(0, len(terms), 2)]
        result.append(value - terms[0])
    return jnp.concatenate(result, axis=1) if tiles > 1 else result[0]


def place_pieces(place, flat, pieces):
    core = lax.axis_index(place.core)
    rows = pieces[0].shape[0]
    for r, piece in enumerate(pieces):
        start = pl.multiple_of(jnp.bitwise_xor(core, r) * rows, PANEL)
        flat[pl.ds(start, rows), :] = piece[...]


def first_half_kernel(place, total, *refs):
    pieces, refs = refs[:2], refs[2:]
    ninv_ref, wa, wl, wr, panel_ref, flat, na, nl, nr = refs
    place_pieces(place, flat, pieces)
    wide, narrow = wa.shape[1], na.shape[1]
    half = LANES
    first, corner, second, square = unpack_squares(flat)
    row, col = iotas((half, half))
    damp = jnp.where(row == col, DAMP, 0.0)
    wa[:PANEL] = jnp.zeros((PANEL, wide), jnp.float32)
    wa[PANEL + wide :] = jnp.zeros((PANEL, wide), jnp.float32)
    na[:PANEL] = jnp.zeros((PANEL, narrow), jnp.float32)
    na[PANEL + narrow :] = jnp.zeros((PANEL, narrow), jnp.float32)
    corner = corner / total
    wa[PANEL : PANEL + half, :half] = first / total + damp
    wa[PANEL : PANEL + half, half:] = corner
    wa[PANEL + half : PANEL + wide, :half] = corner.T
    wa[PANEL + half : PANEL + wide, half:] = second / total + damp
    na[PANEL : PANEL + narrow, :] = square / total + damp
    for ref in (wl, wr, nl, nr):
        ref[...] = jnp.zeros(ref.shape, ref.dtype)

    def both(step, carry):
        wide_panel, narrow_panel = carry
        wide_panel = sweep_panel(wa, wl, wr, 0, step, wide_panel)
        narrow_panel = sweep_panel(na, nl, nr, 0, step, narrow_panel)
        return (wide_panel, narrow_panel)

    start = (wa[PANEL : 2 * PANEL, :], na[PANEL : 2 * PANEL, :])
    panel, _ = lax.fori_loop(0, LANES // PANEL, both, start)
    panel_ref[...] = panel
    trailing_update(na, nl, nr, narrow)
    ninv_ref[...] = -na[PANEL : PANEL + narrow, :]


def later_panels_kernel(begin, end, wa_in, wl_in, wr_in, panel_in, wa, wl, wr, panel_out):
    wa[...] = wa_in[...]
    wl[...] = wl_in[...]
    wr[...] = wr_in[...]

    def only(step, panel):
        return sweep_panel(wa, wl, wr, 1, step, panel)

    panel_out[...] = lax.fori_loop(begin, end, only, panel_in[...])


def last_panels_kernel(begin, wa_in, wl_in, wr_in, panel_in, winv_ref, wa, wl, wr, panel):
    later_panels_kernel(
        begin, LANES // PANEL, wa_in, wl_in, wr_in, panel_in, wa, wl, wr, panel
    )
    wide = wa.shape[1]
    trailing_update(wa, wl, wr, wide)
    winv_ref[...] = -wa[PANEL : PANEL + wide, :]


def sweep_cost(wide):
    return pl.CostEstimate(
        flops=64 * wide * wide * wide, bytes_accessed=16 * wide * wide, transcendentals=0
    )


def first_half(place, pieces, wide, narrow, total):
    splits = 6 * PANEL
    rows = pieces[0].shape[0]
    matrix = (wide + 2 * PANEL, wide)
    return pl.pallas_call(
        functools.partial(first_half_kernel, place, total),
        in_specs=[VMEM] * 2,
        out_specs=[VMEM] * 5,
        out_shape=[
            jax.ShapeDtypeStruct((narrow, narrow), jnp.float32),
            jax.ShapeDtypeStruct(matrix, jnp.float32),
            jax.ShapeDtypeStruct((splits, wide), jnp.bfloat16),
            jax.ShapeDtypeStruct((splits, wide), jnp.bfloat16),
            jax.ShapeDtypeStruct((PANEL, wide), jnp.float32),
        ],
        scratch_shapes=[
            pltpu.VMEM((2 * rows, LANES), jnp.float32),
            pltpu.VMEM((narrow + 2 * PANEL, narrow), jnp.float32),
            pltpu.VMEM((splits, narrow), jnp.bfloat16),
            pltpu.VMEM((splits, narrow), jnp.bfloat16),
        ],
        cost_estimate=sweep_cost(wide),
        compiler_params=PARAMS,
        name="first_half",
    )(*pieces)


def later_panels(state, begin, end):
    return pl.pallas_call(
        functools.partial(later_panels_kernel, begin, end),
        in_specs=[VMEM] * 4,
        out_specs=[VMEM] * 4,
        out_shape=[jax.ShapeDtypeStruct(v.shape, v.dtype) for v in state],
        cost_estimate=sweep_cost(state[0].shape[1]),
        compiler_params=PARAMS,
        name="later_panels",
    )(*state)


def last_panels(state, begin):
    wide = state[0].shape[1]
    return pl.pallas_call(
        functools.partial(last_panels_kernel, begin),
        in_specs=[VMEM] * 4,
        out_specs=VMEM,
        out_shape=jax.ShapeDtypeStruct((wide, wide), jnp.float32),
        scratch_shapes=[pltpu.VMEM(v.shape, v.dtype) for v in state],
        cost_estimate=sweep_cost(wide),
        compiler_params=PARAMS,
        name="last_panels",
    )(*state)


def aligned_rows(ref, index, count):
    if count % PANEL == 0:
        return ref[pl.ds(pl.multiple_of(index * count, count), count), :]
    per_slab = PANEL // count
    slab = ref[pl.ds(pl.multiple_of(index // per_slab * PANEL, PANEL), PANEL), :]
    value = slab[:count]
    for i in range(1, per_slab):
        value = jnp.where(index % per_slab == i, slab[i * count : (i + 1) * count], value)
    return value


def packs(cols, rows):
    return cols == 2 * PANEL and 2 * rows == LANES


def product_kernel(place, total, rows, winv_ref, ninv_ref, mine_ref, other_ref, out_ref, flat):
    place_pieces(place, flat, (mine_ref, other_ref))
    ninv = ninv_ref[...]
    half = flat.shape[0] // 2
    inner = jnp.concatenate(
        [
            transposed_dot(flat[h * half : (h + 1) * half] / total, ninv, HIGHEST)
            for h in range(2)
        ],
        axis=0,
    )
    wide = winv_ref.shape[1]
    cols = wide // 2 ** len(place.dp)
    far, second = lax.axis_index(place.far), lax.axis_index(place.second)
    far_stride = 2 ** (len(place.dp) - 1)
    base = place.index(place.dp) - far * far_stride - second * 2
    _, lane = iotas((PANEL, LANES))
    for j in range(4):
        index = base + (j // 2) * far_stride + (j % 2) * 2
        picked = aligned_rows(winv_ref, index, cols)
        update = lax.dot_general(
            picked,
            inner,
            (((1,), (0,)), ((), ())),
            precision=HIGHEST,
            preferred_element_type=jnp.float32,
        )
        for x in range(2):
            block = 2 * j + x
            out_ref[block, :cols] = picked[:, :LANES]
            out_ref[block, cols : 2 * cols] = picked[:, LANES:]
            if packs(cols, rows):
                upper, lower = update[:PANEL], update[PANEL:]
                if x == 0:
                    lower = pltpu.roll(lower, rows, 1)
                else:
                    upper = pltpu.roll(upper, rows, 1)
                out_ref[block, 2 * cols :] = jnp.where(lane < rows, upper, lower)
            else:
                out_ref[block, 2 * cols :] = update


def products(place, winv, ninv, pieces, cols, rows, total):
    height = 2 * cols + (PANEL if packs(cols, rows) else cols)
    return pl.pallas_call(
        functools.partial(product_kernel, place, total, rows),
        in_specs=[VMEM] * 4,
        out_specs=VMEM,
        out_shape=jax.ShapeDtypeStruct((8, height, LANES), jnp.float32),
        scratch_shapes=[pltpu.VMEM((2 * ninv.shape[0], LANES), jnp.float32)],
        compiler_params=PARAMS,
        name="products",
    )(winv, ninv, *pieces)


def placing_kernel(place, owner_map, got_ref, kept_ref, update_ref):
    layers = got_ref.shape[0]
    slots, cols, wide = kept_ref.shape
    rows = update_ref.shape[2]
    own, dp = place.index(place.own), place.index(place.dp)
    row, col = iotas((cols, wide))
    empty = jnp.where(col == row + dp * cols, 1.0 / DAMP, 0.0)
    count = jnp.int32(0)
    slot = []
    for l in range(layers):
        mine = owner_map[l] == own
        slot.append(jnp.where(mine, count, -1))
        count = count + mine.astype(jnp.int32)
    for h in range(2):
        lanes = slice(h * LANES, (h + 1) * LANES)
        for c in range(slots):
            value = empty[:, lanes]
            for l in range(layers):
                value = jnp.where(slot[l] == c, got_ref[l, h * cols : (h + 1) * cols], value)
            kept_ref[c, :, lanes] = value
    for l in range(layers):
        value = got_ref[l, 2 * cols :]
        if packs(cols, rows):
            update_ref[l, :PANEL] = value[:, :rows]
            update_ref[l, PANEL:] = value[:, rows:]
        else:
            part = value[:, :rows]
            for p in range(1, LANES // rows):
                part = jnp.where(own == p, value[:, p * rows : (p + 1) * rows], part)
            update_ref[l] = part


def placing(place, owner_map, got, wide, cols, slots, rows):
    layers = got.shape[0]
    return pl.pallas_call(
        functools.partial(placing_kernel, place),
        in_specs=[SMEM, VMEM],
        out_specs=[VMEM, VMEM],
        out_shape=[
            jax.ShapeDtypeStruct((slots, cols, wide), jnp.float32),
            jax.ShapeDtypeStruct((layers, cols, rows), jnp.float32),
        ],
        compiler_params=PARAMS,
        name="placing",
    )(owner_map, got)


def swap(value, axis):
    return lax.ppermute(value, axis, [(0, 1), (1, 0)])


def swap_by_core(value, place, stage):
    pairs = []
    for y in range(2):
        for core in range(2):
            for x in range(2):
                flip = 1 if core == stage else 4
                here = y * 4 + core * 2 + x
                pairs.append((here, here ^ flip))
    return lax.ppermute(value, (place.second, place.core, place.first), pairs)


def after(value, *others):
    return lax.optimization_barrier((value,) + others)[0]


def on_device(place, wide_rows, narrow_rows, owner_map):
    layers, rows, wide = wide_rows.shape
    narrow = narrow_rows.shape[2]
    n_dp, n_own = 2 ** len(place.dp), 2 ** len(place.own)
    total = float(rows * n_dp * n_own)

    s_keep, s_send, wides, narrows = squares(place, wide_rows, narrow_rows)
    s_got = swap(s_send, place.core)
    m_keep, m_send = mixed_sums(place, after(wides, s_send), narrows)
    s_keep, m_send = lax.optimization_barrier((s_keep, m_send))

    s = s_keep + s_got
    s_got = swap_by_core(s[2:], place, 0)
    m_got = swap(after(m_send, s), place.core)

    s = s[:2] + s_got
    s_got = swap_by_core(s[1], place, 1)
    m = after(m_keep, s) + m_got
    m_got = swap_by_core(m[2:], place, 0)

    s = s[0] + s_got
    s_got = swap(s[1], place.far)
    m = after(m[:2], s) + m_got
    m_got = swap_by_core(m[1], place, 1)

    s = s[0] + s_got
    if place.extra:
        s = lax.psum(s, place.extra)
    s_got = swap(s, place.near)
    m = after(m[0], s) + m_got
    m_got = swap(m[1], place.far)

    s = s + s_got
    ninv, *state = first_half(place, [s, swap(s, place.core)], wide, narrow, total)
    m = after(m[0], state[0]) + m_got
    if place.extra:
        m = lax.psum(m, place.extra)
    m_got = swap(m, place.near)
    middle = LANES // PANEL // 2
    state = later_panels(state, 0, middle)
    m = after(m, state[0]) + m_got
    m_got = swap(m, place.core)
    winv = last_panels(state, middle)
    m = [m, m_got]
    cols, own_rows = wide // n_dp, narrow // n_own
    sent = products(place, winv, ninv, m, cols, own_rows, total)
    got = lax.all_to_all(sent, (place.far, place.second, place.first), 0, 0)
    kept, update = placing(
        place, owner_map, got, wide, cols, layers // n_own + 1, own_rows
    )
    return (jnp.swapaxes(kept, 1, 2), jnp.swapaxes(update, 1, 2))


def solution(mesh):
    n_dp, n_own = mesh.shape["dp"], mesh.shape["own"]
    dp_names = tuple(f"dp{i}" for i in range(int(np.log2(n_dp))))
    own_names = tuple(f"own{i}" for i in range(int(np.log2(n_own))))
    names = dp_names + own_names
    bits = jax.sharding.Mesh(mesh.devices.reshape((2,) * len(names)), names)
    in_specs = (P(None, names, None), P(None, names, None), P())
    out_specs = (P(own_names, None, dp_names), P(None, own_names, dp_names))
    return jax.shard_map(
        functools.partial(on_device, Place(dp_names, own_names)),
        mesh=bits,
        in_specs=in_specs,
        out_specs=out_specs,
        check_vma=False,
    )
```

```python
import functools

import jax
import jax.numpy as jnp
import numpy as np
from jax import lax
from jax.experimental import pallas as pl
from jax.experimental.pallas import tpu as pltpu
from jax.sharding import PartitionSpec as P

DAMP = 0.5
LANES = 128
PANEL = 8
VMEM_LIMIT = 48 * 1024 * 1024
HIGHEST = lax.Precision.HIGHEST
VMEM = pl.BlockSpec(memory_space=pltpu.VMEM)
SMEM = pl.BlockSpec(memory_space=pltpu.SMEM)
HBM = pl.BlockSpec(memory_space=pltpu.HBM)
PARAMS = pltpu.CompilerParams(vmem_limit_bytes=VMEM_LIMIT)


class Place:
    def __init__(self, dp_names, own_names):
        self.dp, self.own = dp_names, own_names
        self.core, self.second, self.near, self.far = (
            dp_names[-1],
            dp_names[-2],
            dp_names[1],
            dp_names[0],
        )
        self.first = own_names[-1]
        used = (self.core, self.second, self.near, self.far, self.first)
        self.extra = tuple(n for n in dp_names + own_names if n not in used)

    def index(self, names):
        value = jnp.int32(0)
        for name in names:
            value = value * 2 + lax.axis_index(name)
        return value

    def layer(self):
        return self.index((self.far, self.second, self.first))

    def quarter(self):
        return self.index((self.core, self.near))


def transposed_dot(a, b, precision=None):
    return lax.dot_general(
        a, b, (((0,), (0,)), ((), ())), precision=precision, preferred_element_type=jnp.float32
    )


def read_layers(place, sources, buffers, sems):
    layer = place.layer()
    copies = []
    for i in range(buffers[0].shape[0]):
        group = [
            pltpu.make_async_copy(
                source.at[jnp.bitwise_xor(layer, i)], buffer.at[i], sems.at[i, s]
            )
            for s, (source, buffer) in enumerate(zip(sources, buffers))
        ]
        for copy in group:
            copy.start()
        copies.append(group)
    return copies


def write_halves(place, i, flat, keep_ref, send_ref):
    rows = keep_ref.shape[2]
    core = lax.axis_index(place.core)
    z, y, x = i // 4, (i // 2) % 2, i % 2
    mine = jnp.where(core == 0, x * 2 + y, y * 2 + x)
    other = jnp.where(core == 0, y * 2 + x, x * 2 + y)
    kept = pl.multiple_of(core * rows, PANEL)
    sent = pl.multiple_of((1 - core) * rows, PANEL)
    keep_ref[mine, z] = flat[i, pl.ds(kept, rows), :]
    send_ref[other, z] = flat[i, pl.ds(sent, rows), :]


def iotas(shape):
    return (
        lax.broadcasted_iota(jnp.int32, shape, 0),
        lax.broadcasted_iota(jnp.int32, shape, 1),
    )


def pack_pair(first, second):
    row, col = iotas(first.shape)
    return jnp.where(row >= col, first, second)


def unpack_pair(packed, second_diagonal):
    row, col = iotas(packed.shape)
    turned = packed.T
    first = jnp.where(row >= col, packed, turned)
    second = jnp.where(col > row, packed, turned)
    return first, jnp.where(row == col, second_diagonal, second)


def fold(block):
    h = block.shape[0] // 2
    row, col = iotas((h, 2 * h))
    last = pltpu.roll(block[h:], h, 1)
    return jnp.where((col >= h) | (row >= col), block[:h], last)


def unfold(folded, diagonal):
    h, n = folded.shape
    row, col = iotas((n, n))
    block = jnp.concatenate([folded, jnp.zeros((h, n), jnp.float32)], axis=0)
    turned = block.T
    top = jnp.where((col >= h) | (col <= row), block, turned)
    moved = pltpu.roll(pltpu.roll(block, h, 0), h, 1)
    moved_turned = pltpu.roll(pltpu.roll(turned, h, 0), h, 1)
    last = jnp.where(col > row, moved, moved_turned)
    last = jnp.where(row == col, diagonal, last)
    return jnp.where(row < h, top, jnp.where(col < h, turned, last))


def diagonals(blocks, rows):
    n = blocks[0].shape[0]
    row, col = iotas((n, n))
    slab_row, _ = iotas((rows, n))
    slab = jnp.zeros((rows, n), jnp.float32)
    for i, block in enumerate(blocks):
        line = jnp.sum(jnp.where(row == col, block, 0.0), axis=0, keepdims=True)
        slab = jnp.where(slab_row == i, jnp.broadcast_to(line, (rows, n)), slab)
    return slab


EARLY_ROWS = 144
LATE_ROWS = 448


def gram_kernel(place, wide_hbm, narrow_hbm, *refs):
    a_keep, a_send, b_keep, b_send, wides, narrows, a_flat, b_flat, sems = refs
    copies = read_layers(place, (wide_hbm, narrow_hbm), (wides, narrows), sems)
    n = LANES
    for i, group in enumerate(copies):
        for copy in group:
            copy.wait()
        wide = wides[i]
        narrow = narrows[i]
        wcov = transposed_dot(wide, wide)
        ncov = transposed_dot(narrow, narrow)
        mixed = transposed_dot(narrow, wide)
        last = wcov[n:, n:]
        a_flat[i, :n] = pack_pair(wcov[:n, :n], ncov)
        a_flat[i, n:] = diagonals((ncov, last), EARLY_ROWS - n)
        write_halves(place, i, a_flat, a_keep, a_send)
        b_flat[i, :n] = wcov[:n, n:]
        b_flat[i, n : n + n // 2] = fold(last)
        b_flat[i, n + n // 2 : 2 * n + n // 2] = mixed[:, :n]
        b_flat[i, 2 * n + n // 2 :] = mixed[:, n:]
        write_halves(place, i, b_flat, b_keep, b_send)


def gram(place, wide_rows, narrow_rows):
    layers = wide_rows.shape[0]
    early = jax.ShapeDtypeStruct((4, 2, EARLY_ROWS // 2, LANES), jnp.float32)
    late = jax.ShapeDtypeStruct((4, 2, LATE_ROWS // 2, LANES), jnp.float32)
    return pl.pallas_call(
        functools.partial(gram_kernel, place),
        in_specs=[HBM, HBM],
        out_specs=[VMEM] * 4,
        out_shape=[early, early, late, late],
        scratch_shapes=[
            pltpu.VMEM(wide_rows.shape, wide_rows.dtype),
            pltpu.VMEM(narrow_rows.shape, narrow_rows.dtype),
            pltpu.VMEM((layers, EARLY_ROWS, LANES), jnp.float32),
            pltpu.VMEM((layers, LATE_ROWS, LANES), jnp.float32),
            pltpu.SemaphoreType.DMA((layers, 2)),
        ],
        cost_estimate=pl.CostEstimate(
            flops=2 * wide_rows.size * 448,
            bytes_accessed=3 * wide_rows.size,
            transcendentals=0,
        ),
        compiler_params=PARAMS,
        name="gram",
    )(
        pltpu.with_memory_space_constraint(wide_rows, pltpu.HBM),
        pltpu.with_memory_space_constraint(narrow_rows, pltpu.HBM),
    )


def lane_gather(x, index):
    return jnp.take_along_axis(x, index, axis=1, mode="promise_in_bounds")


def trailing_update(a_ref, left_ref, right_ref, base):
    size = a_ref.shape[1]
    a_ref[pl.ds(pl.multiple_of(base, PANEL), PANEL), :] = jnp.zeros((PANEL, size), jnp.float32)
    lane = lax.broadcasted_iota(jnp.int32, (1, size), 1)
    swept = (lane >= base - PANEL) & (lane < base)
    update = transposed_dot(left_ref[...], right_ref[...])
    a_ref[PANEL : PANEL + size, :] = (
        jnp.where(swept, 0.0, a_ref[PANEL : PANEL + size, :]) - update
    )


def sweep_panel(a_ref, left_ref, right_ref, tile, step, panel):
    size = a_ref.shape[1]
    tiles = size // LANES
    first = step * PANEL
    base = tile * LANES + first
    trailing_update(a_ref, left_ref, right_ref, base)

    shape = (PANEL, LANES)
    sub = lax.broadcasted_iota(jnp.int32, shape, 0)
    lane = lax.broadcasted_iota(jnp.int32, shape, 1)
    parts = [panel[:, LANES * t : LANES * (t + 1)] for t in range(tiles)]
    rows = [
        [jnp.broadcast_to(part[k : k + 1, :], shape) for part in parts] for k in range(PANEL)
    ]
    index = [jnp.full(shape, 0, jnp.int32) + (first + i) for i in range(PANEL)]
    d = [[None] * PANEL for _ in range(PANEL)]
    for j in range(PANEL):
        for i in range(j, PANEL):
            d[i][j] = lane_gather(rows[j][tile], index[i])
    own = (lane >= first) & (lane < first + PANEL)
    q = [[None] * tiles for _ in range(PANEL)]
    factor = [[None] * PANEL for _ in range(PANEL)]
    for k in range(PANEL):
        scale = lax.rsqrt(d[k][k])
        for i in range(k + 1, PANEL):
            factor[i][k] = d[i][k] * scale
        for i in range(k + 1, PANEL):
            for j in range(k + 1, i + 1):
                d[i][j] = d[i][j] - factor[i][k] * factor[j][k]
        for t in range(tiles):
            value = rows[k][t]
            if t == tile:
                value = jnp.where(own, jnp.where(lane == first + k, -1.0, 0.0), value)
            for j in range(k):
                value = value - factor[k][j] * q[j][t]
            q[k][t] = value * scale

    packed = []
    for t in range(tiles):
        value = q[0][t]
        for k in range(1, PANEL):
            value = jnp.where(sub == k, q[k][t], value)
        packed.append(value)
    whole = jnp.concatenate(packed, axis=1) if tiles > 1 else packed[0]
    high = whole.astype(jnp.bfloat16).astype(jnp.float32)
    rest = whole - high
    middle = rest.astype(jnp.bfloat16).astype(jnp.float32)
    low = rest - middle
    left = jnp.concatenate([high, high, middle, middle, high, low], axis=0)
    right = jnp.concatenate([high, middle, high, middle, low, high], axis=0)
    left_ref[...] = left.astype(jnp.bfloat16)
    right_ref[...] = right.astype(jnp.bfloat16)

    after = pl.multiple_of(base + 2 * PANEL, PANEL)
    following = a_ref[pl.ds(after, PANEL), :]
    last = first == LANES - PANEL
    next_lane = jnp.where(last, 0, first + PANEL) + sub
    weights = []
    for k in range(PANEL):
        source = q[k][tile]
        if tile + 1 < tiles:
            source = jnp.where(last, q[k][tile + 1], source)
        weights.append(lane_gather(source, next_lane))
    result = []
    for t in range(tiles):
        value = following[:, LANES * t : LANES * (t + 1)]
        if t == tile:
            value = jnp.where(own, 0.0, value)
        terms = [weights[k] * q[k][t] for k in range(PANEL)]
        while len(terms) > 1:
            terms = [terms[i] + terms[i + 1] for i in range(0, len(terms), 2)]
        result.append(value - terms[0])
    return jnp.concatenate(result, axis=1) if tiles > 1 else result[0]


def place_pieces(place, flat, pieces):
    core = lax.axis_index(place.core)
    rows = pieces[0].shape[0]
    for r, piece in enumerate(pieces):
        start = pl.multiple_of(jnp.bitwise_xor(core, r) * rows, PANEL)
        flat[pl.ds(start, rows), :] = piece[...]


def sweep_cost():
    return pl.CostEstimate(flops=1 << 30, bytes_accessed=1 << 20, transcendentals=0)


def load_damped(a_ref, block):
    n = block.shape[0]
    row, col = iotas(block.shape)
    a_ref[:PANEL] = jnp.zeros((PANEL, n), jnp.float32)
    a_ref[PANEL + n :] = jnp.zeros((PANEL, n), jnp.float32)
    a_ref[PANEL : PANEL + n] = block + jnp.where(row == col, DAMP, 0.0)


def sweep_all(works):
    for _, left, right in works:
        left[...] = jnp.zeros(left.shape, left.dtype)
        right[...] = jnp.zeros(right.shape, right.dtype)

    def step(i, panels):
        return tuple(sweep_panel(*work, 0, i, panel) for work, panel in zip(works, panels))

    size = works[0][0].shape[1]
    lax.fori_loop(0, size // PANEL, step, tuple(a[PANEL : 2 * PANEL] for a, _, _ in works))
    for work in works:
        trailing_update(*work, size)
    return [-a[PANEL : PANEL + size] for a, _, _ in works]


def work_shapes(size):
    splits = 6 * PANEL
    return [
        pltpu.VMEM((size + 2 * PANEL, size), jnp.float32),
        pltpu.VMEM((splits, size), jnp.bfloat16),
        pltpu.VMEM((splits, size), jnp.bfloat16),
    ]


def early_kernel(place, total, mine, other, winv_ref, ninv_ref, slab_ref, flat, *works):
    place_pieces(place, flat, (mine, other))
    n = LANES
    slab = flat[n : n + PANEL]
    slab_ref[...] = slab
    first, square = unpack_pair(flat[:n], jnp.broadcast_to(slab[:1], (n, n)))
    load_damped(works[0], first / total)
    load_damped(works[3], square / total)
    winv_ref[...], ninv_ref[...] = sweep_all((works[:3], works[3:]))


def early(place, pieces, total):
    n = LANES
    square = jax.ShapeDtypeStruct((n, n), jnp.float32)
    return pl.pallas_call(
        functools.partial(early_kernel, place, total),
        in_specs=[VMEM] * 2,
        out_specs=[VMEM] * 3,
        out_shape=[square, square, jax.ShapeDtypeStruct((PANEL, n), jnp.float32)],
        scratch_shapes=[
            pltpu.VMEM((EARLY_ROWS, n), jnp.float32),
            *work_shapes(n),
            *work_shapes(n),
        ],
        cost_estimate=sweep_cost(),
        compiler_params=PARAMS,
        name="early",
    )(*pieces)


def aligned_rows(ref, index, count):
    if count % PANEL == 0:
        return ref[pl.ds(pl.multiple_of(index * count, count), count), :]
    per_slab = PANEL // count
    slab = ref[pl.ds(pl.multiple_of(index // per_slab * PANEL, PANEL), PANEL), :]
    value = slab[:count]
    for i in range(1, per_slab):
        value = jnp.where(index % per_slab == i, slab[i * count : (i + 1) * count], value)
    return value


def packs(cols, rows):
    return cols == 2 * PANEL and 2 * rows == LANES


def dot(a, b, last=False):
    return lax.dot_general(
        a,
        b,
        (((1,), (1 if last else 0,)), ((), ())),
        precision=HIGHEST,
        preferred_element_type=jnp.float32,
    )


def late_kernel(place, total, rows, w11_ref, ninv_ref, slab_ref, mine, other, out_ref, *refs):
    flat, winv, inner_ref = refs[:3]
    work = refs[3:]
    place_pieces(place, flat, (mine, other))
    n = LANES
    h = n // 2
    w11 = w11_ref[...]
    corner = flat[:n] / total
    solved = dot(w11, corner)
    schur = transposed_dot(corner, solved, HIGHEST)
    last = unfold(flat[n : n + h], jnp.broadcast_to(slab_ref[1:2], (n, n)))
    load_damped(work[0], last / total - schur)
    ninv = ninv_ref[...]
    for c in range(2):
        start = n + h + c * n
        inner_ref[c * n : (c + 1) * n] = transposed_dot(
            flat[start : start + n] / total, ninv, HIGHEST
        )
    (sinv,) = sweep_all((work,))
    cross = dot(solved, sinv)
    winv[:n, :n] = w11 + dot(cross, solved, last=True)
    winv[:n, n:] = -cross
    winv[n:, :n] = -cross.T
    winv[n:, n:] = sinv
    inner = inner_ref[...]
    wide = winv.shape[1]
    cols = wide // 2 ** len(place.dp)
    far, second = lax.axis_index(place.far), lax.axis_index(place.second)
    far_stride = 2 ** (len(place.dp) - 1)
    base = place.index(place.dp) - far * far_stride - second * 2
    _, lane = iotas((PANEL, LANES))
    for j in range(4):
        index = base + (j // 2) * far_stride + (j % 2) * 2
        picked = aligned_rows(winv, index, cols)
        update = lax.dot_general(
            picked,
            inner,
            (((1,), (0,)), ((), ())),
            precision=HIGHEST,
            preferred_element_type=jnp.float32,
        )
        for x in range(2):
            block = 2 * j + x
            out_ref[block, :cols] = picked[:, :LANES]
            out_ref[block, cols : 2 * cols] = picked[:, LANES:]
            if packs(cols, rows):
                upper, lower = update[:PANEL], update[PANEL:]
                if x == 0:
                    lower = pltpu.roll(lower, rows, 1)
                else:
                    upper = pltpu.roll(upper, rows, 1)
                out_ref[block, 2 * cols :] = jnp.where(lane < rows, upper, lower)
            else:
                out_ref[block, 2 * cols :] = update


def late(place, early_out, pieces, wide, rows, total):
    cols = wide // 2 ** len(place.dp)
    height = 2 * cols + (PANEL if packs(cols, rows) else cols)
    n = LANES
    return pl.pallas_call(
        functools.partial(late_kernel, place, total, rows),
        in_specs=[VMEM] * 5,
        out_specs=VMEM,
        out_shape=jax.ShapeDtypeStruct((8, height, LANES), jnp.float32),
        scratch_shapes=[
            pltpu.VMEM((LATE_ROWS, n), jnp.float32),
            pltpu.VMEM((wide, wide), jnp.float32),
            pltpu.VMEM((wide, n), jnp.float32),
            *work_shapes(n),
        ],
        cost_estimate=sweep_cost(),
        compiler_params=PARAMS,
        name="late",
    )(*early_out, *pieces)


def placing_kernel(place, owner_map, got_ref, kept_ref, update_ref):
    layers = got_ref.shape[0]
    slots, cols, wide = kept_ref.shape
    rows = update_ref.shape[2]
    own, dp = place.index(place.own), place.index(place.dp)
    row, col = iotas((cols, wide))
    empty = jnp.where(col == row + dp * cols, 1.0 / DAMP, 0.0)
    count = jnp.int32(0)
    slot = []
    for l in range(layers):
        mine = owner_map[l] == own
        slot.append(jnp.where(mine, count, -1))
        count = count + mine.astype(jnp.int32)
    for h in range(2):
        lanes = slice(h * LANES, (h + 1) * LANES)
        for c in range(slots):
            value = empty[:, lanes]
            for l in range(layers):
                value = jnp.where(slot[l] == c, got_ref[l, h * cols : (h + 1) * cols], value)
            kept_ref[c, :, lanes] = value
    for l in range(layers):
        value = got_ref[l, 2 * cols :]
        if packs(cols, rows):
            update_ref[l, :PANEL] = value[:, :rows]
            update_ref[l, PANEL:] = value[:, rows:]
        else:
            part = value[:, :rows]
            for p in range(1, LANES // rows):
                part = jnp.where(own == p, value[:, p * rows : (p + 1) * rows], part)
            update_ref[l] = part


def placing(place, owner_map, got, wide, cols, slots, rows):
    layers = got.shape[0]
    return pl.pallas_call(
        functools.partial(placing_kernel, place),
        in_specs=[SMEM, VMEM],
        out_specs=[VMEM, VMEM],
        out_shape=[
            jax.ShapeDtypeStruct((slots, cols, wide), jnp.float32),
            jax.ShapeDtypeStruct((layers, cols, rows), jnp.float32),
        ],
        compiler_params=PARAMS,
        name="placing",
    )(owner_map, got)


def swap(value, axis):
    return lax.ppermute(value, axis, [(0, 1), (1, 0)])


def swap_by_core(value, place, stage):
    pairs = []
    for y in range(2):
        for core in range(2):
            for x in range(2):
                flip = 1 if core == stage else 4
                here = y * 4 + core * 2 + x
                pairs.append((here, here ^ flip))
    return lax.ppermute(value, (place.second, place.core, place.first), pairs)


def after(value, *others):
    return lax.optimization_barrier((value,) + others)[0]


def on_device(place, wide_rows, narrow_rows, owner_map):
    layers, rows, wide = wide_rows.shape
    narrow = narrow_rows.shape[2]
    n_dp, n_own = 2 ** len(place.dp), 2 ** len(place.own)
    total = float(rows * n_dp * n_own)

    a_keep, a_send, b_keep, b_send = gram(place, wide_rows, narrow_rows)
    a_got = swap(a_send, place.core)
    b_got = swap(b_send, place.core)

    a = a_keep + a_got
    a_got = swap_by_core(a[2:], place, 0)
    b = after(b_keep, a) + b_got
    b_got = swap_by_core(b[2:], place, 0)

    a = after(a[:2], b) + a_got
    a_got = swap_by_core(a[1], place, 1)
    a = a[0] + a_got
    a_keep, a_send = a[0], a[1]
    a_got = swap(a_send, place.far)
    b = after(b[:2], a_send) + b_got
    b_got = swap_by_core(b[1], place, 1)

    a = after(a_keep, b) + a_got
    if place.extra:
        a = lax.psum(a, place.extra)
    b = after(b[0], a) + b_got
    b_keep, b_send = b[0], b[1]
    b_got = swap(b_send, place.far)

    a = after(a, b_send)
    a = a + swap(a, place.near)
    early_out = early(place, [a, swap(a, place.core)], total)
    b = after(b_keep, early_out[0]) + b_got
    if place.extra:
        b = lax.psum(b, place.extra)
    b = b + swap(b, place.near)
    cols, own_rows = wide // n_dp, narrow // n_own
    sent = late(place, early_out, [b, swap(b, place.core)], wide, own_rows, total)
    got = lax.all_to_all(sent, (place.far, place.second, place.first), 0, 0)
    kept, update = placing(
        place, owner_map, got, wide, cols, layers // n_own + 1, own_rows
    )
    return (jnp.swapaxes(kept, 1, 2), jnp.swapaxes(update, 1, 2))


def solution(mesh):
    n_dp, n_own = mesh.shape["dp"], mesh.shape["own"]
    dp_names = tuple(f"dp{i}" for i in range(int(np.log2(n_dp))))
    own_names = tuple(f"own{i}" for i in range(int(np.log2(n_own))))
    names = dp_names + own_names
    bits = jax.sharding.Mesh(mesh.devices.reshape((2,) * len(names)), names)
    in_specs = (P(None, names, None), P(None, names, None), P())
    out_specs = (P(own_names, None, dp_names), P(None, own_names, dp_names))
    return jax.shard_map(
        functools.partial(on_device, Place(dp_names, own_names)),
        mesh=bits,
        in_specs=in_specs,
        out_specs=out_specs,
        check_vma=False,
    )
```

```python
import functools

import jax
import jax.numpy as jnp
import numpy as np
from jax import lax
from jax.experimental import pallas as pl
from jax.experimental.pallas import tpu as pltpu
from jax.sharding import PartitionSpec as P

DAMP = 0.5
LANES = 128
PANEL = 8
VMEM_LIMIT = 48 * 1024 * 1024
HIGHEST = lax.Precision.HIGHEST
VMEM = pl.BlockSpec(memory_space=pltpu.VMEM)
SMEM = pl.BlockSpec(memory_space=pltpu.SMEM)
HBM = pl.BlockSpec(memory_space=pltpu.HBM)
PARAMS = pltpu.CompilerParams(vmem_limit_bytes=VMEM_LIMIT)


class Place:
    def __init__(self, dp_names, own_names):
        self.dp, self.own = dp_names, own_names
        self.core, self.second, self.near, self.far = (
            dp_names[-1],
            dp_names[-2],
            dp_names[1],
            dp_names[0],
        )
        self.first = own_names[-1]
        used = (self.core, self.second, self.near, self.far, self.first)
        self.extra = tuple(n for n in dp_names + own_names if n not in used)

    def index(self, names):
        value = jnp.int32(0)
        for name in names:
            value = value * 2 + lax.axis_index(name)
        return value

    def layer(self):
        return self.index((self.far, self.second, self.first))

    def quarter(self):
        return self.index((self.core, self.near))


def transposed_dot(a, b, precision=None):
    return lax.dot_general(
        a, b, (((0,), (0,)), ((), ())), precision=precision, preferred_element_type=jnp.float32
    )


def read_layers(place, sources, buffers, sems):
    layer = place.layer()
    copies = []
    for i in range(buffers[0].shape[0]):
        group = [
            pltpu.make_async_copy(
                source.at[jnp.bitwise_xor(layer, i)], buffer.at[i], sems.at[i, s]
            )
            for s, (source, buffer) in enumerate(zip(sources, buffers))
        ]
        for copy in group:
            copy.start()
        copies.append(group)
    return copies


def write_halves(place, i, first_row, flat, keep_ref, send_ref):
    rows = flat.shape[1] // 2
    core = lax.axis_index(place.core)
    z, y, x = i // 4, (i // 2) % 2, i % 2
    mine = jnp.where(core == 0, x * 2 + y, y * 2 + x)
    other = jnp.where(core == 0, y * 2 + x, x * 2 + y)
    kept = pl.multiple_of(core * rows, PANEL)
    sent = pl.multiple_of((1 - core) * rows, PANEL)
    there = slice(first_row, first_row + rows)
    keep_ref[mine, z, there] = flat[i, pl.ds(kept, rows), :]
    send_ref[other, z, there] = flat[i, pl.ds(sent, rows), :]


def iotas(shape):
    return (
        lax.broadcasted_iota(jnp.int32, shape, 0),
        lax.broadcasted_iota(jnp.int32, shape, 1),
    )


def pack_pair(first, second):
    row, col = iotas(first.shape)
    return jnp.where(row >= col, first, second)


def unpack_pair(packed, second_diagonal):
    row, col = iotas(packed.shape)
    turned = packed.T
    first = jnp.where(row >= col, packed, turned)
    second = jnp.where(col > row, packed, turned)
    return first, jnp.where(row == col, second_diagonal, second)


def fold(block):
    h = block.shape[0] // 2
    row, col = iotas((h, 2 * h))
    last = pltpu.roll(block[h:], h, 1)
    return jnp.where((col >= h) | (row >= col), block[:h], last)


def unfold(folded, diagonal):
    h, n = folded.shape
    row, col = iotas((n, n))
    block = jnp.concatenate([folded, jnp.zeros((h, n), jnp.float32)], axis=0)
    turned = block.T
    top = jnp.where((col >= h) | (col <= row), block, turned)
    moved = pltpu.roll(pltpu.roll(block, h, 0), h, 1)
    moved_turned = pltpu.roll(pltpu.roll(turned, h, 0), h, 1)
    last = jnp.where(col > row, moved, moved_turned)
    last = jnp.where(row == col, diagonal, last)
    return jnp.where(row < h, top, jnp.where(col < h, turned, last))


def diagonals(blocks, rows):
    n = blocks[0].shape[0]
    row, col = iotas((n, n))
    slab_row, _ = iotas((rows, n))
    slab = jnp.zeros((rows, n), jnp.float32)
    for i, block in enumerate(blocks):
        line = jnp.sum(jnp.where(row == col, block, 0.0), axis=0, keepdims=True)
        slab = jnp.where(slab_row == i, jnp.broadcast_to(line, (rows, n)), slab)
    return slab


EARLY_ROWS = 144
LATE_ROWS = 448


def gram_kernel(place, wide_hbm, narrow_hbm, *refs):
    keep, send, wides, narrows, a_flat, b_flat, sems = refs
    copies = read_layers(place, (wide_hbm, narrow_hbm), (wides, narrows), sems)
    n = LANES
    for i, group in enumerate(copies):
        for copy in group:
            copy.wait()
        wide = wides[i]
        narrow = narrows[i]
        wcov = transposed_dot(wide, wide)
        ncov = transposed_dot(narrow, narrow)
        mixed = transposed_dot(narrow, wide)
        last = wcov[n:, n:]
        a_flat[i, :n] = pack_pair(wcov[:n, :n], ncov)
        a_flat[i, n:] = diagonals((ncov, last), EARLY_ROWS - n)
        write_halves(place, i, 0, a_flat, keep, send)
        b_flat[i, :n] = wcov[:n, n:]
        b_flat[i, n : n + n // 2] = fold(last)
        b_flat[i, n + n // 2 : 2 * n + n // 2] = mixed[:, :n]
        b_flat[i, 2 * n + n // 2 :] = mixed[:, n:]
        write_halves(place, i, EARLY_ROWS // 2, b_flat, keep, send)


def gram(place, wide_rows, narrow_rows):
    layers = wide_rows.shape[0]
    half = jax.ShapeDtypeStruct((4, 2, (EARLY_ROWS + LATE_ROWS) // 2, LANES), jnp.float32)
    return pl.pallas_call(
        functools.partial(gram_kernel, place),
        in_specs=[HBM, HBM],
        out_specs=[VMEM] * 2,
        out_shape=[half, half],
        scratch_shapes=[
            pltpu.VMEM(wide_rows.shape, wide_rows.dtype),
            pltpu.VMEM(narrow_rows.shape, narrow_rows.dtype),
            pltpu.VMEM((layers, EARLY_ROWS, LANES), jnp.float32),
            pltpu.VMEM((layers, LATE_ROWS, LANES), jnp.float32),
            pltpu.SemaphoreType.DMA((layers, 2)),
        ],
        cost_estimate=pl.CostEstimate(
            flops=2 * wide_rows.size * 448,
            bytes_accessed=3 * wide_rows.size,
            transcendentals=0,
        ),
        compiler_params=PARAMS,
        name="gram",
    )(
        pltpu.with_memory_space_constraint(wide_rows, pltpu.HBM),
        pltpu.with_memory_space_constraint(narrow_rows, pltpu.HBM),
    )


def lane_gather(x, index):
    return jnp.take_along_axis(x, index, axis=1, mode="promise_in_bounds")


def trailing_update(a_ref, left_ref, right_ref, base):
    size = a_ref.shape[1]
    a_ref[pl.ds(pl.multiple_of(base, PANEL), PANEL), :] = jnp.zeros((PANEL, size), jnp.float32)
    lane = lax.broadcasted_iota(jnp.int32, (1, size), 1)
    swept = (lane >= base - PANEL) & (lane < base)
    update = transposed_dot(left_ref[...], right_ref[...])
    a_ref[PANEL : PANEL + size, :] = (
        jnp.where(swept, 0.0, a_ref[PANEL : PANEL + size, :]) - update
    )


def sweep_panel(a_ref, left_ref, right_ref, tile, step, panel):
    size = a_ref.shape[1]
    tiles = size // LANES
    first = step * PANEL
    base = tile * LANES + first
    trailing_update(a_ref, left_ref, right_ref, base)

    shape = (PANEL, LANES)
    sub = lax.broadcasted_iota(jnp.int32, shape, 0)
    lane = lax.broadcasted_iota(jnp.int32, shape, 1)
    parts = [panel[:, LANES * t : LANES * (t + 1)] for t in range(tiles)]
    rows = [
        [jnp.broadcast_to(part[k : k + 1, :], shape) for part in parts] for k in range(PANEL)
    ]
    index = [jnp.full(shape, 0, jnp.int32) + (first + i) for i in range(PANEL)]
    d = [[None] * PANEL for _ in range(PANEL)]
    for j in range(PANEL):
        for i in range(j, PANEL):
            d[i][j] = lane_gather(rows[j][tile], index[i])
    own = (lane >= first) & (lane < first + PANEL)
    last = first == LANES - PANEL
    next_lane = jnp.where(last, 0, first + PANEL) + sub
    q = [[None] * tiles for _ in range(PANEL)]
    weights = [None] * PANEL
    factor = [[None] * PANEL for _ in range(PANEL)]
    for k in range(PANEL):
        scale = lax.rsqrt(d[k][k])
        for i in range(k + 1, PANEL):
            factor[i][k] = d[i][k] * scale
        for i in range(k + 1, PANEL):
            for j in range(k + 1, i + 1):
                d[i][j] = d[i][j] - factor[i][k] * factor[j][k]
        for t in range(tiles):
            value = rows[k][t]
            if t == tile:
                value = jnp.where(own, jnp.where(lane == first + k, -1.0, 0.0), value)
            for j in range(k):
                value = value - factor[k][j] * q[j][t]
            q[k][t] = value * scale
        source = rows[k][tile]
        if tile + 1 < tiles:
            source = jnp.where(last, rows[k][tile + 1], source)
        value = lane_gather(source, next_lane)
        for j in range(k):
            value = value - factor[k][j] * weights[j]
        weights[k] = value * scale

    packed = []
    for t in range(tiles):
        value = q[0][t]
        for k in range(1, PANEL):
            value = jnp.where(sub == k, q[k][t], value)
        packed.append(value)
    whole = jnp.concatenate(packed, axis=1) if tiles > 1 else packed[0]
    high = whole.astype(jnp.bfloat16).astype(jnp.float32)
    rest = whole - high
    middle = rest.astype(jnp.bfloat16).astype(jnp.float32)
    low = rest - middle
    left = jnp.concatenate([high, high, middle, middle, high, low], axis=0)
    right = jnp.concatenate([high, middle, high, middle, low, high], axis=0)
    left_ref[...] = left.astype(jnp.bfloat16)
    right_ref[...] = right.astype(jnp.bfloat16)

    after = pl.multiple_of(base + 2 * PANEL, PANEL)
    following = a_ref[pl.ds(after, PANEL), :]
    result = []
    for t in range(tiles):
        value = following[:, LANES * t : LANES * (t + 1)]
        if t == tile:
            value = jnp.where(own, 0.0, value)
        terms = [weights[k] * q[k][t] for k in range(PANEL)]
        while len(terms) > 1:
            terms = [terms[i] + terms[i + 1] for i in range(0, len(terms), 2)]
        result.append(value - terms[0])
    return jnp.concatenate(result, axis=1) if tiles > 1 else result[0]


def place_pieces(place, pieces, a_flat, b_flat):
    core = lax.axis_index(place.core)
    a_rows, b_rows = a_flat.shape[0] // 2, b_flat.shape[0] // 2
    for r, piece in enumerate(pieces):
        half = jnp.bitwise_xor(core, r)
        a_flat[pl.ds(pl.multiple_of(half * a_rows, PANEL), a_rows), :] = piece[:a_rows]
        b_flat[pl.ds(pl.multiple_of(half * b_rows, PANEL), b_rows), :] = piece[a_rows:]


def sweep_cost():
    return pl.CostEstimate(flops=1 << 30, bytes_accessed=1 << 20, transcendentals=0)


def load_damped(a_ref, block):
    n = block.shape[0]
    row, col = iotas(block.shape)
    a_ref[:PANEL] = jnp.zeros((PANEL, n), jnp.float32)
    a_ref[PANEL + n :] = jnp.zeros((PANEL, n), jnp.float32)
    a_ref[PANEL : PANEL + n] = block + jnp.where(row == col, DAMP, 0.0)


def sweep_all(works):
    for _, left, right in works:
        left[...] = jnp.zeros(left.shape, left.dtype)
        right[...] = jnp.zeros(right.shape, right.dtype)

    def step(i, panels):
        return tuple(sweep_panel(*work, 0, i, panel) for work, panel in zip(works, panels))

    size = works[0][0].shape[1]
    lax.fori_loop(0, size // PANEL, step, tuple(a[PANEL : 2 * PANEL] for a, _, _ in works))
    for work in works:
        trailing_update(*work, size)
    return [-a[PANEL : PANEL + size] for a, _, _ in works]


def work_shapes(size):
    splits = 6 * PANEL
    return [
        pltpu.VMEM((size + 2 * PANEL, size), jnp.float32),
        pltpu.VMEM((splits, size), jnp.bfloat16),
        pltpu.VMEM((splits, size), jnp.bfloat16),
    ]


def aligned_rows(ref, index, count):
    if count % PANEL == 0:
        return ref[pl.ds(pl.multiple_of(index * count, count), count), :]
    per_slab = PANEL // count
    slab = ref[pl.ds(pl.multiple_of(index // per_slab * PANEL, PANEL), PANEL), :]
    value = slab[:count]
    for i in range(1, per_slab):
        value = jnp.where(index % per_slab == i, slab[i * count : (i + 1) * count], value)
    return value


def packs(cols, rows):
    return cols == 2 * PANEL and 2 * rows == LANES


def dot(a, b, last=False):
    return lax.dot_general(
        a,
        b,
        (((1,), (1 if last else 0,)), ((), ())),
        precision=HIGHEST,
        preferred_element_type=jnp.float32,
    )


def inverse_kernel(place, total, rows, mine, other, out_ref, *refs):
    a_flat, b_flat, winv, inner_ref = refs[:4]
    first_work, narrow_work, last_work = refs[4:7], refs[7:10], refs[10:]
    place_pieces(place, (mine, other), a_flat, b_flat)
    n = LANES
    h = n // 2
    slab = a_flat[n : n + PANEL]
    first, square = unpack_pair(a_flat[:n], jnp.broadcast_to(slab[:1], (n, n)))
    load_damped(first_work[0], first / total)
    load_damped(narrow_work[0], square / total)
    w11, ninv = sweep_all((first_work, narrow_work))
    corner = b_flat[:n] / total
    solved = dot(w11, corner)
    schur = transposed_dot(corner, solved, HIGHEST)
    last = unfold(b_flat[n : n + h], jnp.broadcast_to(slab[1:2], (n, n)))
    load_damped(last_work[0], last / total - schur)
    for c in range(2):
        start = n + h + c * n
        inner_ref[c * n : (c + 1) * n] = transposed_dot(
            b_flat[start : start + n] / total, ninv, HIGHEST
        )
    winv[:n, :n] = w11
    (sinv,) = sweep_all((last_work,))
    cross = dot(solved, sinv)
    winv[:n, :n] += dot(cross, solved, last=True)
    winv[:n, n:] = -cross
    winv[n:, :n] = -cross.T
    winv[n:, n:] = sinv
    inner = inner_ref[...]
    wide = winv.shape[1]
    cols = wide // 2 ** len(place.dp)
    far, second = lax.axis_index(place.far), lax.axis_index(place.second)
    far_stride = 2 ** (len(place.dp) - 1)
    base = place.index(place.dp) - far * far_stride - second * 2
    _, lane = iotas((PANEL, LANES))
    for j in range(4):
        index = base + (j // 2) * far_stride + (j % 2) * 2
        picked = aligned_rows(winv, index, cols)
        update = lax.dot_general(
            picked,
            inner,
            (((1,), (0,)), ((), ())),
            precision=HIGHEST,
            preferred_element_type=jnp.float32,
        )
        for x in range(2):
            block = 2 * j + x
            out_ref[block, :cols] = picked[:, :LANES]
            out_ref[block, cols : 2 * cols] = picked[:, LANES:]
            if packs(cols, rows):
                upper, lower = update[:PANEL], update[PANEL:]
                if x == 0:
                    lower = pltpu.roll(lower, rows, 1)
                else:
                    upper = pltpu.roll(upper, rows, 1)
                out_ref[block, 2 * cols :] = jnp.where(lane < rows, upper, lower)
            else:
                out_ref[block, 2 * cols :] = update


def inverses(place, pieces, wide, rows, total):
    cols = wide // 2 ** len(place.dp)
    height = 2 * cols + (PANEL if packs(cols, rows) else cols)
    n = LANES
    return pl.pallas_call(
        functools.partial(inverse_kernel, place, total, rows),
        in_specs=[VMEM] * 2,
        out_specs=VMEM,
        out_shape=jax.ShapeDtypeStruct((8, height, LANES), jnp.float32),
        scratch_shapes=[
            pltpu.VMEM((EARLY_ROWS, n), jnp.float32),
            pltpu.VMEM((LATE_ROWS, n), jnp.float32),
            pltpu.VMEM((wide, wide), jnp.float32),
            pltpu.VMEM((wide, n), jnp.float32),
            *work_shapes(n),
            *work_shapes(n),
            *work_shapes(n),
        ],
        cost_estimate=sweep_cost(),
        compiler_params=PARAMS,
        name="inverses",
    )(*pieces)


def placing_kernel(place, owner_map, got_ref, kept_ref, update_ref):
    layers = got_ref.shape[0]
    slots, cols, wide = kept_ref.shape
    rows = update_ref.shape[2]
    own, dp = place.index(place.own), place.index(place.dp)
    row, col = iotas((cols, wide))
    empty = jnp.where(col == row + dp * cols, 1.0 / DAMP, 0.0)
    count = jnp.int32(0)
    slot = []
    for l in range(layers):
        mine = owner_map[l] == own
        slot.append(jnp.where(mine, count, -1))
        count = count + mine.astype(jnp.int32)
    for h in range(2):
        lanes = slice(h * LANES, (h + 1) * LANES)
        for c in range(slots):
            value = empty[:, lanes]
            for l in range(layers):
                value = jnp.where(slot[l] == c, got_ref[l, h * cols : (h + 1) * cols], value)
            kept_ref[c, :, lanes] = value
    for l in range(layers):
        value = got_ref[l, 2 * cols :]
        if packs(cols, rows):
            update_ref[l, :PANEL] = value[:, :rows]
            update_ref[l, PANEL:] = value[:, rows:]
        else:
            part = value[:, :rows]
            for p in range(1, LANES // rows):
                part = jnp.where(own == p, value[:, p * rows : (p + 1) * rows], part)
            update_ref[l] = part


def placing(place, owner_map, got, wide, cols, slots, rows):
    layers = got.shape[0]
    return pl.pallas_call(
        functools.partial(placing_kernel, place),
        in_specs=[SMEM, VMEM],
        out_specs=[VMEM, VMEM],
        out_shape=[
            jax.ShapeDtypeStruct((slots, cols, wide), jnp.float32),
            jax.ShapeDtypeStruct((layers, cols, rows), jnp.float32),
        ],
        compiler_params=PARAMS,
        name="placing",
    )(owner_map, got)


def swap(value, axis):
    return lax.ppermute(value, axis, [(0, 1), (1, 0)])


def swap_by_core(value, place, stage):
    pairs = []
    for y in range(2):
        for core in range(2):
            for x in range(2):
                flip = 1 if core == stage else 4
                here = y * 4 + core * 2 + x
                pairs.append((here, here ^ flip))
    return lax.ppermute(value, (place.second, place.core, place.first), pairs)


def in_two(value, exchange):
    return jnp.stack([exchange(value[0]), exchange(value[1])])


def on_device(place, wide_rows, narrow_rows, owner_map):
    layers, rows, wide = wide_rows.shape
    narrow = narrow_rows.shape[2]
    n_dp, n_own = 2 ** len(place.dp), 2 ** len(place.own)
    total = float(rows * n_dp * n_own)

    s_keep, s_send = gram(place, wide_rows, narrow_rows)
    s = s_keep + swap(s_send, place.core)
    s = s[:2] + in_two(s[2:], lambda v: swap_by_core(v, place, 0))
    s = s[0] + in_two(s[1], lambda v: swap_by_core(v, place, 1))
    s = s[0] + swap(s[1], place.far)
    s = s + swap(s, place.near)
    if place.extra:
        s = lax.psum(s, place.extra)
    cols, own_rows = wide // n_dp, narrow // n_own
    sent = inverses(place, [s, swap(s, place.core)], wide, own_rows, total)
    got = lax.all_to_all(sent, (place.far, place.second, place.first), 0, 0)
    kept, update = placing(
        place, owner_map, got, wide, cols, layers // n_own + 1, own_rows
    )
    return (jnp.swapaxes(kept, 1, 2), jnp.swapaxes(update, 1, 2))


def solution(mesh):
    n_dp, n_own = mesh.shape["dp"], mesh.shape["own"]
    dp_names = tuple(f"dp{i}" for i in range(int(np.log2(n_dp))))
    own_names = tuple(f"own{i}" for i in range(int(np.log2(n_own))))
    names = dp_names + own_names
    bits = jax.sharding.Mesh(mesh.devices.reshape((2,) * len(names)), names)
    in_specs = (P(None, names, None), P(None, names, None), P())
    out_specs = (P(own_names, None, dp_names), P(None, own_names, dp_names))
    return jax.shard_map(
        functools.partial(on_device, Place(dp_names, own_names)),
        mesh=bits,
        in_specs=in_specs,
        out_specs=out_specs,
        check_vma=False,
    )
```

```python
import functools

import jax
import jax.numpy as jnp
import numpy as np
from jax import lax
from jax.experimental import pallas as pl
from jax.experimental.pallas import tpu as pltpu
from jax.sharding import PartitionSpec as P

DAMP = 0.5
LANES = 128
PANEL = 8
VMEM_LIMIT = 48 * 1024 * 1024
HIGHEST = lax.Precision.HIGHEST
VMEM = pl.BlockSpec(memory_space=pltpu.VMEM)
SMEM = pl.BlockSpec(memory_space=pltpu.SMEM)
HBM = pl.BlockSpec(memory_space=pltpu.HBM)
PARAMS = pltpu.CompilerParams(vmem_limit_bytes=VMEM_LIMIT)


class Place:
    def __init__(self, dp_names, own_names):
        self.dp, self.own = dp_names, own_names
        self.core, self.second, self.near, self.far = (
            dp_names[-1],
            dp_names[-2],
            dp_names[1],
            dp_names[0],
        )
        self.first = own_names[-1]
        used = (self.core, self.second, self.near, self.far, self.first)
        self.extra = tuple(n for n in dp_names + own_names if n not in used)

    def index(self, names):
        value = jnp.int32(0)
        for name in names:
            value = value * 2 + lax.axis_index(name)
        return value

    def layer(self):
        return self.index((self.near, self.second, self.first))


def transposed_dot(a, b, precision=None):
    return lax.dot_general(
        a, b, (((0,), (0,)), ((), ())), precision=precision, preferred_element_type=jnp.float32
    )


AHEAD = 3


def layer_copies(place, sources, buffers, sems):
    layer = place.layer()
    return [
        [
            pltpu.make_async_copy(
                source.at[jnp.bitwise_xor(layer, i)], buffer.at[i], sems.at[i, s]
            )
            for s, (source, buffer) in enumerate(zip(sources, buffers))
        ]
        for i in range(buffers[0].shape[0])
    ]


def write_halves(place, i, first_row, flat, keep_ref, send_ref):
    rows = flat.shape[1] // 2
    core = lax.axis_index(place.core)
    z, y, x = i // 4, (i // 2) % 2, i % 2
    mine = jnp.where(core == 0, x * 2 + y, y * 2 + x)
    other = jnp.where(core == 0, y * 2 + x, x * 2 + y)
    kept = pl.multiple_of(core * rows, PANEL)
    sent = pl.multiple_of((1 - core) * rows, PANEL)
    there = slice(first_row, first_row + rows)
    keep_ref[mine, z, there] = flat[i, pl.ds(kept, rows), :]
    send_ref[other, z, there] = flat[i, pl.ds(sent, rows), :]


def iotas(shape):
    return (
        lax.broadcasted_iota(jnp.int32, shape, 0),
        lax.broadcasted_iota(jnp.int32, shape, 1),
    )


def pack_pair(first, second):
    row, col = iotas(first.shape)
    return jnp.where(row >= col, first, second)


def unpack_pair(packed, second_diagonal):
    row, col = iotas(packed.shape)
    turned = packed.T
    first = jnp.where(row >= col, packed, turned)
    second = jnp.where(col > row, packed, turned)
    return first, jnp.where(row == col, second_diagonal, second)


def fold(block):
    h = block.shape[0] // 2
    row, col = iotas((h, 2 * h))
    last = pltpu.roll(block[h:], h, 1)
    return jnp.where((col >= h) | (row >= col), block[:h], last)


def unfold(folded, diagonal):
    h, n = folded.shape
    row, col = iotas((n, n))
    block = jnp.concatenate([folded, jnp.zeros((h, n), jnp.float32)], axis=0)
    turned = block.T
    top = jnp.where((col >= h) | (col <= row), block, turned)
    moved = pltpu.roll(pltpu.roll(block, h, 0), h, 1)
    moved_turned = pltpu.roll(pltpu.roll(turned, h, 0), h, 1)
    last = jnp.where(col > row, moved, moved_turned)
    last = jnp.where(row == col, diagonal, last)
    return jnp.where(row < h, top, jnp.where(col < h, turned, last))


def diagonals(blocks, rows):
    n = blocks[0].shape[0]
    row, col = iotas((n, n))
    slab_row, _ = iotas((rows, n))
    slab = jnp.zeros((rows, n), jnp.float32)
    for i, block in enumerate(blocks):
        line = jnp.sum(jnp.where(row == col, block, 0.0), axis=0, keepdims=True)
        slab = jnp.where(slab_row == i, jnp.broadcast_to(line, (rows, n)), slab)
    return slab


EARLY_ROWS = 144
LATE_ROWS = 192


def squares_kernel(place, wide_hbm, narrow_hbm, keep, send, wides, narrows, a_flat, b_flat, sems):
    copies = layer_copies(place, (wide_hbm, narrow_hbm), (wides, narrows), sems)
    for group in copies[:AHEAD]:
        for copy in group:
            copy.start()
    n = LANES
    for i, group in enumerate(copies):
        for copy in group:
            copy.wait()
        if i + AHEAD < len(copies):
            for copy in copies[i + AHEAD]:
                copy.start()
        wide = wides[i]
        narrow = narrows[i]
        wcov = transposed_dot(wide, wide)
        ncov = transposed_dot(narrow, narrow)
        last = wcov[n:, n:]
        a_flat[i, :n] = pack_pair(wcov[:n, :n], ncov)
        a_flat[i, n:] = diagonals((ncov, last), EARLY_ROWS - n)
        write_halves(place, i, 0, a_flat, keep, send)
        b_flat[i, :n] = wcov[:n, n:]
        b_flat[i, n:] = fold(last)
        write_halves(place, i, EARLY_ROWS // 2, b_flat, keep, send)


def mixed_kernel(place, wides, narrows, keep, send, flat):
    n = LANES
    for i in range(wides.shape[0]):
        mixed = transposed_dot(narrows[i], wides[i])
        flat[i, :n] = mixed[:, :n]
        flat[i, n:] = mixed[:, n:]
        write_halves(place, i, 0, flat, keep, send)


def gram_cost(wide_rows, columns):
    return pl.CostEstimate(
        flops=2 * wide_rows.size * columns, bytes_accessed=2 * wide_rows.size, transcendentals=0
    )


def squares(place, wide_rows, narrow_rows):
    layers = wide_rows.shape[0]
    half = jax.ShapeDtypeStruct((4, 2, (EARLY_ROWS + LATE_ROWS) // 2, LANES), jnp.float32)
    return pl.pallas_call(
        functools.partial(squares_kernel, place),
        in_specs=[HBM, HBM],
        out_specs=[VMEM] * 4,
        out_shape=[
            half,
            half,
            jax.ShapeDtypeStruct(wide_rows.shape, wide_rows.dtype),
            jax.ShapeDtypeStruct(narrow_rows.shape, narrow_rows.dtype),
        ],
        scratch_shapes=[
            pltpu.VMEM((layers, EARLY_ROWS, LANES), jnp.float32),
            pltpu.VMEM((layers, LATE_ROWS, LANES), jnp.float32),
            pltpu.SemaphoreType.DMA((layers, 2)),
        ],
        cost_estimate=gram_cost(wide_rows, 320),
        compiler_params=PARAMS,
        name="squares",
    )(
        pltpu.with_memory_space_constraint(wide_rows, pltpu.HBM),
        pltpu.with_memory_space_constraint(narrow_rows, pltpu.HBM),
    )


def mixed_sums(place, wides, narrows):
    layers, _, narrow = narrows.shape
    half = jax.ShapeDtypeStruct((4, 2, narrow, LANES), jnp.float32)
    return pl.pallas_call(
        functools.partial(mixed_kernel, place),
        in_specs=[VMEM, VMEM],
        out_specs=[VMEM, VMEM],
        out_shape=[half, half],
        scratch_shapes=[pltpu.VMEM((layers, 2 * narrow, LANES), jnp.float32)],
        cost_estimate=gram_cost(wides, 128),
        compiler_params=PARAMS,
        name="mixed",
    )(wides, narrows)


def lane_gather(x, index):
    return jnp.take_along_axis(x, index, axis=1, mode="promise_in_bounds")


def trailing_update(a_ref, left_ref, right_ref, base):
    size = a_ref.shape[1]
    a_ref[pl.ds(pl.multiple_of(base, PANEL), PANEL), :] = jnp.zeros((PANEL, size), jnp.float32)
    lane = lax.broadcasted_iota(jnp.int32, (1, size), 1)
    swept = (lane >= base - PANEL) & (lane < base)
    update = transposed_dot(left_ref[...], right_ref[...])
    a_ref[PANEL : PANEL + size, :] = (
        jnp.where(swept, 0.0, a_ref[PANEL : PANEL + size, :]) - update
    )


def sweep_panel(a_ref, left_ref, right_ref, tile, step, panel):
    size = a_ref.shape[1]
    tiles = size // LANES
    first = step * PANEL
    base = tile * LANES + first
    trailing_update(a_ref, left_ref, right_ref, base)

    shape = (PANEL, LANES)
    sub = lax.broadcasted_iota(jnp.int32, shape, 0)
    lane = lax.broadcasted_iota(jnp.int32, shape, 1)
    parts = [panel[:, LANES * t : LANES * (t + 1)] for t in range(tiles)]
    rows = [
        [jnp.broadcast_to(part[k : k + 1, :], shape) for part in parts] for k in range(PANEL)
    ]
    index = [jnp.full(shape, 0, jnp.int32) + (first + i) for i in range(PANEL)]
    d = [[None] * PANEL for _ in range(PANEL)]
    for j in range(PANEL):
        for i in range(j, PANEL):
            d[i][j] = lane_gather(rows[j][tile], index[i])
    own = (lane >= first) & (lane < first + PANEL)
    last = first == LANES - PANEL
    next_lane = jnp.where(last, 0, first + PANEL) + sub
    q = [[None] * tiles for _ in range(PANEL)]
    weights = [None] * PANEL
    factor = [[None] * PANEL for _ in range(PANEL)]
    for k in range(PANEL):
        scale = lax.rsqrt(d[k][k])
        for i in range(k + 1, PANEL):
            factor[i][k] = d[i][k] * scale
        for i in range(k + 1, PANEL):
            for j in range(k + 1, i + 1):
                d[i][j] = d[i][j] - factor[i][k] * factor[j][k]
        for t in range(tiles):
            value = rows[k][t]
            if t == tile:
                value = jnp.where(own, jnp.where(lane == first + k, -1.0, 0.0), value)
            for j in range(k):
                value = value - factor[k][j] * q[j][t]
            q[k][t] = value * scale
        source = rows[k][tile]
        if tile + 1 < tiles:
            source = jnp.where(last, rows[k][tile + 1], source)
        value = lane_gather(source, next_lane)
        for j in range(k):
            value = value - factor[k][j] * weights[j]
        weights[k] = value * scale

    packed = []
    for t in range(tiles):
        value = q[0][t]
        for k in range(1, PANEL):
            value = jnp.where(sub == k, q[k][t], value)
        packed.append(value)
    whole = jnp.concatenate(packed, axis=1) if tiles > 1 else packed[0]
    high = whole.astype(jnp.bfloat16).astype(jnp.float32)
    rest = whole - high
    middle = rest.astype(jnp.bfloat16).astype(jnp.float32)
    low = rest - middle
    left = jnp.concatenate([high, high, middle, middle, high, low], axis=0)
    right = jnp.concatenate([high, middle, high, middle, low, high], axis=0)
    left_ref[...] = left.astype(jnp.bfloat16)
    right_ref[...] = right.astype(jnp.bfloat16)

    after = pl.multiple_of(base + 2 * PANEL, PANEL)
    following = a_ref[pl.ds(after, PANEL), :]
    result = []
    for t in range(tiles):
        value = following[:, LANES * t : LANES * (t + 1)]
        if t == tile:
            value = jnp.where(own, 0.0, value)
        terms = [weights[k] * q[k][t] for k in range(PANEL)]
        while len(terms) > 1:
            terms = [terms[i] + terms[i + 1] for i in range(0, len(terms), 2)]
        result.append(value - terms[0])
    return jnp.concatenate(result, axis=1) if tiles > 1 else result[0]


def place_halves(place, pieces, first_row, flat):
    core = lax.axis_index(place.core)
    rows = flat.shape[0] // 2
    for r, piece in enumerate(pieces):
        start = pl.multiple_of(jnp.bitwise_xor(core, r) * rows, PANEL)
        flat[pl.ds(start, rows), :] = piece[first_row : first_row + rows]


def sweep_cost():
    return pl.CostEstimate(flops=1 << 30, bytes_accessed=1 << 20, transcendentals=0)


def load_damped(a_ref, block):
    n = block.shape[0]
    row, col = iotas(block.shape)
    a_ref[:PANEL] = jnp.zeros((PANEL, n), jnp.float32)
    a_ref[PANEL + n :] = jnp.zeros((PANEL, n), jnp.float32)
    a_ref[PANEL : PANEL + n] = block + jnp.where(row == col, DAMP, 0.0)


def sweep_all(works):
    for _, left, right in works:
        left[...] = jnp.zeros(left.shape, left.dtype)
        right[...] = jnp.zeros(right.shape, right.dtype)

    def step(i, panels):
        return tuple(sweep_panel(*work, 0, i, panel) for work, panel in zip(works, panels))

    size = works[0][0].shape[1]
    lax.fori_loop(0, size // PANEL, step, tuple(a[PANEL : 2 * PANEL] for a, _, _ in works))
    for work in works:
        trailing_update(*work, size)
    return [-a[PANEL : PANEL + size] for a, _, _ in works]


def work_shapes(size):
    splits = 6 * PANEL
    return [
        pltpu.VMEM((size + 2 * PANEL, size), jnp.float32),
        pltpu.VMEM((splits, size), jnp.bfloat16),
        pltpu.VMEM((splits, size), jnp.bfloat16),
    ]


def aligned_rows(ref, index, count):
    if count % PANEL == 0:
        return ref[pl.ds(pl.multiple_of(index * count, count), count), :]
    per_slab = PANEL // count
    slab = ref[pl.ds(pl.multiple_of(index // per_slab * PANEL, PANEL), PANEL), :]
    value = slab[:count]
    for i in range(1, per_slab):
        value = jnp.where(index % per_slab == i, slab[i * count : (i + 1) * count], value)
    return value


def packs(cols, rows):
    return cols == 2 * PANEL and 2 * rows == LANES


def dot(a, b, last=False):
    return lax.dot_general(
        a,
        b,
        (((1,), (1 if last else 0,)), ((), ())),
        precision=HIGHEST,
        preferred_element_type=jnp.float32,
    )


def early_kernel(
    place, total, mine, other, w11_ref, ninv_ref, corner_ref, last_ref, a_flat, b_flat, *works
):
    place_halves(place, (mine, other), 0, a_flat)
    place_halves(place, (mine, other), a_flat.shape[0] // 2, b_flat)
    n = LANES
    slab = a_flat[n : n + PANEL]
    first, square = unpack_pair(a_flat[:n], jnp.broadcast_to(slab[:1], (n, n)))
    load_damped(works[0], first / total)
    load_damped(works[3], square / total)
    corner_ref[...] = b_flat[:n] / total
    last_ref[...] = unfold(b_flat[n:], jnp.broadcast_to(slab[1:2], (n, n))) / total
    w11_ref[...], ninv_ref[...] = sweep_all((works[:3], works[3:]))


def early(place, pieces, total):
    n = LANES
    return pl.pallas_call(
        functools.partial(early_kernel, place, total),
        in_specs=[VMEM] * 2,
        out_specs=[VMEM] * 4,
        out_shape=[jax.ShapeDtypeStruct((n, n), jnp.float32)] * 4,
        scratch_shapes=[
            pltpu.VMEM((EARLY_ROWS, n), jnp.float32),
            pltpu.VMEM((LATE_ROWS, n), jnp.float32),
            *work_shapes(n),
            *work_shapes(n),
        ],
        cost_estimate=sweep_cost(),
        compiler_params=PARAMS,
        name="early",
    )(*pieces)


def late_kernel(w11_ref, corner_ref, last_ref, winv, *work):
    n = LANES
    w11 = w11_ref[...]
    corner = corner_ref[...]
    solved = dot(w11, corner)
    load_damped(work[0], last_ref[...] - transposed_dot(corner, solved, HIGHEST))
    (sinv,) = sweep_all((work,))
    cross = dot(solved, sinv)
    winv[:n, :n] = w11 + dot(cross, solved, last=True)
    winv[:n, n:] = -cross
    winv[n:, :n] = -cross.T
    winv[n:, n:] = sinv


def late(w11, corner, last):
    n = LANES
    return pl.pallas_call(
        late_kernel,
        in_specs=[VMEM] * 3,
        out_specs=VMEM,
        out_shape=jax.ShapeDtypeStruct((2 * n, 2 * n), jnp.float32),
        scratch_shapes=work_shapes(n),
        cost_estimate=sweep_cost(),
        compiler_params=PARAMS,
        name="late",
    )(w11, corner, last)


def product_kernel(place, total, rows, winv, ninv_ref, mine, other, out_ref, flat):
    place_halves(place, (mine, other), 0, flat)
    ninv = ninv_ref[...]
    n = LANES
    inner = jnp.concatenate(
        [
            transposed_dot(flat[c * n : (c + 1) * n] / total, ninv, HIGHEST)
            for c in range(2)
        ],
        axis=0,
    )
    wide = winv.shape[1]
    cols = wide // 2 ** len(place.dp)
    near, second = lax.axis_index(place.near), lax.axis_index(place.second)
    near_stride = 2 ** (len(place.dp) - 2)
    base = place.index(place.dp) - near * near_stride - second * 2
    _, lane = iotas((PANEL, LANES))
    for j in range(4):
        index = base + (j // 2) * near_stride + (j % 2) * 2
        picked = aligned_rows(winv, index, cols)
        update = lax.dot_general(
            picked,
            inner,
            (((1,), (0,)), ((), ())),
            precision=HIGHEST,
            preferred_element_type=jnp.float32,
        )
        for x in range(2):
            block = 2 * j + x
            out_ref[block, :cols] = picked[:, :LANES]
            out_ref[block, cols : 2 * cols] = picked[:, LANES:]
            if packs(cols, rows):
                upper, lower = update[:PANEL], update[PANEL:]
                if x == 0:
                    lower = pltpu.roll(lower, rows, 1)
                else:
                    upper = pltpu.roll(upper, rows, 1)
                out_ref[block, 2 * cols :] = jnp.where(lane < rows, upper, lower)
            else:
                out_ref[block, 2 * cols :] = update


def products(place, winv, ninv, pieces, rows, total):
    wide, narrow = winv.shape[0], ninv.shape[0]
    cols = wide // 2 ** len(place.dp)
    height = 2 * cols + (PANEL if packs(cols, rows) else cols)
    return pl.pallas_call(
        functools.partial(product_kernel, place, total, rows),
        in_specs=[VMEM] * 4,
        out_specs=VMEM,
        out_shape=jax.ShapeDtypeStruct((8, height, LANES), jnp.float32),
        scratch_shapes=[pltpu.VMEM((2 * narrow, LANES), jnp.float32)],
        compiler_params=PARAMS,
        name="products",
    )(winv, ninv, *pieces)


def placing_kernel(place, owner_map, got_ref, kept_ref, update_ref):
    layers = got_ref.shape[0]
    slots, cols, wide = kept_ref.shape
    rows = update_ref.shape[2]
    own, dp = place.index(place.own), place.index(place.dp)
    row, col = iotas((cols, wide))
    empty = jnp.where(col == row + dp * cols, 1.0 / DAMP, 0.0)
    count = jnp.int32(0)
    slot = []
    for l in range(layers):
        mine = owner_map[l] == own
        slot.append(jnp.where(mine, count, -1))
        count = count + mine.astype(jnp.int32)
    for h in range(2):
        lanes = slice(h * LANES, (h + 1) * LANES)
        for c in range(slots):
            value = empty[:, lanes]
            for l in range(layers):
                value = jnp.where(slot[l] == c, got_ref[l, h * cols : (h + 1) * cols], value)
            kept_ref[c, :, lanes] = value
    for l in range(layers):
        value = got_ref[l, 2 * cols :]
        if packs(cols, rows):
            update_ref[l, :PANEL] = value[:, :rows]
            update_ref[l, PANEL:] = value[:, rows:]
        else:
            part = value[:, :rows]
            for p in range(1, LANES // rows):
                part = jnp.where(own == p, value[:, p * rows : (p + 1) * rows], part)
            update_ref[l] = part


def placing(place, owner_map, got, wide, cols, slots, rows):
    layers = got.shape[0]
    return pl.pallas_call(
        functools.partial(placing_kernel, place),
        in_specs=[SMEM, VMEM],
        out_specs=[VMEM, VMEM],
        out_shape=[
            jax.ShapeDtypeStruct((slots, cols, wide), jnp.float32),
            jax.ShapeDtypeStruct((layers, cols, rows), jnp.float32),
        ],
        compiler_params=PARAMS,
        name="placing",
    )(owner_map, got)


def swap(value, axis):
    return lax.ppermute(value, axis, [(0, 1), (1, 0)])


def swap_by_core(value, place, stage):
    pairs = []
    for y in range(2):
        for core in range(2):
            for x in range(2):
                flip = 1 if core == stage else 4
                here = y * 4 + core * 2 + x
                pairs.append((here, here ^ flip))
    return lax.ppermute(value, (place.second, place.core, place.first), pairs)


def after(value, *others):
    return lax.optimization_barrier((value,) + others)[0]


def on_device(place, wide_rows, narrow_rows, owner_map):
    layers, rows, wide = wide_rows.shape
    narrow = narrow_rows.shape[2]
    n_dp, n_own = 2 ** len(place.dp), 2 ** len(place.own)
    total = float(rows * n_dp * n_own)

    s_keep, s_send, wides, narrows = squares(place, wide_rows, narrow_rows)
    s_got = swap(s_send, place.core)
    m_keep, m_send = mixed_sums(place, after(wides, s_send), narrows)
    s_keep, m_send = lax.optimization_barrier((s_keep, m_send))

    s = s_keep + s_got
    s_got = swap_by_core(s[2:], place, 0)
    m_got = swap(after(m_send, s), place.core)

    s = s[:2] + s_got
    s_got = swap_by_core(s[1], place, 1)
    m = after(m_keep, s) + m_got
    m_got = swap_by_core(m[2:], place, 0)

    s = s[0] + s_got
    s_got = swap(s[1], place.near)
    m = after(m[:2], s) + m_got
    m_got = swap_by_core(m[1], place, 1)

    s = s[0] + s_got
    if place.extra:
        s = lax.psum(s, place.extra)
    s_got = swap(s, place.far)
    m = after(m[0], s) + m_got
    m_got = swap(m[1], place.near)

    s = s + s_got
    m = after(m[0], s) + m_got
    if place.extra:
        m = lax.psum(m, place.extra)
    s_got = swap(after(s, m), place.core)
    m_got = swap(m, place.far)

    w11, ninv, corner, last = early(place, [s, s_got], total)
    m = after(m, w11) + m_got
    m_got = swap(m, place.core)
    winv = late(w11, corner, last)
    cols, own_rows = wide // n_dp, narrow // n_own
    sent = products(place, winv, ninv, [m, m_got], own_rows, total)
    got = lax.all_to_all(sent, (place.near, place.second, place.first), 0, 0)
    kept, update = placing(
        place, owner_map, got, wide, cols, layers // n_own + 1, own_rows
    )
    return (jnp.swapaxes(kept, 1, 2), jnp.swapaxes(update, 1, 2))


def solution(mesh):
    n_dp, n_own = mesh.shape["dp"], mesh.shape["own"]
    dp_names = tuple(f"dp{i}" for i in range(int(np.log2(n_dp))))
    own_names = tuple(f"own{i}" for i in range(int(np.log2(n_own))))
    names = dp_names + own_names
    bits = jax.sharding.Mesh(mesh.devices.reshape((2,) * len(names)), names)
    in_specs = (P(None, names, None), P(None, names, None), P())
    out_specs = (P(own_names, None, dp_names), P(None, own_names, dp_names))
    return jax.shard_map(
        functools.partial(on_device, Place(dp_names, own_names)),
        mesh=bits,
        in_specs=in_specs,
        out_specs=out_specs,
        check_vma=False,
    )
```

```python
import functools

import jax
import jax.numpy as jnp
import numpy as np
from jax import lax
from jax.experimental import pallas as pl
from jax.experimental.pallas import tpu as pltpu
from jax.sharding import PartitionSpec as P

DAMP = 0.5
LANES = 128
PANEL = 8
VMEM_LIMIT = 48 * 1024 * 1024
HIGHEST = lax.Precision.HIGHEST
VMEM = pl.BlockSpec(memory_space=pltpu.VMEM)
SMEM = pl.BlockSpec(memory_space=pltpu.SMEM)
HBM = pl.BlockSpec(memory_space=pltpu.HBM)
PARAMS = pltpu.CompilerParams(vmem_limit_bytes=VMEM_LIMIT)


class Place:
    def __init__(self, dp_names, own_names):
        self.dp, self.own = dp_names, own_names
        self.core, self.second, self.near, self.far = (
            dp_names[-1],
            dp_names[-2],
            dp_names[1],
            dp_names[0],
        )
        self.first = own_names[-1]
        used = (self.core, self.second, self.near, self.far, self.first)
        self.extra = tuple(n for n in dp_names + own_names if n not in used)

    def index(self, names):
        value = jnp.int32(0)
        for name in names:
            value = value * 2 + lax.axis_index(name)
        return value

    def layer(self):
        return self.index((self.near, self.second, self.first))


def transposed_dot(a, b, precision=None):
    return lax.dot_general(
        a, b, (((0,), (0,)), ((), ())), precision=precision, preferred_element_type=jnp.float32
    )


AHEAD = 3
STEPS = 2


def layer_copies(place, sources, buffers, sems):
    layer = place.layer()
    return [
        [
            pltpu.make_async_copy(
                source.at[jnp.bitwise_xor(layer, i)], buffer.at[i], sems.at[i, s]
            )
            for s, (source, buffer) in enumerate(zip(sources, buffers))
        ]
        for i in range(buffers[0].shape[0])
    ]


def write_halves(place, i, first_row, flat, keep_ref, send_ref, swapped=False):
    rows = flat.shape[1] // 2
    core = lax.axis_index(place.core)
    z, y, x = i // 4, (i // 2) % 2, i % 2
    orders = (x * 2 + y, y * 2 + x)
    if swapped:
        orders = orders[::-1]
    mine = jnp.where(core == 0, *orders)
    other = jnp.where(core == 1, *orders)
    kept = pl.multiple_of(core * rows, PANEL)
    sent = pl.multiple_of((1 - core) * rows, PANEL)
    there = slice(first_row, first_row + rows)
    keep_ref[mine, z, there] = flat[i, pl.ds(kept, rows), :]
    send_ref[other, z, there] = flat[i, pl.ds(sent, rows), :]


def iotas(shape):
    return (
        lax.broadcasted_iota(jnp.int32, shape, 0),
        lax.broadcasted_iota(jnp.int32, shape, 1),
    )


def pack_pair(first, second):
    row, col = iotas(first.shape)
    return jnp.where(row >= col, first, second)


def unpack_pair(packed, second_diagonal):
    row, col = iotas(packed.shape)
    turned = packed.T
    first = jnp.where(row >= col, packed, turned)
    second = jnp.where(col > row, packed, turned)
    return first, jnp.where(row == col, second_diagonal, second)


def fold(block):
    h = block.shape[0] // 2
    row, col = iotas((h, 2 * h))
    last = pltpu.roll(block[h:], h, 1)
    return jnp.where((col >= h) | (row >= col), block[:h], last)


def unfold(folded, diagonal):
    h, n = folded.shape
    row, col = iotas((n, n))
    block = jnp.concatenate([folded, jnp.zeros((h, n), jnp.float32)], axis=0)
    turned = block.T
    top = jnp.where((col >= h) | (col <= row), block, turned)
    moved = pltpu.roll(pltpu.roll(block, h, 0), h, 1)
    moved_turned = pltpu.roll(pltpu.roll(turned, h, 0), h, 1)
    last = jnp.where(col > row, moved, moved_turned)
    last = jnp.where(row == col, diagonal, last)
    return jnp.where(row < h, top, jnp.where(col < h, turned, last))


def diagonals(blocks, rows):
    n = blocks[0].shape[0]
    row, col = iotas((n, n))
    slab_row, _ = iotas((rows, n))
    slab = jnp.zeros((rows, n), jnp.float32)
    for i, block in enumerate(blocks):
        line = jnp.sum(jnp.where(row == col, block, 0.0), axis=0, keepdims=True)
        slab = jnp.where(slab_row == i, jnp.broadcast_to(line, (rows, n)), slab)
    return slab


EARLY_ROWS = 144
LATE_ROWS = 192


def squares_kernel(place, wide_hbm, narrow_hbm, keep, send, wides, narrows, a_flat, b_flat, sems):
    copies = layer_copies(place, (wide_hbm, narrow_hbm), (wides, narrows), sems)
    for group in copies[:AHEAD]:
        for copy in group:
            copy.start()
    n = LANES

    def pack(i, wcov, ncov):
        last = wcov[n:, n:]
        a_flat[i, :n] = pack_pair(wcov[:n, :n], ncov)
        a_flat[i, n:] = diagonals((ncov, last), EARLY_ROWS - n)
        write_halves(place, i, 0, a_flat, keep, send)
        b_flat[i, :n] = wcov[:n, n:]
        b_flat[i, n:] = fold(last)
        write_halves(place, i, EARLY_ROWS // 2, b_flat, keep, send)

    before = None
    for i, group in enumerate(copies):
        for copy in group:
            copy.wait()
        if i + AHEAD < len(copies):
            for copy in copies[i + AHEAD]:
                copy.start()
        wide = wides[i]
        narrow = narrows[i]
        sums = (transposed_dot(wide, wide), transposed_dot(narrow, narrow))
        if before is not None:
            pack(i - 1, *before)
        before = sums
    pack(len(copies) - 1, *before)


def mixed_kernel(place, wides, narrows, keep, send, flat):
    n = LANES
    for i in range(wides.shape[0]):
        mixed = transposed_dot(narrows[i], wides[i])
        flat[i, :n] = mixed[:, :n]
        flat[i, n:] = mixed[:, n:]
        write_halves(place, i, 0, flat, keep, send, swapped=True)


def gram_cost(wide_rows, columns):
    return pl.CostEstimate(
        flops=2 * wide_rows.size * columns, bytes_accessed=2 * wide_rows.size, transcendentals=0
    )


def squares(place, wide_rows, narrow_rows):
    layers = wide_rows.shape[0]
    half = jax.ShapeDtypeStruct((4, 2, (EARLY_ROWS + LATE_ROWS) // 2, LANES), jnp.float32)
    return pl.pallas_call(
        functools.partial(squares_kernel, place),
        in_specs=[HBM, HBM],
        out_specs=[VMEM] * 4,
        out_shape=[
            half,
            half,
            jax.ShapeDtypeStruct(wide_rows.shape, wide_rows.dtype),
            jax.ShapeDtypeStruct(narrow_rows.shape, narrow_rows.dtype),
        ],
        scratch_shapes=[
            pltpu.VMEM((layers, EARLY_ROWS, LANES), jnp.float32),
            pltpu.VMEM((layers, LATE_ROWS, LANES), jnp.float32),
            pltpu.SemaphoreType.DMA((layers, 2)),
        ],
        cost_estimate=gram_cost(wide_rows, 320),
        compiler_params=PARAMS,
        name="squares",
    )(
        pltpu.with_memory_space_constraint(wide_rows, pltpu.HBM),
        pltpu.with_memory_space_constraint(narrow_rows, pltpu.HBM),
    )


def mixed_sums(place, wides, narrows):
    layers, _, narrow = narrows.shape
    half = jax.ShapeDtypeStruct((4, 2, narrow, LANES), jnp.float32)
    return pl.pallas_call(
        functools.partial(mixed_kernel, place),
        in_specs=[VMEM, VMEM],
        out_specs=[VMEM, VMEM],
        out_shape=[half, half],
        scratch_shapes=[pltpu.VMEM((layers, 2 * narrow, LANES), jnp.float32)],
        cost_estimate=gram_cost(wides, 128),
        compiler_params=PARAMS,
        name="mixed",
    )(wides, narrows)


def lane_gather(x, index):
    return jnp.take_along_axis(x, index, axis=1, mode="promise_in_bounds")


def trailing_update(a_ref, left_ref, right_ref, base):
    size = a_ref.shape[1]
    a_ref[pl.ds(pl.multiple_of(base, PANEL), PANEL), :] = jnp.zeros((PANEL, size), jnp.float32)
    lane = lax.broadcasted_iota(jnp.int32, (1, size), 1)
    swept = (lane >= base - PANEL) & (lane < base)
    update = transposed_dot(left_ref[...], right_ref[...])
    a_ref[PANEL : PANEL + size, :] = (
        jnp.where(swept, 0.0, a_ref[PANEL : PANEL + size, :]) - update
    )


def sweep_panel(a_ref, left_ref, right_ref, tile, step, panel):
    size = a_ref.shape[1]
    tiles = size // LANES
    first = step * PANEL
    base = tile * LANES + first
    trailing_update(a_ref, left_ref, right_ref, base)

    shape = (PANEL, LANES)
    sub = lax.broadcasted_iota(jnp.int32, shape, 0)
    lane = lax.broadcasted_iota(jnp.int32, shape, 1)
    parts = [panel[:, LANES * t : LANES * (t + 1)] for t in range(tiles)]
    rows = [
        [jnp.broadcast_to(part[k : k + 1, :], shape) for part in parts] for k in range(PANEL)
    ]
    index = [jnp.full(shape, 0, jnp.int32) + (first + i) for i in range(PANEL)]
    d = [[None] * PANEL for _ in range(PANEL)]
    for j in range(PANEL):
        for i in range(j, PANEL):
            d[i][j] = lane_gather(rows[j][tile], index[i])
    own = (lane >= first) & (lane < first + PANEL)
    last = first == LANES - PANEL
    next_lane = jnp.where(last, 0, first + PANEL) + sub
    q = [[None] * tiles for _ in range(PANEL)]
    weights = [None] * PANEL
    factor = [[None] * PANEL for _ in range(PANEL)]
    for k in range(PANEL):
        scale = lax.rsqrt(d[k][k])
        for i in range(k + 1, PANEL):
            factor[i][k] = d[i][k] * scale
        for i in range(k + 1, PANEL):
            for j in range(k + 1, i + 1):
                d[i][j] = d[i][j] - factor[i][k] * factor[j][k]
        for t in range(tiles):
            value = rows[k][t]
            if t == tile:
                value = jnp.where(own, jnp.where(lane == first + k, -1.0, 0.0), value)
            for j in range(k):
                value = value - factor[k][j] * q[j][t]
            q[k][t] = value * scale
        source = rows[k][tile]
        if tile + 1 < tiles:
            source = jnp.where(last, rows[k][tile + 1], source)
        value = lane_gather(source, next_lane)
        for j in range(k):
            value = value - factor[k][j] * weights[j]
        weights[k] = value * scale

    packed = []
    for t in range(tiles):
        value = q[0][t]
        for k in range(1, PANEL):
            value = jnp.where(sub == k, q[k][t], value)
        packed.append(value)
    whole = jnp.concatenate(packed, axis=1) if tiles > 1 else packed[0]
    high = whole.astype(jnp.bfloat16).astype(jnp.float32)
    rest = whole - high
    middle = rest.astype(jnp.bfloat16).astype(jnp.float32)
    low = rest - middle
    left = jnp.concatenate([high, high, middle, middle, high, low], axis=0)
    right = jnp.concatenate([high, middle, high, middle, low, high], axis=0)
    left_ref[...] = left.astype(jnp.bfloat16)
    right_ref[...] = right.astype(jnp.bfloat16)

    after = pl.multiple_of(base + 2 * PANEL, PANEL)
    following = a_ref[pl.ds(after, PANEL), :]
    result = []
    for t in range(tiles):
        value = following[:, LANES * t : LANES * (t + 1)]
        if t == tile:
            value = jnp.where(own, 0.0, value)
        terms = [weights[k] * q[k][t] for k in range(PANEL)]
        while len(terms) > 1:
            terms = [terms[i] + terms[i + 1] for i in range(0, len(terms), 2)]
        result.append(value - terms[0])
    return jnp.concatenate(result, axis=1) if tiles > 1 else result[0]


def place_halves(place, pieces, first_row, flat):
    core = lax.axis_index(place.core)
    rows = flat.shape[0] // 2
    for r, piece in enumerate(pieces):
        start = pl.multiple_of(jnp.bitwise_xor(core, r) * rows, PANEL)
        flat[pl.ds(start, rows), :] = piece[first_row : first_row + rows]


def sweep_cost():
    return pl.CostEstimate(flops=1 << 30, bytes_accessed=1 << 20, transcendentals=0)


def load_damped(a_ref, block):
    n = block.shape[0]
    row, col = iotas(block.shape)
    a_ref[:PANEL] = jnp.zeros((PANEL, n), jnp.float32)
    a_ref[PANEL + n :] = jnp.zeros((PANEL, n), jnp.float32)
    a_ref[PANEL : PANEL + n] = block + jnp.where(row == col, DAMP, 0.0)


def sweep_all(works):
    for _, left, right in works:
        left[...] = jnp.zeros(left.shape, left.dtype)
        right[...] = jnp.zeros(right.shape, right.dtype)

    def step(i, panels):
        for j in range(STEPS):
            panels = tuple(
                sweep_panel(*work, 0, i * STEPS + j, panel) for work, panel in zip(works, panels)
            )
        return panels

    size = works[0][0].shape[1]
    trips = size // (PANEL * STEPS)
    lax.fori_loop(0, trips, step, tuple(a[PANEL : 2 * PANEL] for a, _, _ in works))
    for work in works:
        trailing_update(*work, size)
    return [-a[PANEL : PANEL + size] for a, _, _ in works]


def work_shapes(size):
    splits = 6 * PANEL
    return [
        pltpu.VMEM((size + 2 * PANEL, size), jnp.float32),
        pltpu.VMEM((splits, size), jnp.bfloat16),
        pltpu.VMEM((splits, size), jnp.bfloat16),
    ]


def aligned_rows(ref, index, count):
    if count % PANEL == 0:
        return ref[pl.ds(pl.multiple_of(index * count, count), count), :]
    per_slab = PANEL // count
    slab = ref[pl.ds(pl.multiple_of(index // per_slab * PANEL, PANEL), PANEL), :]
    value = slab[:count]
    for i in range(1, per_slab):
        value = jnp.where(index % per_slab == i, slab[i * count : (i + 1) * count], value)
    return value


def packs(cols, rows):
    return cols == 2 * PANEL and 2 * rows == LANES


def dot(a, b, last=False):
    return lax.dot_general(
        a,
        b,
        (((1,), (1 if last else 0,)), ((), ())),
        precision=HIGHEST,
        preferred_element_type=jnp.float32,
    )


def early_kernel(
    place, total, mine, other, w11_ref, ninv_ref, corner_ref, last_ref, a_flat, b_flat, *works
):
    place_halves(place, (mine, other), 0, a_flat)
    place_halves(place, (mine, other), a_flat.shape[0] // 2, b_flat)
    n = LANES
    slab = a_flat[n : n + PANEL]
    first, square = unpack_pair(a_flat[:n], jnp.broadcast_to(slab[:1], (n, n)))
    load_damped(works[0], first / total)
    load_damped(works[3], square / total)
    corner_ref[...] = b_flat[:n] / total
    last_ref[...] = unfold(b_flat[n:], jnp.broadcast_to(slab[1:2], (n, n))) / total
    w11_ref[...], ninv_ref[...] = sweep_all((works[:3], works[3:]))


def early(place, pieces, total):
    n = LANES
    return pl.pallas_call(
        functools.partial(early_kernel, place, total),
        in_specs=[VMEM] * 2,
        out_specs=[VMEM] * 4,
        out_shape=[jax.ShapeDtypeStruct((n, n), jnp.float32)] * 4,
        scratch_shapes=[
            pltpu.VMEM((EARLY_ROWS, n), jnp.float32),
            pltpu.VMEM((LATE_ROWS, n), jnp.float32),
            *work_shapes(n),
            *work_shapes(n),
        ],
        cost_estimate=sweep_cost(),
        compiler_params=PARAMS,
        name="early",
    )(*pieces)


def late_kernel(w11_ref, corner_ref, last_ref, winv, *work):
    n = LANES
    w11 = w11_ref[...]
    corner = corner_ref[...]
    solved = dot(w11, corner)
    load_damped(work[0], last_ref[...] - transposed_dot(corner, solved, HIGHEST))
    (sinv,) = sweep_all((work,))
    cross = dot(solved, sinv)
    winv[:n, :n] = w11 + dot(cross, solved, last=True)
    winv[:n, n:] = -cross
    winv[n:, :n] = -cross.T
    winv[n:, n:] = sinv


def late(w11, corner, last):
    n = LANES
    return pl.pallas_call(
        late_kernel,
        in_specs=[VMEM] * 3,
        out_specs=VMEM,
        out_shape=jax.ShapeDtypeStruct((2 * n, 2 * n), jnp.float32),
        scratch_shapes=work_shapes(n),
        cost_estimate=sweep_cost(),
        compiler_params=PARAMS,
        name="late",
    )(w11, corner, last)


def product_kernel(place, total, rows, winv, ninv_ref, mine, other, out_ref, flat):
    place_halves(place, (mine, other), 0, flat)
    ninv = ninv_ref[...]
    n = LANES
    inner = jnp.concatenate(
        [
            transposed_dot(flat[c * n : (c + 1) * n] / total, ninv, HIGHEST)
            for c in range(2)
        ],
        axis=0,
    )
    wide = winv.shape[1]
    cols = wide // 2 ** len(place.dp)
    near, second = lax.axis_index(place.near), lax.axis_index(place.second)
    near_stride = 2 ** (len(place.dp) - 2)
    base = place.index(place.dp) - near * near_stride - second * 2
    _, lane = iotas((PANEL, LANES))
    for j in range(4):
        index = base + (j // 2) * near_stride + (j % 2) * 2
        picked = aligned_rows(winv, index, cols)
        update = lax.dot_general(
            picked,
            inner,
            (((1,), (0,)), ((), ())),
            precision=HIGHEST,
            preferred_element_type=jnp.float32,
        )
        for x in range(2):
            block = 2 * j + x
            out_ref[block, :cols] = picked[:, :LANES]
            out_ref[block, cols : 2 * cols] = picked[:, LANES:]
            if packs(cols, rows):
                upper, lower = update[:PANEL], update[PANEL:]
                if x == 0:
                    lower = pltpu.roll(lower, rows, 1)
                else:
                    upper = pltpu.roll(upper, rows, 1)
                out_ref[block, 2 * cols :] = jnp.where(lane < rows, upper, lower)
            else:
                out_ref[block, 2 * cols :] = update


def products(place, winv, ninv, pieces, rows, total):
    wide, narrow = winv.shape[0], ninv.shape[0]
    cols = wide // 2 ** len(place.dp)
    height = 2 * cols + (PANEL if packs(cols, rows) else cols)
    return pl.pallas_call(
        functools.partial(product_kernel, place, total, rows),
        in_specs=[VMEM] * 4,
        out_specs=VMEM,
        out_shape=jax.ShapeDtypeStruct((8, height, LANES), jnp.float32),
        scratch_shapes=[pltpu.VMEM((2 * narrow, LANES), jnp.float32)],
        compiler_params=PARAMS,
        name="products",
    )(winv, ninv, *pieces)


def placing_kernel(place, owner_map, got_ref, kept_ref, update_ref):
    layers = got_ref.shape[0]
    slots, cols, wide = kept_ref.shape
    rows = update_ref.shape[2]
    own, dp = place.index(place.own), place.index(place.dp)
    row, col = iotas((cols, wide))
    empty = jnp.where(col == row + dp * cols, 1.0 / DAMP, 0.0)
    count = jnp.int32(0)
    slot = []
    for l in range(layers):
        mine = owner_map[l] == own
        slot.append(jnp.where(mine, count, -1))
        count = count + mine.astype(jnp.int32)
    for h in range(2):
        lanes = slice(h * LANES, (h + 1) * LANES)
        for c in range(slots):
            value = empty[:, lanes]
            for l in range(layers):
                value = jnp.where(slot[l] == c, got_ref[l, h * cols : (h + 1) * cols], value)
            kept_ref[c, :, lanes] = value
    for l in range(layers):
        value = got_ref[l, 2 * cols :]
        if packs(cols, rows):
            update_ref[l, :PANEL] = value[:, :rows]
            update_ref[l, PANEL:] = value[:, rows:]
        else:
            part = value[:, :rows]
            for p in range(1, LANES // rows):
                part = jnp.where(own == p, value[:, p * rows : (p + 1) * rows], part)
            update_ref[l] = part


def placing(place, owner_map, got, wide, cols, slots, rows):
    layers = got.shape[0]
    return pl.pallas_call(
        functools.partial(placing_kernel, place),
        in_specs=[SMEM, VMEM],
        out_specs=[VMEM, VMEM],
        out_shape=[
            jax.ShapeDtypeStruct((slots, cols, wide), jnp.float32),
            jax.ShapeDtypeStruct((layers, cols, rows), jnp.float32),
        ],
        compiler_params=PARAMS,
        name="placing",
    )(owner_map, got)


def swap(value, axis):
    return lax.ppermute(value, axis, [(0, 1), (1, 0)])


def swap_by_core(value, place, stage):
    pairs = []
    for y in range(2):
        for core in range(2):
            for x in range(2):
                flip = 1 if core == stage else 4
                here = y * 4 + core * 2 + x
                pairs.append((here, here ^ flip))
    return lax.ppermute(value, (place.second, place.core, place.first), pairs)


def after(value, *others):
    return lax.optimization_barrier((value,) + others)[0]


def on_device(place, wide_rows, narrow_rows, owner_map):
    layers, rows, wide = wide_rows.shape
    narrow = narrow_rows.shape[2]
    n_dp, n_own = 2 ** len(place.dp), 2 ** len(place.own)
    total = float(rows * n_dp * n_own)

    s_keep, s_send, wides, narrows = squares(place, wide_rows, narrow_rows)
    s_got = swap(s_send, place.core)
    m_keep, m_send = mixed_sums(place, after(wides, s_send), narrows)
    s_keep, m_send = lax.optimization_barrier((s_keep, m_send))

    s = s_keep + s_got
    s_got = swap_by_core(s[2:], place, 0)
    m_got = swap(after(m_send, s), place.core)

    s = s[:2] + s_got
    s_got = swap_by_core(s[1], place, 1)
    m = after(m_keep, s) + m_got
    m_got = swap_by_core(m[2:], place, 1)

    s = s[0] + s_got
    s_got = swap(s[1], place.near)
    m = after(m[:2], s) + m_got
    m_got = swap_by_core(m[1], place, 0)

    s = s[0] + s_got
    if place.extra:
        s = lax.psum(s, place.extra)
    s_got = swap(s, place.far)
    m = after(m[0], s) + m_got
    m_got = swap(m[1], place.near)

    s = s + s_got
    m = after(m[0], s) + m_got
    if place.extra:
        m = lax.psum(m, place.extra)
    s_got = swap(after(s, m), place.core)
    m_got = swap(m, place.far)

    w11, ninv, corner, last = early(place, [s, s_got], total)
    m = after(m, w11) + m_got
    m_got = swap(m, place.core)
    winv = late(w11, corner, last)
    cols, own_rows = wide // n_dp, narrow // n_own
    sent = products(place, winv, ninv, [m, m_got], own_rows, total)
    got = lax.all_to_all(sent, (place.near, place.second, place.first), 0, 0)
    kept, update = placing(
        place, owner_map, got, wide, cols, layers // n_own + 1, own_rows
    )
    return (jnp.swapaxes(kept, 1, 2), jnp.swapaxes(update, 1, 2))


def solution(mesh):
    n_dp, n_own = mesh.shape["dp"], mesh.shape["own"]
    dp_names = tuple(f"dp{i}" for i in range(int(np.log2(n_dp))))
    own_names = tuple(f"own{i}" for i in range(int(np.log2(n_own))))
    names = dp_names + own_names
    bits = jax.sharding.Mesh(mesh.devices.reshape((2,) * len(names)), names)
    in_specs = (P(None, names, None), P(None, names, None), P())
    out_specs = (P(own_names, None, dp_names), P(None, own_names, dp_names))
    return jax.shard_map(
        functools.partial(on_device, Place(dp_names, own_names)),
        mesh=bits,
        in_specs=in_specs,
        out_specs=out_specs,
        check_vma=False,
    )
```

```python
import functools

import jax
import jax.numpy as jnp
import numpy as np
from jax import lax
from jax.experimental import pallas as pl
from jax.experimental.pallas import tpu as pltpu
from jax.sharding import PartitionSpec as P

DAMP = 0.5
LANES = 128
PANEL = 8
VMEM_LIMIT = 48 * 1024 * 1024
HIGHEST = lax.Precision.HIGHEST
VMEM = pl.BlockSpec(memory_space=pltpu.VMEM)
SMEM = pl.BlockSpec(memory_space=pltpu.SMEM)
HBM = pl.BlockSpec(memory_space=pltpu.HBM)
PARAMS = pltpu.CompilerParams(vmem_limit_bytes=VMEM_LIMIT)


class Place:
    def __init__(self, dp_names, own_names):
        self.dp, self.own = dp_names, own_names
        self.core, self.second, self.near, self.far = (
            dp_names[-1],
            dp_names[-2],
            dp_names[1],
            dp_names[0],
        )
        self.first = own_names[-1]
        used = (self.core, self.second, self.near, self.far, self.first)
        self.extra = tuple(n for n in dp_names + own_names if n not in used)

    def index(self, names):
        value = jnp.int32(0)
        for name in names:
            value = value * 2 + lax.axis_index(name)
        return value

    def layer(self):
        return self.index((self.near, self.second, self.first))


def transposed_dot(a, b, precision=None):
    return lax.dot_general(
        a, b, (((0,), (0,)), ((), ())), precision=precision, preferred_element_type=jnp.float32
    )


AHEAD = 3


def layer_copies(place, sources, buffers, sems):
    layer = place.layer()
    return [
        [
            pltpu.make_async_copy(
                source.at[jnp.bitwise_xor(layer, i)], buffer.at[i], sems.at[i, s]
            )
            for s, (source, buffer) in enumerate(zip(sources, buffers))
        ]
        for i in range(buffers[0].shape[0])
    ]


def write_halves(place, i, first_row, flat, keep_ref, send_ref, swapped=False):
    rows = flat.shape[1] // 2
    core = lax.axis_index(place.core)
    z, y, x = i // 4, (i // 2) % 2, i % 2
    orders = (x * 2 + y, y * 2 + x)
    if swapped:
        orders = orders[::-1]
    mine = jnp.where(core == 0, *orders)
    other = jnp.where(core == 1, *orders)
    kept = pl.multiple_of(core * rows, PANEL)
    sent = pl.multiple_of((1 - core) * rows, PANEL)
    there = slice(first_row, first_row + rows)
    keep_ref[mine, z, there] = flat[i, pl.ds(kept, rows), :]
    send_ref[other, z, there] = flat[i, pl.ds(sent, rows), :]


def iotas(shape):
    return (
        lax.broadcasted_iota(jnp.int32, shape, 0),
        lax.broadcasted_iota(jnp.int32, shape, 1),
    )


def pack_pair(first, second):
    row, col = iotas(first.shape)
    return jnp.where(row >= col, first, second)


def unpack_pair(packed, second_diagonal):
    row, col = iotas(packed.shape)
    turned = packed.T
    first = jnp.where(row >= col, packed, turned)
    second = jnp.where(col > row, packed, turned)
    return first, jnp.where(row == col, second_diagonal, second)


def fold(block):
    h = block.shape[0] // 2
    row, col = iotas((h, 2 * h))
    last = pltpu.roll(block[h:], h, 1)
    return jnp.where((col >= h) | (row >= col), block[:h], last)


def unfold(folded, diagonal):
    h, n = folded.shape
    row, col = iotas((n, n))
    block = jnp.concatenate([folded, jnp.zeros((h, n), jnp.float32)], axis=0)
    turned = block.T
    top = jnp.where((col >= h) | (col <= row), block, turned)
    moved = pltpu.roll(pltpu.roll(block, h, 0), h, 1)
    moved_turned = pltpu.roll(pltpu.roll(turned, h, 0), h, 1)
    last = jnp.where(col > row, moved, moved_turned)
    last = jnp.where(row == col, diagonal, last)
    return jnp.where(row < h, top, jnp.where(col < h, turned, last))


def diagonals(blocks, rows):
    n = blocks[0].shape[0]
    row, col = iotas((n, n))
    slab_row, _ = iotas((rows, n))
    slab = jnp.zeros((rows, n), jnp.float32)
    for i, block in enumerate(blocks):
        line = jnp.sum(jnp.where(row == col, block, 0.0), axis=0, keepdims=True)
        slab = jnp.where(slab_row == i, jnp.broadcast_to(line, (rows, n)), slab)
    return slab


EARLY_ROWS = 144
LATE_ROWS = 192


def squares_kernel(place, wide_hbm, narrow_hbm, keep, send, wides, narrows, a_flat, b_flat, sems):
    copies = layer_copies(place, (wide_hbm, narrow_hbm), (wides, narrows), sems)
    for group in copies[:AHEAD]:
        for copy in group:
            copy.start()
    n = LANES

    def pack(i, wcov, ncov):
        last = wcov[n:, n:]
        a_flat[i, :n] = pack_pair(wcov[:n, :n], ncov)
        a_flat[i, n:] = diagonals((ncov, last), EARLY_ROWS - n)
        write_halves(place, i, 0, a_flat, keep, send)
        b_flat[i, :n] = wcov[:n, n:]
        b_flat[i, n:] = fold(last)
        write_halves(place, i, EARLY_ROWS // 2, b_flat, keep, send)

    before = None
    for i, group in enumerate(copies):
        for copy in group:
            copy.wait()
        if i + AHEAD < len(copies):
            for copy in copies[i + AHEAD]:
                copy.start()
        wide = wides[i]
        narrow = narrows[i]
        sums = (transposed_dot(wide, wide), transposed_dot(narrow, narrow))
        if before is not None:
            pack(i - 1, *before)
        before = sums
    pack(len(copies) - 1, *before)


def mixed_kernel(place, wides, narrows, keep, send, flat):
    n = LANES
    for i in range(wides.shape[0]):
        mixed = transposed_dot(narrows[i], wides[i])
        flat[i, :n] = mixed[:, :n]
        flat[i, n:] = mixed[:, n:]
        write_halves(place, i, 0, flat, keep, send, swapped=True)


def dot(a, b, last=False):
    return lax.dot_general(
        a,
        b,
        (((1,), (1 if last else 0,)), ((), ())),
        precision=HIGHEST,
        preferred_element_type=jnp.float32,
    )


def gram_cost(wide_rows, columns):
    return pl.CostEstimate(
        flops=2 * wide_rows.size * columns, bytes_accessed=2 * wide_rows.size, transcendentals=0
    )


def squares(place, wide_rows, narrow_rows):
    layers = wide_rows.shape[0]
    half = jax.ShapeDtypeStruct((4, 2, (EARLY_ROWS + LATE_ROWS) // 2, LANES), jnp.float32)
    return pl.pallas_call(
        functools.partial(squares_kernel, place),
        in_specs=[HBM, HBM],
        out_specs=[VMEM] * 4,
        out_shape=[
            half,
            half,
            jax.ShapeDtypeStruct(wide_rows.shape, wide_rows.dtype),
            jax.ShapeDtypeStruct(narrow_rows.shape, narrow_rows.dtype),
        ],
        scratch_shapes=[
            pltpu.VMEM((layers, EARLY_ROWS, LANES), jnp.float32),
            pltpu.VMEM((layers, LATE_ROWS, LANES), jnp.float32),
            pltpu.SemaphoreType.DMA((layers, 2)),
        ],
        cost_estimate=gram_cost(wide_rows, 320),
        compiler_params=PARAMS,
        name="squares",
    )(
        pltpu.with_memory_space_constraint(wide_rows, pltpu.HBM),
        pltpu.with_memory_space_constraint(narrow_rows, pltpu.HBM),
    )


def mixed_sums(place, wides, narrows):
    layers, _, narrow = narrows.shape
    half = jax.ShapeDtypeStruct((4, 2, narrow, LANES), jnp.float32)
    return pl.pallas_call(
        functools.partial(mixed_kernel, place),
        in_specs=[VMEM, VMEM],
        out_specs=[VMEM, VMEM],
        out_shape=[half, half],
        scratch_shapes=[pltpu.VMEM((layers, 2 * narrow, LANES), jnp.float32)],
        cost_estimate=gram_cost(wides, 128),
        compiler_params=PARAMS,
        name="mixed",
    )(wides, narrows)


def lane_gather(x, index):
    return jnp.take_along_axis(x, index, axis=1, mode="promise_in_bounds")


def spread(x, k):
    return jnp.broadcast_to(x[k : k + 1, :], x.shape)


def trailing_update(a_ref, left_ref, right_ref, base):
    size = a_ref.shape[1]
    a_ref[pl.ds(pl.multiple_of(base, PANEL), PANEL), :] = jnp.zeros((PANEL, size), jnp.float32)
    lane = lax.broadcasted_iota(jnp.int32, (1, size), 1)
    swept = (lane >= base - PANEL) & (lane < base)
    update = transposed_dot(left_ref[...], right_ref[...])
    a_ref[PANEL : PANEL + size, :] = (
        jnp.where(swept, 0.0, a_ref[PANEL : PANEL + size, :]) - update
    )


def store_corner(d_ref, panel, first, corrections):
    shape = panel.shape
    lanes = [jnp.full(shape, 0, jnp.int32) + (first + i) for i in range(PANEL)]
    at = 0
    for j in range(PANEL):
        row = spread(panel, j)
        for i in range(j, PANEL):
            value = lane_gather(row, lanes[i])
            for w in corrections:
                value = value - w[i] * w[j]
            d_ref[at] = value
            at += 1


def sweep_panel(a_ref, left_ref, right_ref, d_ref, step, panel, before):
    first = pl.multiple_of(step * PANEL, PANEL)
    shape = panel.shape
    sub, lane = iotas(shape)
    next_first = jnp.where(first == LANES - PANEL, 0, first + PANEL)
    next_lane = next_first + sub
    following = a_ref[pl.ds(pl.multiple_of(first + 2 * PANEL, PANEL), PANEL), :]
    trailing_update(a_ref, left_ref, right_ref, first)

    following = jnp.where((lane >= first - PANEL) & (lane < first), 0.0, following)
    for k in range(PANEL):
        row = spread(before, k)
        following = following - lane_gather(row, next_lane) * row
    own = (lane >= first) & (lane < first + PANEL)
    following = jnp.where(own, 0.0, following)

    d = [[None] * PANEL for _ in range(PANEL)]
    at = 0
    for j in range(PANEL):
        for i in range(j, PANEL):
            d[i][j] = d_ref[at]
            at += 1
    q = [None] * PANEL
    weights = [None] * PANEL
    factor = [[None] * PANEL for _ in range(PANEL)]
    middle = None
    for k in range(PANEL):
        scale = lax.rsqrt(d[k][k])
        for i in range(k + 1, PANEL):
            factor[i][k] = d[i][k] * scale
        for i in range(k + 1, PANEL):
            for j in range(k + 1, i + 1):
                d[i][j] = d[i][j] - factor[i][k] * factor[j][k]
        row = spread(panel, k)
        value = jnp.where(own, jnp.where(lane == first + k, -1.0, 0.0), row)
        weight = lane_gather(row, next_lane)
        for j in range(k):
            value = value - factor[k][j] * q[j]
            weight = weight - factor[k][j] * weights[j]
        q[k] = value * scale
        weights[k] = weight * scale
        following = following - weights[k] * q[k]
        if k == PANEL // 2 - 1:
            middle = following
    corrections = [[spread(w, i) for i in range(PANEL)] for w in weights[PANEL // 2 :]]
    store_corner(d_ref, middle, next_first, corrections)

    whole = q[0]
    for k in range(1, PANEL):
        whole = jnp.where(sub == k, q[k], whole)
    high = whole.astype(jnp.bfloat16).astype(jnp.float32)
    rest = whole - high
    middle = rest.astype(jnp.bfloat16).astype(jnp.float32)
    low = rest - middle
    left = jnp.concatenate([high, high, middle, middle, high, low], axis=0)
    right = jnp.concatenate([high, middle, high, middle, low, high], axis=0)
    left_ref[...] = left.astype(jnp.bfloat16)
    right_ref[...] = right.astype(jnp.bfloat16)
    return following, whole


def place_halves(place, pieces, first_row, flat):
    core = lax.axis_index(place.core)
    rows = flat.shape[0] // 2
    for r, piece in enumerate(pieces):
        start = pl.multiple_of(jnp.bitwise_xor(core, r) * rows, PANEL)
        flat[pl.ds(start, rows), :] = piece[first_row : first_row + rows]


def sweep_cost():
    return pl.CostEstimate(flops=1 << 30, bytes_accessed=1 << 20, transcendentals=0)


def load_damped(a_ref, block):
    n = block.shape[0]
    row, col = iotas(block.shape)
    a_ref[:PANEL] = jnp.zeros((PANEL, n), jnp.float32)
    a_ref[PANEL + n :] = jnp.zeros((PANEL, n), jnp.float32)
    a_ref[PANEL : PANEL + n] = block + jnp.where(row == col, DAMP, 0.0)


def sweep_all(works):
    carry = []
    for a_ref, left, right, d_ref in works:
        left[...] = jnp.zeros(left.shape, left.dtype)
        right[...] = jnp.zeros(right.shape, right.dtype)
        panel = a_ref[PANEL : 2 * PANEL]
        store_corner(d_ref, panel, 0, ())
        carry.append((panel, jnp.zeros(panel.shape, jnp.float32)))

    def step(i, carry):
        return tuple(sweep_panel(*work, i, *state) for work, state in zip(works, carry))

    lax.fori_loop(0, LANES // PANEL, step, tuple(carry))
    for a_ref, left, right, _ in works:
        trailing_update(a_ref, left, right, LANES)
    return [-work[0][PANEL : PANEL + LANES] for work in works]


def work_shapes():
    splits = 6 * PANEL
    return [
        pltpu.VMEM((LANES + 2 * PANEL, LANES), jnp.float32),
        pltpu.VMEM((splits, LANES), jnp.bfloat16),
        pltpu.VMEM((splits, LANES), jnp.bfloat16),
        pltpu.VMEM((PANEL * (PANEL + 1) // 2, PANEL, LANES), jnp.float32),
    ]


def early_kernel(
    place, total, mine, other, w11_ref, ninv_ref, corner_ref, last_ref, a_flat, b_flat, *works
):
    place_halves(place, (mine, other), 0, a_flat)
    place_halves(place, (mine, other), a_flat.shape[0] // 2, b_flat)
    n = LANES
    slab = a_flat[n : n + PANEL]
    first, square = unpack_pair(a_flat[:n], jnp.broadcast_to(slab[:1], (n, n)))
    load_damped(works[0], first / total)
    load_damped(works[4], square / total)
    corner_ref[...] = b_flat[:n] / total
    last_ref[...] = unfold(b_flat[n:], jnp.broadcast_to(slab[1:2], (n, n))) / total
    w11_ref[...], ninv_ref[...] = sweep_all((works[:4], works[4:]))


def early(place, pieces, total):
    n = LANES
    return pl.pallas_call(
        functools.partial(early_kernel, place, total),
        in_specs=[VMEM] * 2,
        out_specs=[VMEM] * 4,
        out_shape=[jax.ShapeDtypeStruct((n, n), jnp.float32)] * 4,
        scratch_shapes=[
            pltpu.VMEM((EARLY_ROWS, n), jnp.float32),
            pltpu.VMEM((LATE_ROWS, n), jnp.float32),
            *work_shapes(),
            *work_shapes(),
        ],
        cost_estimate=sweep_cost(),
        compiler_params=PARAMS,
        name="early",
    )(*pieces)


def late_kernel(w11_ref, corner_ref, last_ref, winv, *work):
    n = LANES
    w11 = w11_ref[...]
    corner = corner_ref[...]
    solved = dot(w11, corner)
    load_damped(work[0], last_ref[...] - transposed_dot(corner, solved, HIGHEST))
    (sinv,) = sweep_all((work,))
    cross = dot(solved, sinv)
    winv[:n, :n] = w11 + dot(cross, solved, last=True)
    winv[:n, n:] = -cross
    winv[n:, :n] = -cross.T
    winv[n:, n:] = sinv


def late(w11, corner, last):
    n = LANES
    return pl.pallas_call(
        late_kernel,
        in_specs=[VMEM] * 3,
        out_specs=VMEM,
        out_shape=jax.ShapeDtypeStruct((2 * n, 2 * n), jnp.float32),
        scratch_shapes=work_shapes(),
        cost_estimate=sweep_cost(),
        compiler_params=PARAMS,
        name="late",
    )(w11, corner, last)


def aligned_rows(ref, index, count):
    if count % PANEL == 0:
        return ref[pl.ds(pl.multiple_of(index * count, count), count), :]
    per_slab = PANEL // count
    slab = ref[pl.ds(pl.multiple_of(index // per_slab * PANEL, PANEL), PANEL), :]
    value = slab[:count]
    for i in range(1, per_slab):
        value = jnp.where(index % per_slab == i, slab[i * count : (i + 1) * count], value)
    return value


def packs(cols, rows):
    return cols == 2 * PANEL and 2 * rows == LANES


def product_kernel(place, total, rows, winv, ninv_ref, mine, other, out_ref, flat):
    place_halves(place, (mine, other), 0, flat)
    ninv = ninv_ref[...]
    n = LANES
    inner = jnp.concatenate(
        [
            transposed_dot(flat[c * n : (c + 1) * n] / total, ninv, HIGHEST)
            for c in range(2)
        ],
        axis=0,
    )
    wide = winv.shape[1]
    cols = wide // 2 ** len(place.dp)
    near, second = lax.axis_index(place.near), lax.axis_index(place.second)
    near_stride = 2 ** (len(place.dp) - 2)
    base = place.index(place.dp) - near * near_stride - second * 2
    _, lane = iotas((PANEL, LANES))
    for j in range(4):
        index = base + (j // 2) * near_stride + (j % 2) * 2
        picked = aligned_rows(winv, index, cols)
        update = lax.dot_general(
            picked,
            inner,
            (((1,), (0,)), ((), ())),
            precision=HIGHEST,
            preferred_element_type=jnp.float32,
        )
        for x in range(2):
            block = 2 * j + x
            out_ref[block, :cols] = picked[:, :LANES]
            out_ref[block, cols : 2 * cols] = picked[:, LANES:]
            if packs(cols, rows):
                upper, lower = update[:PANEL], update[PANEL:]
                if x == 0:
                    lower = pltpu.roll(lower, rows, 1)
                else:
                    upper = pltpu.roll(upper, rows, 1)
                out_ref[block, 2 * cols :] = jnp.where(lane < rows, upper, lower)
            else:
                out_ref[block, 2 * cols :] = update


def products(place, winv, ninv, pieces, rows, total):
    wide, narrow = winv.shape[0], ninv.shape[0]
    cols = wide // 2 ** len(place.dp)
    height = 2 * cols + (PANEL if packs(cols, rows) else cols)
    return pl.pallas_call(
        functools.partial(product_kernel, place, total, rows),
        in_specs=[VMEM] * 4,
        out_specs=VMEM,
        out_shape=jax.ShapeDtypeStruct((8, height, LANES), jnp.float32),
        scratch_shapes=[pltpu.VMEM((2 * narrow, LANES), jnp.float32)],
        compiler_params=PARAMS,
        name="products",
    )(winv, ninv, *pieces)


def placing_kernel(place, owner_map, got_ref, kept_ref, update_ref):
    layers = got_ref.shape[0]
    slots, cols, wide = kept_ref.shape
    rows = update_ref.shape[2]
    own, dp = place.index(place.own), place.index(place.dp)
    row, col = iotas((cols, wide))
    empty = jnp.where(col == row + dp * cols, 1.0 / DAMP, 0.0)
    count = jnp.int32(0)
    slot = []
    for l in range(layers):
        mine = owner_map[l] == own
        slot.append(jnp.where(mine, count, -1))
        count = count + mine.astype(jnp.int32)
    for h in range(2):
        lanes = slice(h * LANES, (h + 1) * LANES)
        for c in range(slots):
            value = empty[:, lanes]
            for l in range(layers):
                value = jnp.where(slot[l] == c, got_ref[l, h * cols : (h + 1) * cols], value)
            kept_ref[c, :, lanes] = value
    for l in range(layers):
        value = got_ref[l, 2 * cols :]
        if packs(cols, rows):
            update_ref[l, :PANEL] = value[:, :rows]
            update_ref[l, PANEL:] = value[:, rows:]
        else:
            part = value[:, :rows]
            for p in range(1, LANES // rows):
                part = jnp.where(own == p, value[:, p * rows : (p + 1) * rows], part)
            update_ref[l] = part


def placing(place, owner_map, got, wide, cols, slots, rows):
    layers = got.shape[0]
    return pl.pallas_call(
        functools.partial(placing_kernel, place),
        in_specs=[SMEM, VMEM],
        out_specs=[VMEM, VMEM],
        out_shape=[
            jax.ShapeDtypeStruct((slots, cols, wide), jnp.float32),
            jax.ShapeDtypeStruct((layers, cols, rows), jnp.float32),
        ],
        compiler_params=PARAMS,
        name="placing",
    )(owner_map, got)


def swap(value, axis):
    return lax.ppermute(value, axis, [(0, 1), (1, 0)])


def swap_by_core(value, place, stage):
    pairs = []
    for y in range(2):
        for core in range(2):
            for x in range(2):
                flip = 1 if core == stage else 4
                here = y * 4 + core * 2 + x
                pairs.append((here, here ^ flip))
    return lax.ppermute(value, (place.second, place.core, place.first), pairs)


def after(value, *others):
    return lax.optimization_barrier((value,) + others)[0]


def on_device(place, wide_rows, narrow_rows, owner_map):
    layers, rows, wide = wide_rows.shape
    narrow = narrow_rows.shape[2]
    n_dp, n_own = 2 ** len(place.dp), 2 ** len(place.own)
    total = float(rows * n_dp * n_own)

    s_keep, s_send, wides, narrows = squares(place, wide_rows, narrow_rows)
    s_got = swap(s_send, place.core)
    m_keep, m_send = mixed_sums(place, after(wides, s_send), narrows)
    s_keep, m_send = lax.optimization_barrier((s_keep, m_send))

    s = s_keep + s_got
    s_got = swap_by_core(s[2:], place, 0)
    m_got = swap(after(m_send, s), place.core)

    s = s[:2] + s_got
    s_got = swap_by_core(s[1], place, 1)
    m = after(m_keep, s) + m_got
    m_got = swap_by_core(m[2:], place, 1)

    s = s[0] + s_got
    s_got = swap(s[1], place.near)
    m = after(m[:2], s) + m_got
    m_got = swap_by_core(m[1], place, 0)

    s = s[0] + s_got
    if place.extra:
        s = lax.psum(s, place.extra)
    s_got = swap(s, place.far)
    m = after(m[0], s) + m_got
    m_got = swap(m[1], place.near)

    s = s + s_got
    m = after(m[0], s) + m_got
    if place.extra:
        m = lax.psum(m, place.extra)
    s_got = swap(after(s, m), place.core)
    m_got = swap(m, place.far)

    w11, ninv, corner, last = early(place, [s, s_got], total)
    m = after(m, w11) + m_got
    m_got = swap(m, place.core)
    winv = late(w11, corner, last)
    cols, own_rows = wide // n_dp, narrow // n_own
    sent = products(place, winv, ninv, [m, m_got], own_rows, total)
    got = lax.all_to_all(sent, (place.near, place.second, place.first), 0, 0)
    kept, update = placing(
        place, owner_map, got, wide, cols, layers // n_own + 1, own_rows
    )
    return (jnp.swapaxes(kept, 1, 2), jnp.swapaxes(update, 1, 2))


def solution(mesh):
    n_dp, n_own = mesh.shape["dp"], mesh.shape["own"]
    dp_names = tuple(f"dp{i}" for i in range(int(np.log2(n_dp))))
    own_names = tuple(f"own{i}" for i in range(int(np.log2(n_own))))
    names = dp_names + own_names
    bits = jax.sharding.Mesh(mesh.devices.reshape((2,) * len(names)), names)
    in_specs = (P(None, names, None), P(None, names, None), P())
    out_specs = (P(own_names, None, dp_names), P(None, own_names, dp_names))
    return jax.shard_map(
        functools.partial(on_device, Place(dp_names, own_names)),
        mesh=bits,
        in_specs=in_specs,
        out_specs=out_specs,
        check_vma=False,
    )
```

```python
import functools

import jax
import jax.numpy as jnp
import numpy as np
from jax import lax
from jax.experimental import pallas as pl
from jax.experimental.pallas import tpu as pltpu
from jax.sharding import PartitionSpec as P

DAMP = 0.5
LANES = 128
PANEL = 8
VMEM_LIMIT = 48 * 1024 * 1024
HIGHEST = lax.Precision.HIGHEST
VMEM = pl.BlockSpec(memory_space=pltpu.VMEM)
SMEM = pl.BlockSpec(memory_space=pltpu.SMEM)
HBM = pl.BlockSpec(memory_space=pltpu.HBM)
PARAMS = pltpu.CompilerParams(vmem_limit_bytes=VMEM_LIMIT)


class Place:
    def __init__(self, dp_names, own_names):
        self.dp, self.own = dp_names, own_names
        self.core, self.second, self.near, self.far = (
            dp_names[-1],
            dp_names[-2],
            dp_names[1],
            dp_names[0],
        )
        self.first = own_names[-1]
        used = (self.core, self.second, self.near, self.far, self.first)
        self.extra = tuple(n for n in dp_names + own_names if n not in used)

    def index(self, names):
        value = jnp.int32(0)
        for name in names:
            value = value * 2 + lax.axis_index(name)
        return value

    def layer(self):
        return self.index((self.near, self.second, self.first))


def transposed_dot(a, b, precision=None):
    return lax.dot_general(
        a, b, (((0,), (0,)), ((), ())), precision=precision, preferred_element_type=jnp.float32
    )


AHEAD = 3


def layer_copies(place, sources, buffers, sems):
    layer = place.layer()
    return [
        [
            pltpu.make_async_copy(
                source.at[jnp.bitwise_xor(layer, i)], buffer.at[i], sems.at[i, s]
            )
            for s, (source, buffer) in enumerate(zip(sources, buffers))
        ]
        for i in range(buffers[0].shape[0])
    ]


def both_halves(place, flat, i):
    rows = flat.shape[1] // 2
    core = lax.axis_index(place.core)
    kept = pl.multiple_of(core * rows, PANEL)
    sent = pl.multiple_of((1 - core) * rows, PANEL)
    return flat[i, pl.ds(kept, rows), :], flat[i, pl.ds(sent, rows), :]


def by_core(place, first, second):
    core = lax.axis_index(place.core)
    return jnp.where(core == 0, first, second), jnp.where(core == 0, second, first)


def iotas(shape):
    return (
        lax.broadcasted_iota(jnp.int32, shape, 0),
        lax.broadcasted_iota(jnp.int32, shape, 1),
    )


def pack_pair(first, second):
    row, col = iotas(first.shape)
    return jnp.where(row >= col, first, second)


def unpack_pair(packed, second_diagonal):
    row, col = iotas(packed.shape)
    turned = packed.T
    first = jnp.where(row >= col, packed, turned)
    second = jnp.where(col > row, packed, turned)
    return first, jnp.where(row == col, second_diagonal, second)


def fold(block):
    h = block.shape[0] // 2
    row, col = iotas((h, 2 * h))
    last = pltpu.roll(block[h:], h, 1)
    return jnp.where((col >= h) | (row >= col), block[:h], last)


def unfold(folded, diagonal):
    h, n = folded.shape
    row, col = iotas((n, n))
    block = jnp.concatenate([folded, jnp.zeros((h, n), jnp.float32)], axis=0)
    turned = block.T
    top = jnp.where((col >= h) | (col <= row), block, turned)
    moved = pltpu.roll(pltpu.roll(block, h, 0), h, 1)
    moved_turned = pltpu.roll(pltpu.roll(turned, h, 0), h, 1)
    last = jnp.where(col > row, moved, moved_turned)
    last = jnp.where(row == col, diagonal, last)
    return jnp.where(row < h, top, jnp.where(col < h, turned, last))


def diagonals(blocks, rows):
    n = blocks[0].shape[0]
    row, col = iotas((n, n))
    slab_row, _ = iotas((rows, n))
    slab = jnp.zeros((rows, n), jnp.float32)
    for i, block in enumerate(blocks):
        line = jnp.sum(jnp.where(row == col, block, 0.0), axis=0, keepdims=True)
        slab = jnp.where(slab_row == i, jnp.broadcast_to(line, (rows, n)), slab)
    return slab


EARLY_ROWS = 144
LATE_ROWS = 192


HOT = (1, 2, 3, 5, 6, 7)
COLD = (0, 4)


def square_sums(wide, narrow):
    return transposed_dot(wide, wide), transposed_dot(narrow, narrow)


def pack_layer(place, i, wcov, ncov, a_flat, b_flat):
    n = LANES
    last = wcov[n:, n:]
    a_flat[i, :n] = pack_pair(wcov[:n, :n], ncov)
    a_flat[i, n:] = diagonals((ncov, last), EARLY_ROWS - n)
    b_flat[i, :n] = wcov[:n, n:]
    b_flat[i, n:] = fold(last)
    a_kept, a_sent = both_halves(place, a_flat, i)
    b_kept, b_sent = both_halves(place, b_flat, i)
    return (a_kept, b_kept), (a_sent, b_sent)


def put(ref, index, parts):
    rows = EARLY_ROWS // 2
    ref[*index, :rows] = parts[0]
    ref[*index, rows:] = parts[1]


def hot_kernel(place, wide_hbm, narrow_hbm, keep, send, wides, narrows, a_flat, b_flat, sems):
    copies = layer_copies(place, (wide_hbm, narrow_hbm), (wides, narrows), sems)
    order = HOT + COLD
    for i in order[:AHEAD]:
        for copy in copies[i]:
            copy.start()

    def pack(i, sums):
        kept, sent = pack_layer(place, i, *sums, a_flat, b_flat)
        z, y, x = i // 4, (i // 2) % 2, i % 2
        if x and y:
            mine = other = 1
        else:
            mine, other = by_core(place, 0 if x else 2, 2 if x else 0)
        put(keep, (mine, z), kept)
        put(send, (other, z), sent)

    before = None
    for at, i in enumerate(order):
        for copy in copies[i]:
            copy.wait()
        if at + AHEAD < len(order):
            for copy in copies[order[at + AHEAD]]:
                copy.start()
        if before is not None:
            pack(*before)
            before = None
        if i in HOT:
            before = (i, square_sums(wides[i], narrows[i]))


def cold_kernel(place, wides, narrows, keep, send, a_flat, b_flat):
    for i in COLD:
        sums = square_sums(wides[i], narrows[i])
        kept, sent = pack_layer(place, i, *sums, a_flat, b_flat)
        put(keep, (i // 4,), kept)
        put(send, (i // 4,), sent)


def mixed_kernel(place, wides, narrows, keep, send, flat):
    n = LANES
    for i in range(wides.shape[0]):
        mixed = transposed_dot(narrows[i], wides[i])
        flat[i, :n] = mixed[:, :n]
        flat[i, n:] = mixed[:, n:]
        kept, sent = both_halves(place, flat, i)
        z, y, x = i // 4, (i // 2) % 2, i % 2
        mine, other = by_core(place, y * 2 + x, x * 2 + y)
        keep[mine, z] = kept
        send[other, z] = sent


def gram_cost(wide_rows, columns):
    return pl.CostEstimate(
        flops=2 * wide_rows.size * columns, bytes_accessed=2 * wide_rows.size, transcendentals=0
    )


HALF_ROWS = (EARLY_ROWS + LATE_ROWS) // 2


def pack_shapes(layers):
    return [
        pltpu.VMEM((layers, EARLY_ROWS, LANES), jnp.float32),
        pltpu.VMEM((layers, LATE_ROWS, LANES), jnp.float32),
    ]


def hot_squares(place, wide_rows, narrow_rows):
    layers = wide_rows.shape[0]
    half = jax.ShapeDtypeStruct((3, 2, HALF_ROWS, LANES), jnp.float32)
    return pl.pallas_call(
        functools.partial(hot_kernel, place),
        in_specs=[HBM, HBM],
        out_specs=[VMEM] * 4,
        out_shape=[
            half,
            half,
            jax.ShapeDtypeStruct(wide_rows.shape, wide_rows.dtype),
            jax.ShapeDtypeStruct(narrow_rows.shape, narrow_rows.dtype),
        ],
        scratch_shapes=[*pack_shapes(layers), pltpu.SemaphoreType.DMA((layers, 2))],
        cost_estimate=gram_cost(wide_rows, 240),
        compiler_params=PARAMS,
        name="hot_squares",
    )(
        pltpu.with_memory_space_constraint(wide_rows, pltpu.HBM),
        pltpu.with_memory_space_constraint(narrow_rows, pltpu.HBM),
    )


def cold_squares(place, wides, narrows):
    half = jax.ShapeDtypeStruct((2, HALF_ROWS, LANES), jnp.float32)
    return pl.pallas_call(
        functools.partial(cold_kernel, place),
        in_specs=[VMEM, VMEM],
        out_specs=[VMEM, VMEM],
        out_shape=[half, half],
        scratch_shapes=pack_shapes(wides.shape[0]),
        cost_estimate=gram_cost(wides, 80),
        compiler_params=PARAMS,
        name="cold_squares",
    )(wides, narrows)


def mixed_sums(place, wides, narrows):
    layers, _, narrow = narrows.shape
    half = jax.ShapeDtypeStruct((4, 2, narrow, LANES), jnp.float32)
    return pl.pallas_call(
        functools.partial(mixed_kernel, place),
        in_specs=[VMEM, VMEM],
        out_specs=[VMEM, VMEM],
        out_shape=[half, half],
        scratch_shapes=[pltpu.VMEM((layers, 2 * narrow, LANES), jnp.float32)],
        cost_estimate=gram_cost(wides, 128),
        compiler_params=PARAMS,
        name="mixed",
    )(wides, narrows)


def lane_gather(x, index):
    return jnp.take_along_axis(x, index, axis=1, mode="promise_in_bounds")


def trailing_update(a_ref, left_ref, right_ref, base):
    size = a_ref.shape[1]
    a_ref[pl.ds(pl.multiple_of(base, PANEL), PANEL), :] = jnp.zeros((PANEL, size), jnp.float32)
    lane = lax.broadcasted_iota(jnp.int32, (1, size), 1)
    swept = (lane >= base - PANEL) & (lane < base)
    update = transposed_dot(left_ref[...], right_ref[...])
    a_ref[PANEL : PANEL + size, :] = (
        jnp.where(swept, 0.0, a_ref[PANEL : PANEL + size, :]) - update
    )


def sweep_panel(a_ref, left_ref, right_ref, tile, step, panel):
    size = a_ref.shape[1]
    tiles = size // LANES
    first = step * PANEL
    base = tile * LANES + first
    trailing_update(a_ref, left_ref, right_ref, base)

    shape = (PANEL, LANES)
    sub = lax.broadcasted_iota(jnp.int32, shape, 0)
    lane = lax.broadcasted_iota(jnp.int32, shape, 1)
    parts = [panel[:, LANES * t : LANES * (t + 1)] for t in range(tiles)]
    rows = [
        [jnp.broadcast_to(part[k : k + 1, :], shape) for part in parts] for k in range(PANEL)
    ]
    index = [jnp.full(shape, 0, jnp.int32) + (first + i) for i in range(PANEL)]
    d = [[None] * PANEL for _ in range(PANEL)]
    for j in range(PANEL):
        for i in range(j, PANEL):
            d[i][j] = lane_gather(rows[j][tile], index[i])
    own = (lane >= first) & (lane < first + PANEL)
    last = first == LANES - PANEL
    next_lane = jnp.where(last, 0, first + PANEL) + sub
    q = [[None] * tiles for _ in range(PANEL)]
    weights = [None] * PANEL
    factor = [[None] * PANEL for _ in range(PANEL)]
    for k in range(PANEL):
        scale = lax.rsqrt(d[k][k])
        for i in range(k + 1, PANEL):
            factor[i][k] = d[i][k] * scale
        for i in range(k + 1, PANEL):
            for j in range(k + 1, i + 1):
                d[i][j] = d[i][j] - factor[i][k] * factor[j][k]
        for t in range(tiles):
            value = rows[k][t]
            if t == tile:
                value = jnp.where(own, jnp.where(lane == first + k, -1.0, 0.0), value)
            for j in range(k):
                value = value - factor[k][j] * q[j][t]
            q[k][t] = value * scale
        source = rows[k][tile]
        if tile + 1 < tiles:
            source = jnp.where(last, rows[k][tile + 1], source)
        value = lane_gather(source, next_lane)
        for j in range(k):
            value = value - factor[k][j] * weights[j]
        weights[k] = value * scale

    packed = []
    for t in range(tiles):
        value = q[0][t]
        for k in range(1, PANEL):
            value = jnp.where(sub == k, q[k][t], value)
        packed.append(value)
    whole = jnp.concatenate(packed, axis=1) if tiles > 1 else packed[0]
    high = whole.astype(jnp.bfloat16).astype(jnp.float32)
    rest = whole - high
    middle = rest.astype(jnp.bfloat16).astype(jnp.float32)
    low = rest - middle
    left = jnp.concatenate([high, high, middle, middle, high, low], axis=0)
    right = jnp.concatenate([high, middle, high, middle, low, high], axis=0)
    left_ref[...] = left.astype(jnp.bfloat16)
    right_ref[...] = right.astype(jnp.bfloat16)

    after = pl.multiple_of(base + 2 * PANEL, PANEL)
    following = a_ref[pl.ds(after, PANEL), :]
    result = []
    for t in range(tiles):
        value = following[:, LANES * t : LANES * (t + 1)]
        if t == tile:
            value = jnp.where(own, 0.0, value)
        for k in range(PANEL):
            value = value - weights[k] * q[k][t]
        result.append(value)
    return jnp.concatenate(result, axis=1) if tiles > 1 else result[0]


def place_halves(place, pieces, first_row, flat):
    core = lax.axis_index(place.core)
    rows = flat.shape[0] // 2
    for r, piece in enumerate(pieces):
        start = pl.multiple_of(jnp.bitwise_xor(core, r) * rows, PANEL)
        flat[pl.ds(start, rows), :] = piece[first_row : first_row + rows]


def sweep_cost():
    return pl.CostEstimate(flops=1 << 30, bytes_accessed=1 << 20, transcendentals=0)


def clear(work):
    a_ref, left, right = work
    size = a_ref.shape[1]
    a_ref[:PANEL] = jnp.zeros((PANEL, size), jnp.float32)
    a_ref[PANEL + size :] = jnp.zeros((PANEL, size), jnp.float32)
    left[...] = jnp.zeros(left.shape, left.dtype)
    right[...] = jnp.zeros(right.shape, right.dtype)


def work_shapes(size):
    splits = 6 * PANEL
    return [
        pltpu.VMEM((size + 2 * PANEL, size), jnp.float32),
        pltpu.VMEM((splits, size), jnp.bfloat16),
        pltpu.VMEM((splits, size), jnp.bfloat16),
    ]


def aligned_rows(ref, index, count):
    if count % PANEL == 0:
        return ref[pl.ds(pl.multiple_of(index * count, count), count), :]
    per_slab = PANEL // count
    slab = ref[pl.ds(pl.multiple_of(index // per_slab * PANEL, PANEL), PANEL), :]
    value = slab[:count]
    for i in range(1, per_slab):
        value = jnp.where(index % per_slab == i, slab[i * count : (i + 1) * count], value)
    return value


def packs(cols, rows):
    return cols == 2 * PANEL and 2 * rows == LANES


def dot(a, b, last=False):
    return lax.dot_general(
        a,
        b,
        (((1,), (1 if last else 0,)), ((), ())),
        precision=HIGHEST,
        preferred_element_type=jnp.float32,
    )


STEPS = LANES // PANEL


def first_half_kernel(place, total, mine, other, ninv_ref, wa, wl, wr, panel_ref, *refs):
    a_flat, b_flat, na, nl, nr = refs
    wide_work, narrow_work = (wa, wl, wr), (na, nl, nr)
    place_halves(place, (mine, other), 0, a_flat)
    place_halves(place, (mine, other), a_flat.shape[0] // 2, b_flat)
    n = LANES
    slab = a_flat[n : n + PANEL]
    first, square = unpack_pair(a_flat[:n], jnp.broadcast_to(slab[:1], (n, n)))
    corner = b_flat[:n] / total
    last = unfold(b_flat[n:], jnp.broadcast_to(slab[1:2], (n, n)))
    row, col = iotas((n, n))
    damp = jnp.where(row == col, DAMP, 0.0)
    clear(wide_work)
    clear(narrow_work)
    wa[PANEL : PANEL + n, :n] = first / total + damp
    wa[PANEL : PANEL + n, n:] = corner
    wa[PANEL + n : PANEL + 2 * n, :n] = corner.T
    wa[PANEL + n : PANEL + 2 * n, n:] = last / total + damp
    na[PANEL : PANEL + n, :] = square / total + damp

    def step(i, panels):
        return (
            sweep_panel(*wide_work, 0, i, panels[0]),
            sweep_panel(*narrow_work, 0, i, panels[1]),
        )

    start = (wa[PANEL : 2 * PANEL, :], na[PANEL : 2 * PANEL, :])
    panel_ref[...], _ = lax.fori_loop(0, STEPS, step, start)
    trailing_update(*narrow_work, n)
    ninv_ref[...] = -na[PANEL : PANEL + n, :]


def first_half(place, pieces, wide, narrow, total):
    matrix, left, right = work_shapes(wide)
    shapes = [jax.ShapeDtypeStruct((narrow, narrow), jnp.float32)]
    shapes += [jax.ShapeDtypeStruct(v.shape, v.dtype) for v in (matrix, left, right)]
    shapes += [jax.ShapeDtypeStruct((PANEL, wide), jnp.float32)]
    return pl.pallas_call(
        functools.partial(first_half_kernel, place, total),
        in_specs=[VMEM] * 2,
        out_specs=[VMEM] * 5,
        out_shape=shapes,
        scratch_shapes=[
            pltpu.VMEM((EARLY_ROWS, LANES), jnp.float32),
            pltpu.VMEM((LATE_ROWS, LANES), jnp.float32),
            *work_shapes(narrow),
        ],
        cost_estimate=sweep_cost(),
        compiler_params=PARAMS,
        name="first_half",
    )(*pieces)


def second_half_kernel(wa_in, wl_in, wr_in, panel_in, winv, wa, wl, wr):
    wa[...] = wa_in[...]
    wl[...] = wl_in[...]
    wr[...] = wr_in[...]
    wide = wa.shape[1]

    def step(i, panel):
        return sweep_panel(wa, wl, wr, 1, i, panel)

    lax.fori_loop(0, STEPS, step, panel_in[...])
    trailing_update(wa, wl, wr, wide)
    winv[...] = -wa[PANEL : PANEL + wide, :]


def second_half(state):
    wide = state[0].shape[1]
    return pl.pallas_call(
        second_half_kernel,
        in_specs=[VMEM] * 4,
        out_specs=VMEM,
        out_shape=jax.ShapeDtypeStruct((wide, wide), jnp.float32),
        scratch_shapes=work_shapes(wide),
        cost_estimate=sweep_cost(),
        compiler_params=PARAMS,
        name="second_half",
    )(*state)


def product_kernel(place, total, rows, winv, ninv_ref, mine, other, out_ref, flat):
    place_halves(place, (mine, other), 0, flat)
    ninv = ninv_ref[...]
    n = LANES
    inner = jnp.concatenate(
        [
            transposed_dot(flat[c * n : (c + 1) * n] / total, ninv, HIGHEST)
            for c in range(2)
        ],
        axis=0,
    )
    wide = winv.shape[1]
    cols = wide // 2 ** len(place.dp)
    near, second = lax.axis_index(place.near), lax.axis_index(place.second)
    near_stride = 2 ** (len(place.dp) - 2)
    base = place.index(place.dp) - near * near_stride - second * 2
    _, lane = iotas((PANEL, LANES))
    for j in range(4):
        index = base + (j // 2) * near_stride + (j % 2) * 2
        picked = aligned_rows(winv, index, cols)
        update = lax.dot_general(
            picked,
            inner,
            (((1,), (0,)), ((), ())),
            precision=HIGHEST,
            preferred_element_type=jnp.float32,
        )
        for x in range(2):
            block = 2 * j + x
            out_ref[block, :cols] = picked[:, :LANES]
            out_ref[block, cols : 2 * cols] = picked[:, LANES:]
            if packs(cols, rows):
                upper, lower = update[:PANEL], update[PANEL:]
                if x == 0:
                    lower = pltpu.roll(lower, rows, 1)
                else:
                    upper = pltpu.roll(upper, rows, 1)
                out_ref[block, 2 * cols :] = jnp.where(lane < rows, upper, lower)
            else:
                out_ref[block, 2 * cols :] = update


def products(place, winv, ninv, pieces, rows, total):
    wide, narrow = winv.shape[0], ninv.shape[0]
    cols = wide // 2 ** len(place.dp)
    height = 2 * cols + (PANEL if packs(cols, rows) else cols)
    return pl.pallas_call(
        functools.partial(product_kernel, place, total, rows),
        in_specs=[VMEM] * 4,
        out_specs=VMEM,
        out_shape=jax.ShapeDtypeStruct((8, height, LANES), jnp.float32),
        scratch_shapes=[pltpu.VMEM((2 * narrow, LANES), jnp.float32)],
        compiler_params=PARAMS,
        name="products",
    )(winv, ninv, *pieces)


def placing_kernel(place, owner_map, got_ref, kept_ref, update_ref):
    layers = got_ref.shape[0]
    slots, cols, wide = kept_ref.shape
    rows = update_ref.shape[2]
    own, dp = place.index(place.own), place.index(place.dp)
    row, col = iotas((cols, wide))
    empty = jnp.where(col == row + dp * cols, 1.0 / DAMP, 0.0)
    count = jnp.int32(0)
    slot = []
    for l in range(layers):
        mine = owner_map[l] == own
        slot.append(jnp.where(mine, count, -1))
        count = count + mine.astype(jnp.int32)
    for h in range(2):
        lanes = slice(h * LANES, (h + 1) * LANES)
        for c in range(slots):
            value = empty[:, lanes]
            for l in range(layers):
                value = jnp.where(slot[l] == c, got_ref[l, h * cols : (h + 1) * cols], value)
            kept_ref[c, :, lanes] = value
    for l in range(layers):
        value = got_ref[l, 2 * cols :]
        if packs(cols, rows):
            update_ref[l, :PANEL] = value[:, :rows]
            update_ref[l, PANEL:] = value[:, rows:]
        else:
            part = value[:, :rows]
            for p in range(1, LANES // rows):
                part = jnp.where(own == p, value[:, p * rows : (p + 1) * rows], part)
            update_ref[l] = part


def placing(place, owner_map, got, wide, cols, slots, rows):
    layers = got.shape[0]
    return pl.pallas_call(
        functools.partial(placing_kernel, place),
        in_specs=[SMEM, VMEM],
        out_specs=[VMEM, VMEM],
        out_shape=[
            jax.ShapeDtypeStruct((slots, cols, wide), jnp.float32),
            jax.ShapeDtypeStruct((layers, cols, rows), jnp.float32),
        ],
        compiler_params=PARAMS,
        name="placing",
    )(owner_map, got)


def swap(value, axis):
    return lax.ppermute(value, axis, [(0, 1), (1, 0)])


def swap_by_core(value, place, stage):
    pairs = []
    for y in range(2):
        for core in range(2):
            for x in range(2):
                flip = 1 if core == stage else 4
                here = y * 4 + core * 2 + x
                pairs.append((here, here ^ flip))
    return lax.ppermute(value, (place.second, place.core, place.first), pairs)


def after(value, *others):
    return lax.optimization_barrier((value,) + others)[0]


def on_device(place, wide_rows, narrow_rows, owner_map):
    layers, rows, wide = wide_rows.shape
    narrow = narrow_rows.shape[2]
    n_dp, n_own = 2 ** len(place.dp), 2 ** len(place.own)
    total = float(rows * n_dp * n_own)

    h_keep, h_send, wides, narrows = hot_squares(place, wide_rows, narrow_rows)
    h_got = swap(h_send[:2], place.core)
    c_keep, c_send = cold_squares(place, after(wides, h_send), narrows)
    h_keep, c_send = lax.optimization_barrier((h_keep, c_send))

    hot = h_keep[:2] + h_got
    s_got = swap_by_core(hot, place, 0)
    c_got = swap(after(jnp.stack([c_send, h_send[2]]), hot), place.core)
    m_keep, m_send = mixed_sums(place, after(wides, hot), narrows)
    m_got = swap(m_send, place.core)
    s = jnp.stack([c_keep, h_keep[2]]) + after(c_got, m_send)

    s = s + s_got
    s_got = swap_by_core(s[1], place, 1)
    m = after(m_keep, s) + m_got
    m_got = swap_by_core(m[2:], place, 1)

    s = s[0] + s_got
    s_got = swap(s[1], place.near)
    m = after(m[:2], s) + m_got
    m_got = swap_by_core(m[1], place, 0)

    s = s[0] + s_got
    if place.extra:
        s = lax.psum(s, place.extra)
    s_got = swap(s, place.far)
    m = after(m[0], s) + m_got
    m_got = swap(m[1], place.near)

    s = s + s_got
    m = after(m[0], s) + m_got
    if place.extra:
        m = lax.psum(m, place.extra)
    s_got = swap(after(s, m), place.core)
    m_got = swap(m, place.far)

    ninv, *state = first_half(place, [s, s_got], wide, narrow, total)
    m = after(m, ninv) + m_got
    m_got = swap(m, place.core)
    winv = second_half(state)
    cols, own_rows = wide // n_dp, narrow // n_own
    sent = products(place, winv, ninv, [m, m_got], own_rows, total)
    got = lax.all_to_all(sent, (place.near, place.second, place.first), 0, 0)
    kept, update = placing(
        place, owner_map, got, wide, cols, layers // n_own + 1, own_rows
    )
    return (jnp.swapaxes(kept, 1, 2), jnp.swapaxes(update, 1, 2))


def solution(mesh):
    n_dp, n_own = mesh.shape["dp"], mesh.shape["own"]
    dp_names = tuple(f"dp{i}" for i in range(int(np.log2(n_dp))))
    own_names = tuple(f"own{i}" for i in range(int(np.log2(n_own))))
    names = dp_names + own_names
    bits = jax.sharding.Mesh(mesh.devices.reshape((2,) * len(names)), names)
    in_specs = (P(None, names, None), P(None, names, None), P())
    out_specs = (P(own_names, None, dp_names), P(None, own_names, dp_names))
    return jax.shard_map(
        functools.partial(on_device, Place(dp_names, own_names)),
        mesh=bits,
        in_specs=in_specs,
        out_specs=out_specs,
        check_vma=False,
    )
```

```python
import functools

import jax
import jax.numpy as jnp
import numpy as np
from jax import lax
from jax.experimental import pallas as pl
from jax.experimental.pallas import tpu as pltpu
from jax.sharding import PartitionSpec as P

DAMP = 0.5
LANES = 128
PANEL = 8
VMEM_LIMIT = 48 * 1024 * 1024
HIGHEST = lax.Precision.HIGHEST
VMEM = pl.BlockSpec(memory_space=pltpu.VMEM)
SMEM = pl.BlockSpec(memory_space=pltpu.SMEM)
HBM = pl.BlockSpec(memory_space=pltpu.HBM)
PARAMS = pltpu.CompilerParams(vmem_limit_bytes=VMEM_LIMIT)


class Place:
    def __init__(self, dp_names, own_names):
        self.dp, self.own = dp_names, own_names
        self.core, self.second, self.near, self.far = (
            dp_names[-1],
            dp_names[-2],
            dp_names[1],
            dp_names[0],
        )
        self.first = own_names[-1]
        used = (self.core, self.second, self.near, self.far, self.first)
        self.extra = tuple(n for n in dp_names + own_names if n not in used)

    def index(self, names):
        value = jnp.int32(0)
        for name in names:
            value = value * 2 + lax.axis_index(name)
        return value

    def layer(self):
        return self.index((self.near, self.second, self.first))


def transposed_dot(a, b, precision=None):
    return lax.dot_general(
        a, b, (((0,), (0,)), ((), ())), precision=precision, preferred_element_type=jnp.float32
    )


AHEAD = 8


def layer_copies(place, sources, buffers, sems):
    layer = place.layer()
    return [
        [
            pltpu.make_async_copy(
                source.at[jnp.bitwise_xor(layer, i)], buffer.at[i], sems.at[i, s]
            )
            for s, (source, buffer) in enumerate(zip(sources, buffers))
        ]
        for i in range(buffers[0].shape[0])
    ]


def both_halves(place, flat, i):
    rows = flat.shape[1] // 2
    core = lax.axis_index(place.core)
    kept = pl.multiple_of(core * rows, PANEL)
    sent = pl.multiple_of((1 - core) * rows, PANEL)
    return flat[i, pl.ds(kept, rows), :], flat[i, pl.ds(sent, rows), :]


def by_core(place, first, second):
    core = lax.axis_index(place.core)
    return jnp.where(core == 0, first, second), jnp.where(core == 0, second, first)


def iotas(shape):
    return (
        lax.broadcasted_iota(jnp.int32, shape, 0),
        lax.broadcasted_iota(jnp.int32, shape, 1),
    )


def pack_pair(first, second):
    row, col = iotas(first.shape)
    return jnp.where(row >= col, first, second)


def unpack_pair(packed, second_diagonal):
    row, col = iotas(packed.shape)
    turned = packed.T
    first = jnp.where(row >= col, packed, turned)
    second = jnp.where(col > row, packed, turned)
    return first, jnp.where(row == col, second_diagonal, second)


def fold(block):
    h = block.shape[0] // 2
    row, col = iotas((h, 2 * h))
    last = pltpu.roll(block[h:], h, 1)
    return jnp.where((col >= h) | (row >= col), block[:h], last)


def unfold(folded, diagonal):
    h, n = folded.shape
    row, col = iotas((n, n))
    block = jnp.concatenate([folded, jnp.zeros((h, n), jnp.float32)], axis=0)
    turned = block.T
    top = jnp.where((col >= h) | (col <= row), block, turned)
    moved = pltpu.roll(pltpu.roll(block, h, 0), h, 1)
    moved_turned = pltpu.roll(pltpu.roll(turned, h, 0), h, 1)
    last = jnp.where(col > row, moved, moved_turned)
    last = jnp.where(row == col, diagonal, last)
    return jnp.where(row < h, top, jnp.where(col < h, turned, last))


def diagonals(blocks, rows):
    n = blocks[0].shape[0]
    row, col = iotas((n, n))
    slab_row, _ = iotas((rows, n))
    slab = jnp.zeros((rows, n), jnp.float32)
    for i, block in enumerate(blocks):
        line = jnp.sum(jnp.where(row == col, block, 0.0), axis=0, keepdims=True)
        slab = jnp.where(slab_row == i, jnp.broadcast_to(line, (rows, n)), slab)
    return slab


EARLY_ROWS = 144
LATE_ROWS = 192


HOT = (1, 2, 3, 5, 6, 7)
COLD = (0, 4)


def square_sums(wide, narrow):
    return transposed_dot(wide, wide), transposed_dot(narrow, narrow)


def pack_layer(place, i, wcov, ncov, a_flat, b_flat):
    n = LANES
    last = wcov[n:, n:]
    a_flat[i, :n] = pack_pair(wcov[:n, :n], ncov)
    a_flat[i, n:] = diagonals((ncov, last), EARLY_ROWS - n)
    b_flat[i, :n] = wcov[:n, n:]
    b_flat[i, n:] = fold(last)
    a_kept, a_sent = both_halves(place, a_flat, i)
    b_kept, b_sent = both_halves(place, b_flat, i)
    return (a_kept, b_kept), (a_sent, b_sent)


def put(ref, index, parts):
    rows = EARLY_ROWS // 2
    ref[*index, :rows] = parts[0]
    ref[*index, rows:] = parts[1]


def hot_kernel(place, wide_hbm, narrow_hbm, keep, send, wides, narrows, a_flat, b_flat, sems):
    copies = layer_copies(place, (wide_hbm, narrow_hbm), (wides, narrows), sems)
    order = HOT + COLD
    for i in order[:AHEAD]:
        for copy in copies[i]:
            copy.start()

    def pack(i, sums):
        kept, sent = pack_layer(place, i, *sums, a_flat, b_flat)
        z, y, x = i // 4, (i // 2) % 2, i % 2
        if x and y:
            mine = other = 1
        else:
            mine, other = by_core(place, 0 if x else 2, 2 if x else 0)
        put(keep, (mine, z), kept)
        put(send, (other, z), sent)

    before = None
    for at, i in enumerate(order):
        for copy in copies[i]:
            copy.wait()
        if at + AHEAD < len(order):
            for copy in copies[order[at + AHEAD]]:
                copy.start()
        if before is not None:
            pack(*before)
            before = None
        if i in HOT:
            before = (i, square_sums(wides[i], narrows[i]))


def cold_kernel(place, wides, narrows, keep, send, a_flat, b_flat):
    for i in COLD:
        sums = square_sums(wides[i], narrows[i])
        kept, sent = pack_layer(place, i, *sums, a_flat, b_flat)
        put(keep, (i // 4,), kept)
        put(send, (i // 4,), sent)


def mixed_kernel(place, wides, narrows, keep, send, flat):
    n = LANES
    for i in range(wides.shape[0]):
        mixed = transposed_dot(narrows[i], wides[i])
        flat[i, :n] = mixed[:, :n]
        flat[i, n:] = mixed[:, n:]
        kept, sent = both_halves(place, flat, i)
        z, y, x = i // 4, (i // 2) % 2, i % 2
        mine, other = by_core(place, y * 2 + x, x * 2 + y)
        keep[mine, z] = kept
        send[other, z] = sent


def gram_cost(wide_rows, columns):
    return pl.CostEstimate(
        flops=2 * wide_rows.size * columns, bytes_accessed=2 * wide_rows.size, transcendentals=0
    )


HALF_ROWS = (EARLY_ROWS + LATE_ROWS) // 2


def pack_shapes(layers):
    return [
        pltpu.VMEM((layers, EARLY_ROWS, LANES), jnp.float32),
        pltpu.VMEM((layers, LATE_ROWS, LANES), jnp.float32),
    ]


def hot_squares(place, wide_rows, narrow_rows):
    layers = wide_rows.shape[0]
    half = jax.ShapeDtypeStruct((3, 2, HALF_ROWS, LANES), jnp.float32)
    return pl.pallas_call(
        functools.partial(hot_kernel, place),
        in_specs=[HBM, HBM],
        out_specs=[VMEM] * 4,
        out_shape=[
            half,
            half,
            jax.ShapeDtypeStruct(wide_rows.shape, wide_rows.dtype),
            jax.ShapeDtypeStruct(narrow_rows.shape, narrow_rows.dtype),
        ],
        scratch_shapes=[*pack_shapes(layers), pltpu.SemaphoreType.DMA((layers, 2))],
        cost_estimate=gram_cost(wide_rows, 240),
        compiler_params=PARAMS,
        name="hot_squares",
    )(
        pltpu.with_memory_space_constraint(wide_rows, pltpu.HBM),
        pltpu.with_memory_space_constraint(narrow_rows, pltpu.HBM),
    )


def cold_squares(place, wides, narrows):
    half = jax.ShapeDtypeStruct((2, HALF_ROWS, LANES), jnp.float32)
    return pl.pallas_call(
        functools.partial(cold_kernel, place),
        in_specs=[VMEM, VMEM],
        out_specs=[VMEM, VMEM],
        out_shape=[half, half],
        scratch_shapes=pack_shapes(wides.shape[0]),
        cost_estimate=gram_cost(wides, 80),
        compiler_params=PARAMS,
        name="cold_squares",
    )(wides, narrows)


def mixed_sums(place, wides, narrows):
    layers, _, narrow = narrows.shape
    half = jax.ShapeDtypeStruct((4, 2, narrow, LANES), jnp.float32)
    return pl.pallas_call(
        functools.partial(mixed_kernel, place),
        in_specs=[VMEM, VMEM],
        out_specs=[VMEM, VMEM],
        out_shape=[half, half],
        scratch_shapes=[pltpu.VMEM((layers, 2 * narrow, LANES), jnp.float32)],
        cost_estimate=gram_cost(wides, 128),
        compiler_params=PARAMS,
        name="mixed",
    )(wides, narrows)


def lane_gather(x, index):
    return jnp.take_along_axis(x, index, axis=1, mode="promise_in_bounds")


def trailing_update(a_ref, left_ref, right_ref, base):
    size = a_ref.shape[1]
    a_ref[pl.ds(pl.multiple_of(base, PANEL), PANEL), :] = jnp.zeros((PANEL, size), jnp.float32)
    lane = lax.broadcasted_iota(jnp.int32, (1, size), 1)
    swept = (lane >= base - PANEL) & (lane < base)
    update = transposed_dot(left_ref[...], right_ref[...])
    a_ref[PANEL : PANEL + size, :] = (
        jnp.where(swept, 0.0, a_ref[PANEL : PANEL + size, :]) - update
    )


def sweep_panel(a_ref, left_ref, right_ref, tile, step, panel):
    size = a_ref.shape[1]
    tiles = size // LANES
    first = step * PANEL
    base = tile * LANES + first
    trailing_update(a_ref, left_ref, right_ref, base)

    shape = (PANEL, LANES)
    sub = lax.broadcasted_iota(jnp.int32, shape, 0)
    lane = lax.broadcasted_iota(jnp.int32, shape, 1)
    parts = [panel[:, LANES * t : LANES * (t + 1)] for t in range(tiles)]
    rows = [
        [jnp.broadcast_to(part[k : k + 1, :], shape) for part in parts] for k in range(PANEL)
    ]
    index = [jnp.full(shape, 0, jnp.int32) + (first + i) for i in range(PANEL)]
    d = [[None] * PANEL for _ in range(PANEL)]
    for j in range(PANEL):
        for i in range(j, PANEL):
            d[i][j] = lane_gather(rows[j][tile], index[i])
    own = (lane >= first) & (lane < first + PANEL)
    last = first == LANES - PANEL
    next_lane = jnp.where(last, 0, first + PANEL) + sub
    q = [[None] * tiles for _ in range(PANEL)]
    weights = [None] * PANEL
    factor = [[None] * PANEL for _ in range(PANEL)]
    for k in range(PANEL):
        scale = lax.rsqrt(d[k][k])
        for i in range(k + 1, PANEL):
            factor[i][k] = d[i][k] * scale
        for i in range(k + 1, PANEL):
            for j in range(k + 1, i + 1):
                d[i][j] = d[i][j] - factor[i][k] * factor[j][k]
        for t in range(tiles):
            value = rows[k][t]
            if t == tile:
                value = jnp.where(own, jnp.where(lane == first + k, -1.0, 0.0), value)
            for j in range(k):
                value = value - factor[k][j] * q[j][t]
            q[k][t] = value * scale
        source = rows[k][tile]
        if tile + 1 < tiles:
            source = jnp.where(last, rows[k][tile + 1], source)
        value = lane_gather(source, next_lane)
        for j in range(k):
            value = value - factor[k][j] * weights[j]
        weights[k] = value * scale

    packed = []
    for t in range(tiles):
        value = q[0][t]
        for k in range(1, PANEL):
            value = jnp.where(sub == k, q[k][t], value)
        packed.append(value)
    whole = jnp.concatenate(packed, axis=1) if tiles > 1 else packed[0]
    high = whole.astype(jnp.bfloat16).astype(jnp.float32)
    rest = whole - high
    middle = rest.astype(jnp.bfloat16).astype(jnp.float32)
    low = rest - middle
    left = jnp.concatenate([high, high, middle, middle, high, low], axis=0)
    right = jnp.concatenate([high, middle, high, middle, low, high], axis=0)
    left_ref[...] = left.astype(jnp.bfloat16)
    right_ref[...] = right.astype(jnp.bfloat16)

    after = pl.multiple_of(base + 2 * PANEL, PANEL)
    following = a_ref[pl.ds(after, PANEL), :]
    result = []
    for t in range(tiles):
        value = following[:, LANES * t : LANES * (t + 1)]
        if t == tile:
            value = jnp.where(own, 0.0, value)
        for k in range(PANEL):
            value = value - weights[k] * q[k][t]
        result.append(value)
    return jnp.concatenate(result, axis=1) if tiles > 1 else result[0]


def place_halves(place, pieces, first_row, flat):
    core = lax.axis_index(place.core)
    rows = flat.shape[0] // 2
    for r, piece in enumerate(pieces):
        start = pl.multiple_of(jnp.bitwise_xor(core, r) * rows, PANEL)
        flat[pl.ds(start, rows), :] = piece[first_row : first_row + rows]


def sweep_cost():
    return pl.CostEstimate(flops=1 << 30, bytes_accessed=1 << 20, transcendentals=0)


def clear(work):
    a_ref, left, right = work
    size = a_ref.shape[1]
    a_ref[:PANEL] = jnp.zeros((PANEL, size), jnp.float32)
    a_ref[PANEL + size :] = jnp.zeros((PANEL, size), jnp.float32)
    left[...] = jnp.zeros(left.shape, left.dtype)
    right[...] = jnp.zeros(right.shape, right.dtype)


def work_shapes(size):
    splits = 6 * PANEL
    return [
        pltpu.VMEM((size + 2 * PANEL, size), jnp.float32),
        pltpu.VMEM((splits, size), jnp.bfloat16),
        pltpu.VMEM((splits, size), jnp.bfloat16),
    ]


def aligned_rows(ref, index, count):
    if count % PANEL == 0:
        return ref[pl.ds(pl.multiple_of(index * count, count), count), :]
    per_slab = PANEL // count
    slab = ref[pl.ds(pl.multiple_of(index // per_slab * PANEL, PANEL), PANEL), :]
    value = slab[:count]
    for i in range(1, per_slab):
        value = jnp.where(index % per_slab == i, slab[i * count : (i + 1) * count], value)
    return value


def packs(cols, rows):
    return cols == 2 * PANEL and 2 * rows == LANES


def dot(a, b, last=False):
    return lax.dot_general(
        a,
        b,
        (((1,), (1 if last else 0,)), ((), ())),
        precision=HIGHEST,
        preferred_element_type=jnp.float32,
    )


STEPS = LANES // PANEL
FIRST_STEPS = 10
SECOND_STEPS = 10


def sweep_both(wide_work, narrow_work, begin, end, panels):
    def step(i, panels):
        return (
            sweep_panel(*wide_work, 0, i, panels[0]),
            sweep_panel(*narrow_work, 0, i, panels[1]),
        )

    return lax.fori_loop(begin, end, step, panels)


def sweep_wide(work, begin, end, panel):
    return lax.fori_loop(begin, end, lambda i, panel: sweep_panel(*work, 1, i, panel), panel)


def first_kernel(place, total, mine, other, wa, wl, wr, wp, na, nl, nr, np_, a_flat, b_flat):
    wide_work, narrow_work = (wa, wl, wr), (na, nl, nr)
    place_halves(place, (mine, other), 0, a_flat)
    place_halves(place, (mine, other), a_flat.shape[0] // 2, b_flat)
    n = LANES
    slab = a_flat[n : n + PANEL]
    first, square = unpack_pair(a_flat[:n], jnp.broadcast_to(slab[:1], (n, n)))
    corner = b_flat[:n] / total
    last = unfold(b_flat[n:], jnp.broadcast_to(slab[1:2], (n, n)))
    row, col = iotas((n, n))
    damp = jnp.where(row == col, DAMP, 0.0)
    clear(wide_work)
    clear(narrow_work)
    wa[PANEL : PANEL + n, :n] = first / total + damp
    wa[PANEL : PANEL + n, n:] = corner
    wa[PANEL + n : PANEL + 2 * n, :n] = corner.T
    wa[PANEL + n : PANEL + 2 * n, n:] = last / total + damp
    na[PANEL : PANEL + n, :] = square / total + damp
    start = (wa[PANEL : 2 * PANEL, :], na[PANEL : 2 * PANEL, :])
    wp[...], np_[...] = sweep_both(wide_work, narrow_work, 0, FIRST_STEPS, start)


def second_kernel(*refs):
    given, ninv_ref, state, narrow_work = refs[:8], refs[8], refs[9:13], refs[13:]
    wide_work, wp = state[:3], state[3]
    for source, target in zip(given, (*wide_work, None, *narrow_work)):
        if target is not None:
            target[...] = source[...]
    panels = (given[3][...], given[7][...])
    panel, _ = sweep_both(wide_work, narrow_work, FIRST_STEPS, STEPS, panels)
    trailing_update(*narrow_work, LANES)
    ninv_ref[...] = -narrow_work[0][PANEL : PANEL + LANES, :]
    wp[...] = sweep_wide(wide_work, 0, SECOND_STEPS, panel)


def third_kernel(wa_in, wl_in, wr_in, panel_in, winv, wa, wl, wr):
    wa[...] = wa_in[...]
    wl[...] = wl_in[...]
    wr[...] = wr_in[...]
    sweep_wide((wa, wl, wr), SECOND_STEPS, STEPS, panel_in[...])
    wide = wa.shape[1]
    trailing_update(wa, wl, wr, wide)
    winv[...] = -wa[PANEL : PANEL + wide, :]


def state_shapes(size):
    shapes = [jax.ShapeDtypeStruct(v.shape, v.dtype) for v in work_shapes(size)]
    return shapes + [jax.ShapeDtypeStruct((PANEL, size), jnp.float32)]


def sweep_call(kernel, name, args, out_shapes, scratch):
    return pl.pallas_call(
        kernel,
        in_specs=[VMEM] * len(args),
        out_specs=[VMEM] * len(out_shapes),
        out_shape=out_shapes,
        scratch_shapes=scratch,
        cost_estimate=sweep_cost(),
        compiler_params=PARAMS,
        name=name,
    )(*args)


def first_panels(place, pieces, wide, narrow, total):
    return sweep_call(
        functools.partial(first_kernel, place, total),
        "first_panels",
        pieces,
        state_shapes(wide) + state_shapes(narrow),
        [
            pltpu.VMEM((EARLY_ROWS, LANES), jnp.float32),
            pltpu.VMEM((LATE_ROWS, LANES), jnp.float32),
        ],
    )


def second_panels(state, wide, narrow):
    ninv = jax.ShapeDtypeStruct((narrow, narrow), jnp.float32)
    return sweep_call(
        second_kernel,
        "second_panels",
        state,
        [ninv] + state_shapes(wide),
        work_shapes(narrow),
    )


def third_panels(state, wide):
    winv = jax.ShapeDtypeStruct((wide, wide), jnp.float32)
    return sweep_call(third_kernel, "third_panels", state, [winv], work_shapes(wide))[0]


def product_kernel(place, total, rows, winv, ninv_ref, mine, other, out_ref, flat):
    place_halves(place, (mine, other), 0, flat)
    ninv = ninv_ref[...]
    n = LANES
    inner = jnp.concatenate(
        [
            transposed_dot(flat[c * n : (c + 1) * n] / total, ninv, HIGHEST)
            for c in range(2)
        ],
        axis=0,
    )
    wide = winv.shape[1]
    cols = wide // 2 ** len(place.dp)
    near, second = lax.axis_index(place.near), lax.axis_index(place.second)
    near_stride = 2 ** (len(place.dp) - 2)
    base = place.index(place.dp) - near * near_stride - second * 2
    _, lane = iotas((PANEL, LANES))
    for j in range(4):
        index = base + (j // 2) * near_stride + (j % 2) * 2
        picked = aligned_rows(winv, index, cols)
        update = lax.dot_general(
            picked,
            inner,
            (((1,), (0,)), ((), ())),
            precision=HIGHEST,
            preferred_element_type=jnp.float32,
        )
        for x in range(2):
            block = 2 * j + x
            out_ref[block, :cols] = picked[:, :LANES]
            out_ref[block, cols : 2 * cols] = picked[:, LANES:]
            if packs(cols, rows):
                upper, lower = update[:PANEL], update[PANEL:]
                if x == 0:
                    lower = pltpu.roll(lower, rows, 1)
                else:
                    upper = pltpu.roll(upper, rows, 1)
                out_ref[block, 2 * cols :] = jnp.where(lane < rows, upper, lower)
            else:
                out_ref[block, 2 * cols :] = update


def products(place, winv, ninv, pieces, rows, total):
    wide, narrow = winv.shape[0], ninv.shape[0]
    cols = wide // 2 ** len(place.dp)
    height = 2 * cols + (PANEL if packs(cols, rows) else cols)
    return pl.pallas_call(
        functools.partial(product_kernel, place, total, rows),
        in_specs=[VMEM] * 4,
        out_specs=VMEM,
        out_shape=jax.ShapeDtypeStruct((8, height, LANES), jnp.float32),
        scratch_shapes=[pltpu.VMEM((2 * narrow, LANES), jnp.float32)],
        compiler_params=PARAMS,
        name="products",
    )(winv, ninv, *pieces)


def placing_kernel(place, owner_map, got_ref, kept_ref, update_ref):
    layers = got_ref.shape[0]
    slots, cols, wide = kept_ref.shape
    rows = update_ref.shape[2]
    own, dp = place.index(place.own), place.index(place.dp)
    row, col = iotas((cols, wide))
    empty = jnp.where(col == row + dp * cols, 1.0 / DAMP, 0.0)
    count = jnp.int32(0)
    slot = []
    for l in range(layers):
        mine = owner_map[l] == own
        slot.append(jnp.where(mine, count, -1))
        count = count + mine.astype(jnp.int32)
    for h in range(2):
        lanes = slice(h * LANES, (h + 1) * LANES)
        for c in range(slots):
            value = empty[:, lanes]
            for l in range(layers):
                value = jnp.where(slot[l] == c, got_ref[l, h * cols : (h + 1) * cols], value)
            kept_ref[c, :, lanes] = value
    for l in range(layers):
        value = got_ref[l, 2 * cols :]
        if packs(cols, rows):
            update_ref[l, :PANEL] = value[:, :rows]
            update_ref[l, PANEL:] = value[:, rows:]
        else:
            part = value[:, :rows]
            for p in range(1, LANES // rows):
                part = jnp.where(own == p, value[:, p * rows : (p + 1) * rows], part)
            update_ref[l] = part


def placing(place, owner_map, got, wide, cols, slots, rows):
    layers = got.shape[0]
    return pl.pallas_call(
        functools.partial(placing_kernel, place),
        in_specs=[SMEM, VMEM],
        out_specs=[VMEM, VMEM],
        out_shape=[
            jax.ShapeDtypeStruct((slots, cols, wide), jnp.float32),
            jax.ShapeDtypeStruct((layers, cols, rows), jnp.float32),
        ],
        compiler_params=PARAMS,
        name="placing",
    )(owner_map, got)


def swap(value, axis):
    return lax.ppermute(value, axis, [(0, 1), (1, 0)])


def swap_by_core(value, place, stage):
    pairs = []
    for y in range(2):
        for core in range(2):
            for x in range(2):
                flip = 1 if core == stage else 4
                here = y * 4 + core * 2 + x
                pairs.append((here, here ^ flip))
    return lax.ppermute(value, (place.second, place.core, place.first), pairs)


def after(value, *others):
    return lax.optimization_barrier((value,) + others)[0]


def on_device(place, wide_rows, narrow_rows, owner_map):
    layers, rows, wide = wide_rows.shape
    narrow = narrow_rows.shape[2]
    n_dp, n_own = 2 ** len(place.dp), 2 ** len(place.own)
    total = float(rows * n_dp * n_own)

    h_keep, h_send, wides, narrows = hot_squares(place, wide_rows, narrow_rows)
    h_got = swap(h_send[:2], place.core)
    c_keep, c_send = cold_squares(place, after(wides, h_send), narrows)
    h_keep, c_send = lax.optimization_barrier((h_keep, c_send))

    hot = h_keep[:2] + h_got
    s_got = swap_by_core(hot, place, 0)
    c_got = swap(after(jnp.stack([c_send, h_send[2]]), hot), place.core)
    m_keep, m_send = mixed_sums(place, after(wides, hot), narrows)
    m_got = swap(m_send, place.core)
    s = jnp.stack([c_keep, h_keep[2]]) + after(c_got, m_send)

    s = s + s_got
    s_got = swap_by_core(s[1], place, 1)
    m = after(m_keep, s) + m_got
    m_got = swap_by_core(m[2:], place, 1)

    s = s[0] + s_got
    s_got = swap(s[1], place.near)
    m = after(m[:2], s) + m_got
    m_got = swap_by_core(m[1], place, 0)

    s = s[0] + s_got
    if place.extra:
        s = lax.psum(s, place.extra)
    s_got = swap(s, place.far)
    m = after(m[0], s) + m_got
    m_got = swap(m[1], place.near)

    s = s + s_got
    state = first_panels(place, [s, swap(s, place.core)], wide, narrow, total)
    m = after(m[0], state[0]) + m_got
    if place.extra:
        m = lax.psum(m, place.extra)
    m_got = swap(m, place.far)
    ninv, *state = second_panels(state, wide, narrow)
    m = after(m, ninv) + m_got
    m_got = swap(m, place.core)
    winv = third_panels(state, wide)
    cols, own_rows = wide // n_dp, narrow // n_own
    sent = products(place, winv, ninv, [m, m_got], own_rows, total)
    got = lax.all_to_all(sent, (place.near, place.second, place.first), 0, 0)
    kept, update = placing(
        place, owner_map, got, wide, cols, layers // n_own + 1, own_rows
    )
    return (jnp.swapaxes(kept, 1, 2), jnp.swapaxes(update, 1, 2))


def solution(mesh):
    n_dp, n_own = mesh.shape["dp"], mesh.shape["own"]
    dp_names = tuple(f"dp{i}" for i in range(int(np.log2(n_dp))))
    own_names = tuple(f"own{i}" for i in range(int(np.log2(n_own))))
    names = dp_names + own_names
    bits = jax.sharding.Mesh(mesh.devices.reshape((2,) * len(names)), names)
    in_specs = (P(None, names, None), P(None, names, None), P())
    out_specs = (P(own_names, None, dp_names), P(None, own_names, dp_names))
    return jax.shard_map(
        functools.partial(on_device, Place(dp_names, own_names)),
        mesh=bits,
        in_specs=in_specs,
        out_specs=out_specs,
        check_vma=False,
    )
```

```python
import functools

import jax
import jax.numpy as jnp
import numpy as np
from jax import lax
from jax.experimental import pallas as pl
from jax.experimental.pallas import tpu as pltpu
from jax.sharding import PartitionSpec as P

DAMP = 0.5
LANES = 128
PANEL = 8
VMEM_LIMIT = 48 * 1024 * 1024
HIGHEST = lax.Precision.HIGHEST
VMEM = pl.BlockSpec(memory_space=pltpu.VMEM)
SMEM = pl.BlockSpec(memory_space=pltpu.SMEM)
HBM = pl.BlockSpec(memory_space=pltpu.HBM)
PARAMS = pltpu.CompilerParams(vmem_limit_bytes=VMEM_LIMIT)


class Place:
    def __init__(self, dp_names, own_names):
        self.dp, self.own = dp_names, own_names
        self.core, self.second, self.near, self.far = (
            dp_names[-1],
            dp_names[-2],
            dp_names[1],
            dp_names[0],
        )
        self.first = own_names[-1]
        used = (self.core, self.second, self.near, self.far, self.first)
        self.extra = tuple(n for n in dp_names + own_names if n not in used)

    def index(self, names):
        value = jnp.int32(0)
        for name in names:
            value = value * 2 + lax.axis_index(name)
        return value

    def layer(self):
        return self.index((self.near, self.second, self.first))


def transposed_dot(a, b, precision=None):
    return lax.dot_general(
        a, b, (((0,), (0,)), ((), ())), precision=precision, preferred_element_type=jnp.float32
    )


def layer_copies(place, sources, buffers, sems):
    layer = place.layer()
    return [
        [
            pltpu.make_async_copy(
                source.at[jnp.bitwise_xor(layer, i)], buffer.at[i], sems.at[i, s]
            )
            for s, (source, buffer) in enumerate(zip(sources, buffers))
        ]
        for i in range(buffers[0].shape[0])
    ]


def both_halves(place, flat, i):
    rows = flat.shape[1] // 2
    core = lax.axis_index(place.core)
    kept = pl.multiple_of(core * rows, PANEL)
    sent = pl.multiple_of((1 - core) * rows, PANEL)
    return flat[i, pl.ds(kept, rows), :], flat[i, pl.ds(sent, rows), :]


def by_core(place, first, second):
    core = lax.axis_index(place.core)
    return jnp.where(core == 0, first, second), jnp.where(core == 0, second, first)


def iotas(shape):
    return (
        lax.broadcasted_iota(jnp.int32, shape, 0),
        lax.broadcasted_iota(jnp.int32, shape, 1),
    )


def pack_pair(first, second):
    row, col = iotas(first.shape)
    return jnp.where(row >= col, first, second)


def unpack_pair(packed, second_diagonal):
    row, col = iotas(packed.shape)
    turned = packed.T
    first = jnp.where(row >= col, packed, turned)
    second = jnp.where(col > row, packed, turned)
    return first, jnp.where(row == col, second_diagonal, second)


def fold(block):
    h = block.shape[0] // 2
    row, col = iotas((h, 2 * h))
    last = pltpu.roll(block[h:], h, 1)
    return jnp.where((col >= h) | (row >= col), block[:h], last)


def unfold(folded, diagonal):
    h, n = folded.shape
    row, col = iotas((n, n))
    block = jnp.concatenate([folded, jnp.zeros((h, n), jnp.float32)], axis=0)
    turned = block.T
    top = jnp.where((col >= h) | (col <= row), block, turned)
    moved = pltpu.roll(pltpu.roll(block, h, 0), h, 1)
    moved_turned = pltpu.roll(pltpu.roll(turned, h, 0), h, 1)
    last = jnp.where(col > row, moved, moved_turned)
    last = jnp.where(row == col, diagonal, last)
    return jnp.where(row < h, top, jnp.where(col < h, turned, last))


def diagonals(blocks, rows):
    n = blocks[0].shape[0]
    row, col = iotas((n, n))
    slab_row, _ = iotas((rows, n))
    slab = jnp.zeros((rows, n), jnp.float32)
    for i, block in enumerate(blocks):
        line = jnp.sum(jnp.where(row == col, block, 0.0), axis=0, keepdims=True)
        slab = jnp.where(slab_row == i, jnp.broadcast_to(line, (rows, n)), slab)
    return slab


EARLY_ROWS = 144
LATE_ROWS = 192


HOT = (1, 2, 3, 5, 6, 7)
COLD = (0, 4)


def square_sums(wide, narrow):
    return transposed_dot(wide, wide), transposed_dot(narrow, narrow)


def pack_layer(place, i, wcov, ncov, a_flat, b_flat):
    n = LANES
    last = wcov[n:, n:]
    a_flat[i, :n] = pack_pair(wcov[:n, :n], ncov)
    a_flat[i, n:] = diagonals((ncov, last), EARLY_ROWS - n)
    b_flat[i, :n] = wcov[:n, n:]
    b_flat[i, n:] = fold(last)
    a_kept, a_sent = both_halves(place, a_flat, i)
    b_kept, b_sent = both_halves(place, b_flat, i)
    return (a_kept, b_kept), (a_sent, b_sent)


def put(ref, index, parts):
    rows = EARLY_ROWS // 2
    ref[*index, :rows] = parts[0]
    ref[*index, rows:] = parts[1]


def hot_kernel(place, wide_hbm, narrow_hbm, keep, send, wides, narrows, a_flat, b_flat, sems):
    copies = layer_copies(place, (wide_hbm, narrow_hbm), (wides, narrows), sems)
    order = HOT + COLD
    for at, i in enumerate(order):
        for copy in copies[i]:
            copy.start(priority=at % 2)

    def pack(i, sums):
        kept, sent = pack_layer(place, i, *sums, a_flat, b_flat)
        z, y, x = i // 4, (i // 2) % 2, i % 2
        if x and y:
            mine = other = 1
        else:
            mine, other = by_core(place, 0 if x else 2, 2 if x else 0)
        put(keep, (mine, z), kept)
        put(send, (other, z), sent)

    before = None
    for i in order:
        for copy in copies[i]:
            copy.wait()
        if before is not None:
            pack(*before)
            before = None
        if i in HOT:
            before = (i, square_sums(wides[i], narrows[i]))


def cold_kernel(place, wides, narrows, keep, send, a_flat, b_flat):
    for i in COLD:
        sums = square_sums(wides[i], narrows[i])
        kept, sent = pack_layer(place, i, *sums, a_flat, b_flat)
        put(keep, (i // 4,), kept)
        put(send, (i // 4,), sent)


def mixed_kernel(place, wides, narrows, keep, send, flat):
    n = LANES
    for i in range(wides.shape[0]):
        mixed = transposed_dot(narrows[i], wides[i])
        flat[i, :n] = mixed[:, :n]
        flat[i, n:] = mixed[:, n:]
        kept, sent = both_halves(place, flat, i)
        z, y, x = i // 4, (i // 2) % 2, i % 2
        mine, other = by_core(place, y * 2 + x, x * 2 + y)
        keep[mine, z] = kept
        send[other, z] = sent


def gram_cost(wide_rows, columns):
    return pl.CostEstimate(
        flops=2 * wide_rows.size * columns, bytes_accessed=2 * wide_rows.size, transcendentals=0
    )


HALF_ROWS = (EARLY_ROWS + LATE_ROWS) // 2


def pack_shapes(layers):
    return [
        pltpu.VMEM((layers, EARLY_ROWS, LANES), jnp.float32),
        pltpu.VMEM((layers, LATE_ROWS, LANES), jnp.float32),
    ]


def hot_squares(place, wide_rows, narrow_rows):
    layers = wide_rows.shape[0]
    half = jax.ShapeDtypeStruct((3, 2, HALF_ROWS, LANES), jnp.float32)
    return pl.pallas_call(
        functools.partial(hot_kernel, place),
        in_specs=[HBM, HBM],
        out_specs=[VMEM] * 4,
        out_shape=[
            half,
            half,
            jax.ShapeDtypeStruct(wide_rows.shape, wide_rows.dtype),
            jax.ShapeDtypeStruct(narrow_rows.shape, narrow_rows.dtype),
        ],
        scratch_shapes=[*pack_shapes(layers), pltpu.SemaphoreType.DMA((layers, 2))],
        cost_estimate=gram_cost(wide_rows, 240),
        compiler_params=PARAMS,
        name="hot_squares",
    )(
        pltpu.with_memory_space_constraint(wide_rows, pltpu.HBM),
        pltpu.with_memory_space_constraint(narrow_rows, pltpu.HBM),
    )


def cold_squares(place, wides, narrows):
    half = jax.ShapeDtypeStruct((2, HALF_ROWS, LANES), jnp.float32)
    return pl.pallas_call(
        functools.partial(cold_kernel, place),
        in_specs=[VMEM, VMEM],
        out_specs=[VMEM, VMEM],
        out_shape=[half, half],
        scratch_shapes=pack_shapes(wides.shape[0]),
        cost_estimate=gram_cost(wides, 80),
        compiler_params=PARAMS,
        name="cold_squares",
    )(wides, narrows)


def mixed_sums(place, wides, narrows):
    layers, _, narrow = narrows.shape
    half = jax.ShapeDtypeStruct((4, 2, narrow, LANES), jnp.float32)
    return pl.pallas_call(
        functools.partial(mixed_kernel, place),
        in_specs=[VMEM, VMEM],
        out_specs=[VMEM, VMEM],
        out_shape=[half, half],
        scratch_shapes=[pltpu.VMEM((layers, 2 * narrow, LANES), jnp.float32)],
        cost_estimate=gram_cost(wides, 128),
        compiler_params=PARAMS,
        name="mixed",
    )(wides, narrows)


def lane_gather(x, index):
    return jnp.take_along_axis(x, index, axis=1, mode="promise_in_bounds")


def trailing_update(a_ref, left_ref, right_ref, base):
    size = a_ref.shape[1]
    a_ref[pl.ds(pl.multiple_of(base, PANEL), PANEL), :] = jnp.zeros((PANEL, size), jnp.float32)
    lane = lax.broadcasted_iota(jnp.int32, (1, size), 1)
    swept = (lane >= base - PANEL) & (lane < base)
    update = transposed_dot(left_ref[...], right_ref[...])
    a_ref[PANEL : PANEL + size, :] = (
        jnp.where(swept, 0.0, a_ref[PANEL : PANEL + size, :]) - update
    )


def sweep_panel(a_ref, left_ref, right_ref, rows_ref, cols_ref, tile, step, panel):
    size = a_ref.shape[1]
    tiles = size // LANES
    first = step * PANEL
    base = tile * LANES + first
    trailing_update(a_ref, left_ref, right_ref, base)

    shape = (PANEL, LANES)
    sub = lax.broadcasted_iota(jnp.int32, shape, 0)
    lane = lax.broadcasted_iota(jnp.int32, shape, 1)

    def on_all(ref, k, lanes):
        return jnp.broadcast_to(ref[k : k + 1, lanes], shape)

    rows_ref[...] = panel
    lanes = [slice(LANES * t, LANES * (t + 1)) for t in range(tiles)]
    rows = [[on_all(rows_ref, k, part) for part in lanes] for k in range(PANEL)]
    for j in range(PANEL):
        cols_ref[PANEL * j : PANEL * (j + 1)] = lane_gather(rows[j][tile], first + sub)
    d = [[None] * PANEL for _ in range(PANEL)]
    for j in range(PANEL):
        for i in range(j, PANEL):
            d[i][j] = on_all(cols_ref, PANEL * j + i, slice(None))
    own = (lane >= first) & (lane < first + PANEL)
    last = first == LANES - PANEL
    next_lane = jnp.where(last, 0, first + PANEL) + sub
    q = [[None] * tiles for _ in range(PANEL)]
    weights = [None] * PANEL
    factor = [[None] * PANEL for _ in range(PANEL)]
    for k in range(PANEL):
        scale = lax.rsqrt(d[k][k])
        for i in range(k + 1, PANEL):
            factor[i][k] = d[i][k] * scale
        for i in range(k + 1, PANEL):
            for j in range(k + 1, i + 1):
                d[i][j] = d[i][j] - factor[i][k] * factor[j][k]
        for t in range(tiles):
            value = rows[k][t]
            if t == tile:
                value = jnp.where(own, jnp.where(lane == first + k, -1.0, 0.0), value)
            for j in range(k):
                value = value - factor[k][j] * q[j][t]
            q[k][t] = value * scale
        source = rows[k][tile]
        if tile + 1 < tiles:
            source = jnp.where(last, rows[k][tile + 1], source)
        value = lane_gather(source, next_lane)
        for j in range(k):
            value = value - factor[k][j] * weights[j]
        weights[k] = value * scale

    packed = []
    for t in range(tiles):
        value = q[0][t]
        for k in range(1, PANEL):
            value = jnp.where(sub == k, q[k][t], value)
        packed.append(value)
    whole = jnp.concatenate(packed, axis=1) if tiles > 1 else packed[0]
    high = whole.astype(jnp.bfloat16).astype(jnp.float32)
    rest = whole - high
    middle = rest.astype(jnp.bfloat16).astype(jnp.float32)
    low = rest - middle
    left = jnp.concatenate([high, high, middle, middle, high, low], axis=0)
    right = jnp.concatenate([high, middle, high, middle, low, high], axis=0)
    left_ref[...] = left.astype(jnp.bfloat16)
    right_ref[...] = right.astype(jnp.bfloat16)

    after = pl.multiple_of(base + 2 * PANEL, PANEL)
    following = a_ref[pl.ds(after, PANEL), :]
    result = []
    for t in range(tiles):
        value = following[:, LANES * t : LANES * (t + 1)]
        if t == tile:
            value = jnp.where(own, 0.0, value)
        for k in range(PANEL):
            value = value - weights[k] * q[k][t]
        result.append(value)
    return jnp.concatenate(result, axis=1) if tiles > 1 else result[0]


def place_halves(place, pieces, first_row, flat):
    core = lax.axis_index(place.core)
    rows = flat.shape[0] // 2
    for r, piece in enumerate(pieces):
        start = pl.multiple_of(jnp.bitwise_xor(core, r) * rows, PANEL)
        flat[pl.ds(start, rows), :] = piece[first_row : first_row + rows]


def sweep_cost():
    return pl.CostEstimate(flops=1 << 30, bytes_accessed=1 << 20, transcendentals=0)


def clear(work):
    a_ref, left, right = work[:3]
    size = a_ref.shape[1]
    a_ref[:PANEL] = jnp.zeros((PANEL, size), jnp.float32)
    a_ref[PANEL + size :] = jnp.zeros((PANEL, size), jnp.float32)
    left[...] = jnp.zeros(left.shape, left.dtype)
    right[...] = jnp.zeros(right.shape, right.dtype)


def work_shapes(size):
    splits = 6 * PANEL
    return [
        pltpu.VMEM((size + 2 * PANEL, size), jnp.float32),
        pltpu.VMEM((splits, size), jnp.bfloat16),
        pltpu.VMEM((splits, size), jnp.bfloat16),
    ]


def row_shapes(size):
    return [
        pltpu.VMEM((PANEL, size), jnp.float32),
        pltpu.VMEM((PANEL * PANEL, LANES), jnp.float32),
    ]


def aligned_rows(ref, index, count):
    if count % PANEL == 0:
        return ref[pl.ds(pl.multiple_of(index * count, count), count), :]
    per_slab = PANEL // count
    slab = ref[pl.ds(pl.multiple_of(index // per_slab * PANEL, PANEL), PANEL), :]
    value = slab[:count]
    for i in range(1, per_slab):
        value = jnp.where(index % per_slab == i, slab[i * count : (i + 1) * count], value)
    return value


def packs(cols, rows):
    return cols == 2 * PANEL and 2 * rows == LANES


def dot(a, b, last=False):
    return lax.dot_general(
        a,
        b,
        (((1,), (1 if last else 0,)), ((), ())),
        precision=HIGHEST,
        preferred_element_type=jnp.float32,
    )


STEPS = LANES // PANEL
FIRST_STEPS = 10
SECOND_STEPS = 10


def sweep_both(wide_work, narrow_work, begin, end, panels):
    def step(i, panels):
        return (
            sweep_panel(*wide_work, 0, i, panels[0]),
            sweep_panel(*narrow_work, 0, i, panels[1]),
        )

    return lax.fori_loop(begin, end, step, panels)


def sweep_wide(work, begin, end, panel):
    return lax.fori_loop(begin, end, lambda i, panel: sweep_panel(*work, 1, i, panel), panel)


def first_kernel(place, total, mine, other, wa, wl, wr, wp, na, nl, nr, np_, *refs):
    a_flat, b_flat = refs[:2]
    wide_work, narrow_work = (wa, wl, wr, *refs[2:4]), (na, nl, nr, *refs[4:])
    place_halves(place, (mine, other), 0, a_flat)
    place_halves(place, (mine, other), a_flat.shape[0] // 2, b_flat)
    n = LANES
    slab = a_flat[n : n + PANEL]
    first, square = unpack_pair(a_flat[:n], jnp.broadcast_to(slab[:1], (n, n)))
    corner = b_flat[:n] / total
    last = unfold(b_flat[n:], jnp.broadcast_to(slab[1:2], (n, n)))
    row, col = iotas((n, n))
    damp = jnp.where(row == col, DAMP, 0.0)
    clear(wide_work)
    clear(narrow_work)
    wa[PANEL : PANEL + n, :n] = first / total + damp
    wa[PANEL : PANEL + n, n:] = corner
    wa[PANEL + n : PANEL + 2 * n, :n] = corner.T
    wa[PANEL + n : PANEL + 2 * n, n:] = last / total + damp
    na[PANEL : PANEL + n, :] = square / total + damp
    start = (wa[PANEL : 2 * PANEL, :], na[PANEL : 2 * PANEL, :])
    wp[...], np_[...] = sweep_both(wide_work, narrow_work, 0, FIRST_STEPS, start)


def second_kernel(*refs):
    given, ninv_ref, state, narrow_state, wide_rows, narrow_rows = (
        refs[:8],
        refs[8],
        refs[9:13],
        refs[13:16],
        refs[16:18],
        refs[18:],
    )
    for source, target in zip((*given[:3], *given[4:7]), (*state[:3], *narrow_state)):
        target[...] = source[...]
    wide_work, narrow_work = (*state[:3], *wide_rows), (*narrow_state, *narrow_rows)
    wp = state[3]
    panels = (given[3][...], given[7][...])
    panel, _ = sweep_both(wide_work, narrow_work, FIRST_STEPS, STEPS, panels)
    trailing_update(*narrow_work[:3], LANES)
    ninv_ref[...] = -narrow_work[0][PANEL : PANEL + LANES, :]
    wp[...] = sweep_wide(wide_work, 0, SECOND_STEPS, panel)


def third_kernel(wa_in, wl_in, wr_in, panel_in, winv, wa, wl, wr, *rows):
    wa[...] = wa_in[...]
    wl[...] = wl_in[...]
    wr[...] = wr_in[...]
    sweep_wide((wa, wl, wr, *rows), SECOND_STEPS, STEPS, panel_in[...])
    wide = wa.shape[1]
    trailing_update(wa, wl, wr, wide)
    winv[...] = -wa[PANEL : PANEL + wide, :]


def state_shapes(size):
    shapes = [jax.ShapeDtypeStruct(v.shape, v.dtype) for v in work_shapes(size)]
    return shapes + [jax.ShapeDtypeStruct((PANEL, size), jnp.float32)]


def sweep_call(kernel, name, args, out_shapes, scratch):
    return pl.pallas_call(
        kernel,
        in_specs=[VMEM] * len(args),
        out_specs=[VMEM] * len(out_shapes),
        out_shape=out_shapes,
        scratch_shapes=scratch,
        cost_estimate=sweep_cost(),
        compiler_params=PARAMS,
        name=name,
    )(*args)


def first_panels(place, pieces, wide, narrow, total):
    return sweep_call(
        functools.partial(first_kernel, place, total),
        "first_panels",
        pieces,
        state_shapes(wide) + state_shapes(narrow),
        [
            pltpu.VMEM((EARLY_ROWS, LANES), jnp.float32),
            pltpu.VMEM((LATE_ROWS, LANES), jnp.float32),
            *row_shapes(wide),
            *row_shapes(narrow),
        ],
    )


def second_panels(state, wide, narrow):
    ninv = jax.ShapeDtypeStruct((narrow, narrow), jnp.float32)
    return sweep_call(
        second_kernel,
        "second_panels",
        state,
        [ninv] + state_shapes(wide),
        [*work_shapes(narrow), *row_shapes(wide), *row_shapes(narrow)],
    )


def third_panels(state, wide):
    winv = jax.ShapeDtypeStruct((wide, wide), jnp.float32)
    scratch = [*work_shapes(wide), *row_shapes(wide)]
    return sweep_call(third_kernel, "third_panels", state, [winv], scratch)[0]


def product_kernel(place, total, rows, winv, ninv_ref, mine, other, out_ref, flat):
    place_halves(place, (mine, other), 0, flat)
    ninv = ninv_ref[...]
    n = LANES
    inner = jnp.concatenate(
        [
            transposed_dot(flat[c * n : (c + 1) * n] / total, ninv, HIGHEST)
            for c in range(2)
        ],
        axis=0,
    )
    wide = winv.shape[1]
    cols = wide // 2 ** len(place.dp)
    near, second = lax.axis_index(place.near), lax.axis_index(place.second)
    near_stride = 2 ** (len(place.dp) - 2)
    base = place.index(place.dp) - near * near_stride - second * 2
    _, lane = iotas((PANEL, LANES))
    for j in range(4):
        index = base + (j // 2) * near_stride + (j % 2) * 2
        picked = aligned_rows(winv, index, cols)
        update = lax.dot_general(
            picked,
            inner,
            (((1,), (0,)), ((), ())),
            precision=HIGHEST,
            preferred_element_type=jnp.float32,
        )
        for x in range(2):
            block = 2 * j + x
            out_ref[block, :cols] = picked[:, :LANES]
            out_ref[block, cols : 2 * cols] = picked[:, LANES:]
            if packs(cols, rows):
                upper, lower = update[:PANEL], update[PANEL:]
                if x == 0:
                    lower = pltpu.roll(lower, rows, 1)
                else:
                    upper = pltpu.roll(upper, rows, 1)
                out_ref[block, 2 * cols :] = jnp.where(lane < rows, upper, lower)
            else:
                out_ref[block, 2 * cols :] = update


def products(place, winv, ninv, pieces, rows, total):
    wide, narrow = winv.shape[0], ninv.shape[0]
    cols = wide // 2 ** len(place.dp)
    height = 2 * cols + (PANEL if packs(cols, rows) else cols)
    return pl.pallas_call(
        functools.partial(product_kernel, place, total, rows),
        in_specs=[VMEM] * 4,
        out_specs=VMEM,
        out_shape=jax.ShapeDtypeStruct((8, height, LANES), jnp.float32),
        scratch_shapes=[pltpu.VMEM((2 * narrow, LANES), jnp.float32)],
        compiler_params=PARAMS,
        name="products",
    )(winv, ninv, *pieces)


def placing_kernel(place, owner_map, got_ref, kept_ref, update_ref):
    layers = got_ref.shape[0]
    slots, cols, wide = kept_ref.shape
    rows = update_ref.shape[2]
    own, dp = place.index(place.own), place.index(place.dp)
    row, col = iotas((cols, wide))
    empty = jnp.where(col == row + dp * cols, 1.0 / DAMP, 0.0)
    count = jnp.int32(0)
    slot = []
    for l in range(layers):
        mine = owner_map[l] == own
        slot.append(jnp.where(mine, count, -1))
        count = count + mine.astype(jnp.int32)
    for h in range(2):
        lanes = slice(h * LANES, (h + 1) * LANES)
        for c in range(slots):
            value = empty[:, lanes]
            for l in range(layers):
                value = jnp.where(slot[l] == c, got_ref[l, h * cols : (h + 1) * cols], value)
            kept_ref[c, :, lanes] = value
    for l in range(layers):
        value = got_ref[l, 2 * cols :]
        if packs(cols, rows):
            update_ref[l, :PANEL] = value[:, :rows]
            update_ref[l, PANEL:] = value[:, rows:]
        else:
            part = value[:, :rows]
            for p in range(1, LANES // rows):
                part = jnp.where(own == p, value[:, p * rows : (p + 1) * rows], part)
            update_ref[l] = part


def placing(place, owner_map, got, wide, cols, slots, rows):
    layers = got.shape[0]
    return pl.pallas_call(
        functools.partial(placing_kernel, place),
        in_specs=[SMEM, VMEM],
        out_specs=[VMEM, VMEM],
        out_shape=[
            jax.ShapeDtypeStruct((slots, cols, wide), jnp.float32),
            jax.ShapeDtypeStruct((layers, cols, rows), jnp.float32),
        ],
        compiler_params=PARAMS,
        name="placing",
    )(owner_map, got)


def swap(value, axis):
    return lax.ppermute(value, axis, [(0, 1), (1, 0)])


def swap_by_core(value, place, stage):
    pairs = []
    for y in range(2):
        for core in range(2):
            for x in range(2):
                flip = 1 if core == stage else 4
                here = y * 4 + core * 2 + x
                pairs.append((here, here ^ flip))
    return lax.ppermute(value, (place.second, place.core, place.first), pairs)


def after(value, *others):
    return lax.optimization_barrier((value,) + others)[0]


def on_device(place, wide_rows, narrow_rows, owner_map):
    layers, rows, wide = wide_rows.shape
    narrow = narrow_rows.shape[2]
    n_dp, n_own = 2 ** len(place.dp), 2 ** len(place.own)
    total = float(rows * n_dp * n_own)

    h_keep, h_send, wides, narrows = hot_squares(place, wide_rows, narrow_rows)
    h_got = swap(h_send[:2], place.core)
    c_keep, c_send = cold_squares(place, after(wides, h_send), narrows)
    h_keep, c_send = lax.optimization_barrier((h_keep, c_send))

    hot = h_keep[:2] + h_got
    s_got = swap_by_core(hot, place, 0)
    c_got = swap(after(jnp.stack([c_send, h_send[2]]), hot), place.core)
    m_keep, m_send = mixed_sums(place, after(wides, hot), narrows)
    m_got = swap(m_send, place.core)
    s = jnp.stack([c_keep, h_keep[2]]) + after(c_got, m_send)

    s = s + s_got
    s_got = swap_by_core(s[1], place, 1)
    m = after(m_keep, s) + m_got
    m_got = swap_by_core(m[2:], place, 1)

    s = s[0] + s_got
    s_got = swap(s[1], place.near)
    m = after(m[:2], s) + m_got
    m_got = swap_by_core(m[1], place, 0)

    s = s[0] + s_got
    if place.extra:
        s = lax.psum(s, place.extra)
    s_got = swap(s, place.far)
    m = after(m[0], s) + m_got
    m_got = swap(m[1], place.near)

    s = s + s_got
    state = first_panels(place, [s, swap(s, place.core)], wide, narrow, total)
    m = after(m[0], state[0]) + m_got
    if place.extra:
        m = lax.psum(m, place.extra)
    m_got = swap(m, place.far)
    ninv, *state = second_panels(state, wide, narrow)
    m = after(m, ninv) + m_got
    m_got = swap(m, place.core)
    winv = third_panels(state, wide)
    cols, own_rows = wide // n_dp, narrow // n_own
    sent = products(place, winv, ninv, [m, m_got], own_rows, total)
    got = lax.all_to_all(sent, (place.near, place.second, place.first), 0, 0)
    kept, update = placing(
        place, owner_map, got, wide, cols, layers // n_own + 1, own_rows
    )
    return (jnp.swapaxes(kept, 1, 2), jnp.swapaxes(update, 1, 2))


def solution(mesh):
    n_dp, n_own = mesh.shape["dp"], mesh.shape["own"]
    dp_names = tuple(f"dp{i}" for i in range(int(np.log2(n_dp))))
    own_names = tuple(f"own{i}" for i in range(int(np.log2(n_own))))
    names = dp_names + own_names
    bits = jax.sharding.Mesh(mesh.devices.reshape((2,) * len(names)), names)
    in_specs = (P(None, names, None), P(None, names, None), P())
    out_specs = (P(own_names, None, dp_names), P(None, own_names, dp_names))
    return jax.shard_map(
        functools.partial(on_device, Place(dp_names, own_names)),
        mesh=bits,
        in_specs=in_specs,
        out_specs=out_specs,
        check_vma=False,
    )
```

```python
import functools

import jax
import jax.numpy as jnp
import numpy as np
from jax import lax
from jax.experimental import pallas as pl
from jax.experimental.pallas import tpu as pltpu
from jax.sharding import PartitionSpec as P

DAMP = 0.5
LANES = 128
PANEL = 8
VMEM_LIMIT = 48 * 1024 * 1024
HIGHEST = lax.Precision.HIGHEST
VMEM = pl.BlockSpec(memory_space=pltpu.VMEM)
SMEM = pl.BlockSpec(memory_space=pltpu.SMEM)
HBM = pl.BlockSpec(memory_space=pltpu.HBM)
PARAMS = pltpu.CompilerParams(vmem_limit_bytes=VMEM_LIMIT)


class Place:
    def __init__(self, dp_names, own_names):
        self.dp, self.own = dp_names, own_names
        self.core, self.second, self.near, self.far = (
            dp_names[-1],
            dp_names[-2],
            dp_names[1],
            dp_names[0],
        )
        self.first = own_names[-1]
        used = (self.core, self.second, self.near, self.far, self.first)
        self.extra = tuple(n for n in dp_names + own_names if n not in used)

    def index(self, names):
        value = jnp.int32(0)
        for name in names:
            value = value * 2 + lax.axis_index(name)
        return value

    def layer(self):
        return self.index((self.near, self.second, self.first))


def transposed_dot(a, b, precision=None):
    return lax.dot_general(
        a, b, (((0,), (0,)), ((), ())), precision=precision, preferred_element_type=jnp.float32
    )


def layer_copies(place, sources, buffers, sems):
    layer = place.layer()
    return [
        [
            pltpu.make_async_copy(
                source.at[jnp.bitwise_xor(layer, i)], buffer.at[i], sems.at[i, s]
            )
            for s, (source, buffer) in enumerate(zip(sources, buffers))
        ]
        for i in range(buffers[0].shape[0])
    ]


def both_halves(place, flat, i):
    rows = flat.shape[1] // 2
    core = lax.axis_index(place.core)
    kept = pl.multiple_of(core * rows, PANEL)
    sent = pl.multiple_of((1 - core) * rows, PANEL)
    return flat[i, pl.ds(kept, rows), :], flat[i, pl.ds(sent, rows), :]


def by_core(place, first, second):
    core = lax.axis_index(place.core)
    return jnp.where(core == 0, first, second), jnp.where(core == 0, second, first)


def iotas(shape):
    return (
        lax.broadcasted_iota(jnp.int32, shape, 0),
        lax.broadcasted_iota(jnp.int32, shape, 1),
    )


def pack_pair(first, second):
    row, col = iotas(first.shape)
    return jnp.where(row >= col, first, second)


def unpack_pair(packed, second_diagonal):
    row, col = iotas(packed.shape)
    turned = packed.T
    first = jnp.where(row >= col, packed, turned)
    second = jnp.where(col > row, packed, turned)
    return first, jnp.where(row == col, second_diagonal, second)


def fold(block):
    h = block.shape[0] // 2
    row, col = iotas((h, 2 * h))
    last = pltpu.roll(block[h:], h, 1)
    return jnp.where((col >= h) | (row >= col), block[:h], last)


def unfold(folded, diagonal):
    h, n = folded.shape
    row, col = iotas((n, n))
    block = jnp.concatenate([folded, jnp.zeros((h, n), jnp.float32)], axis=0)
    turned = block.T
    top = jnp.where((col >= h) | (col <= row), block, turned)
    moved = pltpu.roll(pltpu.roll(block, h, 0), h, 1)
    moved_turned = pltpu.roll(pltpu.roll(turned, h, 0), h, 1)
    last = jnp.where(col > row, moved, moved_turned)
    last = jnp.where(row == col, diagonal, last)
    return jnp.where(row < h, top, jnp.where(col < h, turned, last))


def diagonals(blocks, rows):
    n = blocks[0].shape[0]
    row, col = iotas((n, n))
    slab_row, _ = iotas((rows, n))
    slab = jnp.zeros((rows, n), jnp.float32)
    for i, block in enumerate(blocks):
        line = jnp.sum(jnp.where(row == col, block, 0.0), axis=0, keepdims=True)
        slab = jnp.where(slab_row == i, jnp.broadcast_to(line, (rows, n)), slab)
    return slab


EARLY_ROWS = 144
LATE_ROWS = 192


HOT = (1, 2, 3, 5, 6, 7)
COLD = (0, 4)


def square_sums(wide, narrow):
    return transposed_dot(wide, wide), transposed_dot(narrow, narrow)


def pack_layer(place, i, wcov, ncov, a_flat, b_flat):
    n = LANES
    last = wcov[n:, n:]
    a_flat[i, :n] = pack_pair(wcov[:n, :n], ncov)
    a_flat[i, n:] = diagonals((ncov, last), EARLY_ROWS - n)
    b_flat[i, :n] = wcov[:n, n:]
    b_flat[i, n:] = fold(last)
    a_kept, a_sent = both_halves(place, a_flat, i)
    b_kept, b_sent = both_halves(place, b_flat, i)
    return (a_kept, b_kept), (a_sent, b_sent)


def put(ref, index, parts):
    rows = EARLY_ROWS // 2
    ref[*index, :rows] = parts[0]
    ref[*index, rows:] = parts[1]


def hot_kernel(place, wide_hbm, narrow_hbm, keep, send, wides, narrows, a_flat, b_flat, sems):
    copies = layer_copies(place, (wide_hbm, narrow_hbm), (wides, narrows), sems)
    order = HOT + COLD
    for i in order:
        for copy in copies[i]:
            copy.start()

    def pack(i, sums):
        kept, sent = pack_layer(place, i, *sums, a_flat, b_flat)
        z, y, x = i // 4, (i // 2) % 2, i % 2
        if x and y:
            mine = other = 1
        else:
            mine, other = by_core(place, 0 if x else 2, 2 if x else 0)
        put(keep, (mine, z), kept)
        put(send, (other, z), sent)

    before = None
    for i in order:
        for copy in copies[i]:
            copy.wait()
        if before is not None:
            pack(*before)
            before = None
        if i in HOT:
            before = (i, square_sums(wides[i], narrows[i]))


def cold_kernel(place, wides, narrows, keep, send, a_flat, b_flat):
    for i in COLD:
        sums = square_sums(wides[i], narrows[i])
        kept, sent = pack_layer(place, i, *sums, a_flat, b_flat)
        put(keep, (i // 4,), kept)
        put(send, (i // 4,), sent)


def mixed_kernel(place, wides, narrows, keep, send, flat):
    n = LANES
    for i in range(wides.shape[0]):
        mixed = transposed_dot(narrows[i], wides[i])
        flat[i, :n] = mixed[:, :n]
        flat[i, n:] = mixed[:, n:]
        kept, sent = both_halves(place, flat, i)
        z, y, x = i // 4, (i // 2) % 2, i % 2
        mine, other = by_core(place, y * 2 + x, x * 2 + y)
        keep[mine, z] = kept
        send[other, z] = sent


def gram_cost(wide_rows, columns):
    return pl.CostEstimate(
        flops=2 * wide_rows.size * columns, bytes_accessed=2 * wide_rows.size, transcendentals=0
    )


HALF_ROWS = (EARLY_ROWS + LATE_ROWS) // 2


def pack_shapes(layers):
    return [
        pltpu.VMEM((layers, EARLY_ROWS, LANES), jnp.float32),
        pltpu.VMEM((layers, LATE_ROWS, LANES), jnp.float32),
    ]


def hot_squares(place, wide_rows, narrow_rows):
    layers = wide_rows.shape[0]
    half = jax.ShapeDtypeStruct((3, 2, HALF_ROWS, LANES), jnp.float32)
    return pl.pallas_call(
        functools.partial(hot_kernel, place),
        in_specs=[HBM, HBM],
        out_specs=[VMEM] * 4,
        out_shape=[
            half,
            half,
            jax.ShapeDtypeStruct(wide_rows.shape, wide_rows.dtype),
            jax.ShapeDtypeStruct(narrow_rows.shape, narrow_rows.dtype),
        ],
        scratch_shapes=[*pack_shapes(layers), pltpu.SemaphoreType.DMA((layers, 2))],
        cost_estimate=gram_cost(wide_rows, 240),
        compiler_params=PARAMS,
        name="hot_squares",
    )(
        pltpu.with_memory_space_constraint(wide_rows, pltpu.HBM),
        pltpu.with_memory_space_constraint(narrow_rows, pltpu.HBM),
    )


def cold_squares(place, wides, narrows):
    half = jax.ShapeDtypeStruct((2, HALF_ROWS, LANES), jnp.float32)
    return pl.pallas_call(
        functools.partial(cold_kernel, place),
        in_specs=[VMEM, VMEM],
        out_specs=[VMEM, VMEM],
        out_shape=[half, half],
        scratch_shapes=pack_shapes(wides.shape[0]),
        cost_estimate=gram_cost(wides, 80),
        compiler_params=PARAMS,
        name="cold_squares",
    )(wides, narrows)


def mixed_sums(place, wides, narrows):
    layers, _, narrow = narrows.shape
    half = jax.ShapeDtypeStruct((4, 2, narrow, LANES), jnp.float32)
    return pl.pallas_call(
        functools.partial(mixed_kernel, place),
        in_specs=[VMEM, VMEM],
        out_specs=[VMEM, VMEM],
        out_shape=[half, half],
        scratch_shapes=[pltpu.VMEM((layers, 2 * narrow, LANES), jnp.float32)],
        cost_estimate=gram_cost(wides, 128),
        compiler_params=PARAMS,
        name="mixed",
    )(wides, narrows)


def lane_gather(x, index):
    return jnp.take_along_axis(x, index, axis=1, mode="promise_in_bounds")


def trailing_update(a_ref, left_ref, right_ref, base):
    size = a_ref.shape[1]
    a_ref[pl.ds(pl.multiple_of(base, PANEL), PANEL), :] = jnp.zeros((PANEL, size), jnp.float32)
    lane = lax.broadcasted_iota(jnp.int32, (1, size), 1)
    swept = (lane >= base - PANEL) & (lane < base)
    update = transposed_dot(left_ref[...], right_ref[...])
    a_ref[PANEL : PANEL + size, :] = (
        jnp.where(swept, 0.0, a_ref[PANEL : PANEL + size, :]) - update
    )


def in_three(x):
    high = x.astype(jnp.bfloat16).astype(jnp.float32)
    rest = x - high
    middle = rest.astype(jnp.bfloat16).astype(jnp.float32)
    return high, middle, rest - middle


def sweep_panel(a_ref, left_ref, right_ref, rows_ref, cols_ref, tile, step, panel):
    size = a_ref.shape[1]
    tiles = size // LANES
    first = step * PANEL
    base = tile * LANES + first
    trailing_update(a_ref, left_ref, right_ref, base)

    shape = (PANEL, LANES)
    sub = lax.broadcasted_iota(jnp.int32, shape, 0)
    lane = lax.broadcasted_iota(jnp.int32, shape, 1)

    def on_all(ref, k, lanes):
        return jnp.broadcast_to(ref[k : k + 1, lanes], shape)

    rows_ref[...] = panel
    lanes = [slice(LANES * t, LANES * (t + 1)) for t in range(tiles)]
    rows = [[on_all(rows_ref, k, part) for part in lanes] for k in range(PANEL)]
    here = panel[:, lanes[tile]]
    for j in range(PANEL):
        column = lane_gather(here, jnp.full(shape, 0, jnp.int32) + (first + j))
        cols_ref[PANEL * j : PANEL * (j + 1)] = column
    d = [[None] * PANEL for _ in range(PANEL)]
    for j in range(PANEL):
        for i in range(j, PANEL):
            d[i][j] = on_all(cols_ref, PANEL * j + i, slice(None))
    own = (lane >= first) & (lane < first + PANEL)
    last = first == LANES - PANEL
    next_lane = jnp.where(last, 0, first + PANEL) + sub
    q = [[None] * tiles for _ in range(PANEL)]
    p = [[None] * tiles for _ in range(PANEL)]
    weights = [None] * PANEL
    factor = [[None] * PANEL for _ in range(PANEL)]

    def substitute(k, scale):
        for t in range(tiles):
            value = rows[k][t]
            if t == tile:
                value = jnp.where(own, jnp.where(lane == first + k, -1.0, 0.0), value)
            for j in range(k):
                value = value - factor[k][j] * q[j][t]
            q[k][t] = value
            p[k][t] = value * scale
        source = rows[k][tile]
        if tile + 1 < tiles:
            source = jnp.where(last, rows[k][tile + 1], source)
        value = lane_gather(source, next_lane)
        for j in range(k):
            value = value - factor[k][j] * weights[j]
        weights[k] = value

    for k in range(0, PANEL, 2):
        m = k + 1
        a, b, c = d[k][k], d[m][k], d[m][m]
        first_scale = 1.0 / a
        second_scale = a * (1.0 / (a * c - b * b))
        factor[m][k] = b * first_scale
        left_over = {i: d[i][m] - d[i][k] * factor[m][k] for i in range(k + 2, PANEL)}
        for i in range(k + 2, PANEL):
            factor[i][k] = d[i][k] * first_scale
            factor[i][m] = left_over[i] * second_scale
        for i in range(k + 2, PANEL):
            for j in range(k + 2, i + 1):
                value = d[i][j] - d[i][k] * factor[j][k]
                d[i][j] = value - (left_over[i] * left_over[j]) * second_scale
        substitute(k, first_scale)
        substitute(m, second_scale)

    def packed(values):
        whole = []
        for t in range(tiles):
            value = values[0][t]
            for k in range(1, PANEL):
                value = jnp.where(sub == k, values[k][t], value)
            whole.append(value)
        return jnp.concatenate(whole, axis=1) if tiles > 1 else whole[0]

    qs, ps = in_three(packed(q)), in_three(packed(p))
    left_ref[...] = jnp.concatenate([qs[i] for i in (0, 0, 1, 1, 0, 2)], axis=0).astype(
        jnp.bfloat16
    )
    right_ref[...] = jnp.concatenate([ps[i] for i in (0, 1, 0, 1, 2, 0)], axis=0).astype(
        jnp.bfloat16
    )

    after = pl.multiple_of(base + 2 * PANEL, PANEL)
    following = a_ref[pl.ds(after, PANEL), :]
    result = []
    for t in range(tiles):
        value = following[:, LANES * t : LANES * (t + 1)]
        if t == tile:
            value = jnp.where(own, 0.0, value)
        for k in range(PANEL):
            value = value - weights[k] * p[k][t]
        result.append(value)
    return jnp.concatenate(result, axis=1) if tiles > 1 else result[0]


def place_halves(place, pieces, first_row, flat):
    core = lax.axis_index(place.core)
    rows = flat.shape[0] // 2
    for r, piece in enumerate(pieces):
        start = pl.multiple_of(jnp.bitwise_xor(core, r) * rows, PANEL)
        flat[pl.ds(start, rows), :] = piece[first_row : first_row + rows]


def sweep_cost():
    return pl.CostEstimate(flops=1 << 30, bytes_accessed=1 << 20, transcendentals=0)


def clear(work):
    a_ref, left, right = work[:3]
    size = a_ref.shape[1]
    a_ref[:PANEL] = jnp.zeros((PANEL, size), jnp.float32)
    a_ref[PANEL + size :] = jnp.zeros((PANEL, size), jnp.float32)
    left[...] = jnp.zeros(left.shape, left.dtype)
    right[...] = jnp.zeros(right.shape, right.dtype)


def work_shapes(size):
    splits = 6 * PANEL
    return [
        pltpu.VMEM((size + 2 * PANEL, size), jnp.float32),
        pltpu.VMEM((splits, size), jnp.bfloat16),
        pltpu.VMEM((splits, size), jnp.bfloat16),
    ]


def row_shapes(size):
    return [
        pltpu.VMEM((PANEL, size), jnp.float32),
        pltpu.VMEM((PANEL * PANEL, LANES), jnp.float32),
    ]


def aligned_rows(ref, index, count):
    if count % PANEL == 0:
        return ref[pl.ds(pl.multiple_of(index * count, count), count), :]
    per_slab = PANEL // count
    slab = ref[pl.ds(pl.multiple_of(index // per_slab * PANEL, PANEL), PANEL), :]
    value = slab[:count]
    for i in range(1, per_slab):
        value = jnp.where(index % per_slab == i, slab[i * count : (i + 1) * count], value)
    return value


def packs(cols, rows):
    return cols == 2 * PANEL and 2 * rows == LANES


def dot(a, b, last=False):
    return lax.dot_general(
        a,
        b,
        (((1,), (1 if last else 0,)), ((), ())),
        precision=HIGHEST,
        preferred_element_type=jnp.float32,
    )


STEPS = LANES // PANEL
FIRST_STEPS = 10
SECOND_STEPS = 10


def sweep_both(wide_work, narrow_work, begin, end, panels):
    def step(i, panels):
        return (
            sweep_panel(*wide_work, 0, i, panels[0]),
            sweep_panel(*narrow_work, 0, i, panels[1]),
        )

    return lax.fori_loop(begin, end, step, panels)


def sweep_wide(work, begin, end, panel):
    return lax.fori_loop(begin, end, lambda i, panel: sweep_panel(*work, 1, i, panel), panel)


def unit_scale(block):
    row, col = iotas(block.shape)
    line = jnp.sum(jnp.where(row == col, block, 0.0), axis=0, keepdims=True)
    return jnp.broadcast_to(lax.rsqrt(line), (PANEL, block.shape[1]))


def scaled(block, down, across):
    columns = jnp.broadcast_to(down[:1], block.shape).T
    return (block * columns) * jnp.broadcast_to(across[:1], block.shape)


def first_kernel(
    place, total, mine, other, wa, wl, wr, wp, na, nl, nr, np_, ws_ref, ns_ref, *refs
):
    a_flat, b_flat = refs[:2]
    wide_work, narrow_work = (wa, wl, wr, *refs[2:4]), (na, nl, nr, *refs[4:])
    place_halves(place, (mine, other), 0, a_flat)
    place_halves(place, (mine, other), a_flat.shape[0] // 2, b_flat)
    n = LANES
    slab = a_flat[n : n + PANEL]
    first, square = unpack_pair(a_flat[:n], jnp.broadcast_to(slab[:1], (n, n)))
    corner = b_flat[:n] / total
    last = unfold(b_flat[n:], jnp.broadcast_to(slab[1:2], (n, n)))
    row, col = iotas((n, n))
    damp = jnp.where(row == col, DAMP, 0.0)
    clear(wide_work)
    clear(narrow_work)
    first, last, square = first / total + damp, last / total + damp, square / total + damp
    by_first, by_last, by_square = (unit_scale(block) for block in (first, last, square))
    ws_ref[:, :n] = by_first
    ws_ref[:, n:] = by_last
    ns_ref[...] = by_square
    corner = scaled(corner, by_first, by_last)
    wa[PANEL : PANEL + n, :n] = scaled(first, by_first, by_first)
    wa[PANEL : PANEL + n, n:] = corner
    wa[PANEL + n : PANEL + 2 * n, :n] = corner.T
    wa[PANEL + n : PANEL + 2 * n, n:] = scaled(last, by_last, by_last)
    na[PANEL : PANEL + n, :] = scaled(square, by_square, by_square)
    start = (wa[PANEL : 2 * PANEL, :], na[PANEL : 2 * PANEL, :])
    wp[...], np_[...] = sweep_both(wide_work, narrow_work, 0, FIRST_STEPS, start)


def second_kernel(*refs):
    given, scale, ninv_ref, state, narrow_state, wide_rows, narrow_rows = (
        refs[:8],
        refs[8],
        refs[9],
        refs[10:14],
        refs[14:17],
        refs[17:19],
        refs[19:],
    )
    for source, target in zip((*given[:3], *given[4:7]), (*state[:3], *narrow_state)):
        target[...] = source[...]
    wide_work, narrow_work = (*state[:3], *wide_rows), (*narrow_state, *narrow_rows)
    wp = state[3]
    panels = (given[3][...], given[7][...])
    panel, _ = sweep_both(wide_work, narrow_work, FIRST_STEPS, STEPS, panels)
    trailing_update(*narrow_work[:3], LANES)
    by_square = scale[...]
    ninv_ref[...] = scaled(-narrow_work[0][PANEL : PANEL + LANES, :], by_square, by_square)
    wp[...] = sweep_wide(wide_work, 0, SECOND_STEPS, panel)


def third_kernel(wa_in, wl_in, wr_in, panel_in, scale, winv, wa, wl, wr, *rows):
    wa[...] = wa_in[...]
    wl[...] = wl_in[...]
    wr[...] = wr_in[...]
    sweep_wide((wa, wl, wr, *rows), SECOND_STEPS, STEPS, panel_in[...])
    wide = wa.shape[1]
    trailing_update(wa, wl, wr, wide)
    parts = [slice(i, i + LANES) for i in range(0, wide, LANES)]
    for i in parts:
        for j in parts:
            block = -wa[PANEL + i.start : PANEL + i.stop, j]
            winv[i, j] = scaled(block, scale[:, i], scale[:, j])


def state_shapes(size):
    shapes = [jax.ShapeDtypeStruct(v.shape, v.dtype) for v in work_shapes(size)]
    return shapes + [jax.ShapeDtypeStruct((PANEL, size), jnp.float32)]


def sweep_call(kernel, name, args, out_shapes, scratch):
    return pl.pallas_call(
        kernel,
        in_specs=[VMEM] * len(args),
        out_specs=[VMEM] * len(out_shapes),
        out_shape=out_shapes,
        scratch_shapes=scratch,
        cost_estimate=sweep_cost(),
        compiler_params=PARAMS,
        name=name,
    )(*args)


def first_panels(place, pieces, wide, narrow, total):
    return sweep_call(
        functools.partial(first_kernel, place, total),
        "first_panels",
        pieces,
        state_shapes(wide)
        + state_shapes(narrow)
        + [jax.ShapeDtypeStruct((PANEL, n), jnp.float32) for n in (wide, narrow)],
        [
            pltpu.VMEM((EARLY_ROWS, LANES), jnp.float32),
            pltpu.VMEM((LATE_ROWS, LANES), jnp.float32),
            *row_shapes(wide),
            *row_shapes(narrow),
        ],
    )


def second_panels(state, wide, narrow):
    ninv = jax.ShapeDtypeStruct((narrow, narrow), jnp.float32)
    return sweep_call(
        second_kernel,
        "second_panels",
        state,
        [ninv] + state_shapes(wide),
        [*work_shapes(narrow), *row_shapes(wide), *row_shapes(narrow)],
    )


def third_panels(state, wide):
    winv = jax.ShapeDtypeStruct((wide, wide), jnp.float32)
    scratch = [*work_shapes(wide), *row_shapes(wide)]
    return sweep_call(third_kernel, "third_panels", state, [winv], scratch)[0]


def product_kernel(place, total, rows, winv, ninv_ref, mine, other, out_ref, flat):
    place_halves(place, (mine, other), 0, flat)
    ninv = ninv_ref[...]
    n = LANES
    inner = jnp.concatenate(
        [
            transposed_dot(flat[c * n : (c + 1) * n] / total, ninv, HIGHEST)
            for c in range(2)
        ],
        axis=0,
    )
    wide = winv.shape[1]
    cols = wide // 2 ** len(place.dp)
    near, second = lax.axis_index(place.near), lax.axis_index(place.second)
    near_stride = 2 ** (len(place.dp) - 2)
    base = place.index(place.dp) - near * near_stride - second * 2
    _, lane = iotas((PANEL, LANES))
    for j in range(4):
        index = base + (j // 2) * near_stride + (j % 2) * 2
        picked = aligned_rows(winv, index, cols)
        update = lax.dot_general(
            picked,
            inner,
            (((1,), (0,)), ((), ())),
            precision=HIGHEST,
            preferred_element_type=jnp.float32,
        )
        for x in range(2):
            block = 2 * j + x
            out_ref[block, :cols] = picked[:, :LANES]
            out_ref[block, cols : 2 * cols] = picked[:, LANES:]
            if packs(cols, rows):
                upper, lower = update[:PANEL], update[PANEL:]
                if x == 0:
                    lower = pltpu.roll(lower, rows, 1)
                else:
                    upper = pltpu.roll(upper, rows, 1)
                out_ref[block, 2 * cols :] = jnp.where(lane < rows, upper, lower)
            else:
                out_ref[block, 2 * cols :] = update


def products(place, winv, ninv, pieces, rows, total):
    wide, narrow = winv.shape[0], ninv.shape[0]
    cols = wide // 2 ** len(place.dp)
    height = 2 * cols + (PANEL if packs(cols, rows) else cols)
    return pl.pallas_call(
        functools.partial(product_kernel, place, total, rows),
        in_specs=[VMEM] * 4,
        out_specs=VMEM,
        out_shape=jax.ShapeDtypeStruct((8, height, LANES), jnp.float32),
        scratch_shapes=[pltpu.VMEM((2 * narrow, LANES), jnp.float32)],
        compiler_params=PARAMS,
        name="products",
    )(winv, ninv, *pieces)


def placing_kernel(place, owner_map, got_ref, kept_ref, update_ref):
    layers = got_ref.shape[0]
    slots, cols, wide = kept_ref.shape
    rows = update_ref.shape[2]
    own, dp = place.index(place.own), place.index(place.dp)
    row, col = iotas((cols, wide))
    empty = jnp.where(col == row + dp * cols, 1.0 / DAMP, 0.0)
    count = jnp.int32(0)
    slot = []
    for l in range(layers):
        mine = owner_map[l] == own
        slot.append(jnp.where(mine, count, -1))
        count = count + mine.astype(jnp.int32)
    for h in range(2):
        lanes = slice(h * LANES, (h + 1) * LANES)
        for c in range(slots):
            value = empty[:, lanes]
            for l in range(layers):
                value = jnp.where(slot[l] == c, got_ref[l, h * cols : (h + 1) * cols], value)
            kept_ref[c, :, lanes] = value
    for l in range(layers):
        value = got_ref[l, 2 * cols :]
        if packs(cols, rows):
            update_ref[l, :PANEL] = value[:, :rows]
            update_ref[l, PANEL:] = value[:, rows:]
        else:
            part = value[:, :rows]
            for p in range(1, LANES // rows):
                part = jnp.where(own == p, value[:, p * rows : (p + 1) * rows], part)
            update_ref[l] = part


def placing(place, owner_map, got, wide, cols, slots, rows):
    layers = got.shape[0]
    return pl.pallas_call(
        functools.partial(placing_kernel, place),
        in_specs=[SMEM, VMEM],
        out_specs=[VMEM, VMEM],
        out_shape=[
            jax.ShapeDtypeStruct((slots, cols, wide), jnp.float32),
            jax.ShapeDtypeStruct((layers, cols, rows), jnp.float32),
        ],
        compiler_params=PARAMS,
        name="placing",
    )(owner_map, got)


def swap(value, axis):
    return lax.ppermute(value, axis, [(0, 1), (1, 0)])


def swap_by_core(value, place, stage):
    pairs = []
    for y in range(2):
        for core in range(2):
            for x in range(2):
                flip = 1 if core == stage else 4
                here = y * 4 + core * 2 + x
                pairs.append((here, here ^ flip))
    return lax.ppermute(value, (place.second, place.core, place.first), pairs)


def after(value, *others):
    return lax.optimization_barrier((value,) + others)[0]


def on_device(place, wide_rows, narrow_rows, owner_map):
    layers, rows, wide = wide_rows.shape
    narrow = narrow_rows.shape[2]
    n_dp, n_own = 2 ** len(place.dp), 2 ** len(place.own)
    total = float(rows * n_dp * n_own)

    h_keep, h_send, wides, narrows = hot_squares(place, wide_rows, narrow_rows)
    h_got = swap(h_send[:2], place.core)
    c_keep, c_send = cold_squares(place, after(wides, h_send), narrows)
    h_keep, c_send = lax.optimization_barrier((h_keep, c_send))

    hot = h_keep[:2] + h_got
    s_got = swap_by_core(hot, place, 0)
    c_got = swap(after(jnp.stack([c_send, h_send[2]]), hot), place.core)
    m_keep, m_send = mixed_sums(place, after(wides, hot), narrows)
    m_got = swap(m_send, place.core)
    s = jnp.stack([c_keep, h_keep[2]]) + after(c_got, m_send)

    s = s + s_got
    s_got = swap_by_core(s[1], place, 1)
    m = after(m_keep, s) + m_got
    m_got = swap_by_core(m[2:], place, 1)

    s = s[0] + s_got
    s_got = swap(s[1], place.near)
    m = after(m[:2], s) + m_got
    m_got = swap_by_core(m[1], place, 0)

    s = s[0] + s_got
    if place.extra:
        s = lax.psum(s, place.extra)
    s_got = swap(s, place.far)
    m = after(m[0], s) + m_got
    m_got = swap(m[1], place.near)

    s = s + s_got
    state = first_panels(place, [s, swap(s, place.core)], wide, narrow, total)
    m = after(m[0], state[0]) + m_got
    if place.extra:
        m = lax.psum(m, place.extra)
    m_got = swap(m, place.far)
    *state, wide_scale, narrow_scale = state
    ninv, *state = second_panels([*state, narrow_scale], wide, narrow)
    m = after(m, ninv) + m_got
    m_got = swap(m, place.core)
    winv = third_panels([*state, wide_scale], wide)
    cols, own_rows = wide // n_dp, narrow // n_own
    sent = products(place, winv, ninv, [m, m_got], own_rows, total)
    got = lax.all_to_all(sent, (place.near, place.second, place.first), 0, 0)
    kept, update = placing(
        place, owner_map, got, wide, cols, layers // n_own + 1, own_rows
    )
    return (jnp.swapaxes(kept, 1, 2), jnp.swapaxes(update, 1, 2))


def solution(mesh):
    n_dp, n_own = mesh.shape["dp"], mesh.shape["own"]
    dp_names = tuple(f"dp{i}" for i in range(int(np.log2(n_dp))))
    own_names = tuple(f"own{i}" for i in range(int(np.log2(n_own))))
    names = dp_names + own_names
    bits = jax.sharding.Mesh(mesh.devices.reshape((2,) * len(names)), names)
    in_specs = (P(None, names, None), P(None, names, None), P())
    out_specs = (P(own_names, None, dp_names), P(None, own_names, dp_names))
    return jax.shard_map(
        functools.partial(on_device, Place(dp_names, own_names)),
        mesh=bits,
        in_specs=in_specs,
        out_specs=out_specs,
        check_vma=False,
    )
```

```python
import functools

import jax
import jax.numpy as jnp
import numpy as np
from jax import lax
from jax.experimental import pallas as pl
from jax.experimental.pallas import tpu as pltpu
from jax.sharding import PartitionSpec as P

DAMP = 0.5
LANES = 128
PANEL = 8
BLOCK = 2 * PANEL
VMEM_LIMIT = 48 * 1024 * 1024
HIGHEST = lax.Precision.HIGHEST
VMEM = pl.BlockSpec(memory_space=pltpu.VMEM)
SMEM = pl.BlockSpec(memory_space=pltpu.SMEM)
HBM = pl.BlockSpec(memory_space=pltpu.HBM)
PARAMS = pltpu.CompilerParams(vmem_limit_bytes=VMEM_LIMIT)


class Place:
    def __init__(self, dp_names, own_names):
        self.dp, self.own = dp_names, own_names
        self.core, self.second, self.near, self.far = (
            dp_names[-1],
            dp_names[-2],
            dp_names[1],
            dp_names[0],
        )
        self.first = own_names[-1]
        used = (self.core, self.second, self.near, self.far, self.first)
        self.extra = tuple(n for n in dp_names + own_names if n not in used)

    def index(self, names):
        value = jnp.int32(0)
        for name in names:
            value = value * 2 + lax.axis_index(name)
        return value

    def layer(self):
        return self.index((self.near, self.second, self.first))


def transposed_dot(a, b, precision=None):
    return lax.dot_general(
        a, b, (((0,), (0,)), ((), ())), precision=precision, preferred_element_type=jnp.float32
    )


def layer_copies(place, sources, buffers, sems):
    layer = place.layer()
    return [
        [
            pltpu.make_async_copy(
                source.at[jnp.bitwise_xor(layer, i)], buffer.at[i], sems.at[i, s]
            )
            for s, (source, buffer) in enumerate(zip(sources, buffers))
        ]
        for i in range(buffers[0].shape[0])
    ]


def both_halves(place, flat, i):
    rows = flat.shape[1] // 2
    core = lax.axis_index(place.core)
    kept = pl.multiple_of(core * rows, PANEL)
    sent = pl.multiple_of((1 - core) * rows, PANEL)
    return flat[i, pl.ds(kept, rows), :], flat[i, pl.ds(sent, rows), :]


def by_core(place, first, second):
    core = lax.axis_index(place.core)
    return jnp.where(core == 0, first, second), jnp.where(core == 0, second, first)


def iotas(shape):
    return (
        lax.broadcasted_iota(jnp.int32, shape, 0),
        lax.broadcasted_iota(jnp.int32, shape, 1),
    )


def pack_pair(first, second):
    row, col = iotas(first.shape)
    return jnp.where(row >= col, first, second)


def unpack_pair(packed, second_diagonal):
    row, col = iotas(packed.shape)
    turned = packed.T
    first = jnp.where(row >= col, packed, turned)
    second = jnp.where(col > row, packed, turned)
    return first, jnp.where(row == col, second_diagonal, second)


def fold(block):
    h = block.shape[0] // 2
    row, col = iotas((h, 2 * h))
    last = pltpu.roll(block[h:], h, 1)
    return jnp.where((col >= h) | (row >= col), block[:h], last)


def unfold(folded, diagonal):
    h, n = folded.shape
    row, col = iotas((n, n))
    block = jnp.concatenate([folded, jnp.zeros((h, n), jnp.float32)], axis=0)
    turned = block.T
    top = jnp.where((col >= h) | (col <= row), block, turned)
    moved = pltpu.roll(pltpu.roll(block, h, 0), h, 1)
    moved_turned = pltpu.roll(pltpu.roll(turned, h, 0), h, 1)
    last = jnp.where(col > row, moved, moved_turned)
    last = jnp.where(row == col, diagonal, last)
    return jnp.where(row < h, top, jnp.where(col < h, turned, last))


def diagonals(blocks, rows):
    n = blocks[0].shape[0]
    row, col = iotas((n, n))
    slab_row, _ = iotas((rows, n))
    slab = jnp.zeros((rows, n), jnp.float32)
    for i, block in enumerate(blocks):
        line = jnp.sum(jnp.where(row == col, block, 0.0), axis=0, keepdims=True)
        slab = jnp.where(slab_row == i, jnp.broadcast_to(line, (rows, n)), slab)
    return slab


EARLY_ROWS = 144
LATE_ROWS = 192


HOT = (1, 2, 3, 5, 6, 7)
COLD = (0, 4)


def square_sums(wide, narrow):
    return transposed_dot(wide, wide), transposed_dot(narrow, narrow)


def pack_layer(place, i, wcov, ncov, a_flat, b_flat):
    n = LANES
    last = wcov[n:, n:]
    a_flat[i, :n] = pack_pair(wcov[:n, :n], ncov)
    a_flat[i, n:] = diagonals((ncov, last), EARLY_ROWS - n)
    b_flat[i, :n] = wcov[:n, n:]
    b_flat[i, n:] = fold(last)
    a_kept, a_sent = both_halves(place, a_flat, i)
    b_kept, b_sent = both_halves(place, b_flat, i)
    return (a_kept, b_kept), (a_sent, b_sent)


def put(ref, index, parts):
    rows = EARLY_ROWS // 2
    ref[*index, :rows] = parts[0]
    ref[*index, rows:] = parts[1]


def hot_kernel(place, wide_hbm, narrow_hbm, keep, send, wides, narrows, a_flat, b_flat, sems):
    copies = layer_copies(place, (wide_hbm, narrow_hbm), (wides, narrows), sems)
    order = HOT + COLD
    for i in order:
        for copy in copies[i]:
            copy.start()

    def pack(i, sums):
        kept, sent = pack_layer(place, i, *sums, a_flat, b_flat)
        z, y, x = i // 4, (i // 2) % 2, i % 2
        if x and y:
            mine = other = 1
        else:
            mine, other = by_core(place, 0 if x else 2, 2 if x else 0)
        put(keep, (mine, z), kept)
        put(send, (other, z), sent)

    before = None
    for i in order:
        for copy in copies[i]:
            copy.wait()
        if before is not None:
            pack(*before)
            before = None
        if i in HOT:
            before = (i, square_sums(wides[i], narrows[i]))


def cold_kernel(place, wides, narrows, keep, send, a_flat, b_flat):
    for i in COLD:
        sums = square_sums(wides[i], narrows[i])
        kept, sent = pack_layer(place, i, *sums, a_flat, b_flat)
        put(keep, (i // 4,), kept)
        put(send, (i // 4,), sent)


def mixed_kernel(place, wides, narrows, keep, send, flat):
    n = LANES
    for i in range(wides.shape[0]):
        mixed = transposed_dot(narrows[i], wides[i])
        flat[i, :n] = mixed[:, :n]
        flat[i, n:] = mixed[:, n:]
        kept, sent = both_halves(place, flat, i)
        z, y, x = i // 4, (i // 2) % 2, i % 2
        mine, other = by_core(place, y * 2 + x, x * 2 + y)
        keep[mine, z] = kept
        send[other, z] = sent


def gram_cost(wide_rows, columns):
    return pl.CostEstimate(
        flops=2 * wide_rows.size * columns, bytes_accessed=2 * wide_rows.size, transcendentals=0
    )


HALF_ROWS = (EARLY_ROWS + LATE_ROWS) // 2


def pack_shapes(layers):
    return [
        pltpu.VMEM((layers, EARLY_ROWS, LANES), jnp.float32),
        pltpu.VMEM((layers, LATE_ROWS, LANES), jnp.float32),
    ]


def hot_squares(place, wide_rows, narrow_rows):
    layers = wide_rows.shape[0]
    half = jax.ShapeDtypeStruct((3, 2, HALF_ROWS, LANES), jnp.float32)
    return pl.pallas_call(
        functools.partial(hot_kernel, place),
        in_specs=[HBM, HBM],
        out_specs=[VMEM] * 4,
        out_shape=[
            half,
            half,
            jax.ShapeDtypeStruct(wide_rows.shape, wide_rows.dtype),
            jax.ShapeDtypeStruct(narrow_rows.shape, narrow_rows.dtype),
        ],
        scratch_shapes=[*pack_shapes(layers), pltpu.SemaphoreType.DMA((layers, 2))],
        cost_estimate=gram_cost(wide_rows, 240),
        compiler_params=PARAMS,
        name="hot_squares",
    )(
        pltpu.with_memory_space_constraint(wide_rows, pltpu.HBM),
        pltpu.with_memory_space_constraint(narrow_rows, pltpu.HBM),
    )


def cold_squares(place, wides, narrows):
    half = jax.ShapeDtypeStruct((2, HALF_ROWS, LANES), jnp.float32)
    return pl.pallas_call(
        functools.partial(cold_kernel, place),
        in_specs=[VMEM, VMEM],
        out_specs=[VMEM, VMEM],
        out_shape=[half, half],
        scratch_shapes=pack_shapes(wides.shape[0]),
        cost_estimate=gram_cost(wides, 80),
        compiler_params=PARAMS,
        name="cold_squares",
    )(wides, narrows)


def mixed_sums(place, wides, narrows):
    layers, _, narrow = narrows.shape
    half = jax.ShapeDtypeStruct((4, 2, narrow, LANES), jnp.float32)
    return pl.pallas_call(
        functools.partial(mixed_kernel, place),
        in_specs=[VMEM, VMEM],
        out_specs=[VMEM, VMEM],
        out_shape=[half, half],
        scratch_shapes=[pltpu.VMEM((layers, 2 * narrow, LANES), jnp.float32)],
        cost_estimate=gram_cost(wides, 128),
        compiler_params=PARAMS,
        name="mixed",
    )(wides, narrows)


def lane_gather(x, index):
    return jnp.take_along_axis(x, index, axis=1, mode="promise_in_bounds")


def trailing_update(a_ref, left_ref, right_ref, base):
    size = a_ref.shape[1]
    a_ref[pl.ds(pl.multiple_of(base, BLOCK), BLOCK), :] = jnp.zeros((BLOCK, size), jnp.float32)
    lane = lax.broadcasted_iota(jnp.int32, (1, size), 1)
    swept = (lane >= base - BLOCK) & (lane < base)
    update = transposed_dot(left_ref[...], right_ref[...])
    a_ref[BLOCK : BLOCK + size, :] = (
        jnp.where(swept, 0.0, a_ref[BLOCK : BLOCK + size, :]) - update
    )


def in_three(x):
    high = x.astype(jnp.bfloat16).astype(jnp.float32)
    rest = x - high
    middle = rest.astype(jnp.bfloat16).astype(jnp.float32)
    return high, middle, rest - middle


def factor_panel(rows_ref, cols_ref, tile, first, panel, targets):
    tiles = panel.shape[1] // LANES
    shape = (PANEL, LANES)
    _, lane = iotas(shape)

    def on_all(ref, k, lanes):
        return jnp.broadcast_to(ref[k : k + 1, lanes], shape)

    rows_ref[...] = panel
    lanes = [slice(LANES * t, LANES * (t + 1)) for t in range(tiles)]
    rows = [[on_all(rows_ref, k, part) for part in lanes] for k in range(PANEL)]
    here = panel[:, lanes[tile]]
    for j in range(PANEL):
        column = lane_gather(here, jnp.full(shape, 0, jnp.int32) + (first + j))
        cols_ref[PANEL * j : PANEL * (j + 1)] = column
    d = [[None] * PANEL for _ in range(PANEL)]
    for j in range(PANEL):
        for i in range(j, PANEL):
            d[i][j] = on_all(cols_ref, PANEL * j + i, slice(None))
    own = (lane >= first) & (lane < first + PANEL)
    q = [[None] * tiles for _ in range(PANEL)]
    p = [[None] * tiles for _ in range(PANEL)]
    weights = [[None] * PANEL for _ in targets]
    factor = [[None] * PANEL for _ in range(PANEL)]

    def substitute(k, scale):
        for t in range(tiles):
            value = rows[k][t]
            if t == tile:
                value = jnp.where(own, jnp.where(lane == first + k, -1.0, 0.0), value)
            for j in range(k):
                value = value - factor[k][j] * q[j][t]
            q[k][t] = value
            p[k][t] = value * scale
        for target, weight in zip(targets, weights):
            source, index = target(rows[k])
            value = lane_gather(source, index)
            for j in range(k):
                value = value - factor[k][j] * weight[j]
            weight[k] = value

    for k in range(0, PANEL, 2):
        m = k + 1
        a, b, c = d[k][k], d[m][k], d[m][m]
        first_scale = 1.0 / a
        second_scale = a * (1.0 / (a * c - b * b))
        factor[m][k] = b * first_scale
        left_over = {i: d[i][m] - d[i][k] * factor[m][k] for i in range(k + 2, PANEL)}
        for i in range(k + 2, PANEL):
            factor[i][k] = d[i][k] * first_scale
            factor[i][m] = left_over[i] * second_scale
        for i in range(k + 2, PANEL):
            for j in range(k + 2, i + 1):
                value = d[i][j] - d[i][k] * factor[j][k]
                d[i][j] = value - (left_over[i] * left_over[j]) * second_scale
        substitute(k, first_scale)
        substitute(m, second_scale)
    return q, p, weights


def packed_rows(values):
    sub, _ = iotas((PANEL, LANES))
    whole = []
    for t in range(len(values[0])):
        value = values[0][t]
        for k in range(1, PANEL):
            value = jnp.where(sub == k, values[k][t], value)
        whole.append(value)
    return whole


def side_by_side(tiles):
    return jnp.concatenate(tiles, axis=1) if len(tiles) > 1 else tiles[0]


def sweep_block(a_ref, left_ref, right_ref, a_rows, a_cols, b_rows, b_cols, tile, step, block):
    size = a_ref.shape[1]
    tiles = size // LANES
    first = step * BLOCK
    second = first + PANEL
    base = tile * LANES + first
    trailing_update(a_ref, left_ref, right_ref, base)

    sub, lane = iotas((PANEL, LANES))
    last = first == LANES - BLOCK
    next_first = jnp.where(last, 0, first + BLOCK)

    def in_block(row):
        return row[tile], second + sub

    def in_next(offset):
        def target(row):
            source = row[tile]
            if tile + 1 < tiles:
                source = jnp.where(last, row[tile + 1], source)
            return source, next_first + offset + sub

        return target

    nexts = [in_next(0), in_next(PANEL)]
    in_a = (lane >= first) & (lane < second)
    in_b = (lane >= second) & (lane < second + PANEL)

    def swept(tiles_of, mask):
        return [jnp.where(mask, 0.0, v) if t == tile else v for t, v in enumerate(tiles_of)]

    def minus(tiles_of, weight, p):
        result = []
        for t, value in enumerate(tiles_of):
            for k in range(PANEL):
                value = value - weight[k] * p[k][t]
            result.append(value)
        return result

    def by_tile(rows):
        return [rows[:, LANES * t : LANES * (t + 1)] for t in range(tiles)]

    qa, pa, (to_b, *to_next_a) = factor_panel(
        a_rows, a_cols, tile, first, block[:PANEL], [in_block, *nexts]
    )
    panel_b = side_by_side(minus(swept(by_tile(block[PANEL:]), in_a), to_b, pa))
    qb, pb, to_next_b = factor_panel(b_rows, b_cols, tile, second, panel_b, nexts)

    left, right = [], []
    for q, p, mask in ((qa, pa, in_b), (qb, pb, None)):
        q, p = packed_rows(q), packed_rows(p)
        if mask is not None:
            q, p = swept(q, mask), swept(p, mask)
        qs, ps = in_three(side_by_side(q)), in_three(side_by_side(p))
        left += [qs[i] for i in (0, 0, 1, 1, 0, 2)]
        right += [ps[i] for i in (0, 1, 0, 1, 2, 0)]
    left_ref[...] = jnp.concatenate(left, axis=0).astype(jnp.bfloat16)
    right_ref[...] = jnp.concatenate(right, axis=0).astype(jnp.bfloat16)

    following = a_ref[pl.ds(pl.multiple_of(base + 2 * BLOCK, BLOCK), BLOCK), :]
    result = []
    for g in range(2):
        rows = by_tile(following[g * PANEL : (g + 1) * PANEL])
        rows = minus(swept(rows, in_a), to_next_a[g], pa)
        rows = minus(swept(rows, in_b), to_next_b[g], pb)
        result.append(side_by_side(rows))
    return jnp.concatenate(result, axis=0)


def place_halves(place, pieces, first_row, flat):
    core = lax.axis_index(place.core)
    rows = flat.shape[0] // 2
    for r, piece in enumerate(pieces):
        start = pl.multiple_of(jnp.bitwise_xor(core, r) * rows, PANEL)
        flat[pl.ds(start, rows), :] = piece[first_row : first_row + rows]


def sweep_cost():
    return pl.CostEstimate(flops=1 << 30, bytes_accessed=1 << 20, transcendentals=0)


def clear(work):
    a_ref, left, right = work[:3]
    size = a_ref.shape[1]
    a_ref[:BLOCK] = jnp.zeros((BLOCK, size), jnp.float32)
    a_ref[BLOCK + size :] = jnp.zeros((BLOCK, size), jnp.float32)
    left[...] = jnp.zeros(left.shape, left.dtype)
    right[...] = jnp.zeros(right.shape, right.dtype)


def work_shapes(size):
    splits = 6 * BLOCK
    return [
        pltpu.VMEM((size + 2 * BLOCK, size), jnp.float32),
        pltpu.VMEM((splits, size), jnp.bfloat16),
        pltpu.VMEM((splits, size), jnp.bfloat16),
    ]


def row_shapes(size):
    return [
        pltpu.VMEM((PANEL, size), jnp.float32),
        pltpu.VMEM((PANEL * PANEL, LANES), jnp.float32),
    ] * 2


def aligned_rows(ref, index, count):
    if count % PANEL == 0:
        return ref[pl.ds(pl.multiple_of(index * count, count), count), :]
    per_slab = PANEL // count
    slab = ref[pl.ds(pl.multiple_of(index // per_slab * PANEL, PANEL), PANEL), :]
    value = slab[:count]
    for i in range(1, per_slab):
        value = jnp.where(index % per_slab == i, slab[i * count : (i + 1) * count], value)
    return value


def packs(cols, rows):
    return cols == 2 * PANEL and 2 * rows == LANES


def dot(a, b, last=False):
    return lax.dot_general(
        a,
        b,
        (((1,), (1 if last else 0,)), ((), ())),
        precision=HIGHEST,
        preferred_element_type=jnp.float32,
    )


STEPS = LANES // BLOCK
FIRST_STEPS = 5
SECOND_STEPS = 5


def sweep_both(wide_work, narrow_work, begin, end, blocks):
    def step(i, blocks):
        return (
            sweep_block(*wide_work, 0, i, blocks[0]),
            sweep_block(*narrow_work, 0, i, blocks[1]),
        )

    return lax.fori_loop(begin, end, step, blocks)


def sweep_wide(work, begin, end, block):
    return lax.fori_loop(begin, end, lambda i, block: sweep_block(*work, 1, i, block), block)


def unit_scale(block):
    row, col = iotas(block.shape)
    line = jnp.sum(jnp.where(row == col, block, 0.0), axis=0, keepdims=True)
    return jnp.broadcast_to(lax.rsqrt(line), (PANEL, block.shape[1]))


def scaled(block, down, across):
    columns = jnp.broadcast_to(down[:1], block.shape).T
    return (block * columns) * jnp.broadcast_to(across[:1], block.shape)


def first_kernel(
    place, total, mine, other, wa, wl, wr, wp, na, nl, nr, np_, ws_ref, ns_ref, *refs
):
    a_flat, b_flat = refs[:2]
    wide_work, narrow_work = (wa, wl, wr, *refs[2:6]), (na, nl, nr, *refs[6:])
    place_halves(place, (mine, other), 0, a_flat)
    place_halves(place, (mine, other), a_flat.shape[0] // 2, b_flat)
    n = LANES
    slab = a_flat[n : n + PANEL]
    first, square = unpack_pair(a_flat[:n], jnp.broadcast_to(slab[:1], (n, n)))
    corner = b_flat[:n] / total
    last = unfold(b_flat[n:], jnp.broadcast_to(slab[1:2], (n, n)))
    row, col = iotas((n, n))
    damp = jnp.where(row == col, DAMP, 0.0)
    clear(wide_work)
    clear(narrow_work)
    first, last, square = first / total + damp, last / total + damp, square / total + damp
    by_first, by_last, by_square = (unit_scale(block) for block in (first, last, square))
    ws_ref[:, :n] = by_first
    ws_ref[:, n:] = by_last
    ns_ref[...] = by_square
    corner = scaled(corner, by_first, by_last)
    wa[BLOCK : BLOCK + n, :n] = scaled(first, by_first, by_first)
    wa[BLOCK : BLOCK + n, n:] = corner
    wa[BLOCK + n : BLOCK + 2 * n, :n] = corner.T
    wa[BLOCK + n : BLOCK + 2 * n, n:] = scaled(last, by_last, by_last)
    na[BLOCK : BLOCK + n, :] = scaled(square, by_square, by_square)
    start = (wa[BLOCK : 2 * BLOCK, :], na[BLOCK : 2 * BLOCK, :])
    wp[...], np_[...] = sweep_both(wide_work, narrow_work, 0, FIRST_STEPS, start)


def second_kernel(*refs):
    given, scale, ninv_ref, state, narrow_state, wide_rows, narrow_rows = (
        refs[:8],
        refs[8],
        refs[9],
        refs[10:14],
        refs[14:17],
        refs[17:21],
        refs[21:],
    )
    for source, target in zip((*given[:3], *given[4:7]), (*state[:3], *narrow_state)):
        target[...] = source[...]
    wide_work, narrow_work = (*state[:3], *wide_rows), (*narrow_state, *narrow_rows)
    wp = state[3]
    panels = (given[3][...], given[7][...])
    panel, _ = sweep_both(wide_work, narrow_work, FIRST_STEPS, STEPS, panels)
    trailing_update(*narrow_work[:3], LANES)
    by_square = scale[...]
    ninv_ref[...] = scaled(-narrow_work[0][BLOCK : BLOCK + LANES, :], by_square, by_square)
    wp[...] = sweep_wide(wide_work, 0, SECOND_STEPS, panel)


def third_kernel(wa_in, wl_in, wr_in, panel_in, scale, winv, wa, wl, wr, *rows):
    wa[...] = wa_in[...]
    wl[...] = wl_in[...]
    wr[...] = wr_in[...]
    sweep_wide((wa, wl, wr, *rows), SECOND_STEPS, STEPS, panel_in[...])
    wide = wa.shape[1]
    trailing_update(wa, wl, wr, wide)
    parts = [slice(i, i + LANES) for i in range(0, wide, LANES)]
    for i in parts:
        for j in parts:
            block = -wa[BLOCK + i.start : BLOCK + i.stop, j]
            winv[i, j] = scaled(block, scale[:, i], scale[:, j])


def state_shapes(size):
    shapes = [jax.ShapeDtypeStruct(v.shape, v.dtype) for v in work_shapes(size)]
    return shapes + [jax.ShapeDtypeStruct((BLOCK, size), jnp.float32)]


def sweep_call(kernel, name, args, out_shapes, scratch):
    return pl.pallas_call(
        kernel,
        in_specs=[VMEM] * len(args),
        out_specs=[VMEM] * len(out_shapes),
        out_shape=out_shapes,
        scratch_shapes=scratch,
        cost_estimate=sweep_cost(),
        compiler_params=PARAMS,
        name=name,
    )(*args)


def first_panels(place, pieces, wide, narrow, total):
    return sweep_call(
        functools.partial(first_kernel, place, total),
        "first_panels",
        pieces,
        state_shapes(wide)
        + state_shapes(narrow)
        + [jax.ShapeDtypeStruct((PANEL, n), jnp.float32) for n in (wide, narrow)],
        [
            pltpu.VMEM((EARLY_ROWS, LANES), jnp.float32),
            pltpu.VMEM((LATE_ROWS, LANES), jnp.float32),
            *row_shapes(wide),
            *row_shapes(narrow),
        ],
    )


def second_panels(state, wide, narrow):
    ninv = jax.ShapeDtypeStruct((narrow, narrow), jnp.float32)
    return sweep_call(
        second_kernel,
        "second_panels",
        state,
        [ninv] + state_shapes(wide),
        [*work_shapes(narrow), *row_shapes(wide), *row_shapes(narrow)],
    )


def third_panels(state, wide):
    winv = jax.ShapeDtypeStruct((wide, wide), jnp.float32)
    scratch = [*work_shapes(wide), *row_shapes(wide)]
    return sweep_call(third_kernel, "third_panels", state, [winv], scratch)[0]


def product_kernel(place, total, rows, winv, ninv_ref, mine, other, out_ref, flat):
    place_halves(place, (mine, other), 0, flat)
    ninv = ninv_ref[...]
    n = LANES
    inner = jnp.concatenate(
        [
            transposed_dot(flat[c * n : (c + 1) * n] / total, ninv, HIGHEST)
            for c in range(2)
        ],
        axis=0,
    )
    wide = winv.shape[1]
    cols = wide // 2 ** len(place.dp)
    near, second = lax.axis_index(place.near), lax.axis_index(place.second)
    near_stride = 2 ** (len(place.dp) - 2)
    base = place.index(place.dp) - near * near_stride - second * 2
    _, lane = iotas((PANEL, LANES))
    for j in range(4):
        index = base + (j // 2) * near_stride + (j % 2) * 2
        picked = aligned_rows(winv, index, cols)
        update = lax.dot_general(
            picked,
            inner,
            (((1,), (0,)), ((), ())),
            precision=HIGHEST,
            preferred_element_type=jnp.float32,
        )
        for x in range(2):
            block = 2 * j + x
            out_ref[block, :cols] = picked[:, :LANES]
            out_ref[block, cols : 2 * cols] = picked[:, LANES:]
            if packs(cols, rows):
                upper, lower = update[:PANEL], update[PANEL:]
                if x == 0:
                    lower = pltpu.roll(lower, rows, 1)
                else:
                    upper = pltpu.roll(upper, rows, 1)
                out_ref[block, 2 * cols :] = jnp.where(lane < rows, upper, lower)
            else:
                out_ref[block, 2 * cols :] = update


def products(place, winv, ninv, pieces, rows, total):
    wide, narrow = winv.shape[0], ninv.shape[0]
    cols = wide // 2 ** len(place.dp)
    height = 2 * cols + (PANEL if packs(cols, rows) else cols)
    return pl.pallas_call(
        functools.partial(product_kernel, place, total, rows),
        in_specs=[VMEM] * 4,
        out_specs=VMEM,
        out_shape=jax.ShapeDtypeStruct((8, height, LANES), jnp.float32),
        scratch_shapes=[pltpu.VMEM((2 * narrow, LANES), jnp.float32)],
        compiler_params=PARAMS,
        name="products",
    )(winv, ninv, *pieces)


def placing_kernel(place, owner_map, got_ref, kept_ref, update_ref):
    layers = got_ref.shape[0]
    slots, cols, wide = kept_ref.shape
    rows = update_ref.shape[2]
    own, dp = place.index(place.own), place.index(place.dp)
    row, col = iotas((cols, wide))
    empty = jnp.where(col == row + dp * cols, 1.0 / DAMP, 0.0)
    count = jnp.int32(0)
    slot = []
    for l in range(layers):
        mine = owner_map[l] == own
        slot.append(jnp.where(mine, count, -1))
        count = count + mine.astype(jnp.int32)
    for h in range(2):
        lanes = slice(h * LANES, (h + 1) * LANES)
        for c in range(slots):
            value = empty[:, lanes]
            for l in range(layers):
                value = jnp.where(slot[l] == c, got_ref[l, h * cols : (h + 1) * cols], value)
            kept_ref[c, :, lanes] = value
    for l in range(layers):
        value = got_ref[l, 2 * cols :]
        if packs(cols, rows):
            update_ref[l, :PANEL] = value[:, :rows]
            update_ref[l, PANEL:] = value[:, rows:]
        else:
            part = value[:, :rows]
            for p in range(1, LANES // rows):
                part = jnp.where(own == p, value[:, p * rows : (p + 1) * rows], part)
            update_ref[l] = part


def placing(place, owner_map, got, wide, cols, slots, rows):
    layers = got.shape[0]
    return pl.pallas_call(
        functools.partial(placing_kernel, place),
        in_specs=[SMEM, VMEM],
        out_specs=[VMEM, VMEM],
        out_shape=[
            jax.ShapeDtypeStruct((slots, cols, wide), jnp.float32),
            jax.ShapeDtypeStruct((layers, cols, rows), jnp.float32),
        ],
        compiler_params=PARAMS,
        name="placing",
    )(owner_map, got)


def swap(value, axis):
    return lax.ppermute(value, axis, [(0, 1), (1, 0)])


def swap_by_core(value, place, stage):
    pairs = []
    for y in range(2):
        for core in range(2):
            for x in range(2):
                flip = 1 if core == stage else 4
                here = y * 4 + core * 2 + x
                pairs.append((here, here ^ flip))
    return lax.ppermute(value, (place.second, place.core, place.first), pairs)


def after(value, *others):
    return lax.optimization_barrier((value,) + others)[0]


def on_device(place, wide_rows, narrow_rows, owner_map):
    layers, rows, wide = wide_rows.shape
    narrow = narrow_rows.shape[2]
    n_dp, n_own = 2 ** len(place.dp), 2 ** len(place.own)
    total = float(rows * n_dp * n_own)

    h_keep, h_send, wides, narrows = hot_squares(place, wide_rows, narrow_rows)
    h_got = swap(h_send[:2], place.core)
    c_keep, c_send = cold_squares(place, after(wides, h_send), narrows)
    h_keep, c_send = lax.optimization_barrier((h_keep, c_send))

    hot = h_keep[:2] + h_got
    s_got = swap_by_core(hot, place, 0)
    c_got = swap(after(jnp.stack([c_send, h_send[2]]), hot), place.core)
    m_keep, m_send = mixed_sums(place, after(wides, hot), narrows)
    m_got = swap(m_send, place.core)
    s = jnp.stack([c_keep, h_keep[2]]) + after(c_got, m_send)

    s = s + s_got
    s_got = swap_by_core(s[1], place, 1)
    m = after(m_keep, s) + m_got
    m_got = swap_by_core(m[2:], place, 1)

    s = s[0] + s_got
    s_got = swap(s[1], place.near)
    m = after(m[:2], s) + m_got
    m_got = swap_by_core(m[1], place, 0)

    s = s[0] + s_got
    if place.extra:
        s = lax.psum(s, place.extra)
    s_got = swap(s, place.far)
    m = after(m[0], s) + m_got
    m_got = swap(m[1], place.near)

    s = s + s_got
    state = first_panels(place, [s, swap(s, place.core)], wide, narrow, total)
    m = after(m[0], state[0]) + m_got
    if place.extra:
        m = lax.psum(m, place.extra)
    m_got = swap(m, place.far)
    *state, wide_scale, narrow_scale = state
    ninv, *state = second_panels([*state, narrow_scale], wide, narrow)
    m = after(m, ninv) + m_got
    m_got = swap(m, place.core)
    winv = third_panels([*state, wide_scale], wide)
    cols, own_rows = wide // n_dp, narrow // n_own
    sent = products(place, winv, ninv, [m, m_got], own_rows, total)
    got = lax.all_to_all(sent, (place.near, place.second, place.first), 0, 0)
    kept, update = placing(
        place, owner_map, got, wide, cols, layers // n_own + 1, own_rows
    )
    return (jnp.swapaxes(kept, 1, 2), jnp.swapaxes(update, 1, 2))


def solution(mesh):
    n_dp, n_own = mesh.shape["dp"], mesh.shape["own"]
    dp_names = tuple(f"dp{i}" for i in range(int(np.log2(n_dp))))
    own_names = tuple(f"own{i}" for i in range(int(np.log2(n_own))))
    names = dp_names + own_names
    bits = jax.sharding.Mesh(mesh.devices.reshape((2,) * len(names)), names)
    in_specs = (P(None, names, None), P(None, names, None), P())
    out_specs = (P(own_names, None, dp_names), P(None, own_names, dp_names))
    return jax.shard_map(
        functools.partial(on_device, Place(dp_names, own_names)),
        mesh=bits,
        in_specs=in_specs,
        out_specs=out_specs,
        check_vma=False,
    )
```

```python
import functools

import jax
import jax.numpy as jnp
import numpy as np
from jax import lax
from jax.experimental import pallas as pl
from jax.experimental.pallas import tpu as pltpu
from jax.sharding import PartitionSpec as P

DAMP = 0.5
LANES = 128
PANEL = 8
BLOCK = 2 * PANEL
VMEM_LIMIT = 48 * 1024 * 1024
HIGHEST = lax.Precision.HIGHEST
VMEM = pl.BlockSpec(memory_space=pltpu.VMEM)
SMEM = pl.BlockSpec(memory_space=pltpu.SMEM)
HBM = pl.BlockSpec(memory_space=pltpu.HBM)
PARAMS = pltpu.CompilerParams(vmem_limit_bytes=VMEM_LIMIT)


class Place:
    def __init__(self, dp_names, own_names):
        self.dp, self.own = dp_names, own_names
        self.core, self.second, self.near, self.far = (
            dp_names[-1],
            dp_names[-2],
            dp_names[1],
            dp_names[0],
        )
        self.first = own_names[-1]
        used = (self.core, self.second, self.near, self.far, self.first)
        self.extra = tuple(n for n in dp_names + own_names if n not in used)

    def index(self, names):
        value = jnp.int32(0)
        for name in names:
            value = value * 2 + lax.axis_index(name)
        return value

    def layer(self):
        return self.index((self.near, self.second, self.first))


def transposed_dot(a, b, precision=None):
    return lax.dot_general(
        a, b, (((0,), (0,)), ((), ())), precision=precision, preferred_element_type=jnp.float32
    )


def layer_copies(place, sources, buffers, sems):
    layer = place.layer()
    return [
        [
            pltpu.make_async_copy(
                source.at[jnp.bitwise_xor(layer, i)], buffer.at[i], sems.at[i, s]
            )
            for s, (source, buffer) in enumerate(zip(sources, buffers))
        ]
        for i in range(buffers[0].shape[0])
    ]


def both_halves(place, flat, i):
    rows = flat.shape[1] // 2
    core = lax.axis_index(place.core)
    kept = pl.multiple_of(core * rows, PANEL)
    sent = pl.multiple_of((1 - core) * rows, PANEL)
    return flat[i, pl.ds(kept, rows), :], flat[i, pl.ds(sent, rows), :]


def by_core(place, first, second):
    core = lax.axis_index(place.core)
    return jnp.where(core == 0, first, second), jnp.where(core == 0, second, first)


def iotas(shape):
    return (
        lax.broadcasted_iota(jnp.int32, shape, 0),
        lax.broadcasted_iota(jnp.int32, shape, 1),
    )


def pack_pair(first, second):
    row, col = iotas(first.shape)
    return jnp.where(row >= col, first, second)


def unpack_pair(packed, second_diagonal):
    row, col = iotas(packed.shape)
    turned = packed.T
    first = jnp.where(row >= col, packed, turned)
    second = jnp.where(col > row, packed, turned)
    return first, jnp.where(row == col, second_diagonal, second)


def fold(block):
    h = block.shape[0] // 2
    row, col = iotas((h, 2 * h))
    last = pltpu.roll(block[h:], h, 1)
    return jnp.where((col >= h) | (row >= col), block[:h], last)


def unfold(folded, diagonal):
    h, n = folded.shape
    row, col = iotas((n, n))
    block = jnp.concatenate([folded, jnp.zeros((h, n), jnp.float32)], axis=0)
    turned = block.T
    top = jnp.where((col >= h) | (col <= row), block, turned)
    moved = pltpu.roll(pltpu.roll(block, h, 0), h, 1)
    moved_turned = pltpu.roll(pltpu.roll(turned, h, 0), h, 1)
    last = jnp.where(col > row, moved, moved_turned)
    last = jnp.where(row == col, diagonal, last)
    return jnp.where(row < h, top, jnp.where(col < h, turned, last))


def diagonals(blocks, rows):
    n = blocks[0].shape[0]
    row, col = iotas((n, n))
    slab_row, _ = iotas((rows, n))
    slab = jnp.zeros((rows, n), jnp.float32)
    for i, block in enumerate(blocks):
        line = jnp.sum(jnp.where(row == col, block, 0.0), axis=0, keepdims=True)
        slab = jnp.where(slab_row == i, jnp.broadcast_to(line, (rows, n)), slab)
    return slab


EARLY_ROWS = 144
LATE_ROWS = 192


HOT = (1, 2, 3, 5, 6, 7)
COLD = (0, 4)


def square_sums(wide, narrow):
    return transposed_dot(wide, wide), transposed_dot(narrow, narrow)


def pack_layer(place, i, wcov, ncov, a_flat, b_flat):
    n = LANES
    last = wcov[n:, n:]
    a_flat[i, :n] = pack_pair(wcov[:n, :n], ncov)
    a_flat[i, n:] = diagonals((ncov, last), EARLY_ROWS - n)
    b_flat[i, :n] = wcov[:n, n:]
    b_flat[i, n:] = fold(last)
    a_kept, a_sent = both_halves(place, a_flat, i)
    b_kept, b_sent = both_halves(place, b_flat, i)
    return (a_kept, b_kept), (a_sent, b_sent)


def put(ref, index, parts):
    rows = EARLY_ROWS // 2
    ref[*index, :rows] = parts[0]
    ref[*index, rows:] = parts[1]


def hot_kernel(place, wide_hbm, narrow_hbm, keep, send, wides, narrows, a_flat, b_flat, sems):
    copies = layer_copies(place, (wide_hbm, narrow_hbm), (wides, narrows), sems)
    order = HOT + COLD
    for i in order:
        for copy in copies[i]:
            copy.start()

    def pack(i, sums):
        kept, sent = pack_layer(place, i, *sums, a_flat, b_flat)
        z, y, x = i // 4, (i // 2) % 2, i % 2
        if x and y:
            mine = other = 1
        else:
            mine, other = by_core(place, 0 if x else 2, 2 if x else 0)
        put(keep, (mine, z), kept)
        put(send, (other, z), sent)

    before = None
    for i in order:
        for copy in copies[i]:
            copy.wait()
        if before is not None:
            pack(*before)
            before = None
        if i in HOT:
            before = (i, square_sums(wides[i], narrows[i]))


def cold_kernel(place, wides, narrows, keep, send, a_flat, b_flat):
    for i in COLD:
        sums = square_sums(wides[i], narrows[i])
        kept, sent = pack_layer(place, i, *sums, a_flat, b_flat)
        put(keep, (i // 4,), kept)
        put(send, (i // 4,), sent)


def write_slots(place, owner_map, slots_ref):
    own = place.index(place.own)
    count = jnp.int32(0)
    for l in range(slots_ref.shape[0]):
        mine = owner_map[l] == own
        slot = jnp.where(mine, count, -1)
        slots_ref[l] = jnp.full(slots_ref.shape[1:], 0, jnp.int32) + slot
        count = count + mine.astype(jnp.int32)


def mixed_kernel(place, owner_map, wides, narrows, keep, send, slots_ref, flat):
    n = LANES
    write_slots(place, owner_map, slots_ref)
    for i in range(wides.shape[0]):
        mixed = transposed_dot(narrows[i], wides[i])
        flat[i, :n] = mixed[:, :n]
        flat[i, n:] = mixed[:, n:]
        kept, sent = both_halves(place, flat, i)
        z, y, x = i // 4, (i // 2) % 2, i % 2
        mine, other = by_core(place, y * 2 + x, x * 2 + y)
        keep[mine, z] = kept
        send[other, z] = sent


def gram_cost(wide_rows, columns):
    return pl.CostEstimate(
        flops=2 * wide_rows.size * columns, bytes_accessed=2 * wide_rows.size, transcendentals=0
    )


HALF_ROWS = (EARLY_ROWS + LATE_ROWS) // 2


def pack_shapes(layers):
    return [
        pltpu.VMEM((layers, EARLY_ROWS, LANES), jnp.float32),
        pltpu.VMEM((layers, LATE_ROWS, LANES), jnp.float32),
    ]


def hot_squares(place, wide_rows, narrow_rows):
    layers = wide_rows.shape[0]
    half = jax.ShapeDtypeStruct((3, 2, HALF_ROWS, LANES), jnp.float32)
    return pl.pallas_call(
        functools.partial(hot_kernel, place),
        in_specs=[HBM, HBM],
        out_specs=[VMEM] * 4,
        out_shape=[
            half,
            half,
            jax.ShapeDtypeStruct(wide_rows.shape, wide_rows.dtype),
            jax.ShapeDtypeStruct(narrow_rows.shape, narrow_rows.dtype),
        ],
        scratch_shapes=[*pack_shapes(layers), pltpu.SemaphoreType.DMA((layers, 2))],
        cost_estimate=gram_cost(wide_rows, 240),
        compiler_params=PARAMS,
        name="hot_squares",
    )(
        pltpu.with_memory_space_constraint(wide_rows, pltpu.HBM),
        pltpu.with_memory_space_constraint(narrow_rows, pltpu.HBM),
    )


def cold_squares(place, wides, narrows):
    half = jax.ShapeDtypeStruct((2, HALF_ROWS, LANES), jnp.float32)
    return pl.pallas_call(
        functools.partial(cold_kernel, place),
        in_specs=[VMEM, VMEM],
        out_specs=[VMEM, VMEM],
        out_shape=[half, half],
        scratch_shapes=pack_shapes(wides.shape[0]),
        cost_estimate=gram_cost(wides, 80),
        compiler_params=PARAMS,
        name="cold_squares",
    )(wides, narrows)


def mixed_sums(place, owner_map, wides, narrows):
    layers, _, narrow = narrows.shape
    half = jax.ShapeDtypeStruct((4, 2, narrow, LANES), jnp.float32)
    return pl.pallas_call(
        functools.partial(mixed_kernel, place),
        in_specs=[SMEM, VMEM, VMEM],
        out_specs=[VMEM] * 3,
        out_shape=[half, half, jax.ShapeDtypeStruct((layers, PANEL, LANES), jnp.int32)],
        scratch_shapes=[pltpu.VMEM((layers, 2 * narrow, LANES), jnp.float32)],
        cost_estimate=gram_cost(wides, 128),
        compiler_params=PARAMS,
        name="mixed",
    )(owner_map, wides, narrows)


def lane_gather(x, index):
    return jnp.take_along_axis(x, index, axis=1, mode="promise_in_bounds")


def trailing_update(a_ref, left_ref, right_ref, base):
    size = a_ref.shape[1]
    a_ref[pl.ds(pl.multiple_of(base, BLOCK), BLOCK), :] = jnp.zeros((BLOCK, size), jnp.float32)
    lane = lax.broadcasted_iota(jnp.int32, (1, size), 1)
    swept = (lane >= base - BLOCK) & (lane < base)
    update = transposed_dot(left_ref[...], right_ref[...])
    a_ref[BLOCK : BLOCK + size, :] = (
        jnp.where(swept, 0.0, a_ref[BLOCK : BLOCK + size, :]) - update
    )


def in_three(x):
    high = x.astype(jnp.bfloat16).astype(jnp.float32)
    rest = x - high
    middle = rest.astype(jnp.bfloat16).astype(jnp.float32)
    return high, middle, rest - middle


def factor_panel(rows_ref, cols_ref, tile, first, panel, targets):
    tiles = panel.shape[1] // LANES
    shape = (PANEL, LANES)
    _, lane = iotas(shape)

    def on_all(ref, k, lanes):
        return jnp.broadcast_to(ref[k : k + 1, lanes], shape)

    rows_ref[...] = panel
    lanes = [slice(LANES * t, LANES * (t + 1)) for t in range(tiles)]
    rows = [[on_all(rows_ref, k, part) for part in lanes] for k in range(PANEL)]
    here = panel[:, lanes[tile]]
    for j in range(PANEL):
        column = lane_gather(here, jnp.full(shape, 0, jnp.int32) + (first + j))
        cols_ref[PANEL * j : PANEL * (j + 1)] = column
    d = [[None] * PANEL for _ in range(PANEL)]
    for j in range(PANEL):
        for i in range(j, PANEL):
            d[i][j] = on_all(cols_ref, PANEL * j + i, slice(None))
    own = (lane >= first) & (lane < first + PANEL)
    q = [[None] * tiles for _ in range(PANEL)]
    p = [[None] * tiles for _ in range(PANEL)]
    weights = [[None] * PANEL for _ in targets]
    factor = [[None] * PANEL for _ in range(PANEL)]

    def substitute(k, scale):
        for t in range(tiles):
            value = rows[k][t]
            if t == tile:
                value = jnp.where(own, jnp.where(lane == first + k, -1.0, 0.0), value)
            for j in range(k):
                value = value - factor[k][j] * q[j][t]
            q[k][t] = value
            p[k][t] = value * scale
        for target, weight in zip(targets, weights):
            source, index = target(rows[k])
            value = lane_gather(source, index)
            for j in range(k):
                value = value - factor[k][j] * weight[j]
            weight[k] = value

    for k in range(0, PANEL, 2):
        m = k + 1
        a, b, c = d[k][k], d[m][k], d[m][m]
        first_scale = 1.0 / a
        second_scale = a * (1.0 / (a * c - b * b))
        factor[m][k] = b * first_scale
        left_over = {i: d[i][m] - d[i][k] * factor[m][k] for i in range(k + 2, PANEL)}
        for i in range(k + 2, PANEL):
            factor[i][k] = d[i][k] * first_scale
            factor[i][m] = left_over[i] * second_scale
        for i in range(k + 2, PANEL):
            for j in range(k + 2, i + 1):
                value = d[i][j] - d[i][k] * factor[j][k]
                d[i][j] = value - (left_over[i] * left_over[j]) * second_scale
        substitute(k, first_scale)
        substitute(m, second_scale)
    return q, p, weights


def packed_rows(values):
    sub, _ = iotas((PANEL, LANES))
    whole = []
    for t in range(len(values[0])):
        value = values[0][t]
        for k in range(1, PANEL):
            value = jnp.where(sub == k, values[k][t], value)
        whole.append(value)
    return whole


def side_by_side(tiles):
    return jnp.concatenate(tiles, axis=1) if len(tiles) > 1 else tiles[0]


def sweep_block(a_ref, left_ref, right_ref, a_rows, a_cols, b_rows, b_cols, tile, step, block):
    size = a_ref.shape[1]
    tiles = size // LANES
    first = step * BLOCK
    second = first + PANEL
    base = tile * LANES + first
    trailing_update(a_ref, left_ref, right_ref, base)

    sub, lane = iotas((PANEL, LANES))
    last = first == LANES - BLOCK
    next_first = jnp.where(last, 0, first + BLOCK)

    def in_block(row):
        return row[tile], second + sub

    def in_next(offset):
        def target(row):
            source = row[tile]
            if tile + 1 < tiles:
                source = jnp.where(last, row[tile + 1], source)
            return source, next_first + offset + sub

        return target

    nexts = [in_next(0), in_next(PANEL)]
    in_a = (lane >= first) & (lane < second)
    in_b = (lane >= second) & (lane < second + PANEL)

    def swept(tiles_of, mask):
        return [jnp.where(mask, 0.0, v) if t == tile else v for t, v in enumerate(tiles_of)]

    def minus(tiles_of, weight, p):
        result = []
        for t, value in enumerate(tiles_of):
            for k in range(PANEL):
                value = value - weight[k] * p[k][t]
            result.append(value)
        return result

    def by_tile(rows):
        return [rows[:, LANES * t : LANES * (t + 1)] for t in range(tiles)]

    qa, pa, (to_b, *to_next_a) = factor_panel(
        a_rows, a_cols, tile, first, block[:PANEL], [in_block, *nexts]
    )
    panel_b = side_by_side(minus(swept(by_tile(block[PANEL:]), in_a), to_b, pa))
    qb, pb, to_next_b = factor_panel(b_rows, b_cols, tile, second, panel_b, nexts)

    left, right = [], []
    for q, p, mask in ((qa, pa, in_b), (qb, pb, None)):
        q, p = packed_rows(q), packed_rows(p)
        if mask is not None:
            q, p = swept(q, mask), swept(p, mask)
        qs, ps = in_three(side_by_side(q)), in_three(side_by_side(p))
        left += [qs[i] for i in (0, 0, 1, 1, 0, 2)]
        right += [ps[i] for i in (0, 1, 0, 1, 2, 0)]
    left_ref[...] = jnp.concatenate(left, axis=0).astype(jnp.bfloat16)
    right_ref[...] = jnp.concatenate(right, axis=0).astype(jnp.bfloat16)

    following = a_ref[pl.ds(pl.multiple_of(base + 2 * BLOCK, BLOCK), BLOCK), :]
    result = []
    for g in range(2):
        rows = by_tile(following[g * PANEL : (g + 1) * PANEL])
        rows = minus(swept(rows, in_a), to_next_a[g], pa)
        rows = minus(swept(rows, in_b), to_next_b[g], pb)
        result.append(side_by_side(rows))
    return jnp.concatenate(result, axis=0)


def place_halves(place, pieces, first_row, flat):
    core = lax.axis_index(place.core)
    rows = flat.shape[0] // 2
    for r, piece in enumerate(pieces):
        start = pl.multiple_of(jnp.bitwise_xor(core, r) * rows, PANEL)
        flat[pl.ds(start, rows), :] = piece[first_row : first_row + rows]


def sweep_cost():
    return pl.CostEstimate(flops=1 << 30, bytes_accessed=1 << 20, transcendentals=0)


def clear(work):
    a_ref, left, right = work[:3]
    size = a_ref.shape[1]
    a_ref[:BLOCK] = jnp.zeros((BLOCK, size), jnp.float32)
    a_ref[BLOCK + size :] = jnp.zeros((BLOCK, size), jnp.float32)
    left[...] = jnp.zeros(left.shape, left.dtype)
    right[...] = jnp.zeros(right.shape, right.dtype)


def work_shapes(size):
    splits = 6 * BLOCK
    return [
        pltpu.VMEM((size + 2 * BLOCK, size), jnp.float32),
        pltpu.VMEM((splits, size), jnp.bfloat16),
        pltpu.VMEM((splits, size), jnp.bfloat16),
    ]


def row_shapes(size):
    return [
        pltpu.VMEM((PANEL, size), jnp.float32),
        pltpu.VMEM((PANEL * PANEL, LANES), jnp.float32),
    ] * 2


def aligned_rows(ref, index, count):
    if count % PANEL == 0:
        return ref[pl.ds(pl.multiple_of(index * count, count), count), :]
    per_slab = PANEL // count
    slab = ref[pl.ds(pl.multiple_of(index // per_slab * PANEL, PANEL), PANEL), :]
    value = slab[:count]
    for i in range(1, per_slab):
        value = jnp.where(index % per_slab == i, slab[i * count : (i + 1) * count], value)
    return value


def packs(cols, rows):
    return cols == 2 * PANEL and 2 * rows == LANES


def dot(a, b, last=False):
    return lax.dot_general(
        a,
        b,
        (((1,), (1 if last else 0,)), ((), ())),
        precision=HIGHEST,
        preferred_element_type=jnp.float32,
    )


STEPS = LANES // BLOCK
FIRST_STEPS = 5
SECOND_STEPS = 5


def sweep_both(wide_work, narrow_work, begin, end, blocks):
    def step(i, blocks):
        return (
            sweep_block(*wide_work, 0, i, blocks[0]),
            sweep_block(*narrow_work, 0, i, blocks[1]),
        )

    return lax.fori_loop(begin, end, step, blocks)


def sweep_wide(work, begin, end, block):
    return lax.fori_loop(begin, end, lambda i, block: sweep_block(*work, 1, i, block), block)


def unit_scale(block):
    row, col = iotas(block.shape)
    line = jnp.sum(jnp.where(row == col, block, 0.0), axis=0, keepdims=True)
    return jnp.broadcast_to(lax.rsqrt(line), (PANEL, block.shape[1]))


def scaled(block, down, across):
    columns = jnp.broadcast_to(down[:1], block.shape).T
    return (block * columns) * jnp.broadcast_to(across[:1], block.shape)


def first_kernel(
    place, total, mine, other, wa, wl, wr, wp, na, nl, nr, np_, ws_ref, ns_ref, *refs
):
    a_flat, b_flat = refs[:2]
    wide_work, narrow_work = (wa, wl, wr, *refs[2:6]), (na, nl, nr, *refs[6:])
    place_halves(place, (mine, other), 0, a_flat)
    place_halves(place, (mine, other), a_flat.shape[0] // 2, b_flat)
    n = LANES
    slab = a_flat[n : n + PANEL]
    first, square = unpack_pair(a_flat[:n], jnp.broadcast_to(slab[:1], (n, n)))
    corner = b_flat[:n] / total
    last = unfold(b_flat[n:], jnp.broadcast_to(slab[1:2], (n, n)))
    row, col = iotas((n, n))
    damp = jnp.where(row == col, DAMP, 0.0)
    clear(wide_work)
    clear(narrow_work)
    first, last, square = first / total + damp, last / total + damp, square / total + damp
    by_first, by_last, by_square = (unit_scale(block) for block in (first, last, square))
    ws_ref[:, :n] = by_first
    ws_ref[:, n:] = by_last
    ns_ref[...] = by_square
    corner = scaled(corner, by_first, by_last)
    wa[BLOCK : BLOCK + n, :n] = scaled(first, by_first, by_first)
    wa[BLOCK : BLOCK + n, n:] = corner
    wa[BLOCK + n : BLOCK + 2 * n, :n] = corner.T
    wa[BLOCK + n : BLOCK + 2 * n, n:] = scaled(last, by_last, by_last)
    na[BLOCK : BLOCK + n, :] = scaled(square, by_square, by_square)
    start = (wa[BLOCK : 2 * BLOCK, :], na[BLOCK : 2 * BLOCK, :])
    wp[...], np_[...] = sweep_both(wide_work, narrow_work, 0, FIRST_STEPS, start)


def second_kernel(*refs):
    given, scale, ninv_ref, state, narrow_state, wide_rows, narrow_rows = (
        refs[:8],
        refs[8],
        refs[9],
        refs[10:14],
        refs[14:17],
        refs[17:21],
        refs[21:],
    )
    for source, target in zip((*given[:3], *given[4:7]), (*state[:3], *narrow_state)):
        target[...] = source[...]
    wide_work, narrow_work = (*state[:3], *wide_rows), (*narrow_state, *narrow_rows)
    wp = state[3]
    panels = (given[3][...], given[7][...])
    panel, _ = sweep_both(wide_work, narrow_work, FIRST_STEPS, STEPS, panels)
    trailing_update(*narrow_work[:3], LANES)
    by_square = scale[...]
    ninv_ref[...] = scaled(-narrow_work[0][BLOCK : BLOCK + LANES, :], by_square, by_square)
    wp[...] = sweep_wide(wide_work, 0, SECOND_STEPS, panel)


def third_kernel(wa_in, wl_in, wr_in, panel_in, scale, winv, wa, wl, wr, *rows):
    wa[...] = wa_in[...]
    wl[...] = wl_in[...]
    wr[...] = wr_in[...]
    sweep_wide((wa, wl, wr, *rows), SECOND_STEPS, STEPS, panel_in[...])
    wide = wa.shape[1]
    trailing_update(wa, wl, wr, wide)
    parts = [slice(i, i + LANES) for i in range(0, wide, LANES)]
    for i in parts:
        for j in parts:
            block = -wa[BLOCK + i.start : BLOCK + i.stop, j]
            winv[i, j] = scaled(block, scale[:, i], scale[:, j])


def state_shapes(size):
    shapes = [jax.ShapeDtypeStruct(v.shape, v.dtype) for v in work_shapes(size)]
    return shapes + [jax.ShapeDtypeStruct((BLOCK, size), jnp.float32)]


def sweep_call(kernel, name, args, out_shapes, scratch):
    return pl.pallas_call(
        kernel,
        in_specs=[VMEM] * len(args),
        out_specs=[VMEM] * len(out_shapes),
        out_shape=out_shapes,
        scratch_shapes=scratch,
        cost_estimate=sweep_cost(),
        compiler_params=PARAMS,
        name=name,
    )(*args)


def first_panels(place, pieces, wide, narrow, total):
    return sweep_call(
        functools.partial(first_kernel, place, total),
        "first_panels",
        pieces,
        state_shapes(wide)
        + state_shapes(narrow)
        + [jax.ShapeDtypeStruct((PANEL, n), jnp.float32) for n in (wide, narrow)],
        [
            pltpu.VMEM((EARLY_ROWS, LANES), jnp.float32),
            pltpu.VMEM((LATE_ROWS, LANES), jnp.float32),
            *row_shapes(wide),
            *row_shapes(narrow),
        ],
    )


def second_panels(state, wide, narrow):
    ninv = jax.ShapeDtypeStruct((narrow, narrow), jnp.float32)
    return sweep_call(
        second_kernel,
        "second_panels",
        state,
        [ninv] + state_shapes(wide),
        [*work_shapes(narrow), *row_shapes(wide), *row_shapes(narrow)],
    )


def third_panels(state, wide):
    winv = jax.ShapeDtypeStruct((wide, wide), jnp.float32)
    scratch = [*work_shapes(wide), *row_shapes(wide)]
    return sweep_call(third_kernel, "third_panels", state, [winv], scratch)[0]


def product_kernel(place, total, rows, winv, ninv_ref, mine, other, out_ref, flat):
    place_halves(place, (mine, other), 0, flat)
    ninv = ninv_ref[...]
    n = LANES
    inner = jnp.concatenate(
        [
            transposed_dot(flat[c * n : (c + 1) * n] / total, ninv, HIGHEST)
            for c in range(2)
        ],
        axis=0,
    )
    wide = winv.shape[1]
    cols = wide // 2 ** len(place.dp)
    near, second = lax.axis_index(place.near), lax.axis_index(place.second)
    near_stride = 2 ** (len(place.dp) - 2)
    base = place.index(place.dp) - near * near_stride - second * 2
    _, lane = iotas((PANEL, LANES))
    for j in range(4):
        index = base + (j // 2) * near_stride + (j % 2) * 2
        picked = aligned_rows(winv, index, cols)
        update = lax.dot_general(
            picked,
            inner,
            (((1,), (0,)), ((), ())),
            precision=HIGHEST,
            preferred_element_type=jnp.float32,
        )
        for x in range(2):
            block = 2 * j + x
            out_ref[block, :cols] = picked[:, :LANES]
            out_ref[block, cols : 2 * cols] = picked[:, LANES:]
            if packs(cols, rows):
                upper, lower = update[:PANEL], update[PANEL:]
                if x == 0:
                    lower = pltpu.roll(lower, rows, 1)
                else:
                    upper = pltpu.roll(upper, rows, 1)
                out_ref[block, 2 * cols :] = jnp.where(lane < rows, upper, lower)
            else:
                out_ref[block, 2 * cols :] = update


def products(place, winv, ninv, pieces, rows, total):
    wide, narrow = winv.shape[0], ninv.shape[0]
    cols = wide // 2 ** len(place.dp)
    height = 2 * cols + (PANEL if packs(cols, rows) else cols)
    return pl.pallas_call(
        functools.partial(product_kernel, place, total, rows),
        in_specs=[VMEM] * 4,
        out_specs=VMEM,
        out_shape=jax.ShapeDtypeStruct((8, height, LANES), jnp.float32),
        scratch_shapes=[pltpu.VMEM((2 * narrow, LANES), jnp.float32)],
        compiler_params=PARAMS,
        name="products",
    )(winv, ninv, *pieces)


def placing_kernel(place, slots_ref, got_ref, kept_ref, update_ref):
    layers = got_ref.shape[0]
    slots, cols, wide = kept_ref.shape
    rows = update_ref.shape[2]
    own, dp = place.index(place.own), place.index(place.dp)
    step = min(cols, PANEL)
    row, col = iotas((step, LANES))
    for h in range(wide // LANES):
        lanes = slice(h * LANES, (h + 1) * LANES)
        for r in range(0, cols, step):
            here = h * cols + r
            empty = jnp.where(col + h * LANES == row + dp * cols + r, 1.0 / DAMP, 0.0)
            for c in range(slots):
                value = empty
                for l in range(layers):
                    taken = slots_ref[l, :step] == c
                    value = jnp.where(taken, got_ref[l, here : here + step], value)
                kept_ref[c, r : r + step, lanes] = value
    for l in range(layers):
        value = got_ref[l, 2 * cols :]
        if packs(cols, rows):
            update_ref[l, :PANEL] = value[:, :rows]
            update_ref[l, PANEL:] = value[:, rows:]
        else:
            part = value[:, :rows]
            for p in range(1, LANES // rows):
                part = jnp.where(own == p, value[:, p * rows : (p + 1) * rows], part)
            update_ref[l] = part


def placing(place, slots_of, got, wide, cols, slots, rows):
    layers = got.shape[0]
    return pl.pallas_call(
        functools.partial(placing_kernel, place),
        in_specs=[VMEM, VMEM],
        out_specs=[VMEM, VMEM],
        out_shape=[
            jax.ShapeDtypeStruct((slots, cols, wide), jnp.float32),
            jax.ShapeDtypeStruct((layers, cols, rows), jnp.float32),
        ],
        compiler_params=PARAMS,
        name="placing",
    )(slots_of, got)


def swap(value, axis):
    return lax.ppermute(value, axis, [(0, 1), (1, 0)])


def swap_by_core(value, place, stage):
    pairs = []
    for y in range(2):
        for core in range(2):
            for x in range(2):
                flip = 1 if core == stage else 4
                here = y * 4 + core * 2 + x
                pairs.append((here, here ^ flip))
    return lax.ppermute(value, (place.second, place.core, place.first), pairs)


def after(value, *others):
    return lax.optimization_barrier((value,) + others)[0]


def on_device(place, wide_rows, narrow_rows, owner_map):
    layers, rows, wide = wide_rows.shape
    narrow = narrow_rows.shape[2]
    n_dp, n_own = 2 ** len(place.dp), 2 ** len(place.own)
    total = float(rows * n_dp * n_own)

    h_keep, h_send, wides, narrows = hot_squares(place, wide_rows, narrow_rows)
    h_got = swap(h_send[:2], place.core)
    c_keep, c_send = cold_squares(place, after(wides, h_send), narrows)
    h_keep, c_send = lax.optimization_barrier((h_keep, c_send))

    hot = h_keep[:2] + h_got
    s_got = swap_by_core(hot, place, 0)
    m_keep, m_send, slots_of = mixed_sums(place, owner_map, after(wides, hot), narrows)
    c_got = swap(after(jnp.stack([c_send, h_send[2]]), m_send), place.core)
    m_got = swap(m_send, place.core)
    s = jnp.stack([c_keep, h_keep[2]]) + s_got
    s = s + after(c_got, s)
    s_got = swap_by_core(s[1], place, 1)
    m = after(m_keep, s) + m_got
    m_got = swap_by_core(m[2:], place, 1)

    s = s[0] + s_got
    s_got = swap(s[1], place.near)
    m = after(m[:2], s) + m_got
    m_got = swap_by_core(m[1], place, 0)

    s = s[0] + s_got
    if place.extra:
        s = lax.psum(s, place.extra)
    s_got = swap(s, place.far)
    m = after(m[0], s) + m_got
    m_got = swap(m[1], place.near)

    s = s + s_got
    state = first_panels(place, [s, swap(s, place.core)], wide, narrow, total)
    m = after(m[0], state[0]) + m_got
    if place.extra:
        m = lax.psum(m, place.extra)
    m_got = swap(m, place.far)
    *state, wide_scale, narrow_scale = state
    ninv, *state = second_panels([*state, narrow_scale], wide, narrow)
    m = after(m, ninv) + m_got
    m_got = swap(m, place.core)
    winv = third_panels([*state, wide_scale], wide)
    cols, own_rows = wide // n_dp, narrow // n_own
    sent = products(place, winv, ninv, [m, m_got], own_rows, total)
    got = lax.all_to_all(sent, (place.near, place.second, place.first), 0, 0)
    kept, update = placing(
        place, slots_of, got, wide, cols, layers // n_own + 1, own_rows
    )
    return (jnp.swapaxes(kept, 1, 2), jnp.swapaxes(update, 1, 2))


def solution(mesh):
    n_dp, n_own = mesh.shape["dp"], mesh.shape["own"]
    dp_names = tuple(f"dp{i}" for i in range(int(np.log2(n_dp))))
    own_names = tuple(f"own{i}" for i in range(int(np.log2(n_own))))
    names = dp_names + own_names
    bits = jax.sharding.Mesh(mesh.devices.reshape((2,) * len(names)), names)
    in_specs = (P(None, names, None), P(None, names, None), P())
    out_specs = (P(own_names, None, dp_names), P(None, own_names, dp_names))
    return jax.shard_map(
        functools.partial(on_device, Place(dp_names, own_names)),
        mesh=bits,
        in_specs=in_specs,
        out_specs=out_specs,
        check_vma=False,
    )
```

```python
import functools

import jax
import jax.numpy as jnp
import numpy as np
from jax import lax
from jax.experimental import pallas as pl
from jax.experimental.pallas import tpu as pltpu
from jax.sharding import PartitionSpec as P

DAMP = 0.5
LANES = 128
PANEL = 8
BLOCK = 2 * PANEL
VMEM_LIMIT = 48 * 1024 * 1024
HIGHEST = lax.Precision.HIGHEST
VMEM = pl.BlockSpec(memory_space=pltpu.VMEM)
SMEM = pl.BlockSpec(memory_space=pltpu.SMEM)
HBM = pl.BlockSpec(memory_space=pltpu.HBM)
PARAMS = pltpu.CompilerParams(vmem_limit_bytes=VMEM_LIMIT)


class Place:
    def __init__(self, dp_names, own_names):
        self.dp, self.own = dp_names, own_names
        self.core, self.second, self.near, self.far = (
            dp_names[-1],
            dp_names[-2],
            dp_names[1],
            dp_names[0],
        )
        self.first = own_names[-1]
        used = (self.core, self.second, self.near, self.far, self.first)
        self.extra = tuple(n for n in dp_names + own_names if n not in used)

    def index(self, names):
        value = jnp.int32(0)
        for name in names:
            value = value * 2 + lax.axis_index(name)
        return value

    def layer(self):
        return self.index((self.near, self.second, self.first))


def transposed_dot(a, b, precision=None):
    return lax.dot_general(
        a, b, (((0,), (0,)), ((), ())), precision=precision, preferred_element_type=jnp.float32
    )


AHEAD = 5


def layer_copies(place, sources, buffers, sems):
    layer = place.layer()
    return [
        [
            pltpu.make_async_copy(
                source.at[jnp.bitwise_xor(layer, i)], buffer.at[i], sems.at[i, s]
            )
            for s, (source, buffer) in enumerate(zip(sources, buffers))
        ]
        for i in range(buffers[0].shape[0])
    ]


def both_halves(place, flat, i):
    rows = flat.shape[1] // 2
    core = lax.axis_index(place.core)
    kept = pl.multiple_of(core * rows, PANEL)
    sent = pl.multiple_of((1 - core) * rows, PANEL)
    return flat[i, pl.ds(kept, rows), :], flat[i, pl.ds(sent, rows), :]


def by_core(place, first, second):
    core = lax.axis_index(place.core)
    return jnp.where(core == 0, first, second), jnp.where(core == 0, second, first)


def iotas(shape):
    return (
        lax.broadcasted_iota(jnp.int32, shape, 0),
        lax.broadcasted_iota(jnp.int32, shape, 1),
    )


def pack_pair(first, second):
    row, col = iotas(first.shape)
    return jnp.where(row >= col, first, second)


def unpack_pair(packed, second_diagonal):
    row, col = iotas(packed.shape)
    turned = packed.T
    first = jnp.where(row >= col, packed, turned)
    second = jnp.where(col > row, packed, turned)
    return first, jnp.where(row == col, second_diagonal, second)


def fold(block):
    h = block.shape[0] // 2
    row, col = iotas((h, 2 * h))
    last = pltpu.roll(block[h:], h, 1)
    return jnp.where((col >= h) | (row >= col), block[:h], last)


def unfold(folded, diagonal):
    h, n = folded.shape
    row, col = iotas((n, n))
    block = jnp.concatenate([folded, jnp.zeros((h, n), jnp.float32)], axis=0)
    turned = block.T
    top = jnp.where((col >= h) | (col <= row), block, turned)
    moved = pltpu.roll(pltpu.roll(block, h, 0), h, 1)
    moved_turned = pltpu.roll(pltpu.roll(turned, h, 0), h, 1)
    last = jnp.where(col > row, moved, moved_turned)
    last = jnp.where(row == col, diagonal, last)
    return jnp.where(row < h, top, jnp.where(col < h, turned, last))


def diagonals(blocks, rows):
    n = blocks[0].shape[0]
    row, col = iotas((n, n))
    slab_row, _ = iotas((rows, n))
    slab = jnp.zeros((rows, n), jnp.float32)
    for i, block in enumerate(blocks):
        line = jnp.sum(jnp.where(row == col, block, 0.0), axis=0, keepdims=True)
        slab = jnp.where(slab_row == i, jnp.broadcast_to(line, (rows, n)), slab)
    return slab


EARLY_ROWS = 144
LATE_ROWS = 192


HOT = (1, 2, 3, 5, 6, 7)
COLD = (0, 4)


def square_sums(wide, narrow):
    return transposed_dot(wide, wide), transposed_dot(narrow, narrow)


def pack_layer(place, i, wcov, ncov, a_flat, b_flat):
    n = LANES
    last = wcov[n:, n:]
    a_flat[i, :n] = pack_pair(wcov[:n, :n], ncov)
    a_flat[i, n:] = diagonals((ncov, last), EARLY_ROWS - n)
    b_flat[i, :n] = wcov[:n, n:]
    b_flat[i, n:] = fold(last)
    a_kept, a_sent = both_halves(place, a_flat, i)
    b_kept, b_sent = both_halves(place, b_flat, i)
    return (a_kept, b_kept), (a_sent, b_sent)


def put(ref, index, parts):
    rows = EARLY_ROWS // 2
    ref[*index, :rows] = parts[0]
    ref[*index, rows:] = parts[1]


def hot_kernel(place, wide_hbm, narrow_hbm, keep, send, wides, narrows, a_flat, b_flat, sems):
    copies = layer_copies(place, (wide_hbm, narrow_hbm), (wides, narrows), sems)
    order = HOT + COLD
    for i in order[:AHEAD]:
        for copy in copies[i]:
            copy.start()

    def pack(i, sums):
        kept, sent = pack_layer(place, i, *sums, a_flat, b_flat)
        z, y, x = i // 4, (i // 2) % 2, i % 2
        if x and y:
            mine = other = 1
        else:
            mine, other = by_core(place, 0 if x else 2, 2 if x else 0)
        put(keep, (mine, z), kept)
        put(send, (other, z), sent)

    before = None
    for at, i in enumerate(order):
        for copy in copies[i]:
            copy.wait()
        if at + AHEAD < len(order):
            for copy in copies[order[at + AHEAD]]:
                copy.start()
        if before is not None:
            pack(*before)
            before = None
        if i in HOT:
            before = (i, square_sums(wides[i], narrows[i]))


def cold_kernel(place, wides, narrows, keep, send, a_flat, b_flat):
    for i in COLD:
        sums = square_sums(wides[i], narrows[i])
        kept, sent = pack_layer(place, i, *sums, a_flat, b_flat)
        put(keep, (i // 4,), kept)
        put(send, (i // 4,), sent)


def write_slots(place, owner_map, slots_ref):
    own = place.index(place.own)
    count = jnp.int32(0)
    for l in range(slots_ref.shape[0]):
        mine = owner_map[l] == own
        slot = jnp.where(mine, count, -1)
        slots_ref[l] = jnp.full(slots_ref.shape[1:], 0, jnp.int32) + slot
        count = count + mine.astype(jnp.int32)


def mixed_kernel(place, owner_map, wides, narrows, keep, send, slots_ref, flat):
    n = LANES
    write_slots(place, owner_map, slots_ref)
    for i in range(wides.shape[0]):
        mixed = transposed_dot(narrows[i], wides[i])
        flat[i, :n] = mixed[:, :n]
        flat[i, n:] = mixed[:, n:]
        kept, sent = both_halves(place, flat, i)
        z, y, x = i // 4, (i // 2) % 2, i % 2
        mine, other = by_core(place, y * 2 + x, x * 2 + y)
        keep[mine, z] = kept
        send[other, z] = sent


def gram_cost(wide_rows, columns):
    return pl.CostEstimate(
        flops=2 * wide_rows.size * columns, bytes_accessed=2 * wide_rows.size, transcendentals=0
    )


HALF_ROWS = (EARLY_ROWS + LATE_ROWS) // 2


def pack_shapes(layers):
    return [
        pltpu.VMEM((layers, EARLY_ROWS, LANES), jnp.float32),
        pltpu.VMEM((layers, LATE_ROWS, LANES), jnp.float32),
    ]


def hot_squares(place, wide_rows, narrow_rows):
    layers = wide_rows.shape[0]
    half = jax.ShapeDtypeStruct((3, 2, HALF_ROWS, LANES), jnp.float32)
    return pl.pallas_call(
        functools.partial(hot_kernel, place),
        in_specs=[HBM, HBM],
        out_specs=[VMEM] * 4,
        out_shape=[
            half,
            half,
            jax.ShapeDtypeStruct(wide_rows.shape, wide_rows.dtype),
            jax.ShapeDtypeStruct(narrow_rows.shape, narrow_rows.dtype),
        ],
        scratch_shapes=[*pack_shapes(layers), pltpu.SemaphoreType.DMA((layers, 2))],
        cost_estimate=gram_cost(wide_rows, 240),
        compiler_params=PARAMS,
        name="hot_squares",
    )(
        pltpu.with_memory_space_constraint(wide_rows, pltpu.HBM),
        pltpu.with_memory_space_constraint(narrow_rows, pltpu.HBM),
    )


def cold_squares(place, wides, narrows):
    half = jax.ShapeDtypeStruct((2, HALF_ROWS, LANES), jnp.float32)
    return pl.pallas_call(
        functools.partial(cold_kernel, place),
        in_specs=[VMEM, VMEM],
        out_specs=[VMEM, VMEM],
        out_shape=[half, half],
        scratch_shapes=pack_shapes(wides.shape[0]),
        cost_estimate=gram_cost(wides, 80),
        compiler_params=PARAMS,
        name="cold_squares",
    )(wides, narrows)


def mixed_sums(place, owner_map, wides, narrows):
    layers, _, narrow = narrows.shape
    half = jax.ShapeDtypeStruct((4, 2, narrow, LANES), jnp.float32)
    return pl.pallas_call(
        functools.partial(mixed_kernel, place),
        in_specs=[SMEM, VMEM, VMEM],
        out_specs=[VMEM] * 3,
        out_shape=[half, half, jax.ShapeDtypeStruct((layers, PANEL, LANES), jnp.int32)],
        scratch_shapes=[pltpu.VMEM((layers, 2 * narrow, LANES), jnp.float32)],
        cost_estimate=gram_cost(wides, 128),
        compiler_params=PARAMS,
        name="mixed",
    )(owner_map, wides, narrows)


def lane_gather(x, index):
    return jnp.take_along_axis(x, index, axis=1, mode="promise_in_bounds")


def trailing_update(a_ref, left_ref, right_ref, base):
    size = a_ref.shape[1]
    a_ref[pl.ds(pl.multiple_of(base, BLOCK), BLOCK), :] = jnp.zeros((BLOCK, size), jnp.float32)
    lane = lax.broadcasted_iota(jnp.int32, (1, size), 1)
    swept = (lane >= base - BLOCK) & (lane < base)
    update = transposed_dot(left_ref[...], right_ref[...])
    a_ref[BLOCK : BLOCK + size, :] = (
        jnp.where(swept, 0.0, a_ref[BLOCK : BLOCK + size, :]) - update
    )


def in_three(x):
    high = x.astype(jnp.bfloat16).astype(jnp.float32)
    rest = x - high
    middle = rest.astype(jnp.bfloat16).astype(jnp.float32)
    return high, middle, rest - middle


def factor_panel(rows_ref, cols_ref, tile, first, panel, targets):
    tiles = panel.shape[1] // LANES
    shape = (PANEL, LANES)
    _, lane = iotas(shape)

    def on_all(ref, k, lanes):
        return jnp.broadcast_to(ref[k : k + 1, lanes], shape)

    rows_ref[...] = panel
    lanes = [slice(LANES * t, LANES * (t + 1)) for t in range(tiles)]
    rows = [[on_all(rows_ref, k, part) for part in lanes] for k in range(PANEL)]
    here = panel[:, lanes[tile]]
    for j in range(PANEL):
        column = lane_gather(here, jnp.full(shape, 0, jnp.int32) + (first + j))
        cols_ref[PANEL * j : PANEL * (j + 1)] = column
    d = [[None] * PANEL for _ in range(PANEL)]
    for j in range(PANEL):
        for i in range(j, PANEL):
            d[i][j] = on_all(cols_ref, PANEL * j + i, slice(None))
    own = (lane >= first) & (lane < first + PANEL)
    q = [[None] * tiles for _ in range(PANEL)]
    p = [[None] * tiles for _ in range(PANEL)]
    weights = [[None] * PANEL for _ in targets]
    factor = [[None] * PANEL for _ in range(PANEL)]

    def substitute(k, scale):
        for t in range(tiles):
            value = rows[k][t]
            if t == tile:
                value = jnp.where(own, jnp.where(lane == first + k, -1.0, 0.0), value)
            for j in range(k):
                value = value - factor[k][j] * q[j][t]
            q[k][t] = value
            p[k][t] = value * scale
        for target, weight in zip(targets, weights):
            source, index = target(rows[k])
            value = lane_gather(source, index)
            for j in range(k):
                value = value - factor[k][j] * weight[j]
            weight[k] = value

    for k in range(0, PANEL, 2):
        m = k + 1
        a, b, c = d[k][k], d[m][k], d[m][m]
        first_scale = 1.0 / a
        second_scale = a * (1.0 / (a * c - b * b))
        factor[m][k] = b * first_scale
        left_over = {i: d[i][m] - d[i][k] * factor[m][k] for i in range(k + 2, PANEL)}
        for i in range(k + 2, PANEL):
            factor[i][k] = d[i][k] * first_scale
            factor[i][m] = left_over[i] * second_scale
        for i in range(k + 2, PANEL):
            for j in range(k + 2, i + 1):
                value = d[i][j] - d[i][k] * factor[j][k]
                d[i][j] = value - (left_over[i] * left_over[j]) * second_scale
        substitute(k, first_scale)
        substitute(m, second_scale)
    return q, p, weights


def packed_rows(values):
    sub, _ = iotas((PANEL, LANES))
    whole = []
    for t in range(len(values[0])):
        value = values[0][t]
        for k in range(1, PANEL):
            value = jnp.where(sub == k, values[k][t], value)
        whole.append(value)
    return whole


def side_by_side(tiles):
    return jnp.concatenate(tiles, axis=1) if len(tiles) > 1 else tiles[0]


def sweep_block(a_ref, left_ref, right_ref, a_rows, a_cols, b_rows, b_cols, tile, step, block):
    size = a_ref.shape[1]
    tiles = size // LANES
    first = step * BLOCK
    second = first + PANEL
    base = tile * LANES + first
    trailing_update(a_ref, left_ref, right_ref, base)

    sub, lane = iotas((PANEL, LANES))
    last = first == LANES - BLOCK
    next_first = jnp.where(last, 0, first + BLOCK)

    def in_block(row):
        return row[tile], second + sub

    def in_next(offset):
        def target(row):
            source = row[tile]
            if tile + 1 < tiles:
                source = jnp.where(last, row[tile + 1], source)
            return source, next_first + offset + sub

        return target

    nexts = [in_next(0), in_next(PANEL)]
    in_a = (lane >= first) & (lane < second)
    in_b = (lane >= second) & (lane < second + PANEL)

    def swept(tiles_of, mask):
        return [jnp.where(mask, 0.0, v) if t == tile else v for t, v in enumerate(tiles_of)]

    def minus(tiles_of, weight, p):
        result = []
        for t, value in enumerate(tiles_of):
            for k in range(PANEL):
                value = value - weight[k] * p[k][t]
            result.append(value)
        return result

    def by_tile(rows):
        return [rows[:, LANES * t : LANES * (t + 1)] for t in range(tiles)]

    qa, pa, (to_b, *to_next_a) = factor_panel(
        a_rows, a_cols, tile, first, block[:PANEL], [in_block, *nexts]
    )
    panel_b = side_by_side(minus(swept(by_tile(block[PANEL:]), in_a), to_b, pa))
    qb, pb, to_next_b = factor_panel(b_rows, b_cols, tile, second, panel_b, nexts)

    left, right = [], []
    for q, p, mask in ((qa, pa, in_b), (qb, pb, None)):
        q, p = packed_rows(q), packed_rows(p)
        if mask is not None:
            q, p = swept(q, mask), swept(p, mask)
        qs, ps = in_three(side_by_side(q)), in_three(side_by_side(p))
        left += [qs[i] for i in (0, 0, 1, 1, 0, 2)]
        right += [ps[i] for i in (0, 1, 0, 1, 2, 0)]
    left_ref[...] = jnp.concatenate(left, axis=0).astype(jnp.bfloat16)
    right_ref[...] = jnp.concatenate(right, axis=0).astype(jnp.bfloat16)

    following = a_ref[pl.ds(pl.multiple_of(base + 2 * BLOCK, BLOCK), BLOCK), :]
    result = []
    for g in range(2):
        rows = by_tile(following[g * PANEL : (g + 1) * PANEL])
        rows = minus(swept(rows, in_a), to_next_a[g], pa)
        rows = minus(swept(rows, in_b), to_next_b[g], pb)
        result.append(side_by_side(rows))
    return jnp.concatenate(result, axis=0)


def place_halves(place, pieces, first_row, flat):
    core = lax.axis_index(place.core)
    rows = flat.shape[0] // 2
    for r, piece in enumerate(pieces):
        start = pl.multiple_of(jnp.bitwise_xor(core, r) * rows, PANEL)
        flat[pl.ds(start, rows), :] = piece[first_row : first_row + rows]


def sweep_cost():
    return pl.CostEstimate(flops=1 << 30, bytes_accessed=1 << 20, transcendentals=0)


def clear(work):
    a_ref, left, right = work[:3]
    size = a_ref.shape[1]
    a_ref[:BLOCK] = jnp.zeros((BLOCK, size), jnp.float32)
    a_ref[BLOCK + size :] = jnp.zeros((BLOCK, size), jnp.float32)
    left[...] = jnp.zeros(left.shape, left.dtype)
    right[...] = jnp.zeros(right.shape, right.dtype)


def work_shapes(size):
    splits = 6 * BLOCK
    return [
        pltpu.VMEM((size + 2 * BLOCK, size), jnp.float32),
        pltpu.VMEM((splits, size), jnp.bfloat16),
        pltpu.VMEM((splits, size), jnp.bfloat16),
    ]


def row_shapes(size):
    return [
        pltpu.VMEM((PANEL, size), jnp.float32),
        pltpu.VMEM((PANEL * PANEL, LANES), jnp.float32),
    ] * 2


def aligned_rows(ref, index, count):
    if count % PANEL == 0:
        return ref[pl.ds(pl.multiple_of(index * count, count), count), :]
    per_slab = PANEL // count
    slab = ref[pl.ds(pl.multiple_of(index // per_slab * PANEL, PANEL), PANEL), :]
    value = slab[:count]
    for i in range(1, per_slab):
        value = jnp.where(index % per_slab == i, slab[i * count : (i + 1) * count], value)
    return value


def packs(cols, rows):
    return cols == 2 * PANEL and 2 * rows == LANES


def dot(a, b, last=False):
    return lax.dot_general(
        a,
        b,
        (((1,), (1 if last else 0,)), ((), ())),
        precision=HIGHEST,
        preferred_element_type=jnp.float32,
    )


STEPS = LANES // BLOCK
FIRST_STEPS = 5
SECOND_STEPS = 6


def sweep_both(wide_work, narrow_work, begin, end, blocks):
    def step(i, blocks):
        return (
            sweep_block(*wide_work, 0, i, blocks[0]),
            sweep_block(*narrow_work, 0, i, blocks[1]),
        )

    return lax.fori_loop(begin, end, step, blocks)


def sweep_wide(work, begin, end, block):
    return lax.fori_loop(begin, end, lambda i, block: sweep_block(*work, 1, i, block), block)


def unit_scale(block):
    row, col = iotas(block.shape)
    line = jnp.sum(jnp.where(row == col, block, 0.0), axis=0, keepdims=True)
    return jnp.broadcast_to(lax.rsqrt(line), (PANEL, block.shape[1]))


def on_rows(scale):
    n = scale.shape[1]
    return jnp.broadcast_to(scale[:1], (n, n))


def scaled(block, down, across):
    return (block * on_rows(down).T) * on_rows(across)


def first_kernel(
    place, total, mine, other, wa, wl, wr, wp, na, nl, nr, np_, ws_ref, ns_ref, *refs
):
    a_flat, b_flat = refs[:2]
    wide_work, narrow_work = (wa, wl, wr, *refs[2:6]), (na, nl, nr, *refs[6:])
    place_halves(place, (mine, other), 0, a_flat)
    place_halves(place, (mine, other), a_flat.shape[0] // 2, b_flat)
    n = LANES
    slab = a_flat[n : n + PANEL]
    first, square = unpack_pair(a_flat[:n], jnp.broadcast_to(slab[:1], (n, n)))
    corner = b_flat[:n] / total
    last = unfold(b_flat[n:], jnp.broadcast_to(slab[1:2], (n, n)))
    row, col = iotas((n, n))
    damp = jnp.where(row == col, DAMP, 0.0)
    clear(wide_work)
    clear(narrow_work)
    first, last, square = first / total + damp, last / total + damp, square / total + damp
    by_first, by_last, by_square = (unit_scale(block) for block in (first, last, square))
    ws_ref[:, :n] = by_first
    ws_ref[:, n:] = by_last
    ns_ref[...] = by_square
    first_across, last_across = on_rows(by_first), on_rows(by_last)
    first_down, last_down = first_across.T, last_across.T
    corner = (corner * first_down) * last_across
    wa[BLOCK : BLOCK + n, :n] = (first * first_down) * first_across
    wa[BLOCK : BLOCK + n, n:] = corner
    wa[BLOCK + n : BLOCK + 2 * n, :n] = corner.T
    wa[BLOCK + n : BLOCK + 2 * n, n:] = (last * last_down) * last_across
    na[BLOCK : BLOCK + n, :] = scaled(square, by_square, by_square)
    start = (wa[BLOCK : 2 * BLOCK, :], na[BLOCK : 2 * BLOCK, :])
    wp[...], np_[...] = sweep_both(wide_work, narrow_work, 0, FIRST_STEPS, start)


def second_kernel(*refs):
    given, scale, ninv_ref, state, narrow_state, wide_rows, narrow_rows = (
        refs[:8],
        refs[8],
        refs[9],
        refs[10:14],
        refs[14:17],
        refs[17:21],
        refs[21:],
    )
    for source, target in zip((*given[:3], *given[4:7]), (*state[:3], *narrow_state)):
        target[...] = source[...]
    wide_work, narrow_work = (*state[:3], *wide_rows), (*narrow_state, *narrow_rows)
    wp = state[3]
    panels = (given[3][...], given[7][...])
    panel, _ = sweep_both(wide_work, narrow_work, FIRST_STEPS, STEPS, panels)
    trailing_update(*narrow_work[:3], LANES)
    by_square = scale[...]
    ninv_ref[...] = scaled(-narrow_work[0][BLOCK : BLOCK + LANES, :], by_square, by_square)
    wp[...] = sweep_wide(wide_work, 0, SECOND_STEPS, panel)


def third_kernel(wa_in, wl_in, wr_in, panel_in, scale, winv, wa, wl, wr, *rows):
    wa[...] = wa_in[...]
    wl[...] = wl_in[...]
    wr[...] = wr_in[...]
    sweep_wide((wa, wl, wr, *rows), SECOND_STEPS, STEPS, panel_in[...])
    wide = wa.shape[1]
    trailing_update(wa, wl, wr, wide)
    parts = [slice(i, i + LANES) for i in range(0, wide, LANES)]
    across = [on_rows(scale[:, i]) for i in parts]
    down = [block.T for block in across]
    for i, rows_scale in zip(parts, down):
        for j, columns_scale in zip(parts, across):
            block = -wa[BLOCK + i.start : BLOCK + i.stop, j]
            winv[i, j] = (block * rows_scale) * columns_scale


def state_shapes(size):
    shapes = [jax.ShapeDtypeStruct(v.shape, v.dtype) for v in work_shapes(size)]
    return shapes + [jax.ShapeDtypeStruct((BLOCK, size), jnp.float32)]


def sweep_call(kernel, name, args, out_shapes, scratch):
    return pl.pallas_call(
        kernel,
        in_specs=[VMEM] * len(args),
        out_specs=[VMEM] * len(out_shapes),
        out_shape=out_shapes,
        scratch_shapes=scratch,
        cost_estimate=sweep_cost(),
        compiler_params=PARAMS,
        name=name,
    )(*args)


def first_panels(place, pieces, wide, narrow, total):
    return sweep_call(
        functools.partial(first_kernel, place, total),
        "first_panels",
        pieces,
        state_shapes(wide)
        + state_shapes(narrow)
        + [jax.ShapeDtypeStruct((PANEL, n), jnp.float32) for n in (wide, narrow)],
        [
            pltpu.VMEM((EARLY_ROWS, LANES), jnp.float32),
            pltpu.VMEM((LATE_ROWS, LANES), jnp.float32),
            *row_shapes(wide),
            *row_shapes(narrow),
        ],
    )


def second_panels(state, wide, narrow):
    ninv = jax.ShapeDtypeStruct((narrow, narrow), jnp.float32)
    return sweep_call(
        second_kernel,
        "second_panels",
        state,
        [ninv] + state_shapes(wide),
        [*work_shapes(narrow), *row_shapes(wide), *row_shapes(narrow)],
    )


def third_panels(state, wide):
    winv = jax.ShapeDtypeStruct((wide, wide), jnp.float32)
    scratch = [*work_shapes(wide), *row_shapes(wide)]
    return sweep_call(third_kernel, "third_panels", state, [winv], scratch)[0]


def product_kernel(place, total, rows, winv, ninv_ref, mine, other, out_ref, flat):
    place_halves(place, (mine, other), 0, flat)
    ninv = ninv_ref[...]
    n = LANES
    inner = jnp.concatenate(
        [
            transposed_dot(flat[c * n : (c + 1) * n] / total, ninv, HIGHEST)
            for c in range(2)
        ],
        axis=0,
    )
    wide = winv.shape[1]
    cols = wide // 2 ** len(place.dp)
    near, second = lax.axis_index(place.near), lax.axis_index(place.second)
    near_stride = 2 ** (len(place.dp) - 2)
    base = place.index(place.dp) - near * near_stride - second * 2
    _, lane = iotas((PANEL, LANES))
    picks = [
        aligned_rows(winv, base + (j // 2) * near_stride + (j % 2) * 2, cols) for j in range(4)
    ]
    if cols % PANEL == 0:
        whole = dot(jnp.concatenate(picks, axis=0), inner)
        updates = [whole[j * cols : (j + 1) * cols] for j in range(4)]
    else:
        updates = [dot(picked, inner) for picked in picks]
    for j, (picked, update) in enumerate(zip(picks, updates)):
        for x in range(2):
            block = 2 * j + x
            out_ref[block, :cols] = picked[:, :LANES]
            out_ref[block, cols : 2 * cols] = picked[:, LANES:]
            if packs(cols, rows):
                upper, lower = update[:PANEL], update[PANEL:]
                if x == 0:
                    lower = pltpu.roll(lower, rows, 1)
                else:
                    upper = pltpu.roll(upper, rows, 1)
                out_ref[block, 2 * cols :] = jnp.where(lane < rows, upper, lower)
            else:
                out_ref[block, 2 * cols :] = update


def products(place, winv, ninv, pieces, rows, total):
    wide, narrow = winv.shape[0], ninv.shape[0]
    cols = wide // 2 ** len(place.dp)
    height = 2 * cols + (PANEL if packs(cols, rows) else cols)
    return pl.pallas_call(
        functools.partial(product_kernel, place, total, rows),
        in_specs=[VMEM] * 4,
        out_specs=VMEM,
        out_shape=jax.ShapeDtypeStruct((8, height, LANES), jnp.float32),
        scratch_shapes=[pltpu.VMEM((2 * narrow, LANES), jnp.float32)],
        compiler_params=PARAMS,
        name="products",
    )(winv, ninv, *pieces)


def placing_kernel(place, slots_ref, got_ref, kept_ref, update_ref):
    layers = got_ref.shape[0]
    slots, cols, wide = kept_ref.shape
    rows = update_ref.shape[2]
    own, dp = place.index(place.own), place.index(place.dp)
    step = min(cols, PANEL)
    row, col = iotas((step, LANES))
    for h in range(wide // LANES):
        lanes = slice(h * LANES, (h + 1) * LANES)
        for r in range(0, cols, step):
            here = h * cols + r
            empty = jnp.where(col + h * LANES == row + dp * cols + r, 1.0 / DAMP, 0.0)
            for c in range(slots):
                value = empty
                for l in range(layers):
                    taken = slots_ref[l, :step] == c
                    value = jnp.where(taken, got_ref[l, here : here + step], value)
                kept_ref[c, r : r + step, lanes] = value
    for l in range(layers):
        value = got_ref[l, 2 * cols :]
        if packs(cols, rows):
            update_ref[l, :PANEL] = value[:, :rows]
            update_ref[l, PANEL:] = value[:, rows:]
        else:
            part = value[:, :rows]
            for p in range(1, LANES // rows):
                part = jnp.where(own == p, value[:, p * rows : (p + 1) * rows], part)
            update_ref[l] = part


def placing(place, slots_of, got, wide, cols, slots, rows):
    layers = got.shape[0]
    return pl.pallas_call(
        functools.partial(placing_kernel, place),
        in_specs=[VMEM, VMEM],
        out_specs=[VMEM, VMEM],
        out_shape=[
            jax.ShapeDtypeStruct((slots, cols, wide), jnp.float32),
            jax.ShapeDtypeStruct((layers, cols, rows), jnp.float32),
        ],
        compiler_params=PARAMS,
        name="placing",
    )(slots_of, got)


def swap(value, axis):
    return lax.ppermute(value, axis, [(0, 1), (1, 0)])


def swap_by_core(value, place, stage):
    pairs = []
    for y in range(2):
        for core in range(2):
            for x in range(2):
                flip = 1 if core == stage else 4
                here = y * 4 + core * 2 + x
                pairs.append((here, here ^ flip))
    return lax.ppermute(value, (place.second, place.core, place.first), pairs)


def after(value, *others):
    return lax.optimization_barrier((value,) + others)[0]


def on_device(place, wide_rows, narrow_rows, owner_map):
    layers, rows, wide = wide_rows.shape
    narrow = narrow_rows.shape[2]
    n_dp, n_own = 2 ** len(place.dp), 2 ** len(place.own)
    total = float(rows * n_dp * n_own)

    h_keep, h_send, wides, narrows = hot_squares(place, wide_rows, narrow_rows)
    h_got = swap(h_send[:2], place.core)
    c_keep, c_send = cold_squares(place, after(wides, h_send), narrows)
    h_keep, c_send = lax.optimization_barrier((h_keep, c_send))

    hot = h_keep[:2] + h_got
    s_got = swap_by_core(hot, place, 0)
    m_keep, m_send, slots_of = mixed_sums(place, owner_map, after(wides, hot), narrows)
    c_got = swap(after(jnp.stack([c_send, h_send[2]]), m_send), place.core)
    m_got = swap(m_send, place.core)
    s = jnp.stack([c_keep, h_keep[2]]) + s_got
    s = s + after(c_got, s)
    s_got = swap_by_core(s[1], place, 1)
    m = after(m_keep, s) + m_got
    m_got = swap_by_core(m[2:], place, 1)

    s = s[0] + s_got
    s_got = swap(s[1], place.near)
    m = after(m[:2], s) + m_got
    m_got = swap_by_core(m[1], place, 0)

    s = s[0] + s_got
    if place.extra:
        s = lax.psum(s, place.extra)
    s_got = swap(s, place.far)
    m = after(m[0], s) + m_got
    m_got = swap(m[1], place.near)

    s = s + s_got
    state = first_panels(place, [s, swap(s, place.core)], wide, narrow, total)
    m = after(m[0], state[0]) + m_got
    if place.extra:
        m = lax.psum(m, place.extra)
    m_got = swap(m, place.far)
    *state, wide_scale, narrow_scale = state
    ninv, *state = second_panels([*state, narrow_scale], wide, narrow)
    m = after(m, ninv) + m_got
    m_got = swap(m, place.core)
    winv = third_panels([*state, wide_scale], wide)
    cols, own_rows = wide // n_dp, narrow // n_own
    sent = products(place, winv, ninv, [m, m_got], own_rows, total)
    got = lax.all_to_all(sent, (place.near, place.second, place.first), 0, 0)
    kept, update = placing(
        place, slots_of, got, wide, cols, layers // n_own + 1, own_rows
    )
    return (jnp.swapaxes(kept, 1, 2), jnp.swapaxes(update, 1, 2))


def solution(mesh):
    n_dp, n_own = mesh.shape["dp"], mesh.shape["own"]
    dp_names = tuple(f"dp{i}" for i in range(int(np.log2(n_dp))))
    own_names = tuple(f"own{i}" for i in range(int(np.log2(n_own))))
    names = dp_names + own_names
    bits = jax.sharding.Mesh(mesh.devices.reshape((2,) * len(names)), names)
    in_specs = (P(None, names, None), P(None, names, None), P())
    out_specs = (P(own_names, None, dp_names), P(None, own_names, dp_names))
    return jax.shard_map(
        functools.partial(on_device, Place(dp_names, own_names)),
        mesh=bits,
        in_specs=in_specs,
        out_specs=out_specs,
        check_vma=False,
    )
```

```python
import functools

import jax
import jax.numpy as jnp
import numpy as np
from jax import lax
from jax.experimental import pallas as pl
from jax.experimental.pallas import tpu as pltpu
from jax.sharding import PartitionSpec as P

DAMP = 0.5
LANES = 128
PANEL = 8
BLOCK = 2 * PANEL
VMEM_LIMIT = 48 * 1024 * 1024
HIGHEST = lax.Precision.HIGHEST
VMEM = pl.BlockSpec(memory_space=pltpu.VMEM)
SMEM = pl.BlockSpec(memory_space=pltpu.SMEM)
HBM = pl.BlockSpec(memory_space=pltpu.HBM)
PARAMS = pltpu.CompilerParams(vmem_limit_bytes=VMEM_LIMIT)


class Place:
    def __init__(self, dp_names, own_names):
        self.dp, self.own = dp_names, own_names
        self.core, self.second, self.near, self.far = (
            dp_names[-1],
            dp_names[-2],
            dp_names[1],
            dp_names[0],
        )
        self.first = own_names[-1]
        used = (self.core, self.second, self.near, self.far, self.first)
        self.extra = tuple(n for n in dp_names + own_names if n not in used)

    def index(self, names):
        value = jnp.int32(0)
        for name in names:
            value = value * 2 + lax.axis_index(name)
        return value

    def layer(self):
        return self.index((self.near, self.second, self.first))


def transposed_dot(a, b, precision=None):
    return lax.dot_general(
        a, b, (((0,), (0,)), ((), ())), precision=precision, preferred_element_type=jnp.float32
    )


AHEAD = 5


def layer_copies(place, sources, buffers, sems):
    layer = place.layer()
    return [
        [
            pltpu.make_async_copy(
                source.at[jnp.bitwise_xor(layer, i)], buffer.at[i], sems.at[i, s]
            )
            for s, (source, buffer) in enumerate(zip(sources, buffers))
        ]
        for i in range(buffers[0].shape[0])
    ]


def both_halves(place, flat, i):
    rows = flat.shape[1] // 2
    core = lax.axis_index(place.core)
    kept = pl.multiple_of(core * rows, PANEL)
    sent = pl.multiple_of((1 - core) * rows, PANEL)
    return flat[i, pl.ds(kept, rows), :], flat[i, pl.ds(sent, rows), :]


ORDERS = (("first", "second", "near"), ("second", "near", "first"))


def position(axes, i):
    bits = {"near": i // 4, "second": (i // 2) % 2, "first": i % 2}
    return bits[axes[0]] * 4 + bits[axes[1]] * 2 + bits[axes[2]]


def positions(place, i, orders):
    core = lax.axis_index(place.core)
    first, second = (position(axes, i) for axes in orders)
    return jnp.where(core == 0, first, second), jnp.where(core == 0, second, first)


def iotas(shape):
    return (
        lax.broadcasted_iota(jnp.int32, shape, 0),
        lax.broadcasted_iota(jnp.int32, shape, 1),
    )


def pack_pair(first, second):
    row, col = iotas(first.shape)
    return jnp.where(row >= col, first, second)


def unpack_pair(packed, second_diagonal):
    row, col = iotas(packed.shape)
    turned = packed.T
    first = jnp.where(row >= col, packed, turned)
    second = jnp.where(col > row, packed, turned)
    return first, jnp.where(row == col, second_diagonal, second)


def fold(block):
    h = block.shape[0] // 2
    row, col = iotas((h, 2 * h))
    last = pltpu.roll(block[h:], h, 1)
    return jnp.where((col >= h) | (row >= col), block[:h], last)


def unfold(folded, diagonal):
    h, n = folded.shape
    row, col = iotas((n, n))
    block = jnp.concatenate([folded, jnp.zeros((h, n), jnp.float32)], axis=0)
    turned = block.T
    top = jnp.where((col >= h) | (col <= row), block, turned)
    moved = pltpu.roll(pltpu.roll(block, h, 0), h, 1)
    moved_turned = pltpu.roll(pltpu.roll(turned, h, 0), h, 1)
    last = jnp.where(col > row, moved, moved_turned)
    last = jnp.where(row == col, diagonal, last)
    return jnp.where(row < h, top, jnp.where(col < h, turned, last))


def diagonals(blocks, rows):
    n = blocks[0].shape[0]
    row, col = iotas((n, n))
    slab_row, _ = iotas((rows, n))
    slab = jnp.zeros((rows, n), jnp.float32)
    for i, block in enumerate(blocks):
        line = jnp.sum(jnp.where(row == col, block, 0.0), axis=0, keepdims=True)
        slab = jnp.where(slab_row == i, jnp.broadcast_to(line, (rows, n)), slab)
    return slab


EARLY_ROWS = 144
LATE_ROWS = 192


HOT = (1, 2, 3, 5, 6, 7)
COLD = (0, 4)


def square_sums(wide, narrow):
    return transposed_dot(wide, wide), transposed_dot(narrow, narrow)


def pack_layer(place, i, wcov, ncov, a_flat, b_flat):
    n = LANES
    last = wcov[n:, n:]
    a_flat[i, :n] = pack_pair(wcov[:n, :n], ncov)
    a_flat[i, n:] = diagonals((ncov, last), EARLY_ROWS - n)
    b_flat[i, :n] = wcov[:n, n:]
    b_flat[i, n:] = fold(last)
    a_kept, a_sent = both_halves(place, a_flat, i)
    b_kept, b_sent = both_halves(place, b_flat, i)
    return (a_kept, b_kept), (a_sent, b_sent)


def put(ref, index, parts):
    rows = EARLY_ROWS // 2
    ref[index, :rows] = parts[0]
    ref[index, rows:] = parts[1]


def put_layer(place, i, sums, a_flat, b_flat, keep, send):
    kept, sent = pack_layer(place, i, *sums, a_flat, b_flat)
    mine, other = positions(place, i, ORDERS)
    put(keep, mine, kept)
    put(send, other, sent)


def clear_others(place, layers, keep, send):
    for i in layers:
        mine, other = positions(place, i, ORDERS)
        keep[mine] = jnp.zeros(keep.shape[1:], jnp.float32)
        send[other] = jnp.zeros(send.shape[1:], jnp.float32)


def hot_kernel(place, wide_hbm, narrow_hbm, keep, send, wides, narrows, a_flat, b_flat, sems):
    copies = layer_copies(place, (wide_hbm, narrow_hbm), (wides, narrows), sems)
    order = HOT + COLD
    for i in order[:AHEAD]:
        for copy in copies[i]:
            copy.start()
    clear_others(place, COLD, keep, send)

    def pack(i, sums):
        put_layer(place, i, sums, a_flat, b_flat, keep, send)

    before = None
    for at, i in enumerate(order):
        for copy in copies[i]:
            copy.wait()
        if at + AHEAD < len(order):
            for copy in copies[order[at + AHEAD]]:
                copy.start()
        if before is not None:
            pack(*before)
            before = None
        if i in HOT:
            before = (i, square_sums(wides[i], narrows[i]))


def cold_kernel(place, wides, narrows, keep, send, a_flat, b_flat):
    for i in COLD:
        put_layer(
            place, i, square_sums(wides[i], narrows[i]), a_flat, b_flat, keep, send
        )
    core = lax.axis_index(place.core)
    stay = [[i for i in HOT if position(axes, i) < 4] for axes in ORDERS]
    for first, second in zip(*stay):
        here = [position(axes, i) for axes, i in zip(ORDERS, (first, second))]
        mine = jnp.where(core == 0, here[0], here[1])
        other = jnp.where(core == 0, here[1], here[0])
        keep[mine] = jnp.zeros(keep.shape[1:], jnp.float32)
        send[other] = jnp.zeros(send.shape[1:], jnp.float32)


def write_slots(place, owner_map, slots_ref):
    own = place.index(place.own)
    count = jnp.int32(0)
    for l in range(slots_ref.shape[0]):
        mine = owner_map[l] == own
        slot = jnp.where(mine, count, -1)
        slots_ref[l] = jnp.full(slots_ref.shape[1:], 0, jnp.int32) + slot
        count = count + mine.astype(jnp.int32)


def mixed_kernel(place, owner_map, wides, narrows, keep, send, slots_ref, flat):
    n = LANES
    write_slots(place, owner_map, slots_ref)
    for i in range(wides.shape[0]):
        mixed = transposed_dot(narrows[i], wides[i])
        flat[i, :n] = mixed[:, :n]
        flat[i, n:] = mixed[:, n:]
        kept, sent = both_halves(place, flat, i)
        mine, other = positions(place, i, ORDERS[::-1])
        keep[mine] = kept
        send[other] = sent


def gram_cost(wide_rows, columns):
    return pl.CostEstimate(
        flops=2 * wide_rows.size * columns, bytes_accessed=2 * wide_rows.size, transcendentals=0
    )


HALF_ROWS = (EARLY_ROWS + LATE_ROWS) // 2


def pack_shapes(layers):
    return [
        pltpu.VMEM((layers, EARLY_ROWS, LANES), jnp.float32),
        pltpu.VMEM((layers, LATE_ROWS, LANES), jnp.float32),
    ]


def hot_squares(place, wide_rows, narrow_rows):
    layers = wide_rows.shape[0]
    half = jax.ShapeDtypeStruct((layers, HALF_ROWS, LANES), jnp.float32)
    return pl.pallas_call(
        functools.partial(hot_kernel, place),
        in_specs=[HBM, HBM],
        out_specs=[VMEM] * 4,
        out_shape=[
            half,
            half,
            jax.ShapeDtypeStruct(wide_rows.shape, wide_rows.dtype),
            jax.ShapeDtypeStruct(narrow_rows.shape, narrow_rows.dtype),
        ],
        scratch_shapes=[*pack_shapes(layers), pltpu.SemaphoreType.DMA((layers, 2))],
        cost_estimate=gram_cost(wide_rows, 240),
        compiler_params=PARAMS,
        name="hot_squares",
    )(
        pltpu.with_memory_space_constraint(wide_rows, pltpu.HBM),
        pltpu.with_memory_space_constraint(narrow_rows, pltpu.HBM),
    )


def cold_squares(place, wides, narrows):
    half = jax.ShapeDtypeStruct((wides.shape[0] // 2, HALF_ROWS, LANES), jnp.float32)
    return pl.pallas_call(
        functools.partial(cold_kernel, place),
        in_specs=[VMEM, VMEM],
        out_specs=[VMEM, VMEM],
        out_shape=[half, half],
        scratch_shapes=pack_shapes(wides.shape[0]),
        cost_estimate=gram_cost(wides, 80),
        compiler_params=PARAMS,
        name="cold_squares",
    )(wides, narrows)


def mixed_sums(place, owner_map, wides, narrows):
    layers, _, narrow = narrows.shape
    half = jax.ShapeDtypeStruct((layers, narrow, LANES), jnp.float32)
    return pl.pallas_call(
        functools.partial(mixed_kernel, place),
        in_specs=[SMEM, VMEM, VMEM],
        out_specs=[VMEM] * 3,
        out_shape=[half, half, jax.ShapeDtypeStruct((layers, PANEL, LANES), jnp.int32)],
        scratch_shapes=[pltpu.VMEM((layers, 2 * narrow, LANES), jnp.float32)],
        cost_estimate=gram_cost(wides, 128),
        compiler_params=PARAMS,
        name="mixed",
    )(owner_map, wides, narrows)


def lane_gather(x, index):
    return jnp.take_along_axis(x, index, axis=1, mode="promise_in_bounds")


def trailing_update(a_ref, left_ref, right_ref, base):
    size = a_ref.shape[1]
    a_ref[pl.ds(pl.multiple_of(base, BLOCK), BLOCK), :] = jnp.zeros((BLOCK, size), jnp.float32)
    lane = lax.broadcasted_iota(jnp.int32, (1, size), 1)
    swept = (lane >= base - BLOCK) & (lane < base)
    update = transposed_dot(left_ref[...], right_ref[...])
    a_ref[BLOCK : BLOCK + size, :] = (
        jnp.where(swept, 0.0, a_ref[BLOCK : BLOCK + size, :]) - update
    )


def in_three(x):
    high = x.astype(jnp.bfloat16).astype(jnp.float32)
    rest = x - high
    middle = rest.astype(jnp.bfloat16).astype(jnp.float32)
    return high, middle, rest - middle


def factor_panel(rows_ref, cols_ref, tile, first, panel, targets):
    tiles = panel.shape[1] // LANES
    shape = (PANEL, LANES)
    _, lane = iotas(shape)

    def on_all(ref, k, lanes):
        return jnp.broadcast_to(ref[k : k + 1, lanes], shape)

    rows_ref[...] = panel
    lanes = [slice(LANES * t, LANES * (t + 1)) for t in range(tiles)]
    rows = [[on_all(rows_ref, k, part) for part in lanes] for k in range(PANEL)]
    here = panel[:, lanes[tile]]
    for j in range(PANEL):
        column = lane_gather(here, jnp.full(shape, 0, jnp.int32) + (first + j))
        cols_ref[PANEL * j : PANEL * (j + 1)] = column
    d = [[None] * PANEL for _ in range(PANEL)]
    for j in range(PANEL):
        for i in range(j, PANEL):
            d[i][j] = on_all(cols_ref, PANEL * j + i, slice(None))
    own = (lane >= first) & (lane < first + PANEL)
    q = [[None] * tiles for _ in range(PANEL)]
    p = [[None] * tiles for _ in range(PANEL)]
    weights = [[None] * PANEL for _ in targets]
    factor = [[None] * PANEL for _ in range(PANEL)]

    def substitute(k, scale):
        for t in range(tiles):
            value = rows[k][t]
            if t == tile:
                value = jnp.where(own, jnp.where(lane == first + k, -1.0, 0.0), value)
            for j in range(k):
                value = value - factor[k][j] * q[j][t]
            q[k][t] = value
            p[k][t] = value * scale
        for target, weight in zip(targets, weights):
            source, index = target(rows[k])
            value = lane_gather(source, index)
            for j in range(k):
                value = value - factor[k][j] * weight[j]
            weight[k] = value

    for k in range(0, PANEL, 2):
        m = k + 1
        a, b, c = d[k][k], d[m][k], d[m][m]
        first_scale = 1.0 / a
        second_scale = a * (1.0 / (a * c - b * b))
        factor[m][k] = b * first_scale
        left_over = {i: d[i][m] - d[i][k] * factor[m][k] for i in range(k + 2, PANEL)}
        for i in range(k + 2, PANEL):
            factor[i][k] = d[i][k] * first_scale
            factor[i][m] = left_over[i] * second_scale
        for i in range(k + 2, PANEL):
            for j in range(k + 2, i + 1):
                value = d[i][j] - d[i][k] * factor[j][k]
                d[i][j] = value - (left_over[i] * left_over[j]) * second_scale
        substitute(k, first_scale)
        substitute(m, second_scale)
    return q, p, weights


def packed_rows(values):
    sub, _ = iotas((PANEL, LANES))
    whole = []
    for t in range(len(values[0])):
        value = values[0][t]
        for k in range(1, PANEL):
            value = jnp.where(sub == k, values[k][t], value)
        whole.append(value)
    return whole


def side_by_side(tiles):
    return jnp.concatenate(tiles, axis=1) if len(tiles) > 1 else tiles[0]


def sweep_block(a_ref, left_ref, right_ref, a_rows, a_cols, b_rows, b_cols, tile, step, block):
    size = a_ref.shape[1]
    tiles = size // LANES
    first = step * BLOCK
    second = first + PANEL
    base = tile * LANES + first
    trailing_update(a_ref, left_ref, right_ref, base)

    sub, lane = iotas((PANEL, LANES))
    last = first == LANES - BLOCK
    next_first = jnp.where(last, 0, first + BLOCK)

    def in_block(row):
        return row[tile], second + sub

    def in_next(offset):
        def target(row):
            source = row[tile]
            if tile + 1 < tiles:
                source = jnp.where(last, row[tile + 1], source)
            return source, next_first + offset + sub

        return target

    nexts = [in_next(0), in_next(PANEL)]
    in_a = (lane >= first) & (lane < second)
    in_b = (lane >= second) & (lane < second + PANEL)

    def swept(tiles_of, mask):
        return [jnp.where(mask, 0.0, v) if t == tile else v for t, v in enumerate(tiles_of)]

    def minus(tiles_of, weight, p):
        result = []
        for t, value in enumerate(tiles_of):
            for k in range(PANEL):
                value = value - weight[k] * p[k][t]
            result.append(value)
        return result

    def by_tile(rows):
        return [rows[:, LANES * t : LANES * (t + 1)] for t in range(tiles)]

    qa, pa, (to_b, *to_next_a) = factor_panel(
        a_rows, a_cols, tile, first, block[:PANEL], [in_block, *nexts]
    )
    panel_b = side_by_side(minus(swept(by_tile(block[PANEL:]), in_a), to_b, pa))
    qb, pb, to_next_b = factor_panel(b_rows, b_cols, tile, second, panel_b, nexts)

    left, right = [], []
    for q, p, mask in ((qa, pa, in_b), (qb, pb, None)):
        q, p = packed_rows(q), packed_rows(p)
        if mask is not None:
            q, p = swept(q, mask), swept(p, mask)
        qs, ps = in_three(side_by_side(q)), in_three(side_by_side(p))
        left += [qs[i] for i in (0, 0, 1, 1, 0, 2)]
        right += [ps[i] for i in (0, 1, 0, 1, 2, 0)]
    left_ref[...] = jnp.concatenate(left, axis=0).astype(jnp.bfloat16)
    right_ref[...] = jnp.concatenate(right, axis=0).astype(jnp.bfloat16)

    following = a_ref[pl.ds(pl.multiple_of(base + 2 * BLOCK, BLOCK), BLOCK), :]
    result = []
    for g in range(2):
        rows = by_tile(following[g * PANEL : (g + 1) * PANEL])
        rows = minus(swept(rows, in_a), to_next_a[g], pa)
        rows = minus(swept(rows, in_b), to_next_b[g], pb)
        result.append(side_by_side(rows))
    return jnp.concatenate(result, axis=0)


def place_halves(place, pieces, first_row, flat):
    core = lax.axis_index(place.core)
    rows = flat.shape[0] // 2
    for r, piece in enumerate(pieces):
        start = pl.multiple_of(jnp.bitwise_xor(core, r) * rows, PANEL)
        flat[pl.ds(start, rows), :] = piece[first_row : first_row + rows]


def sweep_cost():
    return pl.CostEstimate(flops=1 << 30, bytes_accessed=1 << 20, transcendentals=0)


def clear(work):
    a_ref, left, right = work[:3]
    size = a_ref.shape[1]
    a_ref[:BLOCK] = jnp.zeros((BLOCK, size), jnp.float32)
    a_ref[BLOCK + size :] = jnp.zeros((BLOCK, size), jnp.float32)
    left[...] = jnp.zeros(left.shape, left.dtype)
    right[...] = jnp.zeros(right.shape, right.dtype)


def work_shapes(size):
    splits = 6 * BLOCK
    return [
        pltpu.VMEM((size + 2 * BLOCK, size), jnp.float32),
        pltpu.VMEM((splits, size), jnp.bfloat16),
        pltpu.VMEM((splits, size), jnp.bfloat16),
    ]


def row_shapes(size):
    return [
        pltpu.VMEM((PANEL, size), jnp.float32),
        pltpu.VMEM((PANEL * PANEL, LANES), jnp.float32),
    ] * 2


def aligned_rows(ref, index, count):
    if count % PANEL == 0:
        return ref[pl.ds(pl.multiple_of(index * count, count), count), :]
    per_slab = PANEL // count
    slab = ref[pl.ds(pl.multiple_of(index // per_slab * PANEL, PANEL), PANEL), :]
    value = slab[:count]
    for i in range(1, per_slab):
        value = jnp.where(index % per_slab == i, slab[i * count : (i + 1) * count], value)
    return value


def packs(cols, rows):
    return cols == 2 * PANEL and 2 * rows == LANES


def dot(a, b, last=False):
    return lax.dot_general(
        a,
        b,
        (((1,), (1 if last else 0,)), ((), ())),
        precision=HIGHEST,
        preferred_element_type=jnp.float32,
    )


STEPS = LANES // BLOCK
FIRST_STEPS = 5
SECOND_STEPS = 6


def sweep_both(wide_work, narrow_work, begin, end, blocks):
    def step(i, blocks):
        return (
            sweep_block(*wide_work, 0, i, blocks[0]),
            sweep_block(*narrow_work, 0, i, blocks[1]),
        )

    return lax.fori_loop(begin, end, step, blocks)


def sweep_wide(work, begin, end, block):
    return lax.fori_loop(begin, end, lambda i, block: sweep_block(*work, 1, i, block), block)


def unit_scale(block):
    row, col = iotas(block.shape)
    line = jnp.sum(jnp.where(row == col, block, 0.0), axis=0, keepdims=True)
    return jnp.broadcast_to(lax.rsqrt(line), (PANEL, block.shape[1]))


def on_rows(scale):
    n = scale.shape[1]
    return jnp.broadcast_to(scale[:1], (n, n))


def scaled(block, down, across):
    return (block * on_rows(down).T) * on_rows(across)


def first_kernel(
    place, total, mine, other, wa, wl, wr, wp, na, nl, nr, np_, ws_ref, ns_ref, *refs
):
    a_flat, b_flat = refs[:2]
    wide_work, narrow_work = (wa, wl, wr, *refs[2:6]), (na, nl, nr, *refs[6:])
    place_halves(place, (mine, other), 0, a_flat)
    place_halves(place, (mine, other), a_flat.shape[0] // 2, b_flat)
    n = LANES
    slab = a_flat[n : n + PANEL]
    first, square = unpack_pair(a_flat[:n], jnp.broadcast_to(slab[:1], (n, n)))
    corner = b_flat[:n] / total
    last = unfold(b_flat[n:], jnp.broadcast_to(slab[1:2], (n, n)))
    row, col = iotas((n, n))
    damp = jnp.where(row == col, DAMP, 0.0)
    clear(wide_work)
    clear(narrow_work)
    first, last, square = first / total + damp, last / total + damp, square / total + damp
    by_first, by_last, by_square = (unit_scale(block) for block in (first, last, square))
    ws_ref[:, :n] = by_first
    ws_ref[:, n:] = by_last
    ns_ref[...] = by_square
    first_across, last_across = on_rows(by_first), on_rows(by_last)
    first_down, last_down = first_across.T, last_across.T
    corner = (corner * first_down) * last_across
    wa[BLOCK : BLOCK + n, :n] = (first * first_down) * first_across
    wa[BLOCK : BLOCK + n, n:] = corner
    wa[BLOCK + n : BLOCK + 2 * n, :n] = corner.T
    wa[BLOCK + n : BLOCK + 2 * n, n:] = (last * last_down) * last_across
    na[BLOCK : BLOCK + n, :] = scaled(square, by_square, by_square)
    start = (wa[BLOCK : 2 * BLOCK, :], na[BLOCK : 2 * BLOCK, :])
    wp[...], np_[...] = sweep_both(wide_work, narrow_work, 0, FIRST_STEPS, start)


def second_kernel(*refs):
    given, scale, ninv_ref, state, narrow_state, wide_rows, narrow_rows = (
        refs[:8],
        refs[8],
        refs[9],
        refs[10:14],
        refs[14:17],
        refs[17:21],
        refs[21:],
    )
    for source, target in zip((*given[:3], *given[4:7]), (*state[:3], *narrow_state)):
        target[...] = source[...]
    wide_work, narrow_work = (*state[:3], *wide_rows), (*narrow_state, *narrow_rows)
    wp = state[3]
    panels = (given[3][...], given[7][...])
    panel, _ = sweep_both(wide_work, narrow_work, FIRST_STEPS, STEPS, panels)
    trailing_update(*narrow_work[:3], LANES)
    by_square = scale[...]
    ninv_ref[...] = scaled(-narrow_work[0][BLOCK : BLOCK + LANES, :], by_square, by_square)
    wp[...] = sweep_wide(wide_work, 0, SECOND_STEPS, panel)


def third_kernel(wa_in, wl_in, wr_in, panel_in, scale, winv, wa, wl, wr, *rows):
    wa[...] = wa_in[...]
    wl[...] = wl_in[...]
    wr[...] = wr_in[...]
    sweep_wide((wa, wl, wr, *rows), SECOND_STEPS, STEPS, panel_in[...])
    wide = wa.shape[1]
    trailing_update(wa, wl, wr, wide)
    parts = [slice(i, i + LANES) for i in range(0, wide, LANES)]
    across = [on_rows(scale[:, i]) for i in parts]
    down = [block.T for block in across]
    for i, rows_scale in zip(parts, down):
        for j, columns_scale in zip(parts, across):
            block = -wa[BLOCK + i.start : BLOCK + i.stop, j]
            winv[i, j] = (block * rows_scale) * columns_scale


def state_shapes(size):
    shapes = [jax.ShapeDtypeStruct(v.shape, v.dtype) for v in work_shapes(size)]
    return shapes + [jax.ShapeDtypeStruct((BLOCK, size), jnp.float32)]


def sweep_call(kernel, name, args, out_shapes, scratch):
    return pl.pallas_call(
        kernel,
        in_specs=[VMEM] * len(args),
        out_specs=[VMEM] * len(out_shapes),
        out_shape=out_shapes,
        scratch_shapes=scratch,
        cost_estimate=sweep_cost(),
        compiler_params=PARAMS,
        name=name,
    )(*args)


def first_panels(place, pieces, wide, narrow, total):
    return sweep_call(
        functools.partial(first_kernel, place, total),
        "first_panels",
        pieces,
        state_shapes(wide)
        + state_shapes(narrow)
        + [jax.ShapeDtypeStruct((PANEL, n), jnp.float32) for n in (wide, narrow)],
        [
            pltpu.VMEM((EARLY_ROWS, LANES), jnp.float32),
            pltpu.VMEM((LATE_ROWS, LANES), jnp.float32),
            *row_shapes(wide),
            *row_shapes(narrow),
        ],
    )


def second_panels(state, wide, narrow):
    ninv = jax.ShapeDtypeStruct((narrow, narrow), jnp.float32)
    return sweep_call(
        second_kernel,
        "second_panels",
        state,
        [ninv] + state_shapes(wide),
        [*work_shapes(narrow), *row_shapes(wide), *row_shapes(narrow)],
    )


def third_panels(state, wide):
    winv = jax.ShapeDtypeStruct((wide, wide), jnp.float32)
    scratch = [*work_shapes(wide), *row_shapes(wide)]
    return sweep_call(third_kernel, "third_panels", state, [winv], scratch)[0]


def product_kernel(place, total, rows, winv, ninv_ref, mine, other, out_ref, flat):
    place_halves(place, (mine, other), 0, flat)
    ninv = ninv_ref[...]
    n = LANES
    inner = jnp.concatenate(
        [
            transposed_dot(flat[c * n : (c + 1) * n] / total, ninv, HIGHEST)
            for c in range(2)
        ],
        axis=0,
    )
    wide = winv.shape[1]
    cols = wide // 2 ** len(place.dp)
    near, second = lax.axis_index(place.near), lax.axis_index(place.second)
    near_stride = 2 ** (len(place.dp) - 2)
    base = place.index(place.dp) - near * near_stride - second * 2
    _, lane = iotas((PANEL, LANES))
    picks = [
        aligned_rows(winv, base + (j // 2) * near_stride + (j % 2) * 2, cols) for j in range(4)
    ]
    if cols % PANEL == 0:
        whole = dot(jnp.concatenate(picks, axis=0), inner)
        updates = [whole[j * cols : (j + 1) * cols] for j in range(4)]
    else:
        updates = [dot(picked, inner) for picked in picks]
    for j, (picked, update) in enumerate(zip(picks, updates)):
        for x in range(2):
            block = 2 * j + x
            out_ref[block, :cols] = picked[:, :LANES]
            out_ref[block, cols : 2 * cols] = picked[:, LANES:]
            if packs(cols, rows):
                upper, lower = update[:PANEL], update[PANEL:]
                if x == 0:
                    lower = pltpu.roll(lower, rows, 1)
                else:
                    upper = pltpu.roll(upper, rows, 1)
                out_ref[block, 2 * cols :] = jnp.where(lane < rows, upper, lower)
            else:
                out_ref[block, 2 * cols :] = update


def products(place, winv, ninv, pieces, rows, total):
    wide, narrow = winv.shape[0], ninv.shape[0]
    cols = wide // 2 ** len(place.dp)
    height = 2 * cols + (PANEL if packs(cols, rows) else cols)
    return pl.pallas_call(
        functools.partial(product_kernel, place, total, rows),
        in_specs=[VMEM] * 4,
        out_specs=VMEM,
        out_shape=jax.ShapeDtypeStruct((8, height, LANES), jnp.float32),
        scratch_shapes=[pltpu.VMEM((2 * narrow, LANES), jnp.float32)],
        compiler_params=PARAMS,
        name="products",
    )(winv, ninv, *pieces)


def placing_kernel(place, slots_ref, got_ref, kept_ref, update_ref):
    layers = got_ref.shape[0]
    slots, cols, wide = kept_ref.shape
    rows = update_ref.shape[2]
    own, dp = place.index(place.own), place.index(place.dp)
    step = min(cols, PANEL)
    row, col = iotas((step, LANES))
    for h in range(wide // LANES):
        lanes = slice(h * LANES, (h + 1) * LANES)
        for r in range(0, cols, step):
            here = h * cols + r
            empty = jnp.where(col + h * LANES == row + dp * cols + r, 1.0 / DAMP, 0.0)
            for c in range(slots):
                value = empty
                for l in range(layers):
                    taken = slots_ref[l, :step] == c
                    value = jnp.where(taken, got_ref[l, here : here + step], value)
                kept_ref[c, r : r + step, lanes] = value
    for l in range(layers):
        value = got_ref[l, 2 * cols :]
        if packs(cols, rows):
            update_ref[l, :PANEL] = value[:, :rows]
            update_ref[l, PANEL:] = value[:, rows:]
        else:
            part = value[:, :rows]
            for p in range(1, LANES // rows):
                part = jnp.where(own == p, value[:, p * rows : (p + 1) * rows], part)
            update_ref[l] = part


def placing(place, slots_of, got, wide, cols, slots, rows):
    layers = got.shape[0]
    return pl.pallas_call(
        functools.partial(placing_kernel, place),
        in_specs=[VMEM, VMEM],
        out_specs=[VMEM, VMEM],
        out_shape=[
            jax.ShapeDtypeStruct((slots, cols, wide), jnp.float32),
            jax.ShapeDtypeStruct((layers, cols, rows), jnp.float32),
        ],
        compiler_params=PARAMS,
        name="placing",
    )(slots_of, got)


def swap(value, axis):
    return lax.ppermute(value, axis, [(0, 1), (1, 0)])


def swap_by_core(value, place, stage, orders):
    names = (place.near, place.second, place.core, place.first)
    flips = {"near": 8, "second": 4, "first": 1}
    pairs = [(i, i ^ flips[orders[(i >> 1) & 1][stage]]) for i in range(16)]
    return lax.ppermute(value, names, pairs)


def after(value, *others):
    return lax.optimization_barrier((value,) + others)[0]


def on_device(place, wide_rows, narrow_rows, owner_map):
    layers, rows, wide = wide_rows.shape
    narrow = narrow_rows.shape[2]
    n_dp, n_own = 2 ** len(place.dp), 2 ** len(place.own)
    total = float(rows * n_dp * n_own)

    h_keep, h_send, wides, narrows = hot_squares(place, wide_rows, narrow_rows)
    first_send = h_send[4:]
    h_got = swap(first_send, place.core)
    c_keep, c_send = cold_squares(place, after(wides, first_send), narrows)
    h_keep, c_send = lax.optimization_barrier((h_keep, c_send))
    others = ORDERS[::-1]

    hot = h_keep[4:] + h_got
    s_got = swap_by_core(hot, place, 0, ORDERS)
    m_keep, m_send, slots_of = mixed_sums(place, owner_map, after(wides, hot), narrows)
    c_got = swap(after(c_send + h_send[:4], m_send), place.core)
    m_got = swap(m_send, place.core)

    s = (c_keep + h_keep[:4]) + s_got
    s = s + after(c_got, s)
    s_got = swap_by_core(s[2:], place, 1, ORDERS)
    m = after(m_keep, s) + m_got
    m_got = swap_by_core(m[4:], place, 0, others)

    s = s[:2] + s_got
    s_got = swap_by_core(s[1], place, 2, ORDERS)
    m = after(m[:4], s) + m_got
    m_got = swap_by_core(m[2:], place, 1, others)

    s = s[0] + s_got
    if place.extra:
        s = lax.psum(s, place.extra)
    s_got = swap(s, place.far)
    m = after(m[:2], s) + m_got
    m_got = swap_by_core(m[1], place, 2, others)

    s = s + s_got
    state = first_panels(place, [s, swap(s, place.core)], wide, narrow, total)
    m = after(m[0], state[0]) + m_got
    if place.extra:
        m = lax.psum(m, place.extra)
    m_got = swap(m, place.far)
    *state, wide_scale, narrow_scale = state
    ninv, *state = second_panels([*state, narrow_scale], wide, narrow)
    m = after(m, ninv) + m_got
    m_got = swap(m, place.core)
    winv = third_panels([*state, wide_scale], wide)
    cols, own_rows = wide // n_dp, narrow // n_own
    sent = products(place, winv, ninv, [m, m_got], own_rows, total)
    got = lax.all_to_all(sent, (place.near, place.second, place.first), 0, 0)
    kept, update = placing(
        place, slots_of, got, wide, cols, layers // n_own + 1, own_rows
    )
    return (jnp.swapaxes(kept, 1, 2), jnp.swapaxes(update, 1, 2))


def solution(mesh):
    n_dp, n_own = mesh.shape["dp"], mesh.shape["own"]
    dp_names = tuple(f"dp{i}" for i in range(int(np.log2(n_dp))))
    own_names = tuple(f"own{i}" for i in range(int(np.log2(n_own))))
    names = dp_names + own_names
    bits = jax.sharding.Mesh(mesh.devices.reshape((2,) * len(names)), names)
    in_specs = (P(None, names, None), P(None, names, None), P())
    out_specs = (P(own_names, None, dp_names), P(None, own_names, dp_names))
    return jax.shard_map(
        functools.partial(on_device, Place(dp_names, own_names)),
        mesh=bits,
        in_specs=in_specs,
        out_specs=out_specs,
        check_vma=False,
    )
```

```python
import functools

import jax
import jax.numpy as jnp
import numpy as np
from jax import lax
from jax.experimental import pallas as pl
from jax.experimental.pallas import tpu as pltpu
from jax.sharding import PartitionSpec as P

DAMP = 0.5
LANES = 128
PANEL = 8
BLOCK = 2 * PANEL
VMEM_LIMIT = 48 * 1024 * 1024
HIGHEST = lax.Precision.HIGHEST
VMEM = pl.BlockSpec(memory_space=pltpu.VMEM)
SMEM = pl.BlockSpec(memory_space=pltpu.SMEM)
HBM = pl.BlockSpec(memory_space=pltpu.HBM)
PARAMS = pltpu.CompilerParams(vmem_limit_bytes=VMEM_LIMIT)


class Place:
    def __init__(self, dp_names, own_names):
        self.dp, self.own = dp_names, own_names
        self.core, self.second, self.near, self.far = (
            dp_names[-1],
            dp_names[-2],
            dp_names[1],
            dp_names[0],
        )
        self.first = own_names[-1]
        used = (self.core, self.second, self.near, self.far, self.first)
        self.extra = tuple(n for n in dp_names + own_names if n not in used)

    def index(self, names):
        value = jnp.int32(0)
        for name in names:
            value = value * 2 + lax.axis_index(name)
        return value

    def layer(self):
        return self.index((self.near, self.second, self.first))


def transposed_dot(a, b, precision=None):
    return lax.dot_general(
        a, b, (((0,), (0,)), ((), ())), precision=precision, preferred_element_type=jnp.float32
    )


AHEAD = 5


def layer_copies(place, sources, buffers, sems):
    layer = place.layer()
    return [
        [
            pltpu.make_async_copy(
                source.at[jnp.bitwise_xor(layer, i)], buffer.at[i], sems.at[i, s]
            )
            for s, (source, buffer) in enumerate(zip(sources, buffers))
        ]
        for i in range(buffers[0].shape[0])
    ]


def both_halves(place, flat, i):
    rows = flat.shape[1] // 2
    core = lax.axis_index(place.core)
    kept = pl.multiple_of(core * rows, PANEL)
    sent = pl.multiple_of((1 - core) * rows, PANEL)
    return flat[i, pl.ds(kept, rows), :], flat[i, pl.ds(sent, rows), :]


ORDERS = (("first", "second", "near"), ("second", "near", "first"))


def position(axes, i):
    bits = {"near": i // 4, "second": (i // 2) % 2, "first": i % 2}
    return bits[axes[0]] * 4 + bits[axes[1]] * 2 + bits[axes[2]]


def positions(place, i, orders):
    core = lax.axis_index(place.core)
    first, second = (position(axes, i) for axes in orders)
    return jnp.where(core == 0, first, second), jnp.where(core == 0, second, first)


def iotas(shape):
    return (
        lax.broadcasted_iota(jnp.int32, shape, 0),
        lax.broadcasted_iota(jnp.int32, shape, 1),
    )


def pack_pair(first, second):
    row, col = iotas(first.shape)
    return jnp.where(row >= col, first, second)


def unpack_pair(packed, second_diagonal):
    row, col = iotas(packed.shape)
    turned = packed.T
    first = jnp.where(row >= col, packed, turned)
    second = jnp.where(col > row, packed, turned)
    return first, jnp.where(row == col, second_diagonal, second)


def fold(block):
    h = block.shape[0] // 2
    row, col = iotas((h, 2 * h))
    last = pltpu.roll(block[h:], h, 1)
    return jnp.where((col >= h) | (row >= col), block[:h], last)


def unfold(folded, diagonal):
    h, n = folded.shape
    row, col = iotas((n, n))
    block = jnp.concatenate([folded, jnp.zeros((h, n), jnp.float32)], axis=0)
    turned = block.T
    top = jnp.where((col >= h) | (col <= row), block, turned)
    moved = pltpu.roll(pltpu.roll(block, h, 0), h, 1)
    moved_turned = pltpu.roll(pltpu.roll(turned, h, 0), h, 1)
    last = jnp.where(col > row, moved, moved_turned)
    last = jnp.where(row == col, diagonal, last)
    return jnp.where(row < h, top, jnp.where(col < h, turned, last))


def diagonals(blocks, rows):
    n = blocks[0].shape[0]
    row, col = iotas((n, n))
    slab_row, _ = iotas((rows, n))
    slab = jnp.zeros((rows, n), jnp.float32)
    for i, block in enumerate(blocks):
        line = jnp.sum(jnp.where(row == col, block, 0.0), axis=0, keepdims=True)
        slab = jnp.where(slab_row == i, jnp.broadcast_to(line, (rows, n)), slab)
    return slab


EARLY_ROWS = 144
LATE_ROWS = 192


HOT = (1, 2, 3, 5, 6, 7)
COLD = (0, 4)


def square_sums(wide, narrow):
    return transposed_dot(wide, wide), transposed_dot(narrow, narrow)


def pack_layer(place, i, wcov, ncov, a_flat, b_flat):
    n = LANES
    last = wcov[n:, n:]
    a_flat[i, :n] = pack_pair(wcov[:n, :n], ncov)
    a_flat[i, n:] = diagonals((ncov, last), EARLY_ROWS - n)
    b_flat[i, :n] = wcov[:n, n:]
    b_flat[i, n:] = fold(last)
    a_kept, a_sent = both_halves(place, a_flat, i)
    b_kept, b_sent = both_halves(place, b_flat, i)
    return (a_kept, b_kept), (a_sent, b_sent)


def put(ref, index, parts):
    rows = EARLY_ROWS // 2
    ref[index, :rows] = parts[0]
    ref[index, rows:] = parts[1]


def put_layer(place, i, sums, a_flat, b_flat, keep, send):
    kept, sent = pack_layer(place, i, *sums, a_flat, b_flat)
    mine, other = positions(place, i, ORDERS)
    put(keep, mine, kept)
    put(send, other, sent)


def clear_others(place, layers, keep, send):
    for i in layers:
        mine, other = positions(place, i, ORDERS)
        keep[mine] = jnp.zeros(keep.shape[1:], jnp.float32)
        send[other] = jnp.zeros(send.shape[1:], jnp.float32)


def hot_kernel(place, wide_hbm, narrow_hbm, keep, send, wides, narrows, a_flat, b_flat, sems):
    copies = layer_copies(place, (wide_hbm, narrow_hbm), (wides, narrows), sems)
    order = HOT + COLD
    for i in order[:AHEAD]:
        for copy in copies[i]:
            copy.start()
    clear_others(place, COLD, keep, send)

    def pack(i, sums):
        put_layer(place, i, sums, a_flat, b_flat, keep, send)

    before = None
    for at, i in enumerate(order):
        for copy in copies[i]:
            copy.wait()
        if at + AHEAD < len(order):
            for copy in copies[order[at + AHEAD]]:
                copy.start()
        if before is not None:
            pack(*before)
            before = None
        if i in HOT:
            before = (i, square_sums(wides[i], narrows[i]))


def cold_kernel(place, wides, narrows, keep, send, a_flat, b_flat):
    for i in COLD:
        put_layer(
            place, i, square_sums(wides[i], narrows[i]), a_flat, b_flat, keep, send
        )
    core = lax.axis_index(place.core)
    stay = [[i for i in HOT if position(axes, i) < 4] for axes in ORDERS]
    for first, second in zip(*stay):
        here = [position(axes, i) for axes, i in zip(ORDERS, (first, second))]
        mine = jnp.where(core == 0, here[0], here[1])
        other = jnp.where(core == 0, here[1], here[0])
        keep[mine] = jnp.zeros(keep.shape[1:], jnp.float32)
        send[other] = jnp.zeros(send.shape[1:], jnp.float32)


def write_slots(place, owner_map, slots_ref):
    own = place.index(place.own)
    count = jnp.int32(0)
    for l in range(slots_ref.shape[0]):
        mine = owner_map[l] == own
        slot = jnp.where(mine, count, -1)
        slots_ref[l] = jnp.full(slots_ref.shape[1:], 0, jnp.int32) + slot
        count = count + mine.astype(jnp.int32)


def mixed_kernel(place, owner_map, wides, narrows, keep, send, slots_ref, flat):
    n = LANES
    write_slots(place, owner_map, slots_ref)
    for i in range(wides.shape[0]):
        mixed = transposed_dot(narrows[i], wides[i])
        flat[i, :n] = mixed[:, :n]
        flat[i, n:] = mixed[:, n:]
        kept, sent = both_halves(place, flat, i)
        mine, other = positions(place, i, ORDERS[::-1])
        keep[mine] = kept
        send[other] = sent


def gram_cost(wide_rows, columns):
    return pl.CostEstimate(
        flops=2 * wide_rows.size * columns, bytes_accessed=2 * wide_rows.size, transcendentals=0
    )


HALF_ROWS = (EARLY_ROWS + LATE_ROWS) // 2


def pack_shapes(layers):
    return [
        pltpu.VMEM((layers, EARLY_ROWS, LANES), jnp.float32),
        pltpu.VMEM((layers, LATE_ROWS, LANES), jnp.float32),
    ]


def hot_squares(place, wide_rows, narrow_rows):
    layers = wide_rows.shape[0]
    half = jax.ShapeDtypeStruct((layers, HALF_ROWS, LANES), jnp.float32)
    return pl.pallas_call(
        functools.partial(hot_kernel, place),
        in_specs=[HBM, HBM],
        out_specs=[VMEM] * 4,
        out_shape=[
            half,
            half,
            jax.ShapeDtypeStruct(wide_rows.shape, wide_rows.dtype),
            jax.ShapeDtypeStruct(narrow_rows.shape, narrow_rows.dtype),
        ],
        scratch_shapes=[*pack_shapes(layers), pltpu.SemaphoreType.DMA((layers, 2))],
        cost_estimate=gram_cost(wide_rows, 240),
        compiler_params=PARAMS,
        name="hot_squares",
    )(
        pltpu.with_memory_space_constraint(wide_rows, pltpu.HBM),
        pltpu.with_memory_space_constraint(narrow_rows, pltpu.HBM),
    )


def cold_squares(place, wides, narrows):
    half = jax.ShapeDtypeStruct((wides.shape[0] // 2, HALF_ROWS, LANES), jnp.float32)
    return pl.pallas_call(
        functools.partial(cold_kernel, place),
        in_specs=[VMEM, VMEM],
        out_specs=[VMEM, VMEM],
        out_shape=[half, half],
        scratch_shapes=pack_shapes(wides.shape[0]),
        cost_estimate=gram_cost(wides, 80),
        compiler_params=PARAMS,
        name="cold_squares",
    )(wides, narrows)


def mixed_sums(place, owner_map, wides, narrows):
    layers, _, narrow = narrows.shape
    half = jax.ShapeDtypeStruct((layers, narrow, LANES), jnp.float32)
    return pl.pallas_call(
        functools.partial(mixed_kernel, place),
        in_specs=[SMEM, VMEM, VMEM],
        out_specs=[VMEM] * 3,
        out_shape=[half, half, jax.ShapeDtypeStruct((layers, PANEL, LANES), jnp.int32)],
        scratch_shapes=[pltpu.VMEM((layers, 2 * narrow, LANES), jnp.float32)],
        cost_estimate=gram_cost(wides, 128),
        compiler_params=PARAMS,
        name="mixed",
    )(owner_map, wides, narrows)


def lane_gather(x, index):
    return jnp.take_along_axis(x, index, axis=1, mode="promise_in_bounds")


def trailing_update(a_ref, left_ref, right_ref, base):
    size = a_ref.shape[1]
    a_ref[pl.ds(pl.multiple_of(base, BLOCK), BLOCK), :] = jnp.zeros((BLOCK, size), jnp.float32)
    lane = lax.broadcasted_iota(jnp.int32, (1, size), 1)
    swept = (lane >= base - BLOCK) & (lane < base)
    update = transposed_dot(left_ref[...], right_ref[...])
    a_ref[BLOCK : BLOCK + size, :] = (
        jnp.where(swept, 0.0, a_ref[BLOCK : BLOCK + size, :]) - update
    )


def in_three(x):
    high = x.astype(jnp.bfloat16).astype(jnp.float32)
    rest = x - high
    middle = rest.astype(jnp.bfloat16).astype(jnp.float32)
    return high, middle, rest - middle


def factor_panel(rows_ref, cols_ref, tile, first, panel, targets):
    tiles = panel.shape[1] // LANES
    shape = (PANEL, LANES)
    _, lane = iotas(shape)

    def on_all(ref, k, lanes):
        return jnp.broadcast_to(ref[k : k + 1, lanes], shape)

    rows_ref[...] = panel
    lanes = [slice(LANES * t, LANES * (t + 1)) for t in range(tiles)]
    rows = [[on_all(rows_ref, k, part) for part in lanes] for k in range(PANEL)]
    here = panel[:, lanes[tile]]
    for j in range(PANEL):
        column = lane_gather(here, jnp.full(shape, 0, jnp.int32) + (first + j))
        cols_ref[PANEL * j : PANEL * (j + 1)] = column
    d = [[None] * PANEL for _ in range(PANEL)]
    for j in range(PANEL):
        for i in range(j, PANEL):
            d[i][j] = on_all(cols_ref, PANEL * j + i, slice(None))
    own = (lane >= first) & (lane < first + PANEL)
    q = [[None] * tiles for _ in range(PANEL)]
    p = [[None] * tiles for _ in range(PANEL)]
    weights = [[None] * PANEL for _ in targets]
    factor = [[None] * PANEL for _ in range(PANEL)]

    def substitute(k, scale):
        for t in range(tiles):
            value = rows[k][t]
            if t == tile:
                value = jnp.where(own, jnp.where(lane == first + k, -1.0, 0.0), value)
            for j in range(k):
                value = value - factor[k][j] * q[j][t]
            q[k][t] = value
            p[k][t] = value * scale
        for target, weight in zip(targets, weights):
            source, index = target(rows[k])
            value = lane_gather(source, index)
            for j in range(k):
                value = value - factor[k][j] * weight[j]
            weight[k] = value

    for k in range(0, PANEL, 2):
        m = k + 1
        a, b, c = d[k][k], d[m][k], d[m][m]
        first_scale = 1.0 / a
        second_scale = a * (1.0 / (a * c - b * b))
        factor[m][k] = b * first_scale
        left_over = {i: d[i][m] - d[i][k] * factor[m][k] for i in range(k + 2, PANEL)}
        for i in range(k + 2, PANEL):
            factor[i][k] = d[i][k] * first_scale
            factor[i][m] = left_over[i] * second_scale
        for i in range(k + 2, PANEL):
            for j in range(k + 2, i + 1):
                value = d[i][j] - d[i][k] * factor[j][k]
                d[i][j] = value - (left_over[i] * left_over[j]) * second_scale
        substitute(k, first_scale)
        substitute(m, second_scale)
    return q, p, weights


def packed_rows(values):
    sub, _ = iotas((PANEL, LANES))
    whole = []
    for t in range(len(values[0])):
        value = values[0][t]
        for k in range(1, PANEL):
            value = jnp.where(sub == k, values[k][t], value)
        whole.append(value)
    return whole


def side_by_side(tiles):
    return jnp.concatenate(tiles, axis=1) if len(tiles) > 1 else tiles[0]


def sweep_block(a_ref, left_ref, right_ref, a_rows, a_cols, b_rows, b_cols, tile, step, block):
    size = a_ref.shape[1]
    tiles = size // LANES
    first = step * BLOCK
    second = first + PANEL
    base = tile * LANES + first
    trailing_update(a_ref, left_ref, right_ref, base)

    sub, lane = iotas((PANEL, LANES))
    last = first == LANES - BLOCK
    next_first = jnp.where(last, 0, first + BLOCK)

    def in_block(row):
        return row[tile], second + sub

    def in_next(offset):
        def target(row):
            source = row[tile]
            if tile + 1 < tiles:
                source = jnp.where(last, row[tile + 1], source)
            return source, next_first + offset + sub

        return target

    nexts = [in_next(0), in_next(PANEL)]
    in_a = (lane >= first) & (lane < second)
    in_b = (lane >= second) & (lane < second + PANEL)

    def swept(tiles_of, mask):
        return [jnp.where(mask, 0.0, v) if t == tile else v for t, v in enumerate(tiles_of)]

    def minus(tiles_of, weight, p):
        result = []
        for t, value in enumerate(tiles_of):
            for k in range(PANEL):
                value = value - weight[k] * p[k][t]
            result.append(value)
        return result

    def by_tile(rows):
        return [rows[:, LANES * t : LANES * (t + 1)] for t in range(tiles)]

    qa, pa, (to_b, *to_next_a) = factor_panel(
        a_rows, a_cols, tile, first, block[:PANEL], [in_block, *nexts]
    )
    panel_b = side_by_side(minus(swept(by_tile(block[PANEL:]), in_a), to_b, pa))
    qb, pb, to_next_b = factor_panel(b_rows, b_cols, tile, second, panel_b, nexts)

    left, right = [], []
    for q, p, mask in ((qa, pa, in_b), (qb, pb, None)):
        q, p = packed_rows(q), packed_rows(p)
        if mask is not None:
            q, p = swept(q, mask), swept(p, mask)
        qs, ps = in_three(side_by_side(q)), in_three(side_by_side(p))
        left += [qs[i] for i in (0, 0, 1, 1, 0, 2)]
        right += [ps[i] for i in (0, 1, 0, 1, 2, 0)]
    left_ref[...] = jnp.concatenate(left, axis=0).astype(jnp.bfloat16)
    right_ref[...] = jnp.concatenate(right, axis=0).astype(jnp.bfloat16)

    following = a_ref[pl.ds(pl.multiple_of(base + 2 * BLOCK, BLOCK), BLOCK), :]
    result = []
    for g in range(2):
        rows = by_tile(following[g * PANEL : (g + 1) * PANEL])
        rows = minus(swept(rows, in_a), to_next_a[g], pa)
        rows = minus(swept(rows, in_b), to_next_b[g], pb)
        result.append(side_by_side(rows))
    return jnp.concatenate(result, axis=0)


def place_halves(place, pieces, first_row, flat):
    core = lax.axis_index(place.core)
    rows = flat.shape[0] // 2
    for r, piece in enumerate(pieces):
        start = pl.multiple_of(jnp.bitwise_xor(core, r) * rows, PANEL)
        flat[pl.ds(start, rows), :] = piece[first_row : first_row + rows]


def sweep_cost():
    return pl.CostEstimate(flops=1 << 30, bytes_accessed=1 << 20, transcendentals=0)


def clear(work):
    a_ref, left, right = work[:3]
    size = a_ref.shape[1]
    a_ref[:BLOCK] = jnp.zeros((BLOCK, size), jnp.float32)
    a_ref[BLOCK + size :] = jnp.zeros((BLOCK, size), jnp.float32)
    left[...] = jnp.zeros(left.shape, left.dtype)
    right[...] = jnp.zeros(right.shape, right.dtype)


def work_shapes(size):
    splits = 6 * BLOCK
    return [
        pltpu.VMEM((size + 2 * BLOCK, size), jnp.float32),
        pltpu.VMEM((splits, size), jnp.bfloat16),
        pltpu.VMEM((splits, size), jnp.bfloat16),
    ]


def row_shapes(size):
    return [
        pltpu.VMEM((PANEL, size), jnp.float32),
        pltpu.VMEM((PANEL * PANEL, LANES), jnp.float32),
    ] * 2


def aligned_rows(ref, index, count):
    if count % PANEL == 0:
        return ref[pl.ds(pl.multiple_of(index * count, count), count), :]
    per_slab = PANEL // count
    slab = ref[pl.ds(pl.multiple_of(index // per_slab * PANEL, PANEL), PANEL), :]
    value = slab[:count]
    for i in range(1, per_slab):
        value = jnp.where(index % per_slab == i, slab[i * count : (i + 1) * count], value)
    return value


def packs(cols, rows):
    return cols == 2 * PANEL and 2 * rows == LANES


def dot(a, b, last=False):
    return lax.dot_general(
        a,
        b,
        (((1,), (1 if last else 0,)), ((), ())),
        precision=HIGHEST,
        preferred_element_type=jnp.float32,
    )


STEPS = LANES // BLOCK
FIRST_STEPS = 5
SECOND_STEPS = 6


def sweep_both(wide_work, narrow_work, begin, end, blocks):
    def step(i, blocks):
        return (
            sweep_block(*wide_work, 0, i, blocks[0]),
            sweep_block(*narrow_work, 0, i, blocks[1]),
        )

    return lax.fori_loop(begin, end, step, blocks)


def sweep_wide(work, begin, end, block):
    return lax.fori_loop(begin, end, lambda i, block: sweep_block(*work, 1, i, block), block)


def unit_scale(block):
    row, col = iotas(block.shape)
    line = jnp.sum(jnp.where(row == col, block, 0.0), axis=0, keepdims=True)
    return jnp.broadcast_to(lax.rsqrt(line), (PANEL, block.shape[1]))


def on_rows(scale):
    n = scale.shape[1]
    return jnp.broadcast_to(scale[:1], (n, n))


def scaled(block, down, across):
    return (block * on_rows(down).T) * on_rows(across)


def first_kernel(
    place, total, mine, other, wa, wl, wr, wp, na, nl, nr, np_, ws_ref, ns_ref, *refs
):
    a_flat, b_flat = refs[:2]
    wide_work, narrow_work = (wa, wl, wr, *refs[2:6]), (na, nl, nr, *refs[6:])
    place_halves(place, (mine, other), 0, a_flat)
    place_halves(place, (mine, other), a_flat.shape[0] // 2, b_flat)
    n = LANES
    slab = a_flat[n : n + PANEL]
    first, square = unpack_pair(a_flat[:n], jnp.broadcast_to(slab[:1], (n, n)))
    corner = b_flat[:n] / total
    last = unfold(b_flat[n:], jnp.broadcast_to(slab[1:2], (n, n)))
    row, col = iotas((n, n))
    damp = jnp.where(row == col, DAMP, 0.0)
    clear(wide_work)
    clear(narrow_work)
    first, last, square = first / total + damp, last / total + damp, square / total + damp
    by_first, by_last, by_square = (unit_scale(block) for block in (first, last, square))
    ws_ref[:, :n] = by_first
    ws_ref[:, n:] = by_last
    ns_ref[...] = by_square
    first_across, last_across = on_rows(by_first), on_rows(by_last)
    first_down, last_down = first_across.T, last_across.T
    corner = (corner * first_down) * last_across
    wa[BLOCK : BLOCK + n, :n] = (first * first_down) * first_across
    wa[BLOCK : BLOCK + n, n:] = corner
    wa[BLOCK + n : BLOCK + 2 * n, :n] = corner.T
    wa[BLOCK + n : BLOCK + 2 * n, n:] = (last * last_down) * last_across
    na[BLOCK : BLOCK + n, :] = scaled(square, by_square, by_square)
    start = (wa[BLOCK : 2 * BLOCK, :], na[BLOCK : 2 * BLOCK, :])
    wp[...], np_[...] = sweep_both(wide_work, narrow_work, 0, FIRST_STEPS, start)


def second_kernel(*refs):
    given, scale, ninv_ref, state, narrow_state, wide_rows, narrow_rows = (
        refs[:8],
        refs[8],
        refs[9],
        refs[10:14],
        refs[14:17],
        refs[17:21],
        refs[21:],
    )
    for source, target in zip((*given[:3], *given[4:7]), (*state[:3], *narrow_state)):
        target[...] = source[...]
    wide_work, narrow_work = (*state[:3], *wide_rows), (*narrow_state, *narrow_rows)
    wp = state[3]
    panels = (given[3][...], given[7][...])
    panel, _ = sweep_both(wide_work, narrow_work, FIRST_STEPS, STEPS, panels)
    trailing_update(*narrow_work[:3], LANES)
    by_square = scale[...]
    ninv_ref[...] = scaled(-narrow_work[0][BLOCK : BLOCK + LANES, :], by_square, by_square)
    wp[...] = sweep_wide(wide_work, 0, SECOND_STEPS, panel)


def third_kernel(wa_in, wl_in, wr_in, panel_in, scale, winv, wa, wl, wr, *rows):
    wa[...] = wa_in[...]
    wl[...] = wl_in[...]
    wr[...] = wr_in[...]
    sweep_wide((wa, wl, wr, *rows), SECOND_STEPS, STEPS, panel_in[...])
    wide = wa.shape[1]
    trailing_update(wa, wl, wr, wide)
    parts = [slice(i, i + LANES) for i in range(0, wide, LANES)]
    across = [on_rows(scale[:, i]) for i in parts]
    down = [block.T for block in across]
    for i, rows_scale in zip(parts, down):
        for j, columns_scale in zip(parts, across):
            block = -wa[BLOCK + i.start : BLOCK + i.stop, j]
            winv[i, j] = (block * rows_scale) * columns_scale


def state_shapes(size):
    shapes = [jax.ShapeDtypeStruct(v.shape, v.dtype) for v in work_shapes(size)]
    return shapes + [jax.ShapeDtypeStruct((BLOCK, size), jnp.float32)]


def sweep_call(kernel, name, args, out_shapes, scratch):
    return pl.pallas_call(
        kernel,
        in_specs=[VMEM] * len(args),
        out_specs=[VMEM] * len(out_shapes),
        out_shape=out_shapes,
        scratch_shapes=scratch,
        cost_estimate=sweep_cost(),
        compiler_params=PARAMS,
        name=name,
    )(*args)


def first_panels(place, pieces, wide, narrow, total):
    return sweep_call(
        functools.partial(first_kernel, place, total),
        "first_panels",
        pieces,
        state_shapes(wide)
        + state_shapes(narrow)
        + [jax.ShapeDtypeStruct((PANEL, n), jnp.float32) for n in (wide, narrow)],
        [
            pltpu.VMEM((EARLY_ROWS, LANES), jnp.float32),
            pltpu.VMEM((LATE_ROWS, LANES), jnp.float32),
            *row_shapes(wide),
            *row_shapes(narrow),
        ],
    )


def second_panels(state, wide, narrow):
    ninv = jax.ShapeDtypeStruct((narrow, narrow), jnp.float32)
    return sweep_call(
        second_kernel,
        "second_panels",
        state,
        [ninv] + state_shapes(wide),
        [*work_shapes(narrow), *row_shapes(wide), *row_shapes(narrow)],
    )


def third_panels(state, wide):
    winv = jax.ShapeDtypeStruct((wide, wide), jnp.float32)
    scratch = [*work_shapes(wide), *row_shapes(wide)]
    return sweep_call(third_kernel, "third_panels", state, [winv], scratch)[0]


def product_kernel(place, total, rows, winv, ninv_ref, mine, other, out_ref, flat):
    place_halves(place, (mine, other), 0, flat)
    ninv = ninv_ref[...]
    n = LANES
    inner = jnp.concatenate(
        [
            transposed_dot(flat[c * n : (c + 1) * n] / total, ninv, HIGHEST)
            for c in range(2)
        ],
        axis=0,
    )
    wide = winv.shape[1]
    cols = wide // 2 ** len(place.dp)
    near, second = lax.axis_index(place.near), lax.axis_index(place.second)
    near_stride = 2 ** (len(place.dp) - 2)
    base = place.index(place.dp) - near * near_stride - second * 2
    _, lane = iotas((PANEL, LANES))
    picks = [
        aligned_rows(winv, base + (j // 2) * near_stride + (j % 2) * 2, cols) for j in range(4)
    ]
    if cols % PANEL == 0:
        whole = dot(jnp.concatenate(picks, axis=0), inner)
        updates = [whole[j * cols : (j + 1) * cols] for j in range(4)]
    else:
        updates = [dot(picked, inner) for picked in picks]
    for j, (picked, update) in enumerate(zip(picks, updates)):
        for x in range(2):
            block = 2 * j + x
            out_ref[block, :cols] = picked[:, :LANES]
            out_ref[block, cols : 2 * cols] = picked[:, LANES:]
            if packs(cols, rows):
                upper, lower = update[:PANEL], update[PANEL:]
                if x == 0:
                    lower = pltpu.roll(lower, rows, 1)
                else:
                    upper = pltpu.roll(upper, rows, 1)
                out_ref[block, 2 * cols :] = jnp.where(lane < rows, upper, lower)
            else:
                out_ref[block, 2 * cols :] = update


def products(place, winv, ninv, pieces, rows, total):
    wide, narrow = winv.shape[0], ninv.shape[0]
    cols = wide // 2 ** len(place.dp)
    height = 2 * cols + (PANEL if packs(cols, rows) else cols)
    return pl.pallas_call(
        functools.partial(product_kernel, place, total, rows),
        in_specs=[VMEM] * 4,
        out_specs=VMEM,
        out_shape=jax.ShapeDtypeStruct((8, height, LANES), jnp.float32),
        scratch_shapes=[pltpu.VMEM((2 * narrow, LANES), jnp.float32)],
        compiler_params=PARAMS,
        name="products",
    )(winv, ninv, *pieces)


def placing_kernel(place, slots_ref, got_ref, kept_ref, update_ref):
    layers = got_ref.shape[0]
    slots, cols, wide = kept_ref.shape
    rows = update_ref.shape[2]
    own, dp = place.index(place.own), place.index(place.dp)
    step = min(cols, PANEL)
    row, col = iotas((step, LANES))
    for h in range(wide // LANES):
        lanes = slice(h * LANES, (h + 1) * LANES)
        for r in range(0, cols, step):
            here = h * cols + r
            empty = jnp.where(col + h * LANES == row + dp * cols + r, 1.0 / DAMP, 0.0)
            for c in range(slots):
                value = empty
                for l in range(layers):
                    taken = slots_ref[l, :step] == c
                    value = jnp.where(taken, got_ref[l, here : here + step], value)
                kept_ref[c, r : r + step, lanes] = value
    for l in range(layers):
        value = got_ref[l, 2 * cols :]
        if packs(cols, rows):
            update_ref[l, :PANEL] = value[:, :rows]
            update_ref[l, PANEL:] = value[:, rows:]
        else:
            part = value[:, :rows]
            for p in range(1, LANES // rows):
                part = jnp.where(own == p, value[:, p * rows : (p + 1) * rows], part)
            update_ref[l] = part


def placing(place, slots_of, got, wide, cols, slots, rows):
    layers = got.shape[0]
    return pl.pallas_call(
        functools.partial(placing_kernel, place),
        in_specs=[VMEM, VMEM],
        out_specs=[VMEM, VMEM],
        out_shape=[
            jax.ShapeDtypeStruct((slots, cols, wide), jnp.float32),
            jax.ShapeDtypeStruct((layers, cols, rows), jnp.float32),
        ],
        compiler_params=PARAMS,
        name="placing",
    )(slots_of, got)


def swap(value, axis):
    return lax.ppermute(value, axis, [(0, 1), (1, 0)])


def swap_by_core(value, place, stage, orders):
    names = (place.near, place.second, place.core, place.first)
    flips = {"near": 8, "second": 4, "first": 1}
    pairs = [(i, i ^ flips[orders[(i >> 1) & 1][stage]]) for i in range(16)]
    return lax.ppermute(value, names, pairs)


def after(value, *others):
    return lax.optimization_barrier((value,) + others)[0]


def on_device(place, wide_rows, narrow_rows, owner_map):
    layers, rows, wide = wide_rows.shape
    narrow = narrow_rows.shape[2]
    n_dp, n_own = 2 ** len(place.dp), 2 ** len(place.own)
    total = float(rows * n_dp * n_own)

    h_keep, h_send, wides, narrows = hot_squares(place, wide_rows, narrow_rows)
    first_send = h_send[4:]
    h_got = swap(first_send, place.core)
    c_keep, c_send = cold_squares(place, after(wides, first_send), narrows)
    h_keep, c_send = lax.optimization_barrier((h_keep, c_send))
    others = ORDERS[::-1]

    hot = h_keep[4:] + h_got
    s_got = swap_by_core(hot, place, 0, ORDERS)
    m_keep, m_send, slots_of = mixed_sums(place, owner_map, after(wides, hot), narrows)
    c_got = swap(after(c_send + h_send[:4], m_send), place.core)
    m_got = swap(m_send, place.core)

    s = (c_keep + h_keep[:4]) + s_got
    s = s + after(c_got, s)
    s_got = swap_by_core(s[2:], place, 1, ORDERS)
    m = after(m_keep, s) + m_got
    m_got = swap_by_core(m[4:], place, 0, others)

    s = s[:2] + s_got
    s_got = swap_by_core(s[1], place, 2, ORDERS)
    m = after(m[:4], s) + m_got
    m_got = swap_by_core(m[2:], place, 1, others)

    s = s[0] + s_got
    if place.extra:
        s = lax.psum(s, place.extra)
    s_got = swap(s, place.far)
    m = after(m[:2], s) + m_got
    m_got = swap_by_core(m[1], place, 2, others)

    s = s + s_got
    m = after(m[0], s) + m_got
    if place.extra:
        m = lax.psum(m, place.extra)
    s_got = swap(after(s, m), place.core)
    m_got = swap(m, place.far)
    *state, wide_scale, narrow_scale = first_panels(place, [s, s_got], wide, narrow, total)
    ninv, *state = second_panels([*state, narrow_scale], wide, narrow)
    m = after(m, ninv) + m_got
    m_got = swap(m, place.core)
    winv = third_panels([*state, wide_scale], wide)
    cols, own_rows = wide // n_dp, narrow // n_own
    sent = products(place, winv, ninv, [m, m_got], own_rows, total)
    got = lax.all_to_all(sent, (place.near, place.second, place.first), 0, 0)
    kept, update = placing(
        place, slots_of, got, wide, cols, layers // n_own + 1, own_rows
    )
    return (jnp.swapaxes(kept, 1, 2), jnp.swapaxes(update, 1, 2))


def solution(mesh):
    n_dp, n_own = mesh.shape["dp"], mesh.shape["own"]
    dp_names = tuple(f"dp{i}" for i in range(int(np.log2(n_dp))))
    own_names = tuple(f"own{i}" for i in range(int(np.log2(n_own))))
    names = dp_names + own_names
    bits = jax.sharding.Mesh(mesh.devices.reshape((2,) * len(names)), names)
    in_specs = (P(None, names, None), P(None, names, None), P())
    out_specs = (P(own_names, None, dp_names), P(None, own_names, dp_names))
    return jax.shard_map(
        functools.partial(on_device, Place(dp_names, own_names)),
        mesh=bits,
        in_specs=in_specs,
        out_specs=out_specs,
        check_vma=False,
    )
```

```python
import functools

import jax
import jax.numpy as jnp
import numpy as np
from jax import lax
from jax.experimental import pallas as pl
from jax.experimental.pallas import tpu as pltpu
from jax.sharding import PartitionSpec as P

DAMP = 0.5
LANES = 128
PANEL = 8
BLOCK = 2 * PANEL
VMEM_LIMIT = 48 * 1024 * 1024
HIGHEST = lax.Precision.HIGHEST
VMEM = pl.BlockSpec(memory_space=pltpu.VMEM)
SMEM = pl.BlockSpec(memory_space=pltpu.SMEM)
HBM = pl.BlockSpec(memory_space=pltpu.HBM)
PARAMS = pltpu.CompilerParams(vmem_limit_bytes=VMEM_LIMIT)


class Place:
    def __init__(self, dp_names, own_names):
        self.dp, self.own = dp_names, own_names
        self.core, self.second, self.near, self.far = (
            dp_names[-1],
            dp_names[-2],
            dp_names[1],
            dp_names[0],
        )
        self.first = own_names[-1]
        used = (self.core, self.second, self.near, self.far, self.first)
        self.extra = tuple(n for n in dp_names + own_names if n not in used)

    def index(self, names):
        value = jnp.int32(0)
        for name in names:
            value = value * 2 + lax.axis_index(name)
        return value

    def layer(self):
        return self.index((self.near, self.second, self.first))


def transposed_dot(a, b, precision=None):
    return lax.dot_general(
        a, b, (((0,), (0,)), ((), ())), precision=precision, preferred_element_type=jnp.float32
    )


AHEAD = 5


def layer_copies(place, sources, buffers, sems):
    layer = place.layer()
    return [
        [
            pltpu.make_async_copy(
                source.at[jnp.bitwise_xor(layer, i)], buffer.at[i], sems.at[i, s]
            )
            for s, (source, buffer) in enumerate(zip(sources, buffers))
        ]
        for i in range(buffers[0].shape[0])
    ]


def both_halves(place, flat, i):
    rows = flat.shape[1] // 2
    core = lax.axis_index(place.core)
    kept = pl.multiple_of(core * rows, PANEL)
    sent = pl.multiple_of((1 - core) * rows, PANEL)
    return flat[i, pl.ds(kept, rows), :], flat[i, pl.ds(sent, rows), :]


ORDERS = (("first", "second", "near"), ("second", "near", "first"))


def position(axes, i):
    bits = {"near": i // 4, "second": (i // 2) % 2, "first": i % 2}
    return bits[axes[0]] * 4 + bits[axes[1]] * 2 + bits[axes[2]]


def positions(place, i, orders):
    core = lax.axis_index(place.core)
    first, second = (position(axes, i) for axes in orders)
    return jnp.where(core == 0, first, second), jnp.where(core == 0, second, first)


def iotas(shape):
    return (
        lax.broadcasted_iota(jnp.int32, shape, 0),
        lax.broadcasted_iota(jnp.int32, shape, 1),
    )


def pack_pair(first, second):
    row, col = iotas(first.shape)
    return jnp.where(row >= col, first, second)


def unpack_pair(packed, second_diagonal):
    row, col = iotas(packed.shape)
    turned = packed.T
    first = jnp.where(row >= col, packed, turned)
    second = jnp.where(col > row, packed, turned)
    return first, jnp.where(row == col, second_diagonal, second)


def fold(block):
    h = block.shape[0] // 2
    row, col = iotas((h, 2 * h))
    last = pltpu.roll(block[h:], h, 1)
    return jnp.where((col >= h) | (row >= col), block[:h], last)


def unfold(folded, diagonal):
    h, n = folded.shape
    row, col = iotas((n, n))
    block = jnp.concatenate([folded, jnp.zeros((h, n), jnp.float32)], axis=0)
    turned = block.T
    top = jnp.where((col >= h) | (col <= row), block, turned)
    moved = pltpu.roll(pltpu.roll(block, h, 0), h, 1)
    moved_turned = pltpu.roll(pltpu.roll(turned, h, 0), h, 1)
    last = jnp.where(col > row, moved, moved_turned)
    last = jnp.where(row == col, diagonal, last)
    return jnp.where(row < h, top, jnp.where(col < h, turned, last))


def diagonals(blocks, rows):
    n = blocks[0].shape[0]
    row, col = iotas((n, n))
    slab_row, _ = iotas((rows, n))
    slab = jnp.zeros((rows, n), jnp.float32)
    for i, block in enumerate(blocks):
        line = jnp.sum(jnp.where(row == col, block, 0.0), axis=0, keepdims=True)
        slab = jnp.where(slab_row == i, jnp.broadcast_to(line, (rows, n)), slab)
    return slab


EARLY_ROWS = 144
LATE_ROWS = 192


HOT = (1, 2, 3, 5, 6, 7)
COLD = (0, 4)


def square_sums(wide, narrow):
    return transposed_dot(wide, wide), transposed_dot(narrow, narrow)


def pack_layer(place, i, wcov, ncov, a_flat, b_flat):
    n = LANES
    last = wcov[n:, n:]
    a_flat[i, :n] = pack_pair(wcov[:n, :n], ncov)
    a_flat[i, n:] = diagonals((ncov, last), EARLY_ROWS - n)
    b_flat[i, :n] = wcov[:n, n:]
    b_flat[i, n:] = fold(last)
    a_kept, a_sent = both_halves(place, a_flat, i)
    b_kept, b_sent = both_halves(place, b_flat, i)
    return (a_kept, b_kept), (a_sent, b_sent)


def put(ref, index, parts):
    rows = EARLY_ROWS // 2
    ref[index, :rows] = parts[0]
    ref[index, rows:] = parts[1]


def put_layer(place, i, sums, a_flat, b_flat, keep, send):
    kept, sent = pack_layer(place, i, *sums, a_flat, b_flat)
    mine, other = positions(place, i, ORDERS)
    put(keep, mine, kept)
    put(send, other, sent)


def clear_others(place, layers, keep, send):
    for i in layers:
        mine, other = positions(place, i, ORDERS)
        keep[mine] = jnp.zeros(keep.shape[1:], jnp.float32)
        send[other] = jnp.zeros(send.shape[1:], jnp.float32)


def hot_kernel(place, wide_hbm, narrow_hbm, keep, send, wides, narrows, a_flat, b_flat, sems):
    copies = layer_copies(place, (wide_hbm, narrow_hbm), (wides, narrows), sems)
    order = HOT + COLD
    for i in order[:AHEAD]:
        for copy in copies[i]:
            copy.start()
    clear_others(place, COLD, keep, send)

    def pack(i, sums):
        put_layer(place, i, sums, a_flat, b_flat, keep, send)

    before = None
    for at, i in enumerate(order):
        for copy in copies[i]:
            copy.wait()
        if at + AHEAD < len(order):
            for copy in copies[order[at + AHEAD]]:
                copy.start()
        if before is not None:
            pack(*before)
            before = None
        if i in HOT:
            before = (i, square_sums(wides[i], narrows[i]))


def cold_kernel(place, wides, narrows, keep, send, a_flat, b_flat):
    for i in COLD:
        put_layer(
            place, i, square_sums(wides[i], narrows[i]), a_flat, b_flat, keep, send
        )
    core = lax.axis_index(place.core)
    stay = [[i for i in HOT if position(axes, i) < 4] for axes in ORDERS]
    for first, second in zip(*stay):
        here = [position(axes, i) for axes, i in zip(ORDERS, (first, second))]
        mine = jnp.where(core == 0, here[0], here[1])
        other = jnp.where(core == 0, here[1], here[0])
        keep[mine] = jnp.zeros(keep.shape[1:], jnp.float32)
        send[other] = jnp.zeros(send.shape[1:], jnp.float32)


def write_slots(place, owner_map, slots_ref):
    own = place.index(place.own)
    count = jnp.int32(0)
    for l in range(slots_ref.shape[0]):
        mine = owner_map[l] == own
        slot = jnp.where(mine, count, -1)
        slots_ref[l] = jnp.full(slots_ref.shape[1:], 0, jnp.int32) + slot
        count = count + mine.astype(jnp.int32)


def mixed_kernel(place, owner_map, wides, narrows, keep, send, slots_ref, flat):
    n = LANES
    write_slots(place, owner_map, slots_ref)
    for i in range(wides.shape[0]):
        mixed = transposed_dot(narrows[i], wides[i])
        flat[i, :n] = mixed[:, :n]
        flat[i, n:] = mixed[:, n:]
        kept, sent = both_halves(place, flat, i)
        mine, other = positions(place, i, ORDERS[::-1])
        keep[mine] = kept
        send[other] = sent


def gram_cost(wide_rows, columns):
    return pl.CostEstimate(
        flops=2 * wide_rows.size * columns, bytes_accessed=2 * wide_rows.size, transcendentals=0
    )


HALF_ROWS = (EARLY_ROWS + LATE_ROWS) // 2


def pack_shapes(layers):
    return [
        pltpu.VMEM((layers, EARLY_ROWS, LANES), jnp.float32),
        pltpu.VMEM((layers, LATE_ROWS, LANES), jnp.float32),
    ]


def hot_squares(place, wide_rows, narrow_rows):
    layers = wide_rows.shape[0]
    half = jax.ShapeDtypeStruct((layers, HALF_ROWS, LANES), jnp.float32)
    return pl.pallas_call(
        functools.partial(hot_kernel, place),
        in_specs=[HBM, HBM],
        out_specs=[VMEM] * 4,
        out_shape=[
            half,
            half,
            jax.ShapeDtypeStruct(wide_rows.shape, wide_rows.dtype),
            jax.ShapeDtypeStruct(narrow_rows.shape, narrow_rows.dtype),
        ],
        scratch_shapes=[*pack_shapes(layers), pltpu.SemaphoreType.DMA((layers, 2))],
        cost_estimate=gram_cost(wide_rows, 240),
        compiler_params=PARAMS,
        name="hot_squares",
    )(
        pltpu.with_memory_space_constraint(wide_rows, pltpu.HBM),
        pltpu.with_memory_space_constraint(narrow_rows, pltpu.HBM),
    )


def cold_squares(place, wides, narrows):
    half = jax.ShapeDtypeStruct((wides.shape[0] // 2, HALF_ROWS, LANES), jnp.float32)
    return pl.pallas_call(
        functools.partial(cold_kernel, place),
        in_specs=[VMEM, VMEM],
        out_specs=[VMEM, VMEM],
        out_shape=[half, half],
        scratch_shapes=pack_shapes(wides.shape[0]),
        cost_estimate=gram_cost(wides, 80),
        compiler_params=PARAMS,
        name="cold_squares",
    )(wides, narrows)


def mixed_sums(place, owner_map, wides, narrows):
    layers, _, narrow = narrows.shape
    half = jax.ShapeDtypeStruct((layers, narrow, LANES), jnp.float32)
    return pl.pallas_call(
        functools.partial(mixed_kernel, place),
        in_specs=[SMEM, VMEM, VMEM],
        out_specs=[VMEM] * 3,
        out_shape=[half, half, jax.ShapeDtypeStruct((layers, PANEL, LANES), jnp.int32)],
        scratch_shapes=[pltpu.VMEM((layers, 2 * narrow, LANES), jnp.float32)],
        cost_estimate=gram_cost(wides, 128),
        compiler_params=PARAMS,
        name="mixed",
    )(owner_map, wides, narrows)


def lane_gather(x, index):
    return jnp.take_along_axis(x, index, axis=1, mode="promise_in_bounds")


def trailing_update(a_ref, left_ref, right_ref, base):
    size = a_ref.shape[1]
    a_ref[pl.ds(pl.multiple_of(base, BLOCK), BLOCK), :] = jnp.zeros((BLOCK, size), jnp.float32)
    lane = lax.broadcasted_iota(jnp.int32, (1, size), 1)
    swept = (lane >= base - BLOCK) & (lane < base)
    update = transposed_dot(left_ref[...], right_ref[...])
    a_ref[BLOCK : BLOCK + size, :] = (
        jnp.where(swept, 0.0, a_ref[BLOCK : BLOCK + size, :]) - update
    )


def in_three(x):
    high = x.astype(jnp.bfloat16).astype(jnp.float32)
    rest = x - high
    middle = rest.astype(jnp.bfloat16).astype(jnp.float32)
    return high, middle, rest - middle


def factor_panel(rows_ref, cols_ref, tile, first, panel, targets):
    tiles = panel.shape[1] // LANES
    shape = (PANEL, LANES)
    _, lane = iotas(shape)

    def on_all(ref, k, lanes):
        return jnp.broadcast_to(ref[k : k + 1, lanes], shape)

    rows_ref[...] = panel
    lanes = [slice(LANES * t, LANES * (t + 1)) for t in range(tiles)]
    rows = [[on_all(rows_ref, k, part) for part in lanes] for k in range(PANEL)]
    here = panel[:, lanes[tile]]
    for j in range(PANEL):
        column = lane_gather(here, jnp.full(shape, 0, jnp.int32) + (first + j))
        cols_ref[PANEL * j : PANEL * (j + 1)] = column
    d = [[None] * PANEL for _ in range(PANEL)]
    for j in range(PANEL):
        for i in range(j, PANEL):
            d[i][j] = on_all(cols_ref, PANEL * j + i, slice(None))
    own = (lane >= first) & (lane < first + PANEL)
    q = [[None] * tiles for _ in range(PANEL)]
    p = [[None] * tiles for _ in range(PANEL)]
    weights = [[None] * PANEL for _ in targets]
    factor = [[None] * PANEL for _ in range(PANEL)]

    def substitute(k, scale):
        for t in range(tiles):
            value = rows[k][t]
            if t == tile:
                value = jnp.where(own, jnp.where(lane == first + k, -1.0, 0.0), value)
            for j in range(k):
                value = value - factor[k][j] * q[j][t]
            q[k][t] = value
            p[k][t] = value * scale
        for target, weight in zip(targets, weights):
            source, index = target(rows[k])
            value = lane_gather(source, index)
            for j in range(k):
                value = value - factor[k][j] * weight[j]
            weight[k] = value

    for k in range(0, PANEL, 2):
        m = k + 1
        a, b, c = d[k][k], d[m][k], d[m][m]
        first_scale = 1.0 / a
        second_scale = a * (1.0 / (a * c - b * b))
        factor[m][k] = b * first_scale
        left_over = {i: d[i][m] - d[i][k] * factor[m][k] for i in range(k + 2, PANEL)}
        for i in range(k + 2, PANEL):
            factor[i][k] = d[i][k] * first_scale
            factor[i][m] = left_over[i] * second_scale
        for i in range(k + 2, PANEL):
            for j in range(k + 2, i + 1):
                value = d[i][j] - d[i][k] * factor[j][k]
                d[i][j] = value - (left_over[i] * left_over[j]) * second_scale
        substitute(k, first_scale)
        substitute(m, second_scale)
    return q, p, weights


def packed_rows(values):
    sub, _ = iotas((PANEL, LANES))
    whole = []
    for t in range(len(values[0])):
        value = values[0][t]
        for k in range(1, PANEL):
            value = jnp.where(sub == k, values[k][t], value)
        whole.append(value)
    return whole


def side_by_side(tiles):
    return jnp.concatenate(tiles, axis=1) if len(tiles) > 1 else tiles[0]


def sweep_block(a_ref, left_ref, right_ref, a_rows, a_cols, b_rows, b_cols, tile, step, block):
    size = a_ref.shape[1]
    tiles = size // LANES
    first = step * BLOCK
    second = first + PANEL
    base = tile * LANES + first
    trailing_update(a_ref, left_ref, right_ref, base)

    sub, lane = iotas((PANEL, LANES))
    last = first == LANES - BLOCK
    next_first = jnp.where(last, 0, first + BLOCK)

    def in_block(row):
        return row[tile], second + sub

    def in_next(offset):
        def target(row):
            source = row[tile]
            if tile + 1 < tiles:
                source = jnp.where(last, row[tile + 1], source)
            return source, next_first + offset + sub

        return target

    nexts = [in_next(0), in_next(PANEL)]
    in_a = (lane >= first) & (lane < second)
    in_b = (lane >= second) & (lane < second + PANEL)

    def swept(tiles_of, mask):
        return [jnp.where(mask, 0.0, v) if t == tile else v for t, v in enumerate(tiles_of)]

    def minus(tiles_of, weight, p):
        result = []
        for t, value in enumerate(tiles_of):
            for k in range(PANEL):
                value = value - weight[k] * p[k][t]
            result.append(value)
        return result

    def by_tile(rows):
        return [rows[:, LANES * t : LANES * (t + 1)] for t in range(tiles)]

    qa, pa, (to_b, *to_next_a) = factor_panel(
        a_rows, a_cols, tile, first, block[:PANEL], [in_block, *nexts]
    )
    panel_b = side_by_side(minus(swept(by_tile(block[PANEL:]), in_a), to_b, pa))
    qb, pb, to_next_b = factor_panel(b_rows, b_cols, tile, second, panel_b, nexts)

    left, right = [], []
    for q, p, mask in ((qa, pa, in_b), (qb, pb, None)):
        q, p = packed_rows(q), packed_rows(p)
        if mask is not None:
            q, p = swept(q, mask), swept(p, mask)
        qs, ps = in_three(side_by_side(q)), in_three(side_by_side(p))
        left += [qs[i] for i in (0, 0, 1, 1, 0, 2)]
        right += [ps[i] for i in (0, 1, 0, 1, 2, 0)]
    left_ref[...] = jnp.concatenate(left, axis=0).astype(jnp.bfloat16)
    right_ref[...] = jnp.concatenate(right, axis=0).astype(jnp.bfloat16)

    following = a_ref[pl.ds(pl.multiple_of(base + 2 * BLOCK, BLOCK), BLOCK), :]
    result = []
    for g in range(2):
        rows = by_tile(following[g * PANEL : (g + 1) * PANEL])
        rows = minus(swept(rows, in_a), to_next_a[g], pa)
        rows = minus(swept(rows, in_b), to_next_b[g], pb)
        result.append(side_by_side(rows))
    return jnp.concatenate(result, axis=0)


def place_halves(place, pieces, first_row, flat):
    core = lax.axis_index(place.core)
    rows = flat.shape[0] // 2
    for r, piece in enumerate(pieces):
        start = pl.multiple_of(jnp.bitwise_xor(core, r) * rows, PANEL)
        flat[pl.ds(start, rows), :] = piece[first_row : first_row + rows]


def sweep_cost():
    return pl.CostEstimate(flops=1 << 30, bytes_accessed=1 << 20, transcendentals=0)


def clear(work):
    a_ref, left, right = work[:3]
    size = a_ref.shape[1]
    a_ref[:BLOCK] = jnp.zeros((BLOCK, size), jnp.float32)
    a_ref[BLOCK + size :] = jnp.zeros((BLOCK, size), jnp.float32)
    left[...] = jnp.zeros(left.shape, left.dtype)
    right[...] = jnp.zeros(right.shape, right.dtype)


def work_shapes(size):
    splits = 6 * BLOCK
    return [
        pltpu.VMEM((size + 2 * BLOCK, size), jnp.float32),
        pltpu.VMEM((splits, size), jnp.bfloat16),
        pltpu.VMEM((splits, size), jnp.bfloat16),
    ]


def row_shapes(size):
    return [
        pltpu.VMEM((PANEL, size), jnp.float32),
        pltpu.VMEM((PANEL * PANEL, LANES), jnp.float32),
    ] * 2


def aligned_rows(ref, index, count):
    if count % PANEL == 0:
        return ref[pl.ds(pl.multiple_of(index * count, count), count), :]
    per_slab = PANEL // count
    slab = ref[pl.ds(pl.multiple_of(index // per_slab * PANEL, PANEL), PANEL), :]
    value = slab[:count]
    for i in range(1, per_slab):
        value = jnp.where(index % per_slab == i, slab[i * count : (i + 1) * count], value)
    return value


def packs(cols, rows):
    return cols == 2 * PANEL and 2 * rows == LANES


def dot(a, b, last=False):
    return lax.dot_general(
        a,
        b,
        (((1,), (1 if last else 0,)), ((), ())),
        precision=HIGHEST,
        preferred_element_type=jnp.float32,
    )


STEPS = LANES // BLOCK
FIRST_STEPS = 5
SECOND_STEPS = 6


def sweep_both(wide_work, narrow_work, begin, end, blocks):
    def step(i, blocks):
        return (
            sweep_block(*wide_work, 0, i, blocks[0]),
            sweep_block(*narrow_work, 0, i, blocks[1]),
        )

    return lax.fori_loop(begin, end, step, blocks)


def sweep_wide(work, begin, end, block):
    return lax.fori_loop(begin, end, lambda i, block: sweep_block(*work, 1, i, block), block)


def unit_scale(block):
    row, col = iotas(block.shape)
    line = jnp.sum(jnp.where(row == col, block, 0.0), axis=0, keepdims=True)
    return jnp.broadcast_to(lax.rsqrt(line), (PANEL, block.shape[1]))


def on_rows(scale):
    n = scale.shape[1]
    return jnp.broadcast_to(scale[:1], (n, n))


def scaled(block, down, across):
    return (block * on_rows(down).T) * on_rows(across)


def first_kernel(
    place, total, mine, other, wa, wl, wr, wp, na, nl, nr, np_, ws_ref, ns_ref, *refs
):
    a_flat, b_flat = refs[:2]
    wide_work, narrow_work = (wa, wl, wr, *refs[2:6]), (na, nl, nr, *refs[6:])
    place_halves(place, (mine, other), 0, a_flat)
    place_halves(place, (mine, other), a_flat.shape[0] // 2, b_flat)
    n = LANES
    slab = a_flat[n : n + PANEL]
    first, square = unpack_pair(a_flat[:n], jnp.broadcast_to(slab[:1], (n, n)))
    corner = b_flat[:n] / total
    last = unfold(b_flat[n:], jnp.broadcast_to(slab[1:2], (n, n)))
    row, col = iotas((n, n))
    damp = jnp.where(row == col, DAMP, 0.0)
    clear(wide_work)
    clear(narrow_work)
    first, last, square = first / total + damp, last / total + damp, square / total + damp
    by_first, by_last, by_square = (unit_scale(block) for block in (first, last, square))
    ws_ref[:, :n] = by_first
    ws_ref[:, n:] = by_last
    ns_ref[...] = by_square
    first_across, last_across = on_rows(by_first), on_rows(by_last)
    first_down, last_down = first_across.T, last_across.T
    corner = (corner * first_down) * last_across
    wa[BLOCK : BLOCK + n, :n] = (first * first_down) * first_across
    wa[BLOCK : BLOCK + n, n:] = corner
    wa[BLOCK + n : BLOCK + 2 * n, :n] = corner.T
    wa[BLOCK + n : BLOCK + 2 * n, n:] = (last * last_down) * last_across
    na[BLOCK : BLOCK + n, :] = scaled(square, by_square, by_square)
    start = (wa[BLOCK : 2 * BLOCK, :], na[BLOCK : 2 * BLOCK, :])
    wp[...], np_[...] = sweep_both(wide_work, narrow_work, 0, FIRST_STEPS, start)


def second_kernel(*refs):
    given, scale, ninv_ref, state, narrow_state, wide_rows, narrow_rows = (
        refs[:8],
        refs[8],
        refs[9],
        refs[10:14],
        refs[14:17],
        refs[17:21],
        refs[21:],
    )
    for source, target in zip((*given[:3], *given[4:7]), (*state[:3], *narrow_state)):
        target[...] = source[...]
    wide_work, narrow_work = (*state[:3], *wide_rows), (*narrow_state, *narrow_rows)
    wp = state[3]
    panels = (given[3][...], given[7][...])
    panel, _ = sweep_both(wide_work, narrow_work, FIRST_STEPS, STEPS, panels)
    trailing_update(*narrow_work[:3], LANES)
    by_square = scale[...]
    ninv_ref[...] = scaled(-narrow_work[0][BLOCK : BLOCK + LANES, :], by_square, by_square)
    wp[...] = sweep_wide(wide_work, 0, SECOND_STEPS, panel)


def third_kernel(wa_in, wl_in, wr_in, panel_in, scale, winv, wa, wl, wr, *rows):
    wa[...] = wa_in[...]
    wl[...] = wl_in[...]
    wr[...] = wr_in[...]
    sweep_wide((wa, wl, wr, *rows), SECOND_STEPS, STEPS, panel_in[...])
    wide = wa.shape[1]
    trailing_update(wa, wl, wr, wide)
    parts = [slice(i, i + LANES) for i in range(0, wide, LANES)]
    across = [on_rows(scale[:, i]) for i in parts]
    down = [block.T for block in across]
    for i, rows_scale in zip(parts, down):
        for j, columns_scale in zip(parts, across):
            block = -wa[BLOCK + i.start : BLOCK + i.stop, j]
            winv[i, j] = (block * rows_scale) * columns_scale


def state_shapes(size):
    shapes = [jax.ShapeDtypeStruct(v.shape, v.dtype) for v in work_shapes(size)]
    return shapes + [jax.ShapeDtypeStruct((BLOCK, size), jnp.float32)]


def sweep_call(kernel, name, args, out_shapes, scratch):
    return pl.pallas_call(
        kernel,
        in_specs=[VMEM] * len(args),
        out_specs=[VMEM] * len(out_shapes),
        out_shape=out_shapes,
        scratch_shapes=scratch,
        cost_estimate=sweep_cost(),
        compiler_params=PARAMS,
        name=name,
    )(*args)


def first_panels(place, pieces, wide, narrow, total):
    return sweep_call(
        functools.partial(first_kernel, place, total),
        "first_panels",
        pieces,
        state_shapes(wide)
        + state_shapes(narrow)
        + [jax.ShapeDtypeStruct((PANEL, n), jnp.float32) for n in (wide, narrow)],
        [
            pltpu.VMEM((EARLY_ROWS, LANES), jnp.float32),
            pltpu.VMEM((LATE_ROWS, LANES), jnp.float32),
            *row_shapes(wide),
            *row_shapes(narrow),
        ],
    )


def second_panels(state, wide, narrow):
    ninv = jax.ShapeDtypeStruct((narrow, narrow), jnp.float32)
    return sweep_call(
        second_kernel,
        "second_panels",
        state,
        [ninv] + state_shapes(wide),
        [*work_shapes(narrow), *row_shapes(wide), *row_shapes(narrow)],
    )


def third_panels(state, wide):
    winv = jax.ShapeDtypeStruct((wide, wide), jnp.float32)
    scratch = [*work_shapes(wide), *row_shapes(wide)]
    return sweep_call(third_kernel, "third_panels", state, [winv], scratch)[0]


def product_kernel(place, total, rows, winv, ninv_ref, mine, other, out_ref, flat):
    place_halves(place, (mine, other), 0, flat)
    ninv = ninv_ref[...]
    n = LANES
    inner = jnp.concatenate(
        [
            transposed_dot(flat[c * n : (c + 1) * n] / total, ninv, HIGHEST)
            for c in range(2)
        ],
        axis=0,
    )
    wide = winv.shape[1]
    cols = wide // 2 ** len(place.dp)
    near, second = lax.axis_index(place.near), lax.axis_index(place.second)
    near_stride = 2 ** (len(place.dp) - 2)
    base = place.index(place.dp) - near * near_stride - second * 2
    halves = (near * near_stride, (1 - near) * near_stride)
    _, lane = iotas((PANEL, LANES))
    picks = [
        aligned_rows(winv, base + halves[j // 2] + (j % 2) * 2, cols) for j in range(4)
    ]
    if cols % PANEL == 0:
        whole = dot(jnp.concatenate(picks, axis=0), inner)
        updates = [whole[j * cols : (j + 1) * cols] for j in range(4)]
    else:
        updates = [dot(picked, inner) for picked in picks]
    for j, (picked, update) in enumerate(zip(picks, updates)):
        for x in range(2):
            block = (j // 2, 2 * (j % 2) + x)
            out_ref[*block, :cols] = picked[:, :LANES]
            out_ref[*block, cols : 2 * cols] = picked[:, LANES:]
            if packs(cols, rows):
                upper, lower = update[:PANEL], update[PANEL:]
                if x == 0:
                    lower = pltpu.roll(lower, rows, 1)
                else:
                    upper = pltpu.roll(upper, rows, 1)
                out_ref[*block, 2 * cols :] = jnp.where(lane < rows, upper, lower)
            else:
                out_ref[*block, 2 * cols :] = update


def products(place, winv, ninv, pieces, rows, total):
    wide, narrow = winv.shape[0], ninv.shape[0]
    cols = wide // 2 ** len(place.dp)
    height = 2 * cols + (PANEL if packs(cols, rows) else cols)
    return pl.pallas_call(
        functools.partial(product_kernel, place, total, rows),
        in_specs=[VMEM] * 4,
        out_specs=VMEM,
        out_shape=jax.ShapeDtypeStruct((2, 4, height, LANES), jnp.float32),
        scratch_shapes=[pltpu.VMEM((2 * narrow, LANES), jnp.float32)],
        compiler_params=PARAMS,
        name="products",
    )(winv, ninv, *pieces)


def placing_kernel(place, slots_ref, got_ref, kept_ref, update_ref):
    near = lax.axis_index(place.near)
    layers = slots_ref.shape[0]
    got = [(i // 2, i % 2) for i in range(layers)]
    layer = [jnp.bitwise_xor(near, r) * 4 + at for at, r in got]
    slots, cols, wide = kept_ref.shape
    rows = update_ref.shape[2]
    own, dp = place.index(place.own), place.index(place.dp)
    step = min(cols, PANEL)
    row, col = iotas((step, LANES))
    for h in range(wide // LANES):
        lanes = slice(h * LANES, (h + 1) * LANES)
        for r in range(0, cols, step):
            here = h * cols + r
            empty = jnp.where(col + h * LANES == row + dp * cols + r, 1.0 / DAMP, 0.0)
            for c in range(slots):
                value = empty
                for l in range(layers):
                    taken = slots_ref[layer[l], :step] == c
                    value = jnp.where(taken, got_ref[*got[l], here : here + step], value)
                kept_ref[c, r : r + step, lanes] = value
    for l in range(layers):
        value = got_ref[*got[l], 2 * cols :]
        if packs(cols, rows):
            update_ref[layer[l], :PANEL] = value[:, :rows]
            update_ref[layer[l], PANEL:] = value[:, rows:]
        else:
            part = value[:, :rows]
            for p in range(1, LANES // rows):
                part = jnp.where(own == p, value[:, p * rows : (p + 1) * rows], part)
            update_ref[layer[l]] = part


def placing(place, slots_of, got, wide, cols, slots, rows):
    layers = slots_of.shape[0]
    return pl.pallas_call(
        functools.partial(placing_kernel, place),
        in_specs=[VMEM, VMEM],
        out_specs=[VMEM, VMEM],
        out_shape=[
            jax.ShapeDtypeStruct((slots, cols, wide), jnp.float32),
            jax.ShapeDtypeStruct((layers, cols, rows), jnp.float32),
        ],
        compiler_params=PARAMS,
        name="placing",
    )(slots_of, got)


def swap(value, axis):
    return lax.ppermute(value, axis, [(0, 1), (1, 0)])


def swap_by_core(value, place, stage, orders):
    names = (place.near, place.second, place.core, place.first)
    flips = {"near": 8, "second": 4, "first": 1}
    pairs = [(i, i ^ flips[orders[(i >> 1) & 1][stage]]) for i in range(16)]
    return lax.ppermute(value, names, pairs)


def after(value, *others):
    return lax.optimization_barrier((value,) + others)[0]


def on_device(place, wide_rows, narrow_rows, owner_map):
    layers, rows, wide = wide_rows.shape
    narrow = narrow_rows.shape[2]
    n_dp, n_own = 2 ** len(place.dp), 2 ** len(place.own)
    total = float(rows * n_dp * n_own)

    h_keep, h_send, wides, narrows = hot_squares(place, wide_rows, narrow_rows)
    first_send = h_send[4:]
    h_got = swap(first_send, place.core)
    c_keep, c_send = cold_squares(place, after(wides, first_send), narrows)
    h_keep, c_send = lax.optimization_barrier((h_keep, c_send))
    others = ORDERS[::-1]

    hot = h_keep[4:] + h_got
    s_got = swap_by_core(hot, place, 0, ORDERS)
    m_keep, m_send, slots_of = mixed_sums(place, owner_map, after(wides, hot), narrows)
    c_got = swap(after(c_send + h_send[:4], m_send), place.core)
    m_got = swap(m_send, place.core)

    s = (c_keep + h_keep[:4]) + s_got
    s = s + after(c_got, s)
    s_got = swap_by_core(s[2:], place, 1, ORDERS)
    m = after(m_keep, s) + m_got
    m_got = swap_by_core(m[4:], place, 0, others)

    s = s[:2] + s_got
    s_got = swap_by_core(s[1], place, 2, ORDERS)
    m = after(m[:4], s) + m_got
    m_got = swap_by_core(m[2:], place, 1, others)

    s = s[0] + s_got
    if place.extra:
        s = lax.psum(s, place.extra)
    s_got = swap(s, place.far)
    m = after(m[:2], s) + m_got
    m_got = swap_by_core(m[1], place, 2, others)

    s = s + s_got
    state = first_panels(place, [s, swap(s, place.core)], wide, narrow, total)
    m = after(m[0], state[0]) + m_got
    if place.extra:
        m = lax.psum(m, place.extra)
    m_got = swap(m, place.far)
    *state, wide_scale, narrow_scale = state
    ninv, *state = second_panels([*state, narrow_scale], wide, narrow)
    m = after(m, ninv) + m_got
    m_got = swap(m, place.core)
    winv = third_panels([*state, wide_scale], wide)
    cols, own_rows = wide // n_dp, narrow // n_own
    sent = products(place, winv, ninv, [m, m_got], own_rows, total)
    sent = jnp.stack([sent[0], swap(sent[1], place.near)], axis=1)
    got = lax.all_to_all(sent, (place.second, place.first), 0, 0)
    kept, update = placing(
        place, slots_of, got, wide, cols, layers // n_own + 1, own_rows
    )
    return (jnp.swapaxes(kept, 1, 2), jnp.swapaxes(update, 1, 2))


def solution(mesh):
    n_dp, n_own = mesh.shape["dp"], mesh.shape["own"]
    dp_names = tuple(f"dp{i}" for i in range(int(np.log2(n_dp))))
    own_names = tuple(f"own{i}" for i in range(int(np.log2(n_own))))
    names = dp_names + own_names
    bits = jax.sharding.Mesh(mesh.devices.reshape((2,) * len(names)), names)
    in_specs = (P(None, names, None), P(None, names, None), P())
    out_specs = (P(own_names, None, dp_names), P(None, own_names, dp_names))
    return jax.shard_map(
        functools.partial(on_device, Place(dp_names, own_names)),
        mesh=bits,
        in_specs=in_specs,
        out_specs=out_specs,
        check_vma=False,
    )
```

```python
import functools

import jax
import jax.numpy as jnp
import numpy as np
from jax import lax
from jax.experimental import pallas as pl
from jax.experimental.pallas import tpu as pltpu
from jax.sharding import PartitionSpec as P

DAMP = 0.5
LANES = 128
PANEL = 8
BLOCK = 2 * PANEL
VMEM_LIMIT = 48 * 1024 * 1024
HIGHEST = lax.Precision.HIGHEST
VMEM = pl.BlockSpec(memory_space=pltpu.VMEM)
SMEM = pl.BlockSpec(memory_space=pltpu.SMEM)
HBM = pl.BlockSpec(memory_space=pltpu.HBM)
PARAMS = pltpu.CompilerParams(vmem_limit_bytes=VMEM_LIMIT)


class Place:
    def __init__(self, dp_names, own_names):
        self.dp, self.own = dp_names, own_names
        self.core, self.second, self.near, self.far = (
            dp_names[-1],
            dp_names[-2],
            dp_names[1],
            dp_names[0],
        )
        self.first = own_names[-1]
        used = (self.core, self.second, self.near, self.far, self.first)
        self.extra = tuple(n for n in dp_names + own_names if n not in used)

    def index(self, names):
        value = jnp.int32(0)
        for name in names:
            value = value * 2 + lax.axis_index(name)
        return value

    def layer(self):
        return self.index((self.near, self.second, self.first))


def transposed_dot(a, b, precision=None):
    return lax.dot_general(
        a, b, (((0,), (0,)), ((), ())), precision=precision, preferred_element_type=jnp.float32
    )


AHEAD = 5


def layer_copies(place, sources, buffers, sems):
    layer = place.layer()
    return [
        [
            pltpu.make_async_copy(
                source.at[jnp.bitwise_xor(layer, i)], buffer.at[i], sems.at[i, s]
            )
            for s, (source, buffer) in enumerate(zip(sources, buffers))
        ]
        for i in range(buffers[0].shape[0])
    ]


def both_halves(place, flat, i):
    rows = flat.shape[1] // 2
    core = lax.axis_index(place.core)
    kept = pl.multiple_of(core * rows, PANEL)
    sent = pl.multiple_of((1 - core) * rows, PANEL)
    return flat[i, pl.ds(kept, rows), :], flat[i, pl.ds(sent, rows), :]


ORDERS = (("first", "second", "near"), ("second", "near", "first"))
LATE_ORDERS = (("first", "second", "near"), ("near", "first", "second"))


def position(axes, i):
    bits = {"near": i // 4, "second": (i // 2) % 2, "first": i % 2}
    return bits[axes[0]] * 4 + bits[axes[1]] * 2 + bits[axes[2]]


def positions(place, i, orders):
    core = lax.axis_index(place.core)
    first, second = (position(axes, i) for axes in orders)
    return jnp.where(core == 0, first, second), jnp.where(core == 0, second, first)


def iotas(shape):
    return (
        lax.broadcasted_iota(jnp.int32, shape, 0),
        lax.broadcasted_iota(jnp.int32, shape, 1),
    )


def pack_pair(first, second):
    row, col = iotas(first.shape)
    return jnp.where(row >= col, first, second)


def unpack_pair(packed, second_diagonal):
    row, col = iotas(packed.shape)
    turned = packed.T
    first = jnp.where(row >= col, packed, turned)
    second = jnp.where(col > row, packed, turned)
    return first, jnp.where(row == col, second_diagonal, second)


def fold(block):
    h = block.shape[0] // 2
    row, col = iotas((h, 2 * h))
    last = pltpu.roll(block[h:], h, 1)
    return jnp.where((col >= h) | (row >= col), block[:h], last)


def unfold(folded, diagonal):
    h, n = folded.shape
    row, col = iotas((n, n))
    block = jnp.concatenate([folded, jnp.zeros((h, n), jnp.float32)], axis=0)
    turned = block.T
    top = jnp.where((col >= h) | (col <= row), block, turned)
    moved = pltpu.roll(pltpu.roll(block, h, 0), h, 1)
    moved_turned = pltpu.roll(pltpu.roll(turned, h, 0), h, 1)
    last = jnp.where(col > row, moved, moved_turned)
    last = jnp.where(row == col, diagonal, last)
    return jnp.where(row < h, top, jnp.where(col < h, turned, last))


def diagonals(blocks, rows):
    n = blocks[0].shape[0]
    row, col = iotas((n, n))
    slab_row, _ = iotas((rows, n))
    slab = jnp.zeros((rows, n), jnp.float32)
    for i, block in enumerate(blocks):
        line = jnp.sum(jnp.where(row == col, block, 0.0), axis=0, keepdims=True)
        slab = jnp.where(slab_row == i, jnp.broadcast_to(line, (rows, n)), slab)
    return slab


EARLY_ROWS = 144
LATE_ROWS = 192


HOT = (1, 2, 3, 5, 6, 7)
COLD = (0, 4)


def square_sums(wide, narrow):
    return transposed_dot(wide, wide), transposed_dot(narrow, narrow)


def pack_layer(place, i, wcov, ncov, a_flat, b_flat):
    n = LANES
    last = wcov[n:, n:]
    a_flat[i, :n] = pack_pair(wcov[:n, :n], ncov)
    a_flat[i, n:] = diagonals((ncov, last), EARLY_ROWS - n)
    b_flat[i, :n] = wcov[:n, n:]
    b_flat[i, n:] = fold(last)
    a_kept, a_sent = both_halves(place, a_flat, i)
    b_kept, b_sent = both_halves(place, b_flat, i)
    return (a_kept, b_kept), (a_sent, b_sent)


def put(ref, index, parts):
    rows = EARLY_ROWS // 2
    ref[index, :rows] = parts[0]
    ref[index, rows:] = parts[1]


def put_layer(place, i, sums, a_flat, b_flat, keep, send):
    kept, sent = pack_layer(place, i, *sums, a_flat, b_flat)
    mine, other = positions(place, i, ORDERS)
    put(keep, mine, kept)
    put(send, other, sent)


def clear_others(place, layers, keep, send):
    for i in layers:
        mine, other = positions(place, i, ORDERS)
        keep[mine] = jnp.zeros(keep.shape[1:], jnp.float32)
        send[other] = jnp.zeros(send.shape[1:], jnp.float32)


def hot_kernel(place, wide_hbm, narrow_hbm, keep, send, wides, narrows, a_flat, b_flat, sems):
    copies = layer_copies(place, (wide_hbm, narrow_hbm), (wides, narrows), sems)
    order = HOT + COLD
    for i in order[:AHEAD]:
        for copy in copies[i]:
            copy.start()
    clear_others(place, COLD, keep, send)

    def pack(i, sums):
        put_layer(place, i, sums, a_flat, b_flat, keep, send)

    before = None
    for at, i in enumerate(order):
        for copy in copies[i]:
            copy.wait()
        if at + AHEAD < len(order):
            for copy in copies[order[at + AHEAD]]:
                copy.start()
        if before is not None:
            pack(*before)
            before = None
        if i in HOT:
            before = (i, square_sums(wides[i], narrows[i]))


def cold_kernel(place, wides, narrows, keep, send, a_flat, b_flat):
    for i in COLD:
        put_layer(
            place, i, square_sums(wides[i], narrows[i]), a_flat, b_flat, keep, send
        )
    core = lax.axis_index(place.core)
    stay = [[i for i in HOT if position(axes, i) < 4] for axes in ORDERS]
    for first, second in zip(*stay):
        here = [position(axes, i) for axes, i in zip(ORDERS, (first, second))]
        mine = jnp.where(core == 0, here[0], here[1])
        other = jnp.where(core == 0, here[1], here[0])
        keep[mine] = jnp.zeros(keep.shape[1:], jnp.float32)
        send[other] = jnp.zeros(send.shape[1:], jnp.float32)


def write_slots(place, owner_map, slots_ref):
    own = place.index(place.own)
    count = jnp.int32(0)
    for l in range(slots_ref.shape[0]):
        mine = owner_map[l] == own
        slot = jnp.where(mine, count, -1)
        slots_ref[l] = jnp.full(slots_ref.shape[1:], 0, jnp.int32) + slot
        count = count + mine.astype(jnp.int32)


def mixed_kernel(place, owner_map, wides, narrows, keep, send, slots_ref, flat):
    n = LANES
    write_slots(place, owner_map, slots_ref)
    for i in range(wides.shape[0]):
        mixed = transposed_dot(narrows[i], wides[i])
        flat[i, :n] = mixed[:, :n]
        flat[i, n:] = mixed[:, n:]
        kept, sent = both_halves(place, flat, i)
        mine, other = positions(place, i, LATE_ORDERS)
        keep[mine] = kept
        send[other] = sent


def gram_cost(wide_rows, columns):
    return pl.CostEstimate(
        flops=2 * wide_rows.size * columns, bytes_accessed=2 * wide_rows.size, transcendentals=0
    )


HALF_ROWS = (EARLY_ROWS + LATE_ROWS) // 2


def pack_shapes(layers):
    return [
        pltpu.VMEM((layers, EARLY_ROWS, LANES), jnp.float32),
        pltpu.VMEM((layers, LATE_ROWS, LANES), jnp.float32),
    ]


def hot_squares(place, wide_rows, narrow_rows):
    layers = wide_rows.shape[0]
    half = jax.ShapeDtypeStruct((layers, HALF_ROWS, LANES), jnp.float32)
    return pl.pallas_call(
        functools.partial(hot_kernel, place),
        in_specs=[HBM, HBM],
        out_specs=[VMEM] * 4,
        out_shape=[
            half,
            half,
            jax.ShapeDtypeStruct(wide_rows.shape, wide_rows.dtype),
            jax.ShapeDtypeStruct(narrow_rows.shape, narrow_rows.dtype),
        ],
        scratch_shapes=[*pack_shapes(layers), pltpu.SemaphoreType.DMA((layers, 2))],
        cost_estimate=gram_cost(wide_rows, 240),
        compiler_params=PARAMS,
        name="hot_squares",
    )(
        pltpu.with_memory_space_constraint(wide_rows, pltpu.HBM),
        pltpu.with_memory_space_constraint(narrow_rows, pltpu.HBM),
    )


def cold_squares(place, wides, narrows):
    half = jax.ShapeDtypeStruct((wides.shape[0] // 2, HALF_ROWS, LANES), jnp.float32)
    return pl.pallas_call(
        functools.partial(cold_kernel, place),
        in_specs=[VMEM, VMEM],
        out_specs=[VMEM, VMEM],
        out_shape=[half, half],
        scratch_shapes=pack_shapes(wides.shape[0]),
        cost_estimate=gram_cost(wides, 80),
        compiler_params=PARAMS,
        name="cold_squares",
    )(wides, narrows)


def mixed_sums(place, owner_map, wides, narrows):
    layers, _, narrow = narrows.shape
    half = jax.ShapeDtypeStruct((layers, narrow, LANES), jnp.float32)
    return pl.pallas_call(
        functools.partial(mixed_kernel, place),
        in_specs=[SMEM, VMEM, VMEM],
        out_specs=[VMEM] * 3,
        out_shape=[half, half, jax.ShapeDtypeStruct((layers, PANEL, LANES), jnp.int32)],
        scratch_shapes=[pltpu.VMEM((layers, 2 * narrow, LANES), jnp.float32)],
        cost_estimate=gram_cost(wides, 128),
        compiler_params=PARAMS,
        name="mixed",
    )(owner_map, wides, narrows)


def lane_gather(x, index):
    return jnp.take_along_axis(x, index, axis=1, mode="promise_in_bounds")


def trailing_update(a_ref, left_ref, right_ref, base):
    size = a_ref.shape[1]
    a_ref[pl.ds(pl.multiple_of(base, BLOCK), BLOCK), :] = jnp.zeros((BLOCK, size), jnp.float32)
    lane = lax.broadcasted_iota(jnp.int32, (1, size), 1)
    swept = (lane >= base - BLOCK) & (lane < base)
    update = transposed_dot(left_ref[...], right_ref[...])
    a_ref[BLOCK : BLOCK + size, :] = (
        jnp.where(swept, 0.0, a_ref[BLOCK : BLOCK + size, :]) - update
    )


def in_three(x):
    high = x.astype(jnp.bfloat16).astype(jnp.float32)
    rest = x - high
    middle = rest.astype(jnp.bfloat16).astype(jnp.float32)
    return high, middle, rest - middle


def factor_panel(rows_ref, cols_ref, tile, first, panel, targets):
    tiles = panel.shape[1] // LANES
    shape = (PANEL, LANES)
    _, lane = iotas(shape)

    def on_all(ref, k, lanes):
        return jnp.broadcast_to(ref[k : k + 1, lanes], shape)

    rows_ref[...] = panel
    lanes = [slice(LANES * t, LANES * (t + 1)) for t in range(tiles)]
    rows = [[on_all(rows_ref, k, part) for part in lanes] for k in range(PANEL)]
    here = panel[:, lanes[tile]]
    for j in range(PANEL):
        column = lane_gather(here, jnp.full(shape, 0, jnp.int32) + (first + j))
        cols_ref[PANEL * j : PANEL * (j + 1)] = column
    d = [[None] * PANEL for _ in range(PANEL)]
    for j in range(PANEL):
        for i in range(j, PANEL):
            d[i][j] = on_all(cols_ref, PANEL * j + i, slice(None))
    own = (lane >= first) & (lane < first + PANEL)
    q = [[None] * tiles for _ in range(PANEL)]
    p = [[None] * tiles for _ in range(PANEL)]
    weights = [[None] * PANEL for _ in targets]
    factor = [[None] * PANEL for _ in range(PANEL)]

    def substitute(k, scale):
        for t in range(tiles):
            value = rows[k][t]
            if t == tile:
                value = jnp.where(own, jnp.where(lane == first + k, -1.0, 0.0), value)
            for j in range(k):
                value = value - factor[k][j] * q[j][t]
            q[k][t] = value
            p[k][t] = value * scale
        for target, weight in zip(targets, weights):
            source, index = target(rows[k])
            value = lane_gather(source, index)
            for j in range(k):
                value = value - factor[k][j] * weight[j]
            weight[k] = value

    for k in range(0, PANEL, 2):
        m = k + 1
        a, b, c = d[k][k], d[m][k], d[m][m]
        first_scale = 1.0 / a
        second_scale = a * (1.0 / (a * c - b * b))
        factor[m][k] = b * first_scale
        left_over = {i: d[i][m] - d[i][k] * factor[m][k] for i in range(k + 2, PANEL)}
        for i in range(k + 2, PANEL):
            factor[i][k] = d[i][k] * first_scale
            factor[i][m] = left_over[i] * second_scale
        for i in range(k + 2, PANEL):
            for j in range(k + 2, i + 1):
                value = d[i][j] - d[i][k] * factor[j][k]
                d[i][j] = value - (left_over[i] * left_over[j]) * second_scale
        substitute(k, first_scale)
        substitute(m, second_scale)
    return q, p, weights


def packed_rows(values):
    sub, _ = iotas((PANEL, LANES))
    whole = []
    for t in range(len(values[0])):
        value = values[0][t]
        for k in range(1, PANEL):
            value = jnp.where(sub == k, values[k][t], value)
        whole.append(value)
    return whole


def side_by_side(tiles):
    return jnp.concatenate(tiles, axis=1) if len(tiles) > 1 else tiles[0]


def sweep_block(a_ref, left_ref, right_ref, a_rows, a_cols, b_rows, b_cols, tile, step, block):
    size = a_ref.shape[1]
    tiles = size // LANES
    first = step * BLOCK
    second = first + PANEL
    base = tile * LANES + first
    trailing_update(a_ref, left_ref, right_ref, base)

    sub, lane = iotas((PANEL, LANES))
    last = first == LANES - BLOCK
    next_first = jnp.where(last, 0, first + BLOCK)

    def in_block(row):
        return row[tile], second + sub

    def in_next(offset):
        def target(row):
            source = row[tile]
            if tile + 1 < tiles:
                source = jnp.where(last, row[tile + 1], source)
            return source, next_first + offset + sub

        return target

    nexts = [in_next(0), in_next(PANEL)]
    in_a = (lane >= first) & (lane < second)
    in_b = (lane >= second) & (lane < second + PANEL)

    def swept(tiles_of, mask):
        return [jnp.where(mask, 0.0, v) if t == tile else v for t, v in enumerate(tiles_of)]

    def minus(tiles_of, weight, p):
        result = []
        for t, value in enumerate(tiles_of):
            for k in range(PANEL):
                value = value - weight[k] * p[k][t]
            result.append(value)
        return result

    def by_tile(rows):
        return [rows[:, LANES * t : LANES * (t + 1)] for t in range(tiles)]

    qa, pa, (to_b, *to_next_a) = factor_panel(
        a_rows, a_cols, tile, first, block[:PANEL], [in_block, *nexts]
    )
    panel_b = side_by_side(minus(swept(by_tile(block[PANEL:]), in_a), to_b, pa))
    qb, pb, to_next_b = factor_panel(b_rows, b_cols, tile, second, panel_b, nexts)

    left, right = [], []
    for q, p, mask in ((qa, pa, in_b), (qb, pb, None)):
        q, p = packed_rows(q), packed_rows(p)
        if mask is not None:
            q, p = swept(q, mask), swept(p, mask)
        qs, ps = in_three(side_by_side(q)), in_three(side_by_side(p))
        left += [qs[i] for i in (0, 0, 1, 1, 0, 2)]
        right += [ps[i] for i in (0, 1, 0, 1, 2, 0)]
    left_ref[...] = jnp.concatenate(left, axis=0).astype(jnp.bfloat16)
    right_ref[...] = jnp.concatenate(right, axis=0).astype(jnp.bfloat16)

    following = a_ref[pl.ds(pl.multiple_of(base + 2 * BLOCK, BLOCK), BLOCK), :]
    result = []
    for g in range(2):
        rows = by_tile(following[g * PANEL : (g + 1) * PANEL])
        rows = minus(swept(rows, in_a), to_next_a[g], pa)
        rows = minus(swept(rows, in_b), to_next_b[g], pb)
        result.append(side_by_side(rows))
    return jnp.concatenate(result, axis=0)


def place_halves(place, pieces, first_row, flat):
    core = lax.axis_index(place.core)
    rows = flat.shape[0] // 2
    for r, piece in enumerate(pieces):
        start = pl.multiple_of(jnp.bitwise_xor(core, r) * rows, PANEL)
        flat[pl.ds(start, rows), :] = piece[first_row : first_row + rows]


def sweep_cost():
    return pl.CostEstimate(flops=1 << 30, bytes_accessed=1 << 20, transcendentals=0)


def clear(work):
    a_ref, left, right = work[:3]
    size = a_ref.shape[1]
    a_ref[:BLOCK] = jnp.zeros((BLOCK, size), jnp.float32)
    a_ref[BLOCK + size :] = jnp.zeros((BLOCK, size), jnp.float32)
    left[...] = jnp.zeros(left.shape, left.dtype)
    right[...] = jnp.zeros(right.shape, right.dtype)


def work_shapes(size):
    splits = 6 * BLOCK
    return [
        pltpu.VMEM((size + 2 * BLOCK, size), jnp.float32),
        pltpu.VMEM((splits, size), jnp.bfloat16),
        pltpu.VMEM((splits, size), jnp.bfloat16),
    ]


def row_shapes(size):
    return [
        pltpu.VMEM((PANEL, size), jnp.float32),
        pltpu.VMEM((PANEL * PANEL, LANES), jnp.float32),
    ] * 2


def aligned_rows(ref, index, count):
    if count % PANEL == 0:
        return ref[pl.ds(pl.multiple_of(index * count, count), count), :]
    per_slab = PANEL // count
    slab = ref[pl.ds(pl.multiple_of(index // per_slab * PANEL, PANEL), PANEL), :]
    value = slab[:count]
    for i in range(1, per_slab):
        value = jnp.where(index % per_slab == i, slab[i * count : (i + 1) * count], value)
    return value


def packs(cols, rows):
    return cols == 2 * PANEL and 2 * rows == LANES


def dot(a, b, last=False):
    return lax.dot_general(
        a,
        b,
        (((1,), (1 if last else 0,)), ((), ())),
        precision=HIGHEST,
        preferred_element_type=jnp.float32,
    )


STEPS = LANES // BLOCK
FIRST_STEPS = 5
SECOND_STEPS = 6


def sweep_both(wide_work, narrow_work, begin, end, blocks):
    def step(i, blocks):
        return (
            sweep_block(*wide_work, 0, i, blocks[0]),
            sweep_block(*narrow_work, 0, i, blocks[1]),
        )

    return lax.fori_loop(begin, end, step, blocks)


def sweep_wide(work, begin, end, block):
    return lax.fori_loop(begin, end, lambda i, block: sweep_block(*work, 1, i, block), block)


def unit_scale(block):
    row, col = iotas(block.shape)
    line = jnp.sum(jnp.where(row == col, block, 0.0), axis=0, keepdims=True)
    return jnp.broadcast_to(lax.rsqrt(line), (PANEL, block.shape[1]))


def on_rows(scale):
    n = scale.shape[1]
    return jnp.broadcast_to(scale[:1], (n, n))


def scaled(block, down, across):
    return (block * on_rows(down).T) * on_rows(across)


def first_kernel(
    place, total, mine, other, wa, wl, wr, wp, na, nl, nr, np_, ws_ref, ns_ref, *refs
):
    a_flat, b_flat = refs[:2]
    wide_work, narrow_work = (wa, wl, wr, *refs[2:6]), (na, nl, nr, *refs[6:])
    place_halves(place, (mine, other), 0, a_flat)
    place_halves(place, (mine, other), a_flat.shape[0] // 2, b_flat)
    n = LANES
    slab = a_flat[n : n + PANEL]
    first, square = unpack_pair(a_flat[:n], jnp.broadcast_to(slab[:1], (n, n)))
    corner = b_flat[:n] / total
    last = unfold(b_flat[n:], jnp.broadcast_to(slab[1:2], (n, n)))
    row, col = iotas((n, n))
    damp = jnp.where(row == col, DAMP, 0.0)
    clear(wide_work)
    clear(narrow_work)
    first, last, square = first / total + damp, last / total + damp, square / total + damp
    by_first, by_last, by_square = (unit_scale(block) for block in (first, last, square))
    ws_ref[:, :n] = by_first
    ws_ref[:, n:] = by_last
    ns_ref[...] = by_square
    first_across, last_across = on_rows(by_first), on_rows(by_last)
    first_down, last_down = first_across.T, last_across.T
    corner = (corner * first_down) * last_across
    wa[BLOCK : BLOCK + n, :n] = (first * first_down) * first_across
    wa[BLOCK : BLOCK + n, n:] = corner
    wa[BLOCK + n : BLOCK + 2 * n, :n] = corner.T
    wa[BLOCK + n : BLOCK + 2 * n, n:] = (last * last_down) * last_across
    na[BLOCK : BLOCK + n, :] = scaled(square, by_square, by_square)
    start = (wa[BLOCK : 2 * BLOCK, :], na[BLOCK : 2 * BLOCK, :])
    wp[...], np_[...] = sweep_both(wide_work, narrow_work, 0, FIRST_STEPS, start)


def second_kernel(*refs):
    given, scale, ninv_ref, state, narrow_state, wide_rows, narrow_rows = (
        refs[:8],
        refs[8],
        refs[9],
        refs[10:14],
        refs[14:17],
        refs[17:21],
        refs[21:],
    )
    for source, target in zip((*given[:3], *given[4:7]), (*state[:3], *narrow_state)):
        target[...] = source[...]
    wide_work, narrow_work = (*state[:3], *wide_rows), (*narrow_state, *narrow_rows)
    wp = state[3]
    panels = (given[3][...], given[7][...])
    panel, _ = sweep_both(wide_work, narrow_work, FIRST_STEPS, STEPS, panels)
    trailing_update(*narrow_work[:3], LANES)
    by_square = scale[...]
    ninv_ref[...] = scaled(-narrow_work[0][BLOCK : BLOCK + LANES, :], by_square, by_square)
    wp[...] = sweep_wide(wide_work, 0, SECOND_STEPS, panel)


def third_kernel(wa_in, wl_in, wr_in, panel_in, scale, winv, wa, wl, wr, *rows):
    wa[...] = wa_in[...]
    wl[...] = wl_in[...]
    wr[...] = wr_in[...]
    sweep_wide((wa, wl, wr, *rows), SECOND_STEPS, STEPS, panel_in[...])
    wide = wa.shape[1]
    trailing_update(wa, wl, wr, wide)
    parts = [slice(i, i + LANES) for i in range(0, wide, LANES)]
    across = [on_rows(scale[:, i]) for i in parts]
    down = [block.T for block in across]
    for i, rows_scale in zip(parts, down):
        for j, columns_scale in zip(parts, across):
            block = -wa[BLOCK + i.start : BLOCK + i.stop, j]
            winv[i, j] = (block * rows_scale) * columns_scale


def state_shapes(size):
    shapes = [jax.ShapeDtypeStruct(v.shape, v.dtype) for v in work_shapes(size)]
    return shapes + [jax.ShapeDtypeStruct((BLOCK, size), jnp.float32)]


def sweep_call(kernel, name, args, out_shapes, scratch):
    return pl.pallas_call(
        kernel,
        in_specs=[VMEM] * len(args),
        out_specs=[VMEM] * len(out_shapes),
        out_shape=out_shapes,
        scratch_shapes=scratch,
        cost_estimate=sweep_cost(),
        compiler_params=PARAMS,
        name=name,
    )(*args)


def first_panels(place, pieces, wide, narrow, total):
    return sweep_call(
        functools.partial(first_kernel, place, total),
        "first_panels",
        pieces,
        state_shapes(wide)
        + state_shapes(narrow)
        + [jax.ShapeDtypeStruct((PANEL, n), jnp.float32) for n in (wide, narrow)],
        [
            pltpu.VMEM((EARLY_ROWS, LANES), jnp.float32),
            pltpu.VMEM((LATE_ROWS, LANES), jnp.float32),
            *row_shapes(wide),
            *row_shapes(narrow),
        ],
    )


def second_panels(state, wide, narrow):
    ninv = jax.ShapeDtypeStruct((narrow, narrow), jnp.float32)
    return sweep_call(
        second_kernel,
        "second_panels",
        state,
        [ninv] + state_shapes(wide),
        [*work_shapes(narrow), *row_shapes(wide), *row_shapes(narrow)],
    )


def third_panels(state, wide):
    winv = jax.ShapeDtypeStruct((wide, wide), jnp.float32)
    scratch = [*work_shapes(wide), *row_shapes(wide)]
    return sweep_call(third_kernel, "third_panels", state, [winv], scratch)[0]


def product_kernel(place, total, rows, winv, ninv_ref, mine, other, out_ref, flat):
    place_halves(place, (mine, other), 0, flat)
    ninv = ninv_ref[...]
    n = LANES
    inner = jnp.concatenate(
        [
            transposed_dot(flat[c * n : (c + 1) * n] / total, ninv, HIGHEST)
            for c in range(2)
        ],
        axis=0,
    )
    wide = winv.shape[1]
    cols = wide // 2 ** len(place.dp)
    near, second = lax.axis_index(place.near), lax.axis_index(place.second)
    near_stride = 2 ** (len(place.dp) - 2)
    base = place.index(place.dp) - near * near_stride - second * 2
    _, lane = iotas((PANEL, LANES))
    picks = [
        aligned_rows(winv, base + (j // 2) * near_stride + (j % 2) * 2, cols) for j in range(4)
    ]
    if cols % PANEL == 0:
        whole = dot(jnp.concatenate(picks, axis=0), inner)
        updates = [whole[j * cols : (j + 1) * cols] for j in range(4)]
    else:
        updates = [dot(picked, inner) for picked in picks]
    for j, (picked, update) in enumerate(zip(picks, updates)):
        for x in range(2):
            block = 2 * j + x
            out_ref[block, :cols] = picked[:, :LANES]
            out_ref[block, cols : 2 * cols] = picked[:, LANES:]
            if packs(cols, rows):
                upper, lower = update[:PANEL], update[PANEL:]
                if x == 0:
                    lower = pltpu.roll(lower, rows, 1)
                else:
                    upper = pltpu.roll(upper, rows, 1)
                out_ref[block, 2 * cols :] = jnp.where(lane < rows, upper, lower)
            else:
                out_ref[block, 2 * cols :] = update


def products(place, winv, ninv, pieces, rows, total):
    wide, narrow = winv.shape[0], ninv.shape[0]
    cols = wide // 2 ** len(place.dp)
    height = 2 * cols + (PANEL if packs(cols, rows) else cols)
    return pl.pallas_call(
        functools.partial(product_kernel, place, total, rows),
        in_specs=[VMEM] * 4,
        out_specs=VMEM,
        out_shape=jax.ShapeDtypeStruct((8, height, LANES), jnp.float32),
        scratch_shapes=[pltpu.VMEM((2 * narrow, LANES), jnp.float32)],
        compiler_params=PARAMS,
        name="products",
    )(winv, ninv, *pieces)


def placing_kernel(place, slots_ref, got_ref, kept_ref, update_ref):
    layers = got_ref.shape[0]
    slots, cols, wide = kept_ref.shape
    rows = update_ref.shape[2]
    own, dp = place.index(place.own), place.index(place.dp)
    step = min(cols, PANEL)
    row, col = iotas((step, LANES))
    for h in range(wide // LANES):
        lanes = slice(h * LANES, (h + 1) * LANES)
        for r in range(0, cols, step):
            here = h * cols + r
            empty = jnp.where(col + h * LANES == row + dp * cols + r, 1.0 / DAMP, 0.0)
            for c in range(slots):
                value = empty
                for l in range(layers):
                    taken = slots_ref[l, :step] == c
                    value = jnp.where(taken, got_ref[l, here : here + step], value)
                kept_ref[c, r : r + step, lanes] = value
    for l in range(layers):
        value = got_ref[l, 2 * cols :]
        if packs(cols, rows):
            update_ref[l, :PANEL] = value[:, :rows]
            update_ref[l, PANEL:] = value[:, rows:]
        else:
            part = value[:, :rows]
            for p in range(1, LANES // rows):
                part = jnp.where(own == p, value[:, p * rows : (p + 1) * rows], part)
            update_ref[l] = part


def placing(place, slots_of, got, wide, cols, slots, rows):
    layers = got.shape[0]
    return pl.pallas_call(
        functools.partial(placing_kernel, place),
        in_specs=[VMEM, VMEM],
        out_specs=[VMEM, VMEM],
        out_shape=[
            jax.ShapeDtypeStruct((slots, cols, wide), jnp.float32),
            jax.ShapeDtypeStruct((layers, cols, rows), jnp.float32),
        ],
        compiler_params=PARAMS,
        name="placing",
    )(slots_of, got)


def swap(value, axis):
    return lax.ppermute(value, axis, [(0, 1), (1, 0)])


def swap_by_core(value, place, stage, orders):
    names = (place.near, place.second, place.core, place.first)
    flips = {"near": 8, "second": 4, "first": 1}
    pairs = [(i, i ^ flips[orders[(i >> 1) & 1][stage]]) for i in range(16)]
    return lax.ppermute(value, names, pairs)


def after(value, *others):
    return lax.optimization_barrier((value,) + others)[0]


def on_device(place, wide_rows, narrow_rows, owner_map):
    layers, rows, wide = wide_rows.shape
    narrow = narrow_rows.shape[2]
    n_dp, n_own = 2 ** len(place.dp), 2 ** len(place.own)
    total = float(rows * n_dp * n_own)

    h_keep, h_send, wides, narrows = hot_squares(place, wide_rows, narrow_rows)
    first_send = h_send[4:]
    h_got = swap(first_send, place.core)
    c_keep, c_send = cold_squares(place, after(wides, first_send), narrows)
    h_keep, c_send = lax.optimization_barrier((h_keep, c_send))

    hot = h_keep[4:] + h_got
    s_got = swap_by_core(hot, place, 0, ORDERS)
    m_keep, m_send, slots_of = mixed_sums(place, owner_map, after(wides, hot), narrows)
    c_got = swap(after(c_send + h_send[:4], m_send), place.core)
    m_got = swap(m_send, place.core)

    s = (c_keep + h_keep[:4]) + s_got
    s = s + after(c_got, s)
    s_got = swap_by_core(s[2:], place, 1, ORDERS)
    m = after(m_keep, s) + m_got
    m_got = swap_by_core(m[4:], place, 0, LATE_ORDERS)

    s = s[:2] + s_got
    s_got = swap_by_core(s[1], place, 2, ORDERS)
    m = after(m[:4], s) + m_got
    m_got = swap_by_core(m[2:], place, 1, LATE_ORDERS)

    s = s[0] + s_got
    if place.extra:
        s = lax.psum(s, place.extra)
    s_got = swap(s, place.far)
    m = after(m[:2], s) + m_got
    m_got = swap_by_core(m[1], place, 2, LATE_ORDERS)

    s = s + s_got
    state = first_panels(place, [s, swap(s, place.core)], wide, narrow, total)
    m = after(m[0], state[0]) + m_got
    if place.extra:
        m = lax.psum(m, place.extra)
    m_got = swap(m, place.far)
    *state, wide_scale, narrow_scale = state
    ninv, *state = second_panels([*state, narrow_scale], wide, narrow)
    m = after(m, ninv) + m_got
    m_got = swap(m, place.core)
    winv = third_panels([*state, wide_scale], wide)
    cols, own_rows = wide // n_dp, narrow // n_own
    sent = products(place, winv, ninv, [m, m_got], own_rows, total)
    got = lax.all_to_all(sent, (place.near, place.second, place.first), 0, 0)
    kept, update = placing(
        place, slots_of, got, wide, cols, layers // n_own + 1, own_rows
    )
    return (jnp.swapaxes(kept, 1, 2), jnp.swapaxes(update, 1, 2))


def solution(mesh):
    n_dp, n_own = mesh.shape["dp"], mesh.shape["own"]
    dp_names = tuple(f"dp{i}" for i in range(int(np.log2(n_dp))))
    own_names = tuple(f"own{i}" for i in range(int(np.log2(n_own))))
    names = dp_names + own_names
    bits = jax.sharding.Mesh(mesh.devices.reshape((2,) * len(names)), names)
    in_specs = (P(None, names, None), P(None, names, None), P())
    out_specs = (P(own_names, None, dp_names), P(None, own_names, dp_names))
    return jax.shard_map(
        functools.partial(on_device, Place(dp_names, own_names)),
        mesh=bits,
        in_specs=in_specs,
        out_specs=out_specs,
        check_vma=False,
    )
```

```python
import functools

import jax
import jax.numpy as jnp
import numpy as np
from jax import lax
from jax.experimental import pallas as pl
from jax.experimental.pallas import tpu as pltpu
from jax.sharding import PartitionSpec as P

DAMP = 0.5
LANES = 128
PANEL = 8
BLOCK = 2 * PANEL
VMEM_LIMIT = 48 * 1024 * 1024
HIGHEST = lax.Precision.HIGHEST
VMEM = pl.BlockSpec(memory_space=pltpu.VMEM)
SMEM = pl.BlockSpec(memory_space=pltpu.SMEM)
HBM = pl.BlockSpec(memory_space=pltpu.HBM)
PARAMS = pltpu.CompilerParams(vmem_limit_bytes=VMEM_LIMIT)


class Place:
    def __init__(self, dp_names, own_names):
        self.dp, self.own = dp_names, own_names
        self.core, self.second, self.near, self.far = (
            dp_names[-1],
            dp_names[-2],
            dp_names[1],
            dp_names[0],
        )
        self.first = own_names[-1]
        used = (self.core, self.second, self.near, self.far, self.first)
        self.extra = tuple(n for n in dp_names + own_names if n not in used)

    def index(self, names):
        value = jnp.int32(0)
        for name in names:
            value = value * 2 + lax.axis_index(name)
        return value

    def layer(self):
        return self.index((self.near, self.second, self.first))


def transposed_dot(a, b, precision=None):
    return lax.dot_general(
        a, b, (((0,), (0,)), ((), ())), precision=precision, preferred_element_type=jnp.float32
    )


AHEAD = 5


def layer_copies(place, sources, buffers, sems):
    layer = place.layer()
    return [
        [
            pltpu.make_async_copy(
                source.at[jnp.bitwise_xor(layer, i)], buffer.at[i], sems.at[i, s]
            )
            for s, (source, buffer) in enumerate(zip(sources, buffers))
        ]
        for i in range(buffers[0].shape[0])
    ]


def both_halves(place, flat, i):
    rows = flat.shape[1] // 2
    core = lax.axis_index(place.core)
    kept = pl.multiple_of(core * rows, PANEL)
    sent = pl.multiple_of((1 - core) * rows, PANEL)
    return flat[i, pl.ds(kept, rows), :], flat[i, pl.ds(sent, rows), :]


ORDERS = (("first", "second", "near"), ("second", "near", "first"))
LATE_ORDERS = (("first", "second", "near"), ("near", "first", "second"))


def position(axes, i):
    bits = {"near": i // 4, "second": (i // 2) % 2, "first": i % 2}
    return bits[axes[0]] * 4 + bits[axes[1]] * 2 + bits[axes[2]]


def positions(place, i, orders):
    core = lax.axis_index(place.core)
    first, second = (position(axes, i) for axes in orders)
    return jnp.where(core == 0, first, second), jnp.where(core == 0, second, first)


def iotas(shape):
    return (
        lax.broadcasted_iota(jnp.int32, shape, 0),
        lax.broadcasted_iota(jnp.int32, shape, 1),
    )


def pack_pair(first, second):
    row, col = iotas(first.shape)
    return jnp.where(row >= col, first, second)


def unpack_pair(packed, second_diagonal):
    row, col = iotas(packed.shape)
    turned = packed.T
    first = jnp.where(row >= col, packed, turned)
    second = jnp.where(col > row, packed, turned)
    return first, jnp.where(row == col, second_diagonal, second)


def fold(block):
    h = block.shape[0] // 2
    row, col = iotas((h, 2 * h))
    last = pltpu.roll(block[h:], h, 1)
    return jnp.where((col >= h) | (row >= col), block[:h], last)


def unfold(folded, diagonal):
    h, n = folded.shape
    row, col = iotas((n, n))
    block = jnp.concatenate([folded, jnp.zeros((h, n), jnp.float32)], axis=0)
    turned = block.T
    top = jnp.where((col >= h) | (col <= row), block, turned)
    moved = pltpu.roll(pltpu.roll(block, h, 0), h, 1)
    moved_turned = pltpu.roll(pltpu.roll(turned, h, 0), h, 1)
    last = jnp.where(col > row, moved, moved_turned)
    last = jnp.where(row == col, diagonal, last)
    return jnp.where(row < h, top, jnp.where(col < h, turned, last))


def diagonals(blocks, rows):
    n = blocks[0].shape[0]
    row, col = iotas((n, n))
    slab_row, _ = iotas((rows, n))
    slab = jnp.zeros((rows, n), jnp.float32)
    for i, block in enumerate(blocks):
        line = jnp.sum(jnp.where(row == col, block, 0.0), axis=0, keepdims=True)
        slab = jnp.where(slab_row == i, jnp.broadcast_to(line, (rows, n)), slab)
    return slab


EARLY_ROWS = 144
LATE_ROWS = 192


HOT = (1, 2, 3, 5, 6, 7)
COLD = (0, 4)


def square_sums(wide, narrow):
    return transposed_dot(wide, wide), transposed_dot(narrow, narrow)


def pack_layer(place, i, wcov, ncov, a_flat, b_flat):
    n = LANES
    last = wcov[n:, n:]
    a_flat[i, :n] = pack_pair(wcov[:n, :n], ncov)
    a_flat[i, n:] = diagonals((ncov, last), EARLY_ROWS - n)
    b_flat[i, :n] = wcov[:n, n:]
    b_flat[i, n:] = fold(last)
    a_kept, a_sent = both_halves(place, a_flat, i)
    b_kept, b_sent = both_halves(place, b_flat, i)
    return (a_kept, b_kept), (a_sent, b_sent)


def put(ref, index, parts):
    rows = EARLY_ROWS // 2
    ref[index, :rows] = parts[0]
    ref[index, rows:] = parts[1]


def put_layer(place, i, sums, a_flat, b_flat, keep, send):
    kept, sent = pack_layer(place, i, *sums, a_flat, b_flat)
    mine, other = positions(place, i, ORDERS)
    put(keep, mine, kept)
    put(send, other, sent)


def clear_others(place, layers, keep, send):
    for i in layers:
        mine, other = positions(place, i, ORDERS)
        keep[mine] = jnp.zeros(keep.shape[1:], jnp.float32)
        send[other] = jnp.zeros(send.shape[1:], jnp.float32)


def hot_kernel(place, wide_hbm, narrow_hbm, keep, send, wides, narrows, a_flat, b_flat, sems):
    copies = layer_copies(place, (wide_hbm, narrow_hbm), (wides, narrows), sems)
    order = HOT + COLD
    for i in order[:AHEAD]:
        for copy in copies[i]:
            copy.start()
    clear_others(place, COLD, keep, send)

    def pack(i, sums):
        put_layer(place, i, sums, a_flat, b_flat, keep, send)

    before = None
    for at, i in enumerate(order):
        for copy in copies[i]:
            copy.wait()
        if at + AHEAD < len(order):
            for copy in copies[order[at + AHEAD]]:
                copy.start()
        if before is not None:
            pack(*before)
            before = None
        if i in HOT:
            before = (i, square_sums(wides[i], narrows[i]))


def cold_kernel(place, wides, narrows, keep, send, a_flat, b_flat):
    for i in COLD:
        put_layer(
            place, i, square_sums(wides[i], narrows[i]), a_flat, b_flat, keep, send
        )
    core = lax.axis_index(place.core)
    stay = [[i for i in HOT if position(axes, i) < 4] for axes in ORDERS]
    for first, second in zip(*stay):
        here = [position(axes, i) for axes, i in zip(ORDERS, (first, second))]
        mine = jnp.where(core == 0, here[0], here[1])
        other = jnp.where(core == 0, here[1], here[0])
        keep[mine] = jnp.zeros(keep.shape[1:], jnp.float32)
        send[other] = jnp.zeros(send.shape[1:], jnp.float32)


def write_slots(place, owner_map, slots_ref):
    own = place.index(place.own)
    count = jnp.int32(0)
    for l in range(slots_ref.shape[0]):
        mine = owner_map[l] == own
        slot = jnp.where(mine, count, -1)
        slots_ref[l] = jnp.full(slots_ref.shape[1:], 0, jnp.int32) + slot
        count = count + mine.astype(jnp.int32)


def mixed_kernel(place, owner_map, wides, narrows, keep, send, slots_ref, flat):
    n = LANES
    write_slots(place, owner_map, slots_ref)
    for i in range(wides.shape[0]):
        mixed = transposed_dot(narrows[i], wides[i])
        flat[i, :n] = mixed[:, :n]
        flat[i, n:] = mixed[:, n:]
        kept, sent = both_halves(place, flat, i)
        mine, other = positions(place, i, LATE_ORDERS)
        keep[mine] = kept
        send[other] = sent


def gram_cost(wide_rows, columns):
    return pl.CostEstimate(
        flops=2 * wide_rows.size * columns, bytes_accessed=2 * wide_rows.size, transcendentals=0
    )


HALF_ROWS = (EARLY_ROWS + LATE_ROWS) // 2


def pack_shapes(layers):
    return [
        pltpu.VMEM((layers, EARLY_ROWS, LANES), jnp.float32),
        pltpu.VMEM((layers, LATE_ROWS, LANES), jnp.float32),
    ]


def hot_squares(place, wide_rows, narrow_rows):
    layers = wide_rows.shape[0]
    half = jax.ShapeDtypeStruct((layers, HALF_ROWS, LANES), jnp.float32)
    return pl.pallas_call(
        functools.partial(hot_kernel, place),
        in_specs=[HBM, HBM],
        out_specs=[VMEM] * 4,
        out_shape=[
            half,
            half,
            jax.ShapeDtypeStruct(wide_rows.shape, wide_rows.dtype),
            jax.ShapeDtypeStruct(narrow_rows.shape, narrow_rows.dtype),
        ],
        scratch_shapes=[*pack_shapes(layers), pltpu.SemaphoreType.DMA((layers, 2))],
        cost_estimate=gram_cost(wide_rows, 240),
        compiler_params=PARAMS,
        name="hot_squares",
    )(
        pltpu.with_memory_space_constraint(wide_rows, pltpu.HBM),
        pltpu.with_memory_space_constraint(narrow_rows, pltpu.HBM),
    )


def cold_squares(place, wides, narrows):
    half = jax.ShapeDtypeStruct((wides.shape[0] // 2, HALF_ROWS, LANES), jnp.float32)
    return pl.pallas_call(
        functools.partial(cold_kernel, place),
        in_specs=[VMEM, VMEM],
        out_specs=[VMEM, VMEM],
        out_shape=[half, half],
        scratch_shapes=pack_shapes(wides.shape[0]),
        cost_estimate=gram_cost(wides, 80),
        compiler_params=PARAMS,
        name="cold_squares",
    )(wides, narrows)


def mixed_sums(place, owner_map, wides, narrows):
    layers, _, narrow = narrows.shape
    half = jax.ShapeDtypeStruct((layers, narrow, LANES), jnp.float32)
    return pl.pallas_call(
        functools.partial(mixed_kernel, place),
        in_specs=[SMEM, VMEM, VMEM],
        out_specs=[VMEM] * 3,
        out_shape=[half, half, jax.ShapeDtypeStruct((layers, PANEL, LANES), jnp.int32)],
        scratch_shapes=[pltpu.VMEM((layers, 2 * narrow, LANES), jnp.float32)],
        cost_estimate=gram_cost(wides, 128),
        compiler_params=PARAMS,
        name="mixed",
    )(owner_map, wides, narrows)


def lane_gather(x, index):
    return jnp.take_along_axis(x, index, axis=1, mode="promise_in_bounds")


def trailing_update(a_ref, left_ref, right_ref, base):
    size = a_ref.shape[1]
    a_ref[pl.ds(pl.multiple_of(base, BLOCK), BLOCK), :] = jnp.zeros((BLOCK, size), jnp.float32)
    lane = lax.broadcasted_iota(jnp.int32, (1, size), 1)
    swept = (lane >= base - BLOCK) & (lane < base)
    update = transposed_dot(left_ref[...], right_ref[...])
    a_ref[BLOCK : BLOCK + size, :] = (
        jnp.where(swept, 0.0, a_ref[BLOCK : BLOCK + size, :]) - update
    )


def in_three(x):
    high = x.astype(jnp.bfloat16).astype(jnp.float32)
    rest = x - high
    middle = rest.astype(jnp.bfloat16).astype(jnp.float32)
    return high, middle, rest - middle


def factor_panel(rows_ref, cols_ref, tile, first, panel, targets):
    tiles = panel.shape[1] // LANES
    shape = (PANEL, LANES)
    _, lane = iotas(shape)

    def on_all(ref, k, lanes):
        return jnp.broadcast_to(ref[k : k + 1, lanes], shape)

    rows_ref[...] = panel
    lanes = [slice(LANES * t, LANES * (t + 1)) for t in range(tiles)]
    rows = [[on_all(rows_ref, k, part) for part in lanes] for k in range(PANEL)]
    here = panel[:, lanes[tile]]
    for j in range(PANEL):
        column = lane_gather(here, jnp.full(shape, 0, jnp.int32) + (first + j))
        cols_ref[PANEL * j : PANEL * (j + 1)] = column
    d = [[None] * PANEL for _ in range(PANEL)]
    for j in range(PANEL):
        for i in range(j, PANEL):
            d[i][j] = on_all(cols_ref, PANEL * j + i, slice(None))
    own = (lane >= first) & (lane < first + PANEL)
    q = [[None] * tiles for _ in range(PANEL)]
    p = [[None] * tiles for _ in range(PANEL)]
    weights = [[None] * PANEL for _ in targets]
    factor = [[None] * PANEL for _ in range(PANEL)]

    def substitute(k, scale):
        for t in range(tiles):
            value = rows[k][t]
            if t == tile:
                value = jnp.where(own, jnp.where(lane == first + k, -1.0, 0.0), value)
            for j in range(k):
                value = value - factor[k][j] * q[j][t]
            q[k][t] = value
            p[k][t] = value * scale
        for target, weight in zip(targets, weights):
            source, index = target(rows[k])
            value = lane_gather(source, index)
            for j in range(k):
                value = value - factor[k][j] * weight[j]
            weight[k] = value

    for k in range(0, PANEL, 2):
        m = k + 1
        a, b, c = d[k][k], d[m][k], d[m][m]
        first_scale = 1.0 / a
        second_scale = a * (1.0 / (a * c - b * b))
        factor[m][k] = b * first_scale
        left_over = {i: d[i][m] - d[i][k] * factor[m][k] for i in range(k + 2, PANEL)}
        for i in range(k + 2, PANEL):
            factor[i][k] = d[i][k] * first_scale
            factor[i][m] = left_over[i] * second_scale
        for i in range(k + 2, PANEL):
            for j in range(k + 2, i + 1):
                value = d[i][j] - d[i][k] * factor[j][k]
                d[i][j] = value - (left_over[i] * left_over[j]) * second_scale
        substitute(k, first_scale)
        substitute(m, second_scale)
    return q, p, weights


def packed_rows(values):
    sub, _ = iotas((PANEL, LANES))
    whole = []
    for t in range(len(values[0])):
        value = values[0][t]
        for k in range(1, PANEL):
            value = jnp.where(sub == k, values[k][t], value)
        whole.append(value)
    return whole


def side_by_side(tiles):
    return jnp.concatenate(tiles, axis=1) if len(tiles) > 1 else tiles[0]


def sweep_block(a_ref, left_ref, right_ref, a_rows, a_cols, b_rows, b_cols, tile, step, block):
    size = a_ref.shape[1]
    tiles = size // LANES
    first = step * BLOCK
    second = first + PANEL
    base = tile * LANES + first
    trailing_update(a_ref, left_ref, right_ref, base)

    sub, lane = iotas((PANEL, LANES))
    last = first == LANES - BLOCK
    next_first = jnp.where(last, 0, first + BLOCK)

    def in_block(row):
        return row[tile], second + sub

    def in_next(offset):
        def target(row):
            source = row[tile]
            if tile + 1 < tiles:
                source = jnp.where(last, row[tile + 1], source)
            return source, next_first + offset + sub

        return target

    nexts = [in_next(0), in_next(PANEL)]
    in_a = (lane >= first) & (lane < second)
    in_b = (lane >= second) & (lane < second + PANEL)

    def swept(tiles_of, mask):
        return [jnp.where(mask, 0.0, v) if t == tile else v for t, v in enumerate(tiles_of)]

    def minus(tiles_of, weight, p):
        result = []
        for t, value in enumerate(tiles_of):
            for k in range(PANEL):
                value = value - weight[k] * p[k][t]
            result.append(value)
        return result

    def by_tile(rows):
        return [rows[:, LANES * t : LANES * (t + 1)] for t in range(tiles)]

    qa, pa, (to_b, *to_next_a) = factor_panel(
        a_rows, a_cols, tile, first, block[:PANEL], [in_block, *nexts]
    )
    panel_b = side_by_side(minus(swept(by_tile(block[PANEL:]), in_a), to_b, pa))
    qb, pb, to_next_b = factor_panel(b_rows, b_cols, tile, second, panel_b, nexts)

    left, right = [], []
    for q, p, mask in ((qa, pa, in_b), (qb, pb, None)):
        q, p = packed_rows(q), packed_rows(p)
        if mask is not None:
            q, p = swept(q, mask), swept(p, mask)
        qs, ps = in_three(side_by_side(q)), in_three(side_by_side(p))
        left += [qs[i] for i in (0, 0, 1, 1, 0, 2)]
        right += [ps[i] for i in (0, 1, 0, 1, 2, 0)]
    left_ref[...] = jnp.concatenate(left, axis=0).astype(jnp.bfloat16)
    right_ref[...] = jnp.concatenate(right, axis=0).astype(jnp.bfloat16)

    following = a_ref[pl.ds(pl.multiple_of(base + 2 * BLOCK, BLOCK), BLOCK), :]
    result = []
    for g in range(2):
        rows = by_tile(following[g * PANEL : (g + 1) * PANEL])
        rows = minus(swept(rows, in_a), to_next_a[g], pa)
        rows = minus(swept(rows, in_b), to_next_b[g], pb)
        result.append(side_by_side(rows))
    return jnp.concatenate(result, axis=0)


def place_halves(place, pieces, first_row, flat):
    core = lax.axis_index(place.core)
    rows = flat.shape[0] // 2
    for r, piece in enumerate(pieces):
        start = pl.multiple_of(jnp.bitwise_xor(core, r) * rows, PANEL)
        flat[pl.ds(start, rows), :] = piece[first_row : first_row + rows]


def sweep_cost():
    return pl.CostEstimate(flops=1 << 30, bytes_accessed=1 << 20, transcendentals=0)


def clear(work):
    a_ref, left, right = work[:3]
    size = a_ref.shape[1]
    a_ref[:BLOCK] = jnp.zeros((BLOCK, size), jnp.float32)
    a_ref[BLOCK + size :] = jnp.zeros((BLOCK, size), jnp.float32)
    left[...] = jnp.zeros(left.shape, left.dtype)
    right[...] = jnp.zeros(right.shape, right.dtype)


def work_shapes(size):
    splits = 6 * BLOCK
    return [
        pltpu.VMEM((size + 2 * BLOCK, size), jnp.float32),
        pltpu.VMEM((splits, size), jnp.bfloat16),
        pltpu.VMEM((splits, size), jnp.bfloat16),
    ]


def row_shapes(size):
    return [
        pltpu.VMEM((PANEL, size), jnp.float32),
        pltpu.VMEM((PANEL * PANEL, LANES), jnp.float32),
    ] * 2


def aligned_rows(ref, index, count):
    if count % PANEL == 0:
        return ref[pl.ds(pl.multiple_of(index * count, count), count), :]
    per_slab = PANEL // count
    slab = ref[pl.ds(pl.multiple_of(index // per_slab * PANEL, PANEL), PANEL), :]
    value = slab[:count]
    for i in range(1, per_slab):
        value = jnp.where(index % per_slab == i, slab[i * count : (i + 1) * count], value)
    return value


def packs(cols, rows):
    return cols == 2 * PANEL and 2 * rows == LANES


def dot(a, b, last=False):
    return lax.dot_general(
        a,
        b,
        (((1,), (1 if last else 0,)), ((), ())),
        precision=HIGHEST,
        preferred_element_type=jnp.float32,
    )


STEPS = LANES // BLOCK
FIRST_STEPS = 3
SECOND_STEPS = 6


def sweep_both(wide_work, narrow_work, begin, end, blocks):
    def step(i, blocks):
        return (
            sweep_block(*wide_work, 0, i, blocks[0]),
            sweep_block(*narrow_work, 0, i, blocks[1]),
        )

    return lax.fori_loop(begin, end, step, blocks)


def sweep_wide(work, begin, end, block):
    return lax.fori_loop(begin, end, lambda i, block: sweep_block(*work, 1, i, block), block)


def unit_scale(block):
    row, col = iotas(block.shape)
    line = jnp.sum(jnp.where(row == col, block, 0.0), axis=0, keepdims=True)
    return jnp.broadcast_to(lax.rsqrt(line), (PANEL, block.shape[1]))


def on_rows(scale):
    n = scale.shape[1]
    return jnp.broadcast_to(scale[:1], (n, n))


def scaled(block, down, across):
    return (block * on_rows(down).T) * on_rows(across)


def first_kernel(
    place, total, mine, other, wa, wl, wr, wp, na, nl, nr, np_, ws_ref, ns_ref, *refs
):
    a_flat, b_flat = refs[:2]
    wide_work, narrow_work = (wa, wl, wr, *refs[2:6]), (na, nl, nr, *refs[6:])
    place_halves(place, (mine, other), 0, a_flat)
    place_halves(place, (mine, other), a_flat.shape[0] // 2, b_flat)
    n = LANES
    slab = a_flat[n : n + PANEL]
    first, square = unpack_pair(a_flat[:n], jnp.broadcast_to(slab[:1], (n, n)))
    corner = b_flat[:n] / total
    last = unfold(b_flat[n:], jnp.broadcast_to(slab[1:2], (n, n)))
    row, col = iotas((n, n))
    damp = jnp.where(row == col, DAMP, 0.0)
    clear(wide_work)
    clear(narrow_work)
    first, last, square = first / total + damp, last / total + damp, square / total + damp
    by_first, by_last, by_square = (unit_scale(block) for block in (first, last, square))
    ws_ref[:, :n] = by_first
    ws_ref[:, n:] = by_last
    ns_ref[...] = by_square
    first_across, last_across = on_rows(by_first), on_rows(by_last)
    first_down, last_down = first_across.T, last_across.T
    corner = (corner * first_down) * last_across
    wa[BLOCK : BLOCK + n, :n] = (first * first_down) * first_across
    wa[BLOCK : BLOCK + n, n:] = corner
    wa[BLOCK + n : BLOCK + 2 * n, :n] = corner.T
    wa[BLOCK + n : BLOCK + 2 * n, n:] = (last * last_down) * last_across
    na[BLOCK : BLOCK + n, :] = scaled(square, by_square, by_square)
    start = (wa[BLOCK : 2 * BLOCK, :], na[BLOCK : 2 * BLOCK, :])
    wp[...], np_[...] = sweep_both(wide_work, narrow_work, 0, FIRST_STEPS, start)


def second_kernel(*refs):
    given, scale, ninv_ref, state, narrow_state, wide_rows, narrow_rows = (
        refs[:8],
        refs[8],
        refs[9],
        refs[10:14],
        refs[14:17],
        refs[17:21],
        refs[21:],
    )
    for source, target in zip((*given[:3], *given[4:7]), (*state[:3], *narrow_state)):
        target[...] = source[...]
    wide_work, narrow_work = (*state[:3], *wide_rows), (*narrow_state, *narrow_rows)
    wp = state[3]
    panels = (given[3][...], given[7][...])
    panel, _ = sweep_both(wide_work, narrow_work, FIRST_STEPS, STEPS, panels)
    trailing_update(*narrow_work[:3], LANES)
    by_square = scale[...]
    ninv_ref[...] = scaled(-narrow_work[0][BLOCK : BLOCK + LANES, :], by_square, by_square)
    wp[...] = sweep_wide(wide_work, 0, SECOND_STEPS, panel)


def third_kernel(wa_in, wl_in, wr_in, panel_in, scale, winv, wa, wl, wr, *rows):
    wa[...] = wa_in[...]
    wl[...] = wl_in[...]
    wr[...] = wr_in[...]
    sweep_wide((wa, wl, wr, *rows), SECOND_STEPS, STEPS, panel_in[...])
    wide = wa.shape[1]
    trailing_update(wa, wl, wr, wide)
    parts = [slice(i, i + LANES) for i in range(0, wide, LANES)]
    across = [on_rows(scale[:, i]) for i in parts]
    down = [block.T for block in across]
    for i, rows_scale in zip(parts, down):
        for j, columns_scale in zip(parts, across):
            block = -wa[BLOCK + i.start : BLOCK + i.stop, j]
            winv[i, j] = (block * rows_scale) * columns_scale


def state_shapes(size):
    shapes = [jax.ShapeDtypeStruct(v.shape, v.dtype) for v in work_shapes(size)]
    return shapes + [jax.ShapeDtypeStruct((BLOCK, size), jnp.float32)]


def sweep_call(kernel, name, args, out_shapes, scratch):
    return pl.pallas_call(
        kernel,
        in_specs=[VMEM] * len(args),
        out_specs=[VMEM] * len(out_shapes),
        out_shape=out_shapes,
        scratch_shapes=scratch,
        cost_estimate=sweep_cost(),
        compiler_params=PARAMS,
        name=name,
    )(*args)


def first_panels(place, pieces, wide, narrow, total):
    return sweep_call(
        functools.partial(first_kernel, place, total),
        "first_panels",
        pieces,
        state_shapes(wide)
        + state_shapes(narrow)
        + [jax.ShapeDtypeStruct((PANEL, n), jnp.float32) for n in (wide, narrow)],
        [
            pltpu.VMEM((EARLY_ROWS, LANES), jnp.float32),
            pltpu.VMEM((LATE_ROWS, LANES), jnp.float32),
            *row_shapes(wide),
            *row_shapes(narrow),
        ],
    )


def second_panels(state, wide, narrow):
    ninv = jax.ShapeDtypeStruct((narrow, narrow), jnp.float32)
    return sweep_call(
        second_kernel,
        "second_panels",
        state,
        [ninv] + state_shapes(wide),
        [*work_shapes(narrow), *row_shapes(wide), *row_shapes(narrow)],
    )


def third_panels(state, wide):
    winv = jax.ShapeDtypeStruct((wide, wide), jnp.float32)
    scratch = [*work_shapes(wide), *row_shapes(wide)]
    return sweep_call(third_kernel, "third_panels", state, [winv], scratch)[0]


def product_kernel(place, total, rows, winv, ninv_ref, mine, other, out_ref, flat):
    place_halves(place, (mine, other), 0, flat)
    ninv = ninv_ref[...]
    n = LANES
    inner = jnp.concatenate(
        [
            transposed_dot(flat[c * n : (c + 1) * n] / total, ninv, HIGHEST)
            for c in range(2)
        ],
        axis=0,
    )
    wide = winv.shape[1]
    cols = wide // 2 ** len(place.dp)
    near, second = lax.axis_index(place.near), lax.axis_index(place.second)
    near_stride = 2 ** (len(place.dp) - 2)
    base = place.index(place.dp) - near * near_stride - second * 2
    _, lane = iotas((PANEL, LANES))
    picks = [
        aligned_rows(winv, base + (j // 2) * near_stride + (j % 2) * 2, cols) for j in range(4)
    ]
    if cols % PANEL == 0:
        whole = dot(jnp.concatenate(picks, axis=0), inner)
        updates = [whole[j * cols : (j + 1) * cols] for j in range(4)]
    else:
        updates = [dot(picked, inner) for picked in picks]
    for j, (picked, update) in enumerate(zip(picks, updates)):
        for x in range(2):
            block = 2 * j + x
            out_ref[block, :cols] = picked[:, :LANES]
            out_ref[block, cols : 2 * cols] = picked[:, LANES:]
            if packs(cols, rows):
                upper, lower = update[:PANEL], update[PANEL:]
                if x == 0:
                    lower = pltpu.roll(lower, rows, 1)
                else:
                    upper = pltpu.roll(upper, rows, 1)
                out_ref[block, 2 * cols :] = jnp.where(lane < rows, upper, lower)
            else:
                out_ref[block, 2 * cols :] = update


def products(place, winv, ninv, pieces, rows, total):
    wide, narrow = winv.shape[0], ninv.shape[0]
    cols = wide // 2 ** len(place.dp)
    height = 2 * cols + (PANEL if packs(cols, rows) else cols)
    return pl.pallas_call(
        functools.partial(product_kernel, place, total, rows),
        in_specs=[VMEM] * 4,
        out_specs=VMEM,
        out_shape=jax.ShapeDtypeStruct((8, height, LANES), jnp.float32),
        scratch_shapes=[pltpu.VMEM((2 * narrow, LANES), jnp.float32)],
        compiler_params=PARAMS,
        name="products",
    )(winv, ninv, *pieces)


def placing_kernel(place, slots_ref, got_ref, kept_ref, update_ref):
    layers = got_ref.shape[0]
    slots, cols, wide = kept_ref.shape
    rows = update_ref.shape[2]
    own, dp = place.index(place.own), place.index(place.dp)
    step = min(cols, PANEL)
    row, col = iotas((step, LANES))
    for h in range(wide // LANES):
        lanes = slice(h * LANES, (h + 1) * LANES)
        for r in range(0, cols, step):
            here = h * cols + r
            empty = jnp.where(col + h * LANES == row + dp * cols + r, 1.0 / DAMP, 0.0)
            for c in range(slots):
                value = empty
                for l in range(layers):
                    taken = slots_ref[l, :step] == c
                    value = jnp.where(taken, got_ref[l, here : here + step], value)
                kept_ref[c, r : r + step, lanes] = value
    for l in range(layers):
        value = got_ref[l, 2 * cols :]
        if packs(cols, rows):
            update_ref[l, :PANEL] = value[:, :rows]
            update_ref[l, PANEL:] = value[:, rows:]
        else:
            part = value[:, :rows]
            for p in range(1, LANES // rows):
                part = jnp.where(own == p, value[:, p * rows : (p + 1) * rows], part)
            update_ref[l] = part


def placing(place, slots_of, got, wide, cols, slots, rows):
    layers = got.shape[0]
    return pl.pallas_call(
        functools.partial(placing_kernel, place),
        in_specs=[VMEM, VMEM],
        out_specs=[VMEM, VMEM],
        out_shape=[
            jax.ShapeDtypeStruct((slots, cols, wide), jnp.float32),
            jax.ShapeDtypeStruct((layers, cols, rows), jnp.float32),
        ],
        compiler_params=PARAMS,
        name="placing",
    )(slots_of, got)


def swap(value, axis):
    return lax.ppermute(value, axis, [(0, 1), (1, 0)])


def swap_by_core(value, place, stage, orders):
    names = (place.near, place.second, place.core, place.first)
    flips = {"near": 8, "second": 4, "first": 1}
    pairs = [(i, i ^ flips[orders[(i >> 1) & 1][stage]]) for i in range(16)]
    return lax.ppermute(value, names, pairs)


def after(value, *others):
    return lax.optimization_barrier((value,) + others)[0]


def on_device(place, wide_rows, narrow_rows, owner_map):
    layers, rows, wide = wide_rows.shape
    narrow = narrow_rows.shape[2]
    n_dp, n_own = 2 ** len(place.dp), 2 ** len(place.own)
    total = float(rows * n_dp * n_own)

    h_keep, h_send, wides, narrows = hot_squares(place, wide_rows, narrow_rows)
    first_send = h_send[4:]
    h_got = swap(first_send, place.core)
    c_keep, c_send = cold_squares(place, after(wides, first_send), narrows)
    h_keep, c_send = lax.optimization_barrier((h_keep, c_send))

    hot = h_keep[4:] + h_got
    s_got = swap_by_core(hot, place, 0, ORDERS)
    m_keep, m_send, slots_of = mixed_sums(place, owner_map, after(wides, hot), narrows)
    c_got = swap(after(c_send + h_send[:4], m_send), place.core)
    m_got = swap(m_send, place.core)

    s = (c_keep + h_keep[:4]) + s_got
    s = s + after(c_got, s)
    s_got = swap_by_core(s[2:], place, 1, ORDERS)
    m = after(m_keep, s) + m_got
    m_got = swap_by_core(m[4:], place, 0, LATE_ORDERS)

    s = s[:2] + s_got
    s_got = swap_by_core(s[1], place, 2, ORDERS)
    m = after(m[:4], s) + m_got
    m_got = swap_by_core(m[2:], place, 1, LATE_ORDERS)

    s = s[0] + s_got
    if place.extra:
        s = lax.psum(s, place.extra)
    s_got = swap(s, place.far)
    m = after(m[:2], s) + m_got
    m_got = swap_by_core(m[1], place, 2, LATE_ORDERS)

    s = s + s_got
    state = first_panels(place, [s, swap(s, place.core)], wide, narrow, total)
    m = after(m[0], state[0]) + m_got
    if place.extra:
        m = lax.psum(m, place.extra)
    m_got = swap(m, place.far)
    *state, wide_scale, narrow_scale = state
    ninv, *state = second_panels([*state, narrow_scale], wide, narrow)
    m = after(m, ninv) + m_got
    m_got = swap(m, place.core)
    winv = third_panels([*state, wide_scale], wide)
    cols, own_rows = wide // n_dp, narrow // n_own
    sent = products(place, winv, ninv, [m, m_got], own_rows, total)
    got = lax.all_to_all(sent, (place.near, place.second, place.first), 0, 0)
    kept, update = placing(
        place, slots_of, got, wide, cols, layers // n_own + 1, own_rows
    )
    return (jnp.swapaxes(kept, 1, 2), jnp.swapaxes(update, 1, 2))


def solution(mesh):
    n_dp, n_own = mesh.shape["dp"], mesh.shape["own"]
    dp_names = tuple(f"dp{i}" for i in range(int(np.log2(n_dp))))
    own_names = tuple(f"own{i}" for i in range(int(np.log2(n_own))))
    names = dp_names + own_names
    bits = jax.sharding.Mesh(mesh.devices.reshape((2,) * len(names)), names)
    in_specs = (P(None, names, None), P(None, names, None), P())
    out_specs = (P(own_names, None, dp_names), P(None, own_names, dp_names))
    return jax.shard_map(
        functools.partial(on_device, Place(dp_names, own_names)),
        mesh=bits,
        in_specs=in_specs,
        out_specs=out_specs,
        check_vma=False,
    )
```

```python
import functools

import jax
import jax.numpy as jnp
import numpy as np
from jax import lax
from jax.experimental import pallas as pl
from jax.experimental.pallas import tpu as pltpu
from jax.sharding import PartitionSpec as P

DAMP = 0.5
LANES = 128
PANEL = 8
BLOCK = 2 * PANEL
VMEM_LIMIT = 48 * 1024 * 1024
HIGHEST = lax.Precision.HIGHEST
VMEM = pl.BlockSpec(memory_space=pltpu.VMEM)
SMEM = pl.BlockSpec(memory_space=pltpu.SMEM)
HBM = pl.BlockSpec(memory_space=pltpu.HBM)
PARAMS = pltpu.CompilerParams(vmem_limit_bytes=VMEM_LIMIT)


class Place:
    def __init__(self, dp_names, own_names):
        self.dp, self.own = dp_names, own_names
        self.core, self.second, self.near, self.far = (
            dp_names[-1],
            dp_names[-2],
            dp_names[1],
            dp_names[0],
        )
        self.first = own_names[-1]
        used = (self.core, self.second, self.near, self.far, self.first)
        self.extra = tuple(n for n in dp_names + own_names if n not in used)

    def index(self, names):
        value = jnp.int32(0)
        for name in names:
            value = value * 2 + lax.axis_index(name)
        return value

    def layer(self):
        return self.index((self.near, self.second, self.first))


def transposed_dot(a, b, precision=None):
    return lax.dot_general(
        a, b, (((0,), (0,)), ((), ())), precision=precision, preferred_element_type=jnp.float32
    )


AHEAD = 5


def layer_copies(place, sources, buffers, sems):
    layer = place.layer()
    return [
        [
            pltpu.make_async_copy(
                source.at[jnp.bitwise_xor(layer, i)], buffer.at[i], sems.at[i, s]
            )
            for s, (source, buffer) in enumerate(zip(sources, buffers))
        ]
        for i in range(buffers[0].shape[0])
    ]


def both_halves(place, flat, i):
    rows = flat.shape[1] // 2
    core = lax.axis_index(place.core)
    kept = pl.multiple_of(core * rows, PANEL)
    sent = pl.multiple_of((1 - core) * rows, PANEL)
    return flat[i, pl.ds(kept, rows), :], flat[i, pl.ds(sent, rows), :]


ORDERS = (("second", "near", "first"), ("first", "second", "near"))
LATE_ORDERS = (("first", "second", "near"), ("second", "near", "first"))


def position(axes, i):
    bits = {"near": i // 4, "second": (i // 2) % 2, "first": i % 2}
    return bits[axes[0]] * 4 + bits[axes[1]] * 2 + bits[axes[2]]


def positions(place, i, orders):
    core = lax.axis_index(place.core)
    first, second = (position(axes, i) for axes in orders)
    return jnp.where(core == 0, first, second), jnp.where(core == 0, second, first)


def iotas(shape):
    return (
        lax.broadcasted_iota(jnp.int32, shape, 0),
        lax.broadcasted_iota(jnp.int32, shape, 1),
    )


def pack_pair(first, second):
    row, col = iotas(first.shape)
    return jnp.where(row >= col, first, second)


def unpack_pair(packed, second_diagonal):
    row, col = iotas(packed.shape)
    turned = packed.T
    first = jnp.where(row >= col, packed, turned)
    second = jnp.where(col > row, packed, turned)
    return first, jnp.where(row == col, second_diagonal, second)


def fold(block):
    h = block.shape[0] // 2
    row, col = iotas((h, 2 * h))
    last = pltpu.roll(block[h:], h, 1)
    return jnp.where((col >= h) | (row >= col), block[:h], last)


def unfold(folded, diagonal):
    h, n = folded.shape
    row, col = iotas((n, n))
    block = jnp.concatenate([folded, jnp.zeros((h, n), jnp.float32)], axis=0)
    turned = block.T
    top = jnp.where((col >= h) | (col <= row), block, turned)
    moved = pltpu.roll(pltpu.roll(block, h, 0), h, 1)
    moved_turned = pltpu.roll(pltpu.roll(turned, h, 0), h, 1)
    last = jnp.where(col > row, moved, moved_turned)
    last = jnp.where(row == col, diagonal, last)
    return jnp.where(row < h, top, jnp.where(col < h, turned, last))


def diagonals(blocks, rows):
    n = blocks[0].shape[0]
    row, col = iotas((n, n))
    slab_row, _ = iotas((rows, n))
    slab = jnp.zeros((rows, n), jnp.float32)
    for i, block in enumerate(blocks):
        line = jnp.sum(jnp.where(row == col, block, 0.0), axis=0, keepdims=True)
        slab = jnp.where(slab_row == i, jnp.broadcast_to(line, (rows, n)), slab)
    return slab


EARLY_ROWS = 144
LATE_ROWS = 192


HOT = (1, 2, 3, 5, 6, 7)
COLD = (0, 4)


def square_sums(wide, narrow):
    return transposed_dot(wide, wide), transposed_dot(narrow, narrow)


def pack_layer(place, i, wcov, ncov, a_flat, b_flat):
    n = LANES
    last = wcov[n:, n:]
    a_flat[i, :n] = pack_pair(wcov[:n, :n], ncov)
    a_flat[i, n:] = diagonals((ncov, last), EARLY_ROWS - n)
    b_flat[i, :n] = wcov[:n, n:]
    b_flat[i, n:] = fold(last)
    a_kept, a_sent = both_halves(place, a_flat, i)
    b_kept, b_sent = both_halves(place, b_flat, i)
    return (a_kept, b_kept), (a_sent, b_sent)


def put(ref, index, parts):
    rows = EARLY_ROWS // 2
    ref[index, :rows] = parts[0]
    ref[index, rows:] = parts[1]


def put_layer(place, i, sums, a_flat, b_flat, keep, send):
    kept, sent = pack_layer(place, i, *sums, a_flat, b_flat)
    mine, other = positions(place, i, ORDERS)
    put(keep, mine, kept)
    put(send, other, sent)


def clear_others(place, layers, keep, send):
    for i in layers:
        mine, other = positions(place, i, ORDERS)
        keep[mine] = jnp.zeros(keep.shape[1:], jnp.float32)
        send[other] = jnp.zeros(send.shape[1:], jnp.float32)


def hot_kernel(place, wide_hbm, narrow_hbm, keep, send, wides, narrows, a_flat, b_flat, sems):
    copies = layer_copies(place, (wide_hbm, narrow_hbm), (wides, narrows), sems)
    order = HOT + COLD
    for i in order[:AHEAD]:
        for copy in copies[i]:
            copy.start()
    clear_others(place, COLD, keep, send)

    def pack(i, sums):
        put_layer(place, i, sums, a_flat, b_flat, keep, send)

    before = None
    for at, i in enumerate(order):
        for copy in copies[i]:
            copy.wait()
        if at + AHEAD < len(order):
            for copy in copies[order[at + AHEAD]]:
                copy.start()
        if before is not None:
            pack(*before)
            before = None
        if i in HOT:
            before = (i, square_sums(wides[i], narrows[i]))


def cold_kernel(place, wides, narrows, keep, send, a_flat, b_flat):
    for i in COLD:
        put_layer(
            place, i, square_sums(wides[i], narrows[i]), a_flat, b_flat, keep, send
        )
    core = lax.axis_index(place.core)
    stay = [[i for i in HOT if position(axes, i) < 4] for axes in ORDERS]
    for first, second in zip(*stay):
        here = [position(axes, i) for axes, i in zip(ORDERS, (first, second))]
        mine = jnp.where(core == 0, here[0], here[1])
        other = jnp.where(core == 0, here[1], here[0])
        keep[mine] = jnp.zeros(keep.shape[1:], jnp.float32)
        send[other] = jnp.zeros(send.shape[1:], jnp.float32)


def write_slots(place, owner_map, slots_ref):
    own = place.index(place.own)
    count = jnp.int32(0)
    for l in range(slots_ref.shape[0]):
        mine = owner_map[l] == own
        slot = jnp.where(mine, count, -1)
        slots_ref[l] = jnp.full(slots_ref.shape[1:], 0, jnp.int32) + slot
        count = count + mine.astype(jnp.int32)


def mixed_kernel(place, owner_map, wides, narrows, keep, send, slots_ref, flat):
    n = LANES
    write_slots(place, owner_map, slots_ref)
    for i in range(wides.shape[0]):
        mixed = transposed_dot(narrows[i], wides[i])
        flat[i, :n] = mixed[:, :n]
        flat[i, n:] = mixed[:, n:]
        kept, sent = both_halves(place, flat, i)
        mine, other = positions(place, i, LATE_ORDERS)
        keep[mine] = kept
        send[other] = sent


def gram_cost(wide_rows, columns):
    return pl.CostEstimate(
        flops=2 * wide_rows.size * columns, bytes_accessed=2 * wide_rows.size, transcendentals=0
    )


HALF_ROWS = (EARLY_ROWS + LATE_ROWS) // 2


def pack_shapes(layers):
    return [
        pltpu.VMEM((layers, EARLY_ROWS, LANES), jnp.float32),
        pltpu.VMEM((layers, LATE_ROWS, LANES), jnp.float32),
    ]


def hot_squares(place, wide_rows, narrow_rows):
    layers = wide_rows.shape[0]
    half = jax.ShapeDtypeStruct((layers, HALF_ROWS, LANES), jnp.float32)
    return pl.pallas_call(
        functools.partial(hot_kernel, place),
        in_specs=[HBM, HBM],
        out_specs=[VMEM] * 4,
        out_shape=[
            half,
            half,
            jax.ShapeDtypeStruct(wide_rows.shape, wide_rows.dtype),
            jax.ShapeDtypeStruct(narrow_rows.shape, narrow_rows.dtype),
        ],
        scratch_shapes=[*pack_shapes(layers), pltpu.SemaphoreType.DMA((layers, 2))],
        cost_estimate=gram_cost(wide_rows, 240),
        compiler_params=PARAMS,
        name="hot_squares",
    )(
        pltpu.with_memory_space_constraint(wide_rows, pltpu.HBM),
        pltpu.with_memory_space_constraint(narrow_rows, pltpu.HBM),
    )


def cold_squares(place, wides, narrows):
    half = jax.ShapeDtypeStruct((wides.shape[0] // 2, HALF_ROWS, LANES), jnp.float32)
    return pl.pallas_call(
        functools.partial(cold_kernel, place),
        in_specs=[VMEM, VMEM],
        out_specs=[VMEM, VMEM],
        out_shape=[half, half],
        scratch_shapes=pack_shapes(wides.shape[0]),
        cost_estimate=gram_cost(wides, 80),
        compiler_params=PARAMS,
        name="cold_squares",
    )(wides, narrows)


def mixed_sums(place, owner_map, wides, narrows):
    layers, _, narrow = narrows.shape
    half = jax.ShapeDtypeStruct((layers, narrow, LANES), jnp.float32)
    return pl.pallas_call(
        functools.partial(mixed_kernel, place),
        in_specs=[SMEM, VMEM, VMEM],
        out_specs=[VMEM] * 3,
        out_shape=[half, half, jax.ShapeDtypeStruct((layers, PANEL, LANES), jnp.int32)],
        scratch_shapes=[pltpu.VMEM((layers, 2 * narrow, LANES), jnp.float32)],
        cost_estimate=gram_cost(wides, 128),
        compiler_params=PARAMS,
        name="mixed",
    )(owner_map, wides, narrows)


def lane_gather(x, index):
    return jnp.take_along_axis(x, index, axis=1, mode="promise_in_bounds")


def trailing_update(a_ref, left_ref, right_ref, base):
    size = a_ref.shape[1]
    a_ref[pl.ds(pl.multiple_of(base, BLOCK), BLOCK), :] = jnp.zeros((BLOCK, size), jnp.float32)
    lane = lax.broadcasted_iota(jnp.int32, (1, size), 1)
    swept = (lane >= base - BLOCK) & (lane < base)
    update = transposed_dot(left_ref[...], right_ref[...])
    a_ref[BLOCK : BLOCK + size, :] = (
        jnp.where(swept, 0.0, a_ref[BLOCK : BLOCK + size, :]) - update
    )


def in_three(x):
    high = x.astype(jnp.bfloat16).astype(jnp.float32)
    rest = x - high
    middle = rest.astype(jnp.bfloat16).astype(jnp.float32)
    return high, middle, rest - middle


def factor_panel(rows_ref, cols_ref, tile, first, panel, targets):
    tiles = panel.shape[1] // LANES
    shape = (PANEL, LANES)
    _, lane = iotas(shape)

    def on_all(ref, k, lanes):
        return jnp.broadcast_to(ref[k : k + 1, lanes], shape)

    rows_ref[...] = panel
    lanes = [slice(LANES * t, LANES * (t + 1)) for t in range(tiles)]
    rows = [[on_all(rows_ref, k, part) for part in lanes] for k in range(PANEL)]
    here = panel[:, lanes[tile]]
    for j in range(PANEL):
        column = lane_gather(here, jnp.full(shape, 0, jnp.int32) + (first + j))
        cols_ref[PANEL * j : PANEL * (j + 1)] = column
    d = [[None] * PANEL for _ in range(PANEL)]
    for j in range(PANEL):
        for i in range(j, PANEL):
            d[i][j] = on_all(cols_ref, PANEL * j + i, slice(None))
    own = (lane >= first) & (lane < first + PANEL)
    q = [[None] * tiles for _ in range(PANEL)]
    p = [[None] * tiles for _ in range(PANEL)]
    weights = [[None] * PANEL for _ in targets]
    factor = [[None] * PANEL for _ in range(PANEL)]

    def substitute(k, scale):
        for t in range(tiles):
            value = rows[k][t]
            if t == tile:
                value = jnp.where(own, jnp.where(lane == first + k, -1.0, 0.0), value)
            for j in range(k):
                value = value - factor[k][j] * q[j][t]
            q[k][t] = value
            p[k][t] = value * scale
        for target, weight in zip(targets, weights):
            source, index = target(rows[k])
            value = lane_gather(source, index)
            for j in range(k):
                value = value - factor[k][j] * weight[j]
            weight[k] = value

    for k in range(0, PANEL, 2):
        m = k + 1
        a, b, c = d[k][k], d[m][k], d[m][m]
        first_scale = 1.0 / a
        second_scale = a * (1.0 / (a * c - b * b))
        factor[m][k] = b * first_scale
        left_over = {i: d[i][m] - d[i][k] * factor[m][k] for i in range(k + 2, PANEL)}
        for i in range(k + 2, PANEL):
            factor[i][k] = d[i][k] * first_scale
            factor[i][m] = left_over[i] * second_scale
        for i in range(k + 2, PANEL):
            for j in range(k + 2, i + 1):
                value = d[i][j] - d[i][k] * factor[j][k]
                d[i][j] = value - (left_over[i] * left_over[j]) * second_scale
        substitute(k, first_scale)
        substitute(m, second_scale)
    return q, p, weights


def packed_rows(values):
    sub, _ = iotas((PANEL, LANES))
    whole = []
    for t in range(len(values[0])):
        value = values[0][t]
        for k in range(1, PANEL):
            value = jnp.where(sub == k, values[k][t], value)
        whole.append(value)
    return whole


def side_by_side(tiles):
    return jnp.concatenate(tiles, axis=1) if len(tiles) > 1 else tiles[0]


def sweep_block(a_ref, left_ref, right_ref, a_rows, a_cols, b_rows, b_cols, tile, step, block):
    size = a_ref.shape[1]
    tiles = size // LANES
    first = step * BLOCK
    second = first + PANEL
    base = tile * LANES + first
    trailing_update(a_ref, left_ref, right_ref, base)

    sub, lane = iotas((PANEL, LANES))
    last = first == LANES - BLOCK
    next_first = jnp.where(last, 0, first + BLOCK)

    def in_block(row):
        return row[tile], second + sub

    def in_next(offset):
        def target(row):
            source = row[tile]
            if tile + 1 < tiles:
                source = jnp.where(last, row[tile + 1], source)
            return source, next_first + offset + sub

        return target

    nexts = [in_next(0), in_next(PANEL)]
    in_a = (lane >= first) & (lane < second)
    in_b = (lane >= second) & (lane < second + PANEL)

    def swept(tiles_of, mask):
        return [jnp.where(mask, 0.0, v) if t == tile else v for t, v in enumerate(tiles_of)]

    def minus(tiles_of, weight, p):
        result = []
        for t, value in enumerate(tiles_of):
            for k in range(PANEL):
                value = value - weight[k] * p[k][t]
            result.append(value)
        return result

    def by_tile(rows):
        return [rows[:, LANES * t : LANES * (t + 1)] for t in range(tiles)]

    qa, pa, (to_b, *to_next_a) = factor_panel(
        a_rows, a_cols, tile, first, block[:PANEL], [in_block, *nexts]
    )
    panel_b = side_by_side(minus(swept(by_tile(block[PANEL:]), in_a), to_b, pa))
    qb, pb, to_next_b = factor_panel(b_rows, b_cols, tile, second, panel_b, nexts)

    left, right = [], []
    for q, p, mask in ((qa, pa, in_b), (qb, pb, None)):
        q, p = packed_rows(q), packed_rows(p)
        if mask is not None:
            q, p = swept(q, mask), swept(p, mask)
        qs, ps = in_three(side_by_side(q)), in_three(side_by_side(p))
        left += [qs[i] for i in (0, 0, 1, 1, 0, 2)]
        right += [ps[i] for i in (0, 1, 0, 1, 2, 0)]
    left_ref[...] = jnp.concatenate(left, axis=0).astype(jnp.bfloat16)
    right_ref[...] = jnp.concatenate(right, axis=0).astype(jnp.bfloat16)

    following = a_ref[pl.ds(pl.multiple_of(base + 2 * BLOCK, BLOCK), BLOCK), :]
    result = []
    for g in range(2):
        rows = by_tile(following[g * PANEL : (g + 1) * PANEL])
        rows = minus(swept(rows, in_a), to_next_a[g], pa)
        rows = minus(swept(rows, in_b), to_next_b[g], pb)
        result.append(side_by_side(rows))
    return jnp.concatenate(result, axis=0)


def place_halves(place, pieces, first_row, flat):
    core = lax.axis_index(place.core)
    rows = flat.shape[0] // 2
    for r, piece in enumerate(pieces):
        start = pl.multiple_of(jnp.bitwise_xor(core, r) * rows, PANEL)
        flat[pl.ds(start, rows), :] = piece[first_row : first_row + rows]


def sweep_cost():
    return pl.CostEstimate(flops=1 << 30, bytes_accessed=1 << 20, transcendentals=0)


def clear(work):
    a_ref, left, right = work[:3]
    size = a_ref.shape[1]
    a_ref[:BLOCK] = jnp.zeros((BLOCK, size), jnp.float32)
    a_ref[BLOCK + size :] = jnp.zeros((BLOCK, size), jnp.float32)
    left[...] = jnp.zeros(left.shape, left.dtype)
    right[...] = jnp.zeros(right.shape, right.dtype)


def work_shapes(size):
    splits = 6 * BLOCK
    return [
        pltpu.VMEM((size + 2 * BLOCK, size), jnp.float32),
        pltpu.VMEM((splits, size), jnp.bfloat16),
        pltpu.VMEM((splits, size), jnp.bfloat16),
    ]


def row_shapes(size):
    return [
        pltpu.VMEM((PANEL, size), jnp.float32),
        pltpu.VMEM((PANEL * PANEL, LANES), jnp.float32),
    ] * 2


def aligned_rows(ref, index, count):
    if count % PANEL == 0:
        return ref[pl.ds(pl.multiple_of(index * count, count), count), :]
    per_slab = PANEL // count
    slab = ref[pl.ds(pl.multiple_of(index // per_slab * PANEL, PANEL), PANEL), :]
    value = slab[:count]
    for i in range(1, per_slab):
        value = jnp.where(index % per_slab == i, slab[i * count : (i + 1) * count], value)
    return value


def packs(cols, rows):
    return cols == 2 * PANEL and 2 * rows == LANES


def dot(a, b, last=False):
    return lax.dot_general(
        a,
        b,
        (((1,), (1 if last else 0,)), ((), ())),
        precision=HIGHEST,
        preferred_element_type=jnp.float32,
    )


STEPS = LANES // BLOCK
FIRST_STEPS = 5
SECOND_STEPS = 6


def sweep_both(wide_work, narrow_work, begin, end, blocks):
    def step(i, blocks):
        return (
            sweep_block(*wide_work, 0, i, blocks[0]),
            sweep_block(*narrow_work, 0, i, blocks[1]),
        )

    return lax.fori_loop(begin, end, step, blocks)


def sweep_wide(work, begin, end, block):
    return lax.fori_loop(begin, end, lambda i, block: sweep_block(*work, 1, i, block), block)


def unit_scale(block):
    row, col = iotas(block.shape)
    line = jnp.sum(jnp.where(row == col, block, 0.0), axis=0, keepdims=True)
    return jnp.broadcast_to(lax.rsqrt(line), (PANEL, block.shape[1]))


def on_rows(scale):
    n = scale.shape[1]
    return jnp.broadcast_to(scale[:1], (n, n))


def scaled(block, down, across):
    return (block * on_rows(down).T) * on_rows(across)


def first_kernel(
    place, total, mine, other, wa, wl, wr, wp, na, nl, nr, np_, ws_ref, ns_ref, *refs
):
    a_flat, b_flat = refs[:2]
    wide_work, narrow_work = (wa, wl, wr, *refs[2:6]), (na, nl, nr, *refs[6:])
    place_halves(place, (mine, other), 0, a_flat)
    place_halves(place, (mine, other), a_flat.shape[0] // 2, b_flat)
    n = LANES
    slab = a_flat[n : n + PANEL]
    first, square = unpack_pair(a_flat[:n], jnp.broadcast_to(slab[:1], (n, n)))
    corner = b_flat[:n] / total
    last = unfold(b_flat[n:], jnp.broadcast_to(slab[1:2], (n, n)))
    row, col = iotas((n, n))
    damp = jnp.where(row == col, DAMP, 0.0)
    clear(wide_work)
    clear(narrow_work)
    first, last, square = first / total + damp, last / total + damp, square / total + damp
    by_first, by_last, by_square = (unit_scale(block) for block in (first, last, square))
    ws_ref[:, :n] = by_first
    ws_ref[:, n:] = by_last
    ns_ref[...] = by_square
    first_across, last_across = on_rows(by_first), on_rows(by_last)
    first_down, last_down = first_across.T, last_across.T
    corner = (corner * first_down) * last_across
    wa[BLOCK : BLOCK + n, :n] = (first * first_down) * first_across
    wa[BLOCK : BLOCK + n, n:] = corner
    wa[BLOCK + n : BLOCK + 2 * n, :n] = corner.T
    wa[BLOCK + n : BLOCK + 2 * n, n:] = (last * last_down) * last_across
    na[BLOCK : BLOCK + n, :] = scaled(square, by_square, by_square)
    start = (wa[BLOCK : 2 * BLOCK, :], na[BLOCK : 2 * BLOCK, :])
    wp[...], np_[...] = sweep_both(wide_work, narrow_work, 0, FIRST_STEPS, start)


def second_kernel(*refs):
    given, scale, ninv_ref, state, narrow_state, wide_rows, narrow_rows = (
        refs[:8],
        refs[8],
        refs[9],
        refs[10:14],
        refs[14:17],
        refs[17:21],
        refs[21:],
    )
    for source, target in zip((*given[:3], *given[4:7]), (*state[:3], *narrow_state)):
        target[...] = source[...]
    wide_work, narrow_work = (*state[:3], *wide_rows), (*narrow_state, *narrow_rows)
    wp = state[3]
    panels = (given[3][...], given[7][...])
    panel, _ = sweep_both(wide_work, narrow_work, FIRST_STEPS, STEPS, panels)
    trailing_update(*narrow_work[:3], LANES)
    by_square = scale[...]
    ninv_ref[...] = scaled(-narrow_work[0][BLOCK : BLOCK + LANES, :], by_square, by_square)
    wp[...] = sweep_wide(wide_work, 0, SECOND_STEPS, panel)


def third_kernel(wa_in, wl_in, wr_in, panel_in, scale, winv, wa, wl, wr, *rows):
    wa[...] = wa_in[...]
    wl[...] = wl_in[...]
    wr[...] = wr_in[...]
    sweep_wide((wa, wl, wr, *rows), SECOND_STEPS, STEPS, panel_in[...])
    wide = wa.shape[1]
    trailing_update(wa, wl, wr, wide)
    parts = [slice(i, i + LANES) for i in range(0, wide, LANES)]
    across = [on_rows(scale[:, i]) for i in parts]
    down = [block.T for block in across]
    for i, rows_scale in zip(parts, down):
        for j, columns_scale in zip(parts, across):
            block = -wa[BLOCK + i.start : BLOCK + i.stop, j]
            winv[i, j] = (block * rows_scale) * columns_scale


def state_shapes(size):
    shapes = [jax.ShapeDtypeStruct(v.shape, v.dtype) for v in work_shapes(size)]
    return shapes + [jax.ShapeDtypeStruct((BLOCK, size), jnp.float32)]


def sweep_call(kernel, name, args, out_shapes, scratch):
    return pl.pallas_call(
        kernel,
        in_specs=[VMEM] * len(args),
        out_specs=[VMEM] * len(out_shapes),
        out_shape=out_shapes,
        scratch_shapes=scratch,
        cost_estimate=sweep_cost(),
        compiler_params=PARAMS,
        name=name,
    )(*args)


def first_panels(place, pieces, wide, narrow, total):
    return sweep_call(
        functools.partial(first_kernel, place, total),
        "first_panels",
        pieces,
        state_shapes(wide)
        + state_shapes(narrow)
        + [jax.ShapeDtypeStruct((PANEL, n), jnp.float32) for n in (wide, narrow)],
        [
            pltpu.VMEM((EARLY_ROWS, LANES), jnp.float32),
            pltpu.VMEM((LATE_ROWS, LANES), jnp.float32),
            *row_shapes(wide),
            *row_shapes(narrow),
        ],
    )


def second_panels(state, wide, narrow):
    ninv = jax.ShapeDtypeStruct((narrow, narrow), jnp.float32)
    return sweep_call(
        second_kernel,
        "second_panels",
        state,
        [ninv] + state_shapes(wide),
        [*work_shapes(narrow), *row_shapes(wide), *row_shapes(narrow)],
    )


def third_panels(state, wide):
    winv = jax.ShapeDtypeStruct((wide, wide), jnp.float32)
    scratch = [*work_shapes(wide), *row_shapes(wide)]
    return sweep_call(third_kernel, "third_panels", state, [winv], scratch)[0]


def product_kernel(place, total, rows, winv, ninv_ref, mine, other, out_ref, flat):
    place_halves(place, (mine, other), 0, flat)
    ninv = ninv_ref[...]
    n = LANES
    inner = jnp.concatenate(
        [
            transposed_dot(flat[c * n : (c + 1) * n] / total, ninv, HIGHEST)
            for c in range(2)
        ],
        axis=0,
    )
    wide = winv.shape[1]
    cols = wide // 2 ** len(place.dp)
    near, second = lax.axis_index(place.near), lax.axis_index(place.second)
    near_stride = 2 ** (len(place.dp) - 2)
    base = place.index(place.dp) - near * near_stride - second * 2
    _, lane = iotas((PANEL, LANES))
    picks = [
        aligned_rows(winv, base + (j // 2) * near_stride + (j % 2) * 2, cols) for j in range(4)
    ]
    if cols % PANEL == 0:
        whole = dot(jnp.concatenate(picks, axis=0), inner)
        updates = [whole[j * cols : (j + 1) * cols] for j in range(4)]
    else:
        updates = [dot(picked, inner) for picked in picks]
    for j, (picked, update) in enumerate(zip(picks, updates)):
        for x in range(2):
            block = 2 * j + x
            out_ref[block, :cols] = picked[:, :LANES]
            out_ref[block, cols : 2 * cols] = picked[:, LANES:]
            if packs(cols, rows):
                upper, lower = update[:PANEL], update[PANEL:]
                if x == 0:
                    lower = pltpu.roll(lower, rows, 1)
                else:
                    upper = pltpu.roll(upper, rows, 1)
                out_ref[block, 2 * cols :] = jnp.where(lane < rows, upper, lower)
            else:
                out_ref[block, 2 * cols :] = update


def products(place, winv, ninv, pieces, rows, total):
    wide, narrow = winv.shape[0], ninv.shape[0]
    cols = wide // 2 ** len(place.dp)
    height = 2 * cols + (PANEL if packs(cols, rows) else cols)
    return pl.pallas_call(
        functools.partial(product_kernel, place, total, rows),
        in_specs=[VMEM] * 4,
        out_specs=VMEM,
        out_shape=jax.ShapeDtypeStruct((8, height, LANES), jnp.float32),
        scratch_shapes=[pltpu.VMEM((2 * narrow, LANES), jnp.float32)],
        compiler_params=PARAMS,
        name="products",
    )(winv, ninv, *pieces)


def placing_kernel(place, slots_ref, got_ref, kept_ref, update_ref):
    layers = got_ref.shape[0]
    slots, cols, wide = kept_ref.shape
    rows = update_ref.shape[2]
    own, dp = place.index(place.own), place.index(place.dp)
    step = min(cols, PANEL)
    row, col = iotas((step, LANES))
    for h in range(wide // LANES):
        lanes = slice(h * LANES, (h + 1) * LANES)
        for r in range(0, cols, step):
            here = h * cols + r
            empty = jnp.where(col + h * LANES == row + dp * cols + r, 1.0 / DAMP, 0.0)
            for c in range(slots):
                value = empty
                for l in range(layers):
                    taken = slots_ref[l, :step] == c
                    value = jnp.where(taken, got_ref[l, here : here + step], value)
                kept_ref[c, r : r + step, lanes] = value
    for l in range(layers):
        value = got_ref[l, 2 * cols :]
        if packs(cols, rows):
            update_ref[l, :PANEL] = value[:, :rows]
            update_ref[l, PANEL:] = value[:, rows:]
        else:
            part = value[:, :rows]
            for p in range(1, LANES // rows):
                part = jnp.where(own == p, value[:, p * rows : (p + 1) * rows], part)
            update_ref[l] = part


def placing(place, slots_of, got, wide, cols, slots, rows):
    layers = got.shape[0]
    return pl.pallas_call(
        functools.partial(placing_kernel, place),
        in_specs=[VMEM, VMEM],
        out_specs=[VMEM, VMEM],
        out_shape=[
            jax.ShapeDtypeStruct((slots, cols, wide), jnp.float32),
            jax.ShapeDtypeStruct((layers, cols, rows), jnp.float32),
        ],
        compiler_params=PARAMS,
        name="placing",
    )(slots_of, got)


def swap(value, axis):
    return lax.ppermute(value, axis, [(0, 1), (1, 0)])


def swap_by_core(value, place, stage, orders):
    names = (place.near, place.second, place.core, place.first)
    flips = {"near": 8, "second": 4, "first": 1}
    pairs = [(i, i ^ flips[orders[(i >> 1) & 1][stage]]) for i in range(16)]
    return lax.ppermute(value, names, pairs)


def after(value, *others):
    return lax.optimization_barrier((value,) + others)[0]


def on_device(place, wide_rows, narrow_rows, owner_map):
    layers, rows, wide = wide_rows.shape
    narrow = narrow_rows.shape[2]
    n_dp, n_own = 2 ** len(place.dp), 2 ** len(place.own)
    total = float(rows * n_dp * n_own)

    h_keep, h_send, wides, narrows = hot_squares(place, wide_rows, narrow_rows)
    first_send = h_send[4:]
    h_got = swap(first_send, place.core)
    c_keep, c_send = cold_squares(place, after(wides, first_send), narrows)
    h_keep, c_send = lax.optimization_barrier((h_keep, c_send))

    hot = h_keep[4:] + h_got
    s_got = swap_by_core(hot, place, 0, ORDERS)
    m_keep, m_send, slots_of = mixed_sums(place, owner_map, after(wides, hot), narrows)
    c_got = swap(after(c_send + h_send[:4], m_send), place.core)
    m_got = swap(m_send, place.core)

    s = (c_keep + h_keep[:4]) + s_got
    s = s + after(c_got, s)
    s_got = swap_by_core(s[2:], place, 1, ORDERS)
    m = after(m_keep, s) + m_got
    m_got = swap_by_core(m[4:], place, 0, LATE_ORDERS)

    s = s[:2] + s_got
    s_got = swap_by_core(s[1], place, 2, ORDERS)
    m = after(m[:4], s) + m_got
    m_got = swap_by_core(m[2:], place, 1, LATE_ORDERS)

    s = s[0] + s_got
    if place.extra:
        s = lax.psum(s, place.extra)
    s_got = swap(s, place.far)
    m = after(m[:2], s) + m_got
    m_got = swap_by_core(m[1], place, 2, LATE_ORDERS)

    s = s + s_got
    state = first_panels(place, [s, swap(s, place.core)], wide, narrow, total)
    m = after(m[0], state[0]) + m_got
    if place.extra:
        m = lax.psum(m, place.extra)
    m_got = swap(m, place.far)
    *state, wide_scale, narrow_scale = state
    ninv, *state = second_panels([*state, narrow_scale], wide, narrow)
    m = after(m, ninv) + m_got
    m_got = swap(m, place.core)
    winv = third_panels([*state, wide_scale], wide)
    cols, own_rows = wide // n_dp, narrow // n_own
    sent = products(place, winv, ninv, [m, m_got], own_rows, total)
    got = lax.all_to_all(sent, (place.near, place.second, place.first), 0, 0)
    kept, update = placing(
        place, slots_of, got, wide, cols, layers // n_own + 1, own_rows
    )
    return (jnp.swapaxes(kept, 1, 2), jnp.swapaxes(update, 1, 2))


def solution(mesh):
    n_dp, n_own = mesh.shape["dp"], mesh.shape["own"]
    dp_names = tuple(f"dp{i}" for i in range(int(np.log2(n_dp))))
    own_names = tuple(f"own{i}" for i in range(int(np.log2(n_own))))
    names = dp_names + own_names
    bits = jax.sharding.Mesh(mesh.devices.reshape((2,) * len(names)), names)
    in_specs = (P(None, names, None), P(None, names, None), P())
    out_specs = (P(own_names, None, dp_names), P(None, own_names, dp_names))
    return jax.shard_map(
        functools.partial(on_device, Place(dp_names, own_names)),
        mesh=bits,
        in_specs=in_specs,
        out_specs=out_specs,
        check_vma=False,
    )
```

```python
import functools

import jax
import jax.numpy as jnp
import numpy as np
from jax import lax
from jax.experimental import pallas as pl
from jax.experimental.pallas import tpu as pltpu
from jax.sharding import PartitionSpec as P

DAMP = 0.5
LANES = 128
PANEL = 8
BLOCK = 2 * PANEL
VMEM_LIMIT = 48 * 1024 * 1024
HIGHEST = lax.Precision.HIGHEST
VMEM = pl.BlockSpec(memory_space=pltpu.VMEM)
SMEM = pl.BlockSpec(memory_space=pltpu.SMEM)
HBM = pl.BlockSpec(memory_space=pltpu.HBM)
PARAMS = pltpu.CompilerParams(vmem_limit_bytes=VMEM_LIMIT)


class Place:
    def __init__(self, dp_names, own_names):
        self.dp, self.own = dp_names, own_names
        self.core, self.second, self.near, self.far = (
            dp_names[-1],
            dp_names[-2],
            dp_names[1],
            dp_names[0],
        )
        self.first = own_names[-1]
        used = (self.core, self.second, self.near, self.far, self.first)
        self.extra = tuple(n for n in dp_names + own_names if n not in used)

    def index(self, names):
        value = jnp.int32(0)
        for name in names:
            value = value * 2 + lax.axis_index(name)
        return value

    def layer(self):
        return self.index((self.near, self.second, self.first))


def transposed_dot(a, b, precision=None):
    return lax.dot_general(
        a, b, (((0,), (0,)), ((), ())), precision=precision, preferred_element_type=jnp.float32
    )


AHEAD = 5


def layer_copies(place, sources, buffers, sems):
    layer = place.layer()
    return [
        [
            pltpu.make_async_copy(
                source.at[jnp.bitwise_xor(layer, i)], buffer.at[i], sems.at[i, s]
            )
            for s, (source, buffer) in enumerate(zip(sources, buffers))
        ]
        for i in range(buffers[0].shape[0])
    ]


def both_halves(place, flat, i):
    rows = flat.shape[1] // 2
    core = lax.axis_index(place.core)
    kept = pl.multiple_of(core * rows, PANEL)
    sent = pl.multiple_of((1 - core) * rows, PANEL)
    return flat[i, pl.ds(kept, rows), :], flat[i, pl.ds(sent, rows), :]


ORDERS = (("first", "second", "near"), ("second", "near", "first"))
LATE_ORDERS = (("first", "second", "near"), ("near", "first", "second"))


def position(axes, i):
    bits = {"near": i // 4, "second": (i // 2) % 2, "first": i % 2}
    return bits[axes[0]] * 4 + bits[axes[1]] * 2 + bits[axes[2]]


def positions(place, i, orders):
    core = lax.axis_index(place.core)
    first, second = (position(axes, i) for axes in orders)
    return jnp.where(core == 0, first, second), jnp.where(core == 0, second, first)


def iotas(shape):
    return (
        lax.broadcasted_iota(jnp.int32, shape, 0),
        lax.broadcasted_iota(jnp.int32, shape, 1),
    )


def pack_pair(first, second):
    row, col = iotas(first.shape)
    return jnp.where(row >= col, first, second)


def unpack_pair(packed, second_diagonal):
    row, col = iotas(packed.shape)
    turned = packed.T
    first = jnp.where(row >= col, packed, turned)
    second = jnp.where(col > row, packed, turned)
    return first, jnp.where(row == col, second_diagonal, second)


def fold(block):
    h = block.shape[0] // 2
    row, col = iotas((h, 2 * h))
    last = pltpu.roll(block[h:], h, 1)
    return jnp.where((col >= h) | (row >= col), block[:h], last)


def unfold(folded, diagonal):
    h, n = folded.shape
    row, col = iotas((n, n))
    block = jnp.concatenate([folded, jnp.zeros((h, n), jnp.float32)], axis=0)
    turned = block.T
    top = jnp.where((col >= h) | (col <= row), block, turned)
    moved = pltpu.roll(pltpu.roll(block, h, 0), h, 1)
    moved_turned = pltpu.roll(pltpu.roll(turned, h, 0), h, 1)
    last = jnp.where(col > row, moved, moved_turned)
    last = jnp.where(row == col, diagonal, last)
    return jnp.where(row < h, top, jnp.where(col < h, turned, last))


def diagonals(blocks, rows):
    n = blocks[0].shape[0]
    row, col = iotas((n, n))
    slab_row, _ = iotas((rows, n))
    slab = jnp.zeros((rows, n), jnp.float32)
    for i, block in enumerate(blocks):
        line = jnp.sum(jnp.where(row == col, block, 0.0), axis=0, keepdims=True)
        slab = jnp.where(slab_row == i, jnp.broadcast_to(line, (rows, n)), slab)
    return slab


EARLY_ROWS = 144
LATE_ROWS = 192


HOT = (1, 2, 3, 5, 6, 7)
COLD = (0, 4)


def square_sums(wide, narrow):
    return transposed_dot(wide, wide), transposed_dot(narrow, narrow)


def pack_layer(place, i, wcov, ncov, a_flat, b_flat):
    n = LANES
    last = wcov[n:, n:]
    a_flat[i, :n] = pack_pair(wcov[:n, :n], ncov)
    a_flat[i, n:] = diagonals((ncov, last), EARLY_ROWS - n)
    b_flat[i, :n] = wcov[:n, n:]
    b_flat[i, n:] = fold(last)
    a_kept, a_sent = both_halves(place, a_flat, i)
    b_kept, b_sent = both_halves(place, b_flat, i)
    return (a_kept, b_kept), (a_sent, b_sent)


def put(ref, index, parts):
    rows = EARLY_ROWS // 2
    ref[index, :rows] = parts[0]
    ref[index, rows:] = parts[1]


def put_layer(place, i, sums, a_flat, b_flat, keep, send):
    kept, sent = pack_layer(place, i, *sums, a_flat, b_flat)
    mine, other = positions(place, i, ORDERS)
    put(keep, mine, kept)
    put(send, other, sent)


def clear_others(place, layers, keep, send):
    for i in layers:
        mine, other = positions(place, i, ORDERS)
        keep[mine] = jnp.zeros(keep.shape[1:], jnp.float32)
        send[other] = jnp.zeros(send.shape[1:], jnp.float32)


def hot_kernel(place, wide_hbm, narrow_hbm, keep, send, wides, narrows, a_flat, b_flat, sems):
    copies = layer_copies(place, (wide_hbm, narrow_hbm), (wides, narrows), sems)
    order = HOT + COLD
    for i in order[:AHEAD]:
        for copy in copies[i]:
            copy.start()
    clear_others(place, COLD, keep, send)

    def pack(i, sums):
        put_layer(place, i, sums, a_flat, b_flat, keep, send)

    before = None
    for at, i in enumerate(order):
        for copy in copies[i]:
            copy.wait()
        if at + AHEAD < len(order):
            for copy in copies[order[at + AHEAD]]:
                copy.start()
        if before is not None:
            pack(*before)
            before = None
        if i in HOT:
            before = (i, square_sums(wides[i], narrows[i]))


def cold_kernel(place, wides, narrows, keep, send, a_flat, b_flat):
    for i in COLD:
        put_layer(
            place, i, square_sums(wides[i], narrows[i]), a_flat, b_flat, keep, send
        )
    core = lax.axis_index(place.core)
    stay = [[i for i in HOT if position(axes, i) < 4] for axes in ORDERS]
    for first, second in zip(*stay):
        here = [position(axes, i) for axes, i in zip(ORDERS, (first, second))]
        mine = jnp.where(core == 0, here[0], here[1])
        other = jnp.where(core == 0, here[1], here[0])
        keep[mine] = jnp.zeros(keep.shape[1:], jnp.float32)
        send[other] = jnp.zeros(send.shape[1:], jnp.float32)


def write_slots(place, owner_map, slots_ref):
    own = place.index(place.own)
    count = jnp.int32(0)
    for l in range(slots_ref.shape[0]):
        mine = owner_map[l] == own
        slot = jnp.where(mine, count, -1)
        slots_ref[l] = jnp.full(slots_ref.shape[1:], 0, jnp.int32) + slot
        count = count + mine.astype(jnp.int32)


def mixed_kernel(place, owner_map, wides, narrows, keep, send, slots_ref, flat):
    n = LANES
    write_slots(place, owner_map, slots_ref)
    for i in range(wides.shape[0]):
        mixed = transposed_dot(narrows[i], wides[i])
        flat[i, :n] = mixed[:, :n]
        flat[i, n:] = mixed[:, n:]
        kept, sent = both_halves(place, flat, i)
        mine, other = positions(place, i, LATE_ORDERS)
        keep[mine] = kept
        send[other] = sent


def gram_cost(wide_rows, columns):
    return pl.CostEstimate(
        flops=2 * wide_rows.size * columns, bytes_accessed=2 * wide_rows.size, transcendentals=0
    )


HALF_ROWS = (EARLY_ROWS + LATE_ROWS) // 2


def pack_shapes(layers):
    return [
        pltpu.VMEM((layers, EARLY_ROWS, LANES), jnp.float32),
        pltpu.VMEM((layers, LATE_ROWS, LANES), jnp.float32),
    ]


def hot_squares(place, wide_rows, narrow_rows):
    layers = wide_rows.shape[0]
    half = jax.ShapeDtypeStruct((layers, HALF_ROWS, LANES), jnp.float32)
    return pl.pallas_call(
        functools.partial(hot_kernel, place),
        in_specs=[HBM, HBM],
        out_specs=[VMEM] * 4,
        out_shape=[
            half,
            half,
            jax.ShapeDtypeStruct(wide_rows.shape, wide_rows.dtype),
            jax.ShapeDtypeStruct(narrow_rows.shape, narrow_rows.dtype),
        ],
        scratch_shapes=[*pack_shapes(layers), pltpu.SemaphoreType.DMA((layers, 2))],
        cost_estimate=gram_cost(wide_rows, 240),
        compiler_params=PARAMS,
        name="hot_squares",
    )(
        pltpu.with_memory_space_constraint(wide_rows, pltpu.HBM),
        pltpu.with_memory_space_constraint(narrow_rows, pltpu.HBM),
    )


def cold_squares(place, wides, narrows):
    half = jax.ShapeDtypeStruct((wides.shape[0] // 2, HALF_ROWS, LANES), jnp.float32)
    return pl.pallas_call(
        functools.partial(cold_kernel, place),
        in_specs=[VMEM, VMEM],
        out_specs=[VMEM, VMEM],
        out_shape=[half, half],
        scratch_shapes=pack_shapes(wides.shape[0]),
        cost_estimate=gram_cost(wides, 80),
        compiler_params=PARAMS,
        name="cold_squares",
    )(wides, narrows)


def mixed_sums(place, owner_map, wides, narrows):
    layers, _, narrow = narrows.shape
    half = jax.ShapeDtypeStruct((layers, narrow, LANES), jnp.float32)
    return pl.pallas_call(
        functools.partial(mixed_kernel, place),
        in_specs=[SMEM, VMEM, VMEM],
        out_specs=[VMEM] * 3,
        out_shape=[half, half, jax.ShapeDtypeStruct((layers, PANEL, LANES), jnp.int32)],
        scratch_shapes=[pltpu.VMEM((layers, 2 * narrow, LANES), jnp.float32)],
        cost_estimate=gram_cost(wides, 128),
        compiler_params=PARAMS,
        name="mixed",
    )(owner_map, wides, narrows)


def lane_gather(x, index):
    return jnp.take_along_axis(x, index, axis=1, mode="promise_in_bounds")


def trailing_update(a_ref, left_ref, right_ref, base):
    size = a_ref.shape[1]
    a_ref[pl.ds(pl.multiple_of(base, BLOCK), BLOCK), :] = jnp.zeros((BLOCK, size), jnp.float32)
    lane = lax.broadcasted_iota(jnp.int32, (1, size), 1)
    swept = (lane >= base - BLOCK) & (lane < base)
    update = transposed_dot(left_ref[...], right_ref[...])
    a_ref[BLOCK : BLOCK + size, :] = (
        jnp.where(swept, 0.0, a_ref[BLOCK : BLOCK + size, :]) - update
    )


def in_three(x):
    high = x.astype(jnp.bfloat16).astype(jnp.float32)
    rest = x - high
    middle = rest.astype(jnp.bfloat16).astype(jnp.float32)
    return high, middle, rest - middle


def factor_panel(rows_ref, cols_ref, tile, first, panel, targets):
    tiles = panel.shape[1] // LANES
    shape = (PANEL, LANES)
    _, lane = iotas(shape)

    def on_all(ref, k, lanes):
        return jnp.broadcast_to(ref[k : k + 1, lanes], shape)

    rows_ref[...] = panel
    lanes = [slice(LANES * t, LANES * (t + 1)) for t in range(tiles)]
    rows = [[on_all(rows_ref, k, part) for part in lanes] for k in range(PANEL)]
    here = panel[:, lanes[tile]]
    for j in range(PANEL):
        column = lane_gather(here, jnp.full(shape, 0, jnp.int32) + (first + j))
        cols_ref[PANEL * j : PANEL * (j + 1)] = column
    d = [[None] * PANEL for _ in range(PANEL)]
    for j in range(PANEL):
        for i in range(j, PANEL):
            d[i][j] = on_all(cols_ref, PANEL * j + i, slice(None))
    own = (lane >= first) & (lane < first + PANEL)
    q = [[None] * tiles for _ in range(PANEL)]
    p = [[None] * tiles for _ in range(PANEL)]
    weights = [[None] * PANEL for _ in targets]
    factor = [[None] * PANEL for _ in range(PANEL)]

    def substitute(k, scale):
        for t in range(tiles):
            value = rows[k][t]
            if t == tile:
                value = jnp.where(own, jnp.where(lane == first + k, -1.0, 0.0), value)
            for j in range(k):
                value = value - factor[k][j] * q[j][t]
            q[k][t] = value
            p[k][t] = value * scale
        for target, weight in zip(targets, weights):
            source, index = target(rows[k])
            value = lane_gather(source, index)
            for j in range(k):
                value = value - factor[k][j] * weight[j]
            weight[k] = value

    for k in range(0, PANEL, 2):
        m = k + 1
        a, b, c = d[k][k], d[m][k], d[m][m]
        first_scale = 1.0 / a
        second_scale = a * (1.0 / (a * c - b * b))
        factor[m][k] = b * first_scale
        left_over = {i: d[i][m] - d[i][k] * factor[m][k] for i in range(k + 2, PANEL)}
        for i in range(k + 2, PANEL):
            factor[i][k] = d[i][k] * first_scale
            factor[i][m] = left_over[i] * second_scale
        for i in range(k + 2, PANEL):
            for j in range(k + 2, i + 1):
                value = d[i][j] - d[i][k] * factor[j][k]
                d[i][j] = value - (left_over[i] * left_over[j]) * second_scale
        substitute(k, first_scale)
        substitute(m, second_scale)
    return q, p, weights


def packed_rows(values):
    sub, _ = iotas((PANEL, LANES))
    whole = []
    for t in range(len(values[0])):
        value = values[0][t]
        for k in range(1, PANEL):
            value = jnp.where(sub == k, values[k][t], value)
        whole.append(value)
    return whole


def side_by_side(tiles):
    return jnp.concatenate(tiles, axis=1) if len(tiles) > 1 else tiles[0]


def sweep_block(a_ref, left_ref, right_ref, a_rows, a_cols, b_rows, b_cols, tile, step, block):
    size = a_ref.shape[1]
    tiles = size // LANES
    first = step * BLOCK
    second = first + PANEL
    base = tile * LANES + first
    trailing_update(a_ref, left_ref, right_ref, base)

    sub, lane = iotas((PANEL, LANES))
    last = first == LANES - BLOCK
    next_first = jnp.where(last, 0, first + BLOCK)

    def in_block(row):
        return row[tile], second + sub

    def in_next(offset):
        def target(row):
            source = row[tile]
            if tile + 1 < tiles:
                source = jnp.where(last, row[tile + 1], source)
            return source, next_first + offset + sub

        return target

    nexts = [in_next(0), in_next(PANEL)]
    in_a = (lane >= first) & (lane < second)
    in_b = (lane >= second) & (lane < second + PANEL)

    def swept(tiles_of, mask):
        return [jnp.where(mask, 0.0, v) if t == tile else v for t, v in enumerate(tiles_of)]

    def minus(tiles_of, weight, p):
        result = []
        for t, value in enumerate(tiles_of):
            for k in range(PANEL):
                value = value - weight[k] * p[k][t]
            result.append(value)
        return result

    def by_tile(rows):
        return [rows[:, LANES * t : LANES * (t + 1)] for t in range(tiles)]

    qa, pa, (to_b, *to_next_a) = factor_panel(
        a_rows, a_cols, tile, first, block[:PANEL], [in_block, *nexts]
    )
    panel_b = side_by_side(minus(swept(by_tile(block[PANEL:]), in_a), to_b, pa))
    qb, pb, to_next_b = factor_panel(b_rows, b_cols, tile, second, panel_b, nexts)

    left, right = [], []
    for q, p, mask in ((qa, pa, in_b), (qb, pb, None)):
        q, p = packed_rows(q), packed_rows(p)
        if mask is not None:
            q, p = swept(q, mask), swept(p, mask)
        qs, ps = in_three(side_by_side(q)), in_three(side_by_side(p))
        left += [qs[i] for i in (0, 0, 1, 1, 0, 2)]
        right += [ps[i] for i in (0, 1, 0, 1, 2, 0)]
    left_ref[...] = jnp.concatenate(left, axis=0).astype(jnp.bfloat16)
    right_ref[...] = jnp.concatenate(right, axis=0).astype(jnp.bfloat16)

    following = a_ref[pl.ds(pl.multiple_of(base + 2 * BLOCK, BLOCK), BLOCK), :]
    result = []
    for g in range(2):
        rows = by_tile(following[g * PANEL : (g + 1) * PANEL])
        rows = minus(swept(rows, in_a), to_next_a[g], pa)
        rows = minus(swept(rows, in_b), to_next_b[g], pb)
        result.append(side_by_side(rows))
    return jnp.concatenate(result, axis=0)


def place_halves(place, pieces, first_row, flat):
    core = lax.axis_index(place.core)
    rows = flat.shape[0] // 2
    for r, piece in enumerate(pieces):
        start = pl.multiple_of(jnp.bitwise_xor(core, r) * rows, PANEL)
        flat[pl.ds(start, rows), :] = piece[first_row : first_row + rows]


def sweep_cost():
    return pl.CostEstimate(flops=1 << 30, bytes_accessed=1 << 20, transcendentals=0)


def clear(work):
    a_ref, left, right = work[:3]
    size = a_ref.shape[1]
    a_ref[:BLOCK] = jnp.zeros((BLOCK, size), jnp.float32)
    a_ref[BLOCK + size :] = jnp.zeros((BLOCK, size), jnp.float32)
    left[...] = jnp.zeros(left.shape, left.dtype)
    right[...] = jnp.zeros(right.shape, right.dtype)


def work_shapes(size):
    splits = 6 * BLOCK
    return [
        pltpu.VMEM((size + 2 * BLOCK, size), jnp.float32),
        pltpu.VMEM((splits, size), jnp.bfloat16),
        pltpu.VMEM((splits, size), jnp.bfloat16),
    ]


def row_shapes(size):
    return [
        pltpu.VMEM((PANEL, size), jnp.float32),
        pltpu.VMEM((PANEL * PANEL, LANES), jnp.float32),
    ] * 2


def aligned_rows(ref, index, count):
    if count % PANEL == 0:
        return ref[pl.ds(pl.multiple_of(index * count, count), count), :]
    per_slab = PANEL // count
    slab = ref[pl.ds(pl.multiple_of(index // per_slab * PANEL, PANEL), PANEL), :]
    value = slab[:count]
    for i in range(1, per_slab):
        value = jnp.where(index % per_slab == i, slab[i * count : (i + 1) * count], value)
    return value


def packs(cols, rows):
    return cols == 2 * PANEL and 2 * rows == LANES


def dot(a, b, last=False):
    return lax.dot_general(
        a,
        b,
        (((1,), (1 if last else 0,)), ((), ())),
        precision=HIGHEST,
        preferred_element_type=jnp.float32,
    )


STEPS = LANES // BLOCK
FIRST_STEPS = 7
SECOND_STEPS = 6


def sweep_both(wide_work, narrow_work, begin, end, blocks):
    def step(i, blocks):
        return (
            sweep_block(*wide_work, 0, i, blocks[0]),
            sweep_block(*narrow_work, 0, i, blocks[1]),
        )

    return lax.fori_loop(begin, end, step, blocks)


def sweep_wide(work, begin, end, block):
    return lax.fori_loop(begin, end, lambda i, block: sweep_block(*work, 1, i, block), block)


def unit_scale(block):
    row, col = iotas(block.shape)
    line = jnp.sum(jnp.where(row == col, block, 0.0), axis=0, keepdims=True)
    return jnp.broadcast_to(lax.rsqrt(line), (PANEL, block.shape[1]))


def on_rows(scale):
    n = scale.shape[1]
    return jnp.broadcast_to(scale[:1], (n, n))


def scaled(block, down, across):
    return (block * on_rows(down).T) * on_rows(across)


def first_kernel(
    place, total, mine, other, wa, wl, wr, wp, na, nl, nr, np_, ws_ref, ns_ref, *refs
):
    a_flat, b_flat = refs[:2]
    wide_work, narrow_work = (wa, wl, wr, *refs[2:6]), (na, nl, nr, *refs[6:])
    place_halves(place, (mine, other), 0, a_flat)
    place_halves(place, (mine, other), a_flat.shape[0] // 2, b_flat)
    n = LANES
    slab = a_flat[n : n + PANEL]
    first, square = unpack_pair(a_flat[:n], jnp.broadcast_to(slab[:1], (n, n)))
    corner = b_flat[:n] / total
    last = unfold(b_flat[n:], jnp.broadcast_to(slab[1:2], (n, n)))
    row, col = iotas((n, n))
    damp = jnp.where(row == col, DAMP, 0.0)
    clear(wide_work)
    clear(narrow_work)
    first, last, square = first / total + damp, last / total + damp, square / total + damp
    by_first, by_last, by_square = (unit_scale(block) for block in (first, last, square))
    ws_ref[:, :n] = by_first
    ws_ref[:, n:] = by_last
    ns_ref[...] = by_square
    first_across, last_across = on_rows(by_first), on_rows(by_last)
    first_down, last_down = first_across.T, last_across.T
    corner = (corner * first_down) * last_across
    wa[BLOCK : BLOCK + n, :n] = (first * first_down) * first_across
    wa[BLOCK : BLOCK + n, n:] = corner
    wa[BLOCK + n : BLOCK + 2 * n, :n] = corner.T
    wa[BLOCK + n : BLOCK + 2 * n, n:] = (last * last_down) * last_across
    na[BLOCK : BLOCK + n, :] = scaled(square, by_square, by_square)
    start = (wa[BLOCK : 2 * BLOCK, :], na[BLOCK : 2 * BLOCK, :])
    wp[...], np_[...] = sweep_both(wide_work, narrow_work, 0, FIRST_STEPS, start)


def second_kernel(*refs):
    given, scale, ninv_ref, state, narrow_state, wide_rows, narrow_rows = (
        refs[:8],
        refs[8],
        refs[9],
        refs[10:14],
        refs[14:17],
        refs[17:21],
        refs[21:],
    )
    for source, target in zip((*given[:3], *given[4:7]), (*state[:3], *narrow_state)):
        target[...] = source[...]
    wide_work, narrow_work = (*state[:3], *wide_rows), (*narrow_state, *narrow_rows)
    wp = state[3]
    panels = (given[3][...], given[7][...])
    panel, _ = sweep_both(wide_work, narrow_work, FIRST_STEPS, STEPS, panels)
    trailing_update(*narrow_work[:3], LANES)
    by_square = scale[...]
    ninv_ref[...] = scaled(-narrow_work[0][BLOCK : BLOCK + LANES, :], by_square, by_square)
    wp[...] = sweep_wide(wide_work, 0, SECOND_STEPS, panel)


def third_kernel(wa_in, wl_in, wr_in, panel_in, scale, winv, wa, wl, wr, *rows):
    wa[...] = wa_in[...]
    wl[...] = wl_in[...]
    wr[...] = wr_in[...]
    sweep_wide((wa, wl, wr, *rows), SECOND_STEPS, STEPS, panel_in[...])
    wide = wa.shape[1]
    trailing_update(wa, wl, wr, wide)
    parts = [slice(i, i + LANES) for i in range(0, wide, LANES)]
    across = [on_rows(scale[:, i]) for i in parts]
    down = [block.T for block in across]
    for i, rows_scale in zip(parts, down):
        for j, columns_scale in zip(parts, across):
            block = -wa[BLOCK + i.start : BLOCK + i.stop, j]
            winv[i, j] = (block * rows_scale) * columns_scale


def state_shapes(size):
    shapes = [jax.ShapeDtypeStruct(v.shape, v.dtype) for v in work_shapes(size)]
    return shapes + [jax.ShapeDtypeStruct((BLOCK, size), jnp.float32)]


def sweep_call(kernel, name, args, out_shapes, scratch):
    return pl.pallas_call(
        kernel,
        in_specs=[VMEM] * len(args),
        out_specs=[VMEM] * len(out_shapes),
        out_shape=out_shapes,
        scratch_shapes=scratch,
        cost_estimate=sweep_cost(),
        compiler_params=PARAMS,
        name=name,
    )(*args)


def first_panels(place, pieces, wide, narrow, total):
    return sweep_call(
        functools.partial(first_kernel, place, total),
        "first_panels",
        pieces,
        state_shapes(wide)
        + state_shapes(narrow)
        + [jax.ShapeDtypeStruct((PANEL, n), jnp.float32) for n in (wide, narrow)],
        [
            pltpu.VMEM((EARLY_ROWS, LANES), jnp.float32),
            pltpu.VMEM((LATE_ROWS, LANES), jnp.float32),
            *row_shapes(wide),
            *row_shapes(narrow),
        ],
    )


def second_panels(state, wide, narrow):
    ninv = jax.ShapeDtypeStruct((narrow, narrow), jnp.float32)
    return sweep_call(
        second_kernel,
        "second_panels",
        state,
        [ninv] + state_shapes(wide),
        [*work_shapes(narrow), *row_shapes(wide), *row_shapes(narrow)],
    )


def third_panels(state, wide):
    winv = jax.ShapeDtypeStruct((wide, wide), jnp.float32)
    scratch = [*work_shapes(wide), *row_shapes(wide)]
    return sweep_call(third_kernel, "third_panels", state, [winv], scratch)[0]


def product_kernel(place, total, rows, winv, ninv_ref, mine, other, out_ref, flat):
    place_halves(place, (mine, other), 0, flat)
    ninv = ninv_ref[...]
    n = LANES
    inner = jnp.concatenate(
        [
            transposed_dot(flat[c * n : (c + 1) * n] / total, ninv, HIGHEST)
            for c in range(2)
        ],
        axis=0,
    )
    wide = winv.shape[1]
    cols = wide // 2 ** len(place.dp)
    near, second = lax.axis_index(place.near), lax.axis_index(place.second)
    near_stride = 2 ** (len(place.dp) - 2)
    base = place.index(place.dp) - near * near_stride - second * 2
    _, lane = iotas((PANEL, LANES))
    picks = [
        aligned_rows(winv, base + (j // 2) * near_stride + (j % 2) * 2, cols) for j in range(4)
    ]
    if cols % PANEL == 0:
        whole = dot(jnp.concatenate(picks, axis=0), inner)
        updates = [whole[j * cols : (j + 1) * cols] for j in range(4)]
    else:
        updates = [dot(picked, inner) for picked in picks]
    for j, (picked, update) in enumerate(zip(picks, updates)):
        for x in range(2):
            block = 2 * j + x
            out_ref[block, :cols] = picked[:, :LANES]
            out_ref[block, cols : 2 * cols] = picked[:, LANES:]
            if packs(cols, rows):
                upper, lower = update[:PANEL], update[PANEL:]
                if x == 0:
                    lower = pltpu.roll(lower, rows, 1)
                else:
                    upper = pltpu.roll(upper, rows, 1)
                out_ref[block, 2 * cols :] = jnp.where(lane < rows, upper, lower)
            else:
                out_ref[block, 2 * cols :] = update


def products(place, winv, ninv, pieces, rows, total):
    wide, narrow = winv.shape[0], ninv.shape[0]
    cols = wide // 2 ** len(place.dp)
    height = 2 * cols + (PANEL if packs(cols, rows) else cols)
    return pl.pallas_call(
        functools.partial(product_kernel, place, total, rows),
        in_specs=[VMEM] * 4,
        out_specs=VMEM,
        out_shape=jax.ShapeDtypeStruct((8, height, LANES), jnp.float32),
        scratch_shapes=[pltpu.VMEM((2 * narrow, LANES), jnp.float32)],
        compiler_params=PARAMS,
        name="products",
    )(winv, ninv, *pieces)


def placing_kernel(place, slots_ref, got_ref, kept_ref, update_ref):
    layers = got_ref.shape[0]
    slots, cols, wide = kept_ref.shape
    rows = update_ref.shape[2]
    own, dp = place.index(place.own), place.index(place.dp)
    step = min(cols, PANEL)
    row, col = iotas((step, LANES))
    for h in range(wide // LANES):
        lanes = slice(h * LANES, (h + 1) * LANES)
        for r in range(0, cols, step):
            here = h * cols + r
            empty = jnp.where(col + h * LANES == row + dp * cols + r, 1.0 / DAMP, 0.0)
            for c in range(slots):
                value = empty
                for l in range(layers):
                    taken = slots_ref[l, :step] == c
                    value = jnp.where(taken, got_ref[l, here : here + step], value)
                kept_ref[c, r : r + step, lanes] = value
    for l in range(layers):
        value = got_ref[l, 2 * cols :]
        if packs(cols, rows):
            update_ref[l, :PANEL] = value[:, :rows]
            update_ref[l, PANEL:] = value[:, rows:]
        else:
            part = value[:, :rows]
            for p in range(1, LANES // rows):
                part = jnp.where(own == p, value[:, p * rows : (p + 1) * rows], part)
            update_ref[l] = part


def placing(place, slots_of, got, wide, cols, slots, rows):
    layers = got.shape[0]
    return pl.pallas_call(
        functools.partial(placing_kernel, place),
        in_specs=[VMEM, VMEM],
        out_specs=[VMEM, VMEM],
        out_shape=[
            jax.ShapeDtypeStruct((slots, cols, wide), jnp.float32),
            jax.ShapeDtypeStruct((layers, cols, rows), jnp.float32),
        ],
        compiler_params=PARAMS,
        name="placing",
    )(slots_of, got)


def swap(value, axis):
    return lax.ppermute(value, axis, [(0, 1), (1, 0)])


def swap_by_core(value, place, stage, orders):
    names = (place.near, place.second, place.core, place.first)
    flips = {"near": 8, "second": 4, "first": 1}
    pairs = [(i, i ^ flips[orders[(i >> 1) & 1][stage]]) for i in range(16)]
    return lax.ppermute(value, names, pairs)


def after(value, *others):
    return lax.optimization_barrier((value,) + others)[0]


def on_device(place, wide_rows, narrow_rows, owner_map):
    layers, rows, wide = wide_rows.shape
    narrow = narrow_rows.shape[2]
    n_dp, n_own = 2 ** len(place.dp), 2 ** len(place.own)
    total = float(rows * n_dp * n_own)

    h_keep, h_send, wides, narrows = hot_squares(place, wide_rows, narrow_rows)
    first_send = h_send[4:]
    h_got = swap(first_send, place.core)
    c_keep, c_send = cold_squares(place, after(wides, first_send), narrows)
    h_keep, c_send = lax.optimization_barrier((h_keep, c_send))

    hot = h_keep[4:] + h_got
    s_got = swap_by_core(hot, place, 0, ORDERS)
    m_keep, m_send, slots_of = mixed_sums(place, owner_map, after(wides, hot), narrows)
    c_got = swap(after(c_send + h_send[:4], m_send), place.core)
    m_got = swap(m_send, place.core)

    s = (c_keep + h_keep[:4]) + s_got
    s = s + after(c_got, s)
    s_got = swap_by_core(s[2:], place, 1, ORDERS)
    m = after(m_keep, s) + m_got
    m_got = swap_by_core(m[4:], place, 0, LATE_ORDERS)

    s = s[:2] + s_got
    s_got = swap_by_core(s[1], place, 2, ORDERS)
    m = after(m[:4], s) + m_got
    m_got = swap_by_core(m[2:], place, 1, LATE_ORDERS)

    s = s[0] + s_got
    if place.extra:
        s = lax.psum(s, place.extra)
    s_got = swap(s, place.far)
    m = after(m[:2], s) + m_got
    m_got = swap_by_core(m[1], place, 2, LATE_ORDERS)

    s = s + s_got
    state = first_panels(place, [s, swap(s, place.core)], wide, narrow, total)
    m = after(m[0], state[0]) + m_got
    if place.extra:
        m = lax.psum(m, place.extra)
    m_got = swap(m, place.far)
    *state, wide_scale, narrow_scale = state
    ninv, *state = second_panels([*state, narrow_scale], wide, narrow)
    m = after(m, ninv) + m_got
    m_got = swap(m, place.core)
    winv = third_panels([*state, wide_scale], wide)
    cols, own_rows = wide // n_dp, narrow // n_own
    sent = products(place, winv, ninv, [m, m_got], own_rows, total)
    got = lax.all_to_all(sent, (place.near, place.second, place.first), 0, 0)
    kept, update = placing(
        place, slots_of, got, wide, cols, layers // n_own + 1, own_rows
    )
    return (jnp.swapaxes(kept, 1, 2), jnp.swapaxes(update, 1, 2))


def solution(mesh):
    n_dp, n_own = mesh.shape["dp"], mesh.shape["own"]
    dp_names = tuple(f"dp{i}" for i in range(int(np.log2(n_dp))))
    own_names = tuple(f"own{i}" for i in range(int(np.log2(n_own))))
    names = dp_names + own_names
    bits = jax.sharding.Mesh(mesh.devices.reshape((2,) * len(names)), names)
    in_specs = (P(None, names, None), P(None, names, None), P())
    out_specs = (P(own_names, None, dp_names), P(None, own_names, dp_names))
    return jax.shard_map(
        functools.partial(on_device, Place(dp_names, own_names)),
        mesh=bits,
        in_specs=in_specs,
        out_specs=out_specs,
        check_vma=False,
    )
```

```python
import functools

import jax
import jax.numpy as jnp
import numpy as np
from jax import lax
from jax.experimental import pallas as pl
from jax.experimental.pallas import tpu as pltpu
from jax.sharding import PartitionSpec as P

DAMP = 0.5
LANES = 128
PANEL = 8
BLOCK = 2 * PANEL
VMEM_LIMIT = 48 * 1024 * 1024
HIGHEST = lax.Precision.HIGHEST
VMEM = pl.BlockSpec(memory_space=pltpu.VMEM)
SMEM = pl.BlockSpec(memory_space=pltpu.SMEM)
HBM = pl.BlockSpec(memory_space=pltpu.HBM)
PARAMS = pltpu.CompilerParams(vmem_limit_bytes=VMEM_LIMIT)


class Place:
    def __init__(self, dp_names, own_names):
        self.dp, self.own = dp_names, own_names
        self.core, self.second, self.near, self.far = (
            dp_names[-1],
            dp_names[-2],
            dp_names[1],
            dp_names[0],
        )
        self.first = own_names[-1]
        used = (self.core, self.second, self.near, self.far, self.first)
        self.extra = tuple(n for n in dp_names + own_names if n not in used)

    def index(self, names):
        value = jnp.int32(0)
        for name in names:
            value = value * 2 + lax.axis_index(name)
        return value

    def layer(self):
        return self.index((self.near, self.second, self.first))


def transposed_dot(a, b, precision=None):
    return lax.dot_general(
        a, b, (((0,), (0,)), ((), ())), precision=precision, preferred_element_type=jnp.float32
    )


AHEAD = 5


def layer_copies(place, sources, buffers, sems):
    layer = place.layer()
    return [
        [
            pltpu.make_async_copy(
                source.at[jnp.bitwise_xor(layer, i)], buffer.at[i], sems.at[i, s]
            )
            for s, (source, buffer) in enumerate(zip(sources, buffers))
        ]
        for i in range(buffers[0].shape[0])
    ]


def both_halves(place, flat, i):
    rows = flat.shape[1] // 2
    core = lax.axis_index(place.core)
    kept = pl.multiple_of(core * rows, PANEL)
    sent = pl.multiple_of((1 - core) * rows, PANEL)
    return flat[i, pl.ds(kept, rows), :], flat[i, pl.ds(sent, rows), :]


ORDERS = (("first", "second", "near"), ("second", "near", "first"))
LATE_ORDERS = (("first", "second", "near"), ("near", "first", "second"))


def position(axes, i):
    bits = {"near": i // 4, "second": (i // 2) % 2, "first": i % 2}
    return bits[axes[0]] * 4 + bits[axes[1]] * 2 + bits[axes[2]]


def positions(place, i, orders):
    core = lax.axis_index(place.core)
    first, second = (position(axes, i) for axes in orders)
    return jnp.where(core == 0, first, second), jnp.where(core == 0, second, first)


def iotas(shape):
    return (
        lax.broadcasted_iota(jnp.int32, shape, 0),
        lax.broadcasted_iota(jnp.int32, shape, 1),
    )


def pack_pair(first, second):
    row, col = iotas(first.shape)
    return jnp.where(row >= col, first, second)


def unpack_pair(packed, second_diagonal):
    row, col = iotas(packed.shape)
    turned = packed.T
    first = jnp.where(row >= col, packed, turned)
    second = jnp.where(col > row, packed, turned)
    return first, jnp.where(row == col, second_diagonal, second)


def fold(block):
    h = block.shape[0] // 2
    row, col = iotas((h, 2 * h))
    last = pltpu.roll(block[h:], h, 1)
    return jnp.where((col >= h) | (row >= col), block[:h], last)


def unfold(folded, diagonal):
    h, n = folded.shape
    row, col = iotas((n, n))
    block = jnp.concatenate([folded, jnp.zeros((h, n), jnp.float32)], axis=0)
    turned = block.T
    top = jnp.where((col >= h) | (col <= row), block, turned)
    moved = pltpu.roll(pltpu.roll(block, h, 0), h, 1)
    moved_turned = pltpu.roll(pltpu.roll(turned, h, 0), h, 1)
    last = jnp.where(col > row, moved, moved_turned)
    last = jnp.where(row == col, diagonal, last)
    return jnp.where(row < h, top, jnp.where(col < h, turned, last))


def diagonals(blocks, rows):
    n = blocks[0].shape[0]
    row, col = iotas((n, n))
    slab_row, _ = iotas((rows, n))
    slab = jnp.zeros((rows, n), jnp.float32)
    for i, block in enumerate(blocks):
        line = jnp.sum(jnp.where(row == col, block, 0.0), axis=0, keepdims=True)
        slab = jnp.where(slab_row == i, jnp.broadcast_to(line, (rows, n)), slab)
    return slab


EARLY_ROWS = 144
LATE_ROWS = 192


HOT = (1, 2, 3, 5, 6, 7)
COLD = (0, 4)


def square_sums(wide, narrow):
    return transposed_dot(wide, wide), transposed_dot(narrow, narrow)


def pack_layer(place, i, wcov, ncov, a_flat, b_flat):
    n = LANES
    last = wcov[n:, n:]
    a_flat[i, :n] = pack_pair(wcov[:n, :n], ncov)
    a_flat[i, n:] = diagonals((ncov, last), EARLY_ROWS - n)
    b_flat[i, :n] = wcov[:n, n:]
    b_flat[i, n:] = fold(last)
    a_kept, a_sent = both_halves(place, a_flat, i)
    b_kept, b_sent = both_halves(place, b_flat, i)
    return (a_kept, b_kept), (a_sent, b_sent)


def put(ref, index, parts):
    rows = EARLY_ROWS // 2
    ref[index, :rows] = parts[0]
    ref[index, rows:] = parts[1]


def put_layer(place, i, sums, a_flat, b_flat, keep, send):
    kept, sent = pack_layer(place, i, *sums, a_flat, b_flat)
    mine, other = positions(place, i, ORDERS)
    put(keep, mine, kept)
    put(send, other, sent)


def clear_others(place, layers, keep, send):
    for i in layers:
        mine, other = positions(place, i, ORDERS)
        keep[mine] = jnp.zeros(keep.shape[1:], jnp.float32)
        send[other] = jnp.zeros(send.shape[1:], jnp.float32)


def hot_kernel(place, wide_hbm, narrow_hbm, keep, send, wides, narrows, a_flat, b_flat, sems):
    copies = layer_copies(place, (wide_hbm, narrow_hbm), (wides, narrows), sems)
    order = HOT + COLD
    for i in order[:AHEAD]:
        for copy in copies[i]:
            copy.start()
    clear_others(place, COLD, keep, send)

    def pack(i, sums):
        put_layer(place, i, sums, a_flat, b_flat, keep, send)

    before = None
    for at, i in enumerate(order):
        wide_copy, narrow_copy = copies[i]
        wide_copy.wait()
        if at + AHEAD < len(order):
            for copy in copies[order[at + AHEAD]]:
                copy.start()
        if i in HOT:
            wcov = transposed_dot(wides[i], wides[i])
        if before is not None:
            pack(*before)
            before = None
        narrow_copy.wait()
        if i in HOT:
            before = (i, (wcov, transposed_dot(narrows[i], narrows[i])))


def cold_kernel(place, wides, narrows, keep, send, a_flat, b_flat):
    for i in COLD:
        put_layer(
            place, i, square_sums(wides[i], narrows[i]), a_flat, b_flat, keep, send
        )
    core = lax.axis_index(place.core)
    stay = [[i for i in HOT if position(axes, i) < 4] for axes in ORDERS]
    for first, second in zip(*stay):
        here = [position(axes, i) for axes, i in zip(ORDERS, (first, second))]
        mine = jnp.where(core == 0, here[0], here[1])
        other = jnp.where(core == 0, here[1], here[0])
        keep[mine] = jnp.zeros(keep.shape[1:], jnp.float32)
        send[other] = jnp.zeros(send.shape[1:], jnp.float32)


def write_slots(place, owner_map, slots_ref):
    own = place.index(place.own)
    count = jnp.int32(0)
    for l in range(slots_ref.shape[0]):
        mine = owner_map[l] == own
        slot = jnp.where(mine, count, -1)
        slots_ref[l] = jnp.full(slots_ref.shape[1:], 0, jnp.int32) + slot
        count = count + mine.astype(jnp.int32)


def mixed_kernel(place, owner_map, wides, narrows, keep, send, slots_ref, flat):
    n = LANES
    write_slots(place, owner_map, slots_ref)
    for i in range(wides.shape[0]):
        mixed = transposed_dot(narrows[i], wides[i])
        flat[i, :n] = mixed[:, :n]
        flat[i, n:] = mixed[:, n:]
        kept, sent = both_halves(place, flat, i)
        mine, other = positions(place, i, LATE_ORDERS)
        keep[mine] = kept
        send[other] = sent


def gram_cost(wide_rows, columns):
    return pl.CostEstimate(
        flops=2 * wide_rows.size * columns, bytes_accessed=2 * wide_rows.size, transcendentals=0
    )


HALF_ROWS = (EARLY_ROWS + LATE_ROWS) // 2


def pack_shapes(layers):
    return [
        pltpu.VMEM((layers, EARLY_ROWS, LANES), jnp.float32),
        pltpu.VMEM((layers, LATE_ROWS, LANES), jnp.float32),
    ]


def hot_squares(place, wide_rows, narrow_rows):
    layers = wide_rows.shape[0]
    half = jax.ShapeDtypeStruct((layers, HALF_ROWS, LANES), jnp.float32)
    return pl.pallas_call(
        functools.partial(hot_kernel, place),
        in_specs=[HBM, HBM],
        out_specs=[VMEM] * 4,
        out_shape=[
            half,
            half,
            jax.ShapeDtypeStruct(wide_rows.shape, wide_rows.dtype),
            jax.ShapeDtypeStruct(narrow_rows.shape, narrow_rows.dtype),
        ],
        scratch_shapes=[*pack_shapes(layers), pltpu.SemaphoreType.DMA((layers, 2))],
        cost_estimate=gram_cost(wide_rows, 240),
        compiler_params=PARAMS,
        name="hot_squares",
    )(
        pltpu.with_memory_space_constraint(wide_rows, pltpu.HBM),
        pltpu.with_memory_space_constraint(narrow_rows, pltpu.HBM),
    )


def cold_squares(place, wides, narrows):
    half = jax.ShapeDtypeStruct((wides.shape[0] // 2, HALF_ROWS, LANES), jnp.float32)
    return pl.pallas_call(
        functools.partial(cold_kernel, place),
        in_specs=[VMEM, VMEM],
        out_specs=[VMEM, VMEM],
        out_shape=[half, half],
        scratch_shapes=pack_shapes(wides.shape[0]),
        cost_estimate=gram_cost(wides, 80),
        compiler_params=PARAMS,
        name="cold_squares",
    )(wides, narrows)


def mixed_sums(place, owner_map, wides, narrows):
    layers, _, narrow = narrows.shape
    half = jax.ShapeDtypeStruct((layers, narrow, LANES), jnp.float32)
    return pl.pallas_call(
        functools.partial(mixed_kernel, place),
        in_specs=[SMEM, VMEM, VMEM],
        out_specs=[VMEM] * 3,
        out_shape=[half, half, jax.ShapeDtypeStruct((layers, PANEL, LANES), jnp.int32)],
        scratch_shapes=[pltpu.VMEM((layers, 2 * narrow, LANES), jnp.float32)],
        cost_estimate=gram_cost(wides, 128),
        compiler_params=PARAMS,
        name="mixed",
    )(owner_map, wides, narrows)


def lane_gather(x, index):
    return jnp.take_along_axis(x, index, axis=1, mode="promise_in_bounds")


def trailing_update(a_ref, left_ref, right_ref, base):
    size = a_ref.shape[1]
    a_ref[pl.ds(pl.multiple_of(base, BLOCK), BLOCK), :] = jnp.zeros((BLOCK, size), jnp.float32)
    lane = lax.broadcasted_iota(jnp.int32, (1, size), 1)
    swept = (lane >= base - BLOCK) & (lane < base)
    update = transposed_dot(left_ref[...], right_ref[...])
    a_ref[BLOCK : BLOCK + size, :] = (
        jnp.where(swept, 0.0, a_ref[BLOCK : BLOCK + size, :]) - update
    )


def in_three(x):
    high = x.astype(jnp.bfloat16).astype(jnp.float32)
    rest = x - high
    middle = rest.astype(jnp.bfloat16).astype(jnp.float32)
    return high, middle, rest - middle


def factor_panel(rows_ref, cols_ref, tile, first, panel, targets):
    tiles = panel.shape[1] // LANES
    shape = (PANEL, LANES)
    _, lane = iotas(shape)

    def on_all(ref, k, lanes):
        return jnp.broadcast_to(ref[k : k + 1, lanes], shape)

    rows_ref[...] = panel
    lanes = [slice(LANES * t, LANES * (t + 1)) for t in range(tiles)]
    rows = [[on_all(rows_ref, k, part) for part in lanes] for k in range(PANEL)]
    here = panel[:, lanes[tile]]
    for j in range(PANEL):
        column = lane_gather(here, jnp.full(shape, 0, jnp.int32) + (first + j))
        cols_ref[PANEL * j : PANEL * (j + 1)] = column
    d = [[None] * PANEL for _ in range(PANEL)]
    for j in range(PANEL):
        for i in range(j, PANEL):
            d[i][j] = on_all(cols_ref, PANEL * j + i, slice(None))
    own = (lane >= first) & (lane < first + PANEL)
    q = [[None] * tiles for _ in range(PANEL)]
    p = [[None] * tiles for _ in range(PANEL)]
    weights = [[None] * PANEL for _ in targets]
    factor = [[None] * PANEL for _ in range(PANEL)]

    def substitute(k, scale):
        for t in range(tiles):
            value = rows[k][t]
            if t == tile:
                value = jnp.where(own, jnp.where(lane == first + k, -1.0, 0.0), value)
            for j in range(k):
                value = value - factor[k][j] * q[j][t]
            q[k][t] = value
            p[k][t] = value * scale
        for target, weight in zip(targets, weights):
            source, index = target(rows[k])
            value = lane_gather(source, index)
            for j in range(k):
                value = value - factor[k][j] * weight[j]
            weight[k] = value

    for k in range(0, PANEL, 2):
        m = k + 1
        a, b, c = d[k][k], d[m][k], d[m][m]
        first_scale = 1.0 / a
        second_scale = a * (1.0 / (a * c - b * b))
        factor[m][k] = b * first_scale
        left_over = {i: d[i][m] - d[i][k] * factor[m][k] for i in range(k + 2, PANEL)}
        for i in range(k + 2, PANEL):
            factor[i][k] = d[i][k] * first_scale
            factor[i][m] = left_over[i] * second_scale
        for i in range(k + 2, PANEL):
            for j in range(k + 2, i + 1):
                value = d[i][j] - d[i][k] * factor[j][k]
                d[i][j] = value - (left_over[i] * left_over[j]) * second_scale
        substitute(k, first_scale)
        substitute(m, second_scale)
    return q, p, weights


def packed_rows(values):
    sub, _ = iotas((PANEL, LANES))
    whole = []
    for t in range(len(values[0])):
        value = values[0][t]
        for k in range(1, PANEL):
            value = jnp.where(sub == k, values[k][t], value)
        whole.append(value)
    return whole


def side_by_side(tiles):
    return jnp.concatenate(tiles, axis=1) if len(tiles) > 1 else tiles[0]


def sweep_block(a_ref, left_ref, right_ref, a_rows, a_cols, b_rows, b_cols, tile, step, block):
    size = a_ref.shape[1]
    tiles = size // LANES
    first = step * BLOCK
    second = first + PANEL
    base = tile * LANES + first
    trailing_update(a_ref, left_ref, right_ref, base)

    sub, lane = iotas((PANEL, LANES))
    last = first == LANES - BLOCK
    next_first = jnp.where(last, 0, first + BLOCK)

    def in_block(row):
        return row[tile], second + sub

    def in_next(offset):
        def target(row):
            source = row[tile]
            if tile + 1 < tiles:
                source = jnp.where(last, row[tile + 1], source)
            return source, next_first + offset + sub

        return target

    nexts = [in_next(0), in_next(PANEL)]
    in_a = (lane >= first) & (lane < second)
    in_b = (lane >= second) & (lane < second + PANEL)

    def swept(tiles_of, mask):
        return [jnp.where(mask, 0.0, v) if t == tile else v for t, v in enumerate(tiles_of)]

    def minus(tiles_of, weight, p):
        result = []
        for t, value in enumerate(tiles_of):
            for k in range(PANEL):
                value = value - weight[k] * p[k][t]
            result.append(value)
        return result

    def by_tile(rows):
        return [rows[:, LANES * t : LANES * (t + 1)] for t in range(tiles)]

    qa, pa, (to_b, *to_next_a) = factor_panel(
        a_rows, a_cols, tile, first, block[:PANEL], [in_block, *nexts]
    )
    panel_b = side_by_side(minus(swept(by_tile(block[PANEL:]), in_a), to_b, pa))
    qb, pb, to_next_b = factor_panel(b_rows, b_cols, tile, second, panel_b, nexts)

    left, right = [], []
    for q, p, mask in ((qa, pa, in_b), (qb, pb, None)):
        q, p = packed_rows(q), packed_rows(p)
        if mask is not None:
            q, p = swept(q, mask), swept(p, mask)
        qs, ps = in_three(side_by_side(q)), in_three(side_by_side(p))
        left += [qs[i] for i in (0, 0, 1, 1, 0, 2)]
        right += [ps[i] for i in (0, 1, 0, 1, 2, 0)]
    left_ref[...] = jnp.concatenate(left, axis=0).astype(jnp.bfloat16)
    right_ref[...] = jnp.concatenate(right, axis=0).astype(jnp.bfloat16)

    following = a_ref[pl.ds(pl.multiple_of(base + 2 * BLOCK, BLOCK), BLOCK), :]
    result = []
    for g in range(2):
        rows = by_tile(following[g * PANEL : (g + 1) * PANEL])
        rows = minus(swept(rows, in_a), to_next_a[g], pa)
        rows = minus(swept(rows, in_b), to_next_b[g], pb)
        result.append(side_by_side(rows))
    return jnp.concatenate(result, axis=0)


def place_halves(place, pieces, first_row, flat):
    core = lax.axis_index(place.core)
    rows = flat.shape[0] // 2
    for r, piece in enumerate(pieces):
        start = pl.multiple_of(jnp.bitwise_xor(core, r) * rows, PANEL)
        flat[pl.ds(start, rows), :] = piece[first_row : first_row + rows]


def sweep_cost():
    return pl.CostEstimate(flops=1 << 30, bytes_accessed=1 << 20, transcendentals=0)


def clear(work):
    a_ref, left, right = work[:3]
    size = a_ref.shape[1]
    a_ref[:BLOCK] = jnp.zeros((BLOCK, size), jnp.float32)
    a_ref[BLOCK + size :] = jnp.zeros((BLOCK, size), jnp.float32)
    left[...] = jnp.zeros(left.shape, left.dtype)
    right[...] = jnp.zeros(right.shape, right.dtype)


def work_shapes(size):
    splits = 6 * BLOCK
    return [
        pltpu.VMEM((size + 2 * BLOCK, size), jnp.float32),
        pltpu.VMEM((splits, size), jnp.bfloat16),
        pltpu.VMEM((splits, size), jnp.bfloat16),
    ]


def row_shapes(size):
    return [
        pltpu.VMEM((PANEL, size), jnp.float32),
        pltpu.VMEM((PANEL * PANEL, LANES), jnp.float32),
    ] * 2


def aligned_rows(ref, index, count):
    if count % PANEL == 0:
        return ref[pl.ds(pl.multiple_of(index * count, count), count), :]
    per_slab = PANEL // count
    slab = ref[pl.ds(pl.multiple_of(index // per_slab * PANEL, PANEL), PANEL), :]
    value = slab[:count]
    for i in range(1, per_slab):
        value = jnp.where(index % per_slab == i, slab[i * count : (i + 1) * count], value)
    return value


def packs(cols, rows):
    return cols == 2 * PANEL and 2 * rows == LANES


def dot(a, b, last=False):
    return lax.dot_general(
        a,
        b,
        (((1,), (1 if last else 0,)), ((), ())),
        precision=HIGHEST,
        preferred_element_type=jnp.float32,
    )


STEPS = LANES // BLOCK
FIRST_STEPS = 5
SECOND_STEPS = 6


def sweep_both(wide_work, narrow_work, begin, end, blocks):
    def step(i, blocks):
        return (
            sweep_block(*wide_work, 0, i, blocks[0]),
            sweep_block(*narrow_work, 0, i, blocks[1]),
        )

    return lax.fori_loop(begin, end, step, blocks)


def sweep_wide(work, begin, end, block):
    return lax.fori_loop(begin, end, lambda i, block: sweep_block(*work, 1, i, block), block)


def unit_scale(block):
    row, col = iotas(block.shape)
    line = jnp.sum(jnp.where(row == col, block, 0.0), axis=0, keepdims=True)
    return jnp.broadcast_to(lax.rsqrt(line), (PANEL, block.shape[1]))


def on_rows(scale):
    n = scale.shape[1]
    return jnp.broadcast_to(scale[:1], (n, n))


def scaled(block, down, across):
    return (block * on_rows(down).T) * on_rows(across)


def first_kernel(
    place, total, mine, other, wa, wl, wr, wp, na, nl, nr, np_, ws_ref, ns_ref, *refs
):
    a_flat, b_flat = refs[:2]
    wide_work, narrow_work = (wa, wl, wr, *refs[2:6]), (na, nl, nr, *refs[6:])
    place_halves(place, (mine, other), 0, a_flat)
    place_halves(place, (mine, other), a_flat.shape[0] // 2, b_flat)
    n = LANES
    slab = a_flat[n : n + PANEL]
    first, square = unpack_pair(a_flat[:n], jnp.broadcast_to(slab[:1], (n, n)))
    corner = b_flat[:n]
    last = unfold(b_flat[n:], jnp.broadcast_to(slab[1:2], (n, n)))
    row, col = iotas((n, n))
    damp = jnp.where(row == col, DAMP * total, 0.0)
    clear(wide_work)
    clear(narrow_work)
    first, last, square = first + damp, last + damp, square + damp
    by_first, by_last, by_square = (unit_scale(block) for block in (first, last, square))
    root = total**0.5
    ws_ref[:, :n] = by_first * root
    ws_ref[:, n:] = by_last * root
    ns_ref[...] = by_square * root
    first_across, last_across = on_rows(by_first), on_rows(by_last)
    first_down, last_down = first_across.T, last_across.T
    corner = (corner * first_down) * last_across
    wa[BLOCK : BLOCK + n, :n] = (first * first_down) * first_across
    wa[BLOCK : BLOCK + n, n:] = corner
    wa[BLOCK + n : BLOCK + 2 * n, :n] = corner.T
    wa[BLOCK + n : BLOCK + 2 * n, n:] = (last * last_down) * last_across
    na[BLOCK : BLOCK + n, :] = scaled(square, by_square, by_square)
    start = (wa[BLOCK : 2 * BLOCK, :], na[BLOCK : 2 * BLOCK, :])
    wp[...], np_[...] = sweep_both(wide_work, narrow_work, 0, FIRST_STEPS, start)


def second_kernel(*refs):
    given, scale, ninv_ref, state, narrow_state, wide_rows, narrow_rows = (
        refs[:8],
        refs[8],
        refs[9],
        refs[10:14],
        refs[14:17],
        refs[17:21],
        refs[21:],
    )
    for source, target in zip((*given[:3], *given[4:7]), (*state[:3], *narrow_state)):
        target[...] = source[...]
    wide_work, narrow_work = (*state[:3], *wide_rows), (*narrow_state, *narrow_rows)
    wp = state[3]
    panels = (given[3][...], given[7][...])
    panel, _ = sweep_both(wide_work, narrow_work, FIRST_STEPS, STEPS, panels)
    trailing_update(*narrow_work[:3], LANES)
    by_square = scale[...]
    ninv_ref[...] = scaled(-narrow_work[0][BLOCK : BLOCK + LANES, :], by_square, by_square)
    wp[...] = sweep_wide(wide_work, 0, SECOND_STEPS, panel)


def third_kernel(wa_in, wl_in, wr_in, panel_in, scale, winv, wa, wl, wr, *rows):
    wa[...] = wa_in[...]
    wl[...] = wl_in[...]
    wr[...] = wr_in[...]
    sweep_wide((wa, wl, wr, *rows), SECOND_STEPS, STEPS, panel_in[...])
    wide = wa.shape[1]
    trailing_update(wa, wl, wr, wide)
    parts = [slice(i, i + LANES) for i in range(0, wide, LANES)]
    across = [on_rows(scale[:, i]) for i in parts]
    down = [block.T for block in across]
    for i, rows_scale in zip(parts, down):
        for j, columns_scale in zip(parts, across):
            block = -wa[BLOCK + i.start : BLOCK + i.stop, j]
            winv[i, j] = (block * rows_scale) * columns_scale


def state_shapes(size):
    shapes = [jax.ShapeDtypeStruct(v.shape, v.dtype) for v in work_shapes(size)]
    return shapes + [jax.ShapeDtypeStruct((BLOCK, size), jnp.float32)]


def sweep_call(kernel, name, args, out_shapes, scratch):
    return pl.pallas_call(
        kernel,
        in_specs=[VMEM] * len(args),
        out_specs=[VMEM] * len(out_shapes),
        out_shape=out_shapes,
        scratch_shapes=scratch,
        cost_estimate=sweep_cost(),
        compiler_params=PARAMS,
        name=name,
    )(*args)


def first_panels(place, pieces, wide, narrow, total):
    return sweep_call(
        functools.partial(first_kernel, place, total),
        "first_panels",
        pieces,
        state_shapes(wide)
        + state_shapes(narrow)
        + [jax.ShapeDtypeStruct((PANEL, n), jnp.float32) for n in (wide, narrow)],
        [
            pltpu.VMEM((EARLY_ROWS, LANES), jnp.float32),
            pltpu.VMEM((LATE_ROWS, LANES), jnp.float32),
            *row_shapes(wide),
            *row_shapes(narrow),
        ],
    )


def second_panels(state, wide, narrow):
    ninv = jax.ShapeDtypeStruct((narrow, narrow), jnp.float32)
    return sweep_call(
        second_kernel,
        "second_panels",
        state,
        [ninv] + state_shapes(wide),
        [*work_shapes(narrow), *row_shapes(wide), *row_shapes(narrow)],
    )


def third_panels(state, wide):
    winv = jax.ShapeDtypeStruct((wide, wide), jnp.float32)
    scratch = [*work_shapes(wide), *row_shapes(wide)]
    return sweep_call(third_kernel, "third_panels", state, [winv], scratch)[0]


def product_kernel(place, total, rows, winv, ninv_ref, mine, other, out_ref, flat):
    place_halves(place, (mine, other), 0, flat)
    ninv = ninv_ref[...]
    n = LANES
    inner = jnp.concatenate(
        [
            transposed_dot(flat[c * n : (c + 1) * n] / total, ninv, HIGHEST)
            for c in range(2)
        ],
        axis=0,
    )
    wide = winv.shape[1]
    cols = wide // 2 ** len(place.dp)
    near, second = lax.axis_index(place.near), lax.axis_index(place.second)
    near_stride = 2 ** (len(place.dp) - 2)
    base = place.index(place.dp) - near * near_stride - second * 2
    _, lane = iotas((PANEL, LANES))
    picks = [
        aligned_rows(winv, base + (j // 2) * near_stride + (j % 2) * 2, cols) for j in range(4)
    ]
    if cols % PANEL == 0:
        whole = dot(jnp.concatenate(picks, axis=0), inner)
        updates = [whole[j * cols : (j + 1) * cols] for j in range(4)]
    else:
        updates = [dot(picked, inner) for picked in picks]
    for j, (picked, update) in enumerate(zip(picks, updates)):
        for x in range(2):
            block = 2 * j + x
            out_ref[block, :cols] = picked[:, :LANES]
            out_ref[block, cols : 2 * cols] = picked[:, LANES:]
            if packs(cols, rows):
                upper, lower = update[:PANEL], update[PANEL:]
                if x == 0:
                    lower = pltpu.roll(lower, rows, 1)
                else:
                    upper = pltpu.roll(upper, rows, 1)
                out_ref[block, 2 * cols :] = jnp.where(lane < rows, upper, lower)
            else:
                out_ref[block, 2 * cols :] = update


def products(place, winv, ninv, pieces, rows, total):
    wide, narrow = winv.shape[0], ninv.shape[0]
    cols = wide // 2 ** len(place.dp)
    height = 2 * cols + (PANEL if packs(cols, rows) else cols)
    return pl.pallas_call(
        functools.partial(product_kernel, place, total, rows),
        in_specs=[VMEM] * 4,
        out_specs=VMEM,
        out_shape=jax.ShapeDtypeStruct((8, height, LANES), jnp.float32),
        scratch_shapes=[pltpu.VMEM((2 * narrow, LANES), jnp.float32)],
        compiler_params=PARAMS,
        name="products",
    )(winv, ninv, *pieces)


def placing_kernel(place, slots_ref, got_ref, kept_ref, update_ref):
    layers = got_ref.shape[0]
    slots, cols, wide = kept_ref.shape
    rows = update_ref.shape[2]
    own, dp = place.index(place.own), place.index(place.dp)
    step = min(cols, PANEL)
    row, col = iotas((step, LANES))
    for h in range(wide // LANES):
        lanes = slice(h * LANES, (h + 1) * LANES)
        for r in range(0, cols, step):
            here = h * cols + r
            empty = jnp.where(col + h * LANES == row + dp * cols + r, 1.0 / DAMP, 0.0)
            for c in range(slots):
                value = empty
                for l in range(layers):
                    taken = slots_ref[l, :step] == c
                    value = jnp.where(taken, got_ref[l, here : here + step], value)
                kept_ref[c, r : r + step, lanes] = value
    for l in range(layers):
        value = got_ref[l, 2 * cols :]
        if packs(cols, rows):
            update_ref[l, :PANEL] = value[:, :rows]
            update_ref[l, PANEL:] = value[:, rows:]
        else:
            part = value[:, :rows]
            for p in range(1, LANES // rows):
                part = jnp.where(own == p, value[:, p * rows : (p + 1) * rows], part)
            update_ref[l] = part


def placing(place, slots_of, got, wide, cols, slots, rows):
    layers = got.shape[0]
    return pl.pallas_call(
        functools.partial(placing_kernel, place),
        in_specs=[VMEM, VMEM],
        out_specs=[VMEM, VMEM],
        out_shape=[
            jax.ShapeDtypeStruct((slots, cols, wide), jnp.float32),
            jax.ShapeDtypeStruct((layers, cols, rows), jnp.float32),
        ],
        compiler_params=PARAMS,
        name="placing",
    )(slots_of, got)


def swap(value, axis):
    return lax.ppermute(value, axis, [(0, 1), (1, 0)])


def swap_by_core(value, place, stage, orders):
    names = (place.near, place.second, place.core, place.first)
    flips = {"near": 8, "second": 4, "first": 1}
    pairs = [(i, i ^ flips[orders[(i >> 1) & 1][stage]]) for i in range(16)]
    return lax.ppermute(value, names, pairs)


def after(value, *others):
    return lax.optimization_barrier((value,) + others)[0]


def on_device(place, wide_rows, narrow_rows, owner_map):
    layers, rows, wide = wide_rows.shape
    narrow = narrow_rows.shape[2]
    n_dp, n_own = 2 ** len(place.dp), 2 ** len(place.own)
    total = float(rows * n_dp * n_own)

    h_keep, h_send, wides, narrows = hot_squares(place, wide_rows, narrow_rows)
    first_send = h_send[4:]
    h_got = swap(first_send, place.core)
    c_keep, c_send = cold_squares(place, after(wides, first_send), narrows)
    h_keep, c_send = lax.optimization_barrier((h_keep, c_send))

    hot = h_keep[4:] + h_got
    s_got = swap_by_core(hot, place, 0, ORDERS)
    m_keep, m_send, slots_of = mixed_sums(place, owner_map, after(wides, hot), narrows)
    c_got = swap(after(c_send + h_send[:4], m_send), place.core)
    m_got = swap(m_send, place.core)

    s = (c_keep + h_keep[:4]) + s_got
    s = s + after(c_got, s)
    s_got = swap_by_core(s[2:], place, 1, ORDERS)
    m = after(m_keep, s) + m_got
    m_got = swap_by_core(m[4:], place, 0, LATE_ORDERS)

    s = s[:2] + s_got
    s_got = swap_by_core(s[1], place, 2, ORDERS)
    m = after(m[:4], s) + m_got
    m_got = swap_by_core(m[2:], place, 1, LATE_ORDERS)

    s = s[0] + s_got
    if place.extra:
        s = lax.psum(s, place.extra)
    s_got = swap(s, place.far)
    m = after(m[:2], s) + m_got
    m_got = swap_by_core(m[1], place, 2, LATE_ORDERS)

    s = s + s_got
    state = first_panels(place, [s, swap(s, place.core)], wide, narrow, total)
    m = after(m[0], state[0]) + m_got
    if place.extra:
        m = lax.psum(m, place.extra)
    m_got = swap(m, place.far)
    *state, wide_scale, narrow_scale = state
    ninv, *state = second_panels([*state, narrow_scale], wide, narrow)
    m = after(m, ninv) + m_got
    m_got = swap(m, place.core)
    winv = third_panels([*state, wide_scale], wide)
    cols, own_rows = wide // n_dp, narrow // n_own
    sent = products(place, winv, ninv, [m, m_got], own_rows, total)
    got = lax.all_to_all(sent, (place.near, place.second, place.first), 0, 0)
    kept, update = placing(
        place, slots_of, got, wide, cols, layers // n_own + 1, own_rows
    )
    return (jnp.swapaxes(kept, 1, 2), jnp.swapaxes(update, 1, 2))


def solution(mesh):
    n_dp, n_own = mesh.shape["dp"], mesh.shape["own"]
    dp_names = tuple(f"dp{i}" for i in range(int(np.log2(n_dp))))
    own_names = tuple(f"own{i}" for i in range(int(np.log2(n_own))))
    names = dp_names + own_names
    bits = jax.sharding.Mesh(mesh.devices.reshape((2,) * len(names)), names)
    in_specs = (P(None, names, None), P(None, names, None), P())
    out_specs = (P(own_names, None, dp_names), P(None, own_names, dp_names))
    return jax.shard_map(
        functools.partial(on_device, Place(dp_names, own_names)),
        mesh=bits,
        in_specs=in_specs,
        out_specs=out_specs,
        check_vma=False,
    )
```

```python
import functools

import jax
import jax.numpy as jnp
import numpy as np
from jax import lax
from jax.experimental import pallas as pl
from jax.experimental.pallas import tpu as pltpu
from jax.sharding import PartitionSpec as P

DAMP = 0.5
LANES = 128
PANEL = 8
BLOCK = 2 * PANEL
VMEM_LIMIT = 48 * 1024 * 1024
HIGHEST = lax.Precision.HIGHEST
VMEM = pl.BlockSpec(memory_space=pltpu.VMEM)
SMEM = pl.BlockSpec(memory_space=pltpu.SMEM)
HBM = pl.BlockSpec(memory_space=pltpu.HBM)
PARAMS = pltpu.CompilerParams(vmem_limit_bytes=VMEM_LIMIT)


class Place:
    def __init__(self, dp_names, own_names):
        self.dp, self.own = dp_names, own_names
        self.core, self.second, self.near, self.far = (
            dp_names[-1],
            dp_names[-2],
            dp_names[1],
            dp_names[0],
        )
        self.first = own_names[-1]
        used = (self.core, self.second, self.near, self.far, self.first)
        self.extra = tuple(n for n in dp_names + own_names if n not in used)

    def index(self, names):
        value = jnp.int32(0)
        for name in names:
            value = value * 2 + lax.axis_index(name)
        return value

    def layer(self):
        return self.index((self.near, self.second, self.first))


def transposed_dot(a, b, precision=None):
    return lax.dot_general(
        a, b, (((0,), (0,)), ((), ())), precision=precision, preferred_element_type=jnp.float32
    )


def layer_copies(place, sources, buffers, sems):
    layer = place.layer()
    return [
        [
            pltpu.make_async_copy(
                source.at[jnp.bitwise_xor(layer, i)], buffer.at[i], sems.at[i, s]
            )
            for s, (source, buffer) in enumerate(zip(sources, buffers))
        ]
        for i in range(buffers[0].shape[0])
    ]


def both_halves(place, flat, i):
    rows = flat.shape[1] // 2
    core = lax.axis_index(place.core)
    kept = pl.multiple_of(core * rows, PANEL)
    sent = pl.multiple_of((1 - core) * rows, PANEL)
    return flat[i, pl.ds(kept, rows), :], flat[i, pl.ds(sent, rows), :]


ORDERS = (("first", "second", "near"), ("second", "near", "first"))
LATE_ORDERS = (("first", "second", "near"), ("near", "first", "second"))


def position(axes, i):
    bits = {"near": i // 4, "second": (i // 2) % 2, "first": i % 2}
    return bits[axes[0]] * 4 + bits[axes[1]] * 2 + bits[axes[2]]


def positions(place, i, orders):
    core = lax.axis_index(place.core)
    first, second = (position(axes, i) for axes in orders)
    return jnp.where(core == 0, first, second), jnp.where(core == 0, second, first)


def iotas(shape):
    return (
        lax.broadcasted_iota(jnp.int32, shape, 0),
        lax.broadcasted_iota(jnp.int32, shape, 1),
    )


def pack_pair(first, second):
    row, col = iotas(first.shape)
    return jnp.where(row >= col, first, second)


def unpack_pair(packed, second_diagonal):
    row, col = iotas(packed.shape)
    turned = packed.T
    first = jnp.where(row >= col, packed, turned)
    second = jnp.where(col > row, packed, turned)
    return first, jnp.where(row == col, second_diagonal, second)


def fold(block):
    h = block.shape[0] // 2
    row, col = iotas((h, 2 * h))
    last = pltpu.roll(block[h:], h, 1)
    return jnp.where((col >= h) | (row >= col), block[:h], last)


def unfold(folded, diagonal):
    h, n = folded.shape
    row, col = iotas((n, n))
    block = jnp.concatenate([folded, jnp.zeros((h, n), jnp.float32)], axis=0)
    turned = block.T
    top = jnp.where((col >= h) | (col <= row), block, turned)
    moved = pltpu.roll(pltpu.roll(block, h, 0), h, 1)
    moved_turned = pltpu.roll(pltpu.roll(turned, h, 0), h, 1)
    last = jnp.where(col > row, moved, moved_turned)
    last = jnp.where(row == col, diagonal, last)
    return jnp.where(row < h, top, jnp.where(col < h, turned, last))


def diagonals(blocks, rows):
    n = blocks[0].shape[0]
    row, col = iotas((n, n))
    slab_row, _ = iotas((rows, n))
    slab = jnp.zeros((rows, n), jnp.float32)
    for i, block in enumerate(blocks):
        line = jnp.sum(jnp.where(row == col, block, 0.0), axis=0, keepdims=True)
        slab = jnp.where(slab_row == i, jnp.broadcast_to(line, (rows, n)), slab)
    return slab


EARLY_ROWS = 144
LATE_ROWS = 192


HOT = (1, 2, 3, 5, 6, 7)
COLD = (0, 4)


def square_sums(wide, narrow):
    return transposed_dot(wide, wide), transposed_dot(narrow, narrow)


def pack_layer(place, i, wcov, ncov, a_flat, b_flat):
    n = LANES
    last = wcov[n:, n:]
    a_flat[i, :n] = pack_pair(wcov[:n, :n], ncov)
    a_flat[i, n:] = diagonals((ncov, last), EARLY_ROWS - n)
    b_flat[i, :n] = wcov[:n, n:]
    b_flat[i, n:] = fold(last)
    a_kept, a_sent = both_halves(place, a_flat, i)
    b_kept, b_sent = both_halves(place, b_flat, i)
    return (a_kept, b_kept), (a_sent, b_sent)


def put(ref, index, parts):
    rows = EARLY_ROWS // 2
    ref[index, :rows] = parts[0]
    ref[index, rows:] = parts[1]


def put_layer(place, i, sums, a_flat, b_flat, keep, send):
    kept, sent = pack_layer(place, i, *sums, a_flat, b_flat)
    mine, other = positions(place, i, ORDERS)
    put(keep, mine, kept)
    put(send, other, sent)


def clear_others(place, layers, keep, send):
    for i in layers:
        mine, other = positions(place, i, ORDERS)
        keep[mine] = jnp.zeros(keep.shape[1:], jnp.float32)
        send[other] = jnp.zeros(send.shape[1:], jnp.float32)


def hot_kernel(place, wide_hbm, narrow_hbm, keep, send, wides, narrows, a_flat, b_flat, sems):
    copies = layer_copies(place, (wide_hbm, narrow_hbm), (wides, narrows), sems)
    for i in HOT + COLD:
        for copy in copies[i]:
            copy.start()
    clear_others(place, COLD, keep, send)
    for group in (HOT[:3], HOT[3:], COLD):
        for i in group:
            for copy in copies[i]:
                copy.wait()
        if group is not COLD:
            for i in group:
                sums = square_sums(wides[i], narrows[i])
                put_layer(place, i, sums, a_flat, b_flat, keep, send)


def cold_kernel(place, wides, narrows, keep, send, a_flat, b_flat):
    for i in COLD:
        put_layer(
            place, i, square_sums(wides[i], narrows[i]), a_flat, b_flat, keep, send
        )
    core = lax.axis_index(place.core)
    stay = [[i for i in HOT if position(axes, i) < 4] for axes in ORDERS]
    for first, second in zip(*stay):
        here = [position(axes, i) for axes, i in zip(ORDERS, (first, second))]
        mine = jnp.where(core == 0, here[0], here[1])
        other = jnp.where(core == 0, here[1], here[0])
        keep[mine] = jnp.zeros(keep.shape[1:], jnp.float32)
        send[other] = jnp.zeros(send.shape[1:], jnp.float32)


def write_slots(place, owner_map, slots_ref):
    own = place.index(place.own)
    count = jnp.int32(0)
    for l in range(slots_ref.shape[0]):
        mine = owner_map[l] == own
        slot = jnp.where(mine, count, -1)
        slots_ref[l] = jnp.full(slots_ref.shape[1:], 0, jnp.int32) + slot
        count = count + mine.astype(jnp.int32)


def mixed_kernel(place, owner_map, wides, narrows, keep, send, slots_ref, flat):
    n = LANES
    write_slots(place, owner_map, slots_ref)
    for i in range(wides.shape[0]):
        mixed = transposed_dot(narrows[i], wides[i])
        flat[i, :n] = mixed[:, :n]
        flat[i, n:] = mixed[:, n:]
        kept, sent = both_halves(place, flat, i)
        mine, other = positions(place, i, LATE_ORDERS)
        keep[mine] = kept
        send[other] = sent


def gram_cost(wide_rows, columns):
    return pl.CostEstimate(
        flops=2 * wide_rows.size * columns, bytes_accessed=2 * wide_rows.size, transcendentals=0
    )


HALF_ROWS = (EARLY_ROWS + LATE_ROWS) // 2


def pack_shapes(layers):
    return [
        pltpu.VMEM((layers, EARLY_ROWS, LANES), jnp.float32),
        pltpu.VMEM((layers, LATE_ROWS, LANES), jnp.float32),
    ]


def hot_squares(place, wide_rows, narrow_rows):
    layers = wide_rows.shape[0]
    half = jax.ShapeDtypeStruct((layers, HALF_ROWS, LANES), jnp.float32)
    return pl.pallas_call(
        functools.partial(hot_kernel, place),
        in_specs=[HBM, HBM],
        out_specs=[VMEM] * 4,
        out_shape=[
            half,
            half,
            jax.ShapeDtypeStruct(wide_rows.shape, wide_rows.dtype),
            jax.ShapeDtypeStruct(narrow_rows.shape, narrow_rows.dtype),
        ],
        scratch_shapes=[*pack_shapes(layers), pltpu.SemaphoreType.DMA((layers, 2))],
        cost_estimate=gram_cost(wide_rows, 240),
        compiler_params=PARAMS,
        name="hot_squares",
    )(
        pltpu.with_memory_space_constraint(wide_rows, pltpu.HBM),
        pltpu.with_memory_space_constraint(narrow_rows, pltpu.HBM),
    )


def cold_squares(place, wides, narrows):
    half = jax.ShapeDtypeStruct((wides.shape[0] // 2, HALF_ROWS, LANES), jnp.float32)
    return pl.pallas_call(
        functools.partial(cold_kernel, place),
        in_specs=[VMEM, VMEM],
        out_specs=[VMEM, VMEM],
        out_shape=[half, half],
        scratch_shapes=pack_shapes(wides.shape[0]),
        cost_estimate=gram_cost(wides, 80),
        compiler_params=PARAMS,
        name="cold_squares",
    )(wides, narrows)


def mixed_sums(place, owner_map, wides, narrows):
    layers, _, narrow = narrows.shape
    half = jax.ShapeDtypeStruct((layers, narrow, LANES), jnp.float32)
    return pl.pallas_call(
        functools.partial(mixed_kernel, place),
        in_specs=[SMEM, VMEM, VMEM],
        out_specs=[VMEM] * 3,
        out_shape=[half, half, jax.ShapeDtypeStruct((layers, PANEL, LANES), jnp.int32)],
        scratch_shapes=[pltpu.VMEM((layers, 2 * narrow, LANES), jnp.float32)],
        cost_estimate=gram_cost(wides, 128),
        compiler_params=PARAMS,
        name="mixed",
    )(owner_map, wides, narrows)


def lane_gather(x, index):
    return jnp.take_along_axis(x, index, axis=1, mode="promise_in_bounds")


def trailing_update(a_ref, left_ref, right_ref, base):
    size = a_ref.shape[1]
    a_ref[pl.ds(pl.multiple_of(base, BLOCK), BLOCK), :] = jnp.zeros((BLOCK, size), jnp.float32)
    lane = lax.broadcasted_iota(jnp.int32, (1, size), 1)
    swept = (lane >= base - BLOCK) & (lane < base)
    update = transposed_dot(left_ref[...], right_ref[...])
    a_ref[BLOCK : BLOCK + size, :] = (
        jnp.where(swept, 0.0, a_ref[BLOCK : BLOCK + size, :]) - update
    )


def in_three(x):
    high = x.astype(jnp.bfloat16).astype(jnp.float32)
    rest = x - high
    middle = rest.astype(jnp.bfloat16).astype(jnp.float32)
    return high, middle, rest - middle


def factor_panel(rows_ref, cols_ref, tile, first, panel, targets):
    tiles = panel.shape[1] // LANES
    shape = (PANEL, LANES)
    _, lane = iotas(shape)

    def on_all(ref, k, lanes):
        return jnp.broadcast_to(ref[k : k + 1, lanes], shape)

    rows_ref[...] = panel
    lanes = [slice(LANES * t, LANES * (t + 1)) for t in range(tiles)]
    rows = [[on_all(rows_ref, k, part) for part in lanes] for k in range(PANEL)]
    here = panel[:, lanes[tile]]
    for j in range(PANEL):
        column = lane_gather(here, jnp.full(shape, 0, jnp.int32) + (first + j))
        cols_ref[PANEL * j : PANEL * (j + 1)] = column
    d = [[None] * PANEL for _ in range(PANEL)]
    for j in range(PANEL):
        for i in range(j, PANEL):
            d[i][j] = on_all(cols_ref, PANEL * j + i, slice(None))
    own = (lane >= first) & (lane < first + PANEL)
    q = [[None] * tiles for _ in range(PANEL)]
    p = [[None] * tiles for _ in range(PANEL)]
    weights = [[None] * PANEL for _ in targets]
    factor = [[None] * PANEL for _ in range(PANEL)]

    def substitute(k, scale):
        for t in range(tiles):
            value = rows[k][t]
            if t == tile:
                value = jnp.where(own, jnp.where(lane == first + k, -1.0, 0.0), value)
            for j in range(k):
                value = value - factor[k][j] * q[j][t]
            q[k][t] = value
            p[k][t] = value * scale
        for target, weight in zip(targets, weights):
            source, index = target(rows[k])
            value = lane_gather(source, index)
            for j in range(k):
                value = value - factor[k][j] * weight[j]
            weight[k] = value

    for k in range(0, PANEL, 2):
        m = k + 1
        a, b, c = d[k][k], d[m][k], d[m][m]
        first_scale = 1.0 / a
        second_scale = a * (1.0 / (a * c - b * b))
        factor[m][k] = b * first_scale
        left_over = {i: d[i][m] - d[i][k] * factor[m][k] for i in range(k + 2, PANEL)}
        for i in range(k + 2, PANEL):
            factor[i][k] = d[i][k] * first_scale
            factor[i][m] = left_over[i] * second_scale
        for i in range(k + 2, PANEL):
            for j in range(k + 2, i + 1):
                value = d[i][j] - d[i][k] * factor[j][k]
                d[i][j] = value - (left_over[i] * left_over[j]) * second_scale
        substitute(k, first_scale)
        substitute(m, second_scale)
    return q, p, weights


def packed_rows(values):
    sub, _ = iotas((PANEL, LANES))
    whole = []
    for t in range(len(values[0])):
        value = values[0][t]
        for k in range(1, PANEL):
            value = jnp.where(sub == k, values[k][t], value)
        whole.append(value)
    return whole


def side_by_side(tiles):
    return jnp.concatenate(tiles, axis=1) if len(tiles) > 1 else tiles[0]


def sweep_block(a_ref, left_ref, right_ref, a_rows, a_cols, b_rows, b_cols, tile, step, block):
    size = a_ref.shape[1]
    tiles = size // LANES
    first = step * BLOCK
    second = first + PANEL
    base = tile * LANES + first
    trailing_update(a_ref, left_ref, right_ref, base)

    sub, lane = iotas((PANEL, LANES))
    last = first == LANES - BLOCK
    next_first = jnp.where(last, 0, first + BLOCK)

    def in_block(row):
        return row[tile], second + sub

    def in_next(offset):
        def target(row):
            source = row[tile]
            if tile + 1 < tiles:
                source = jnp.where(last, row[tile + 1], source)
            return source, next_first + offset + sub

        return target

    nexts = [in_next(0), in_next(PANEL)]
    in_a = (lane >= first) & (lane < second)
    in_b = (lane >= second) & (lane < second + PANEL)

    def swept(tiles_of, mask):
        return [jnp.where(mask, 0.0, v) if t == tile else v for t, v in enumerate(tiles_of)]

    def minus(tiles_of, weight, p):
        result = []
        for t, value in enumerate(tiles_of):
            for k in range(PANEL):
                value = value - weight[k] * p[k][t]
            result.append(value)
        return result

    def by_tile(rows):
        return [rows[:, LANES * t : LANES * (t + 1)] for t in range(tiles)]

    qa, pa, (to_b, *to_next_a) = factor_panel(
        a_rows, a_cols, tile, first, block[:PANEL], [in_block, *nexts]
    )
    panel_b = side_by_side(minus(swept(by_tile(block[PANEL:]), in_a), to_b, pa))
    qb, pb, to_next_b = factor_panel(b_rows, b_cols, tile, second, panel_b, nexts)

    left, right = [], []
    for q, p, mask in ((qa, pa, in_b), (qb, pb, None)):
        q, p = packed_rows(q), packed_rows(p)
        if mask is not None:
            q, p = swept(q, mask), swept(p, mask)
        qs, ps = in_three(side_by_side(q)), in_three(side_by_side(p))
        left += [qs[i] for i in (0, 0, 1, 1, 0, 2)]
        right += [ps[i] for i in (0, 1, 0, 1, 2, 0)]
    left_ref[...] = jnp.concatenate(left, axis=0).astype(jnp.bfloat16)
    right_ref[...] = jnp.concatenate(right, axis=0).astype(jnp.bfloat16)

    following = a_ref[pl.ds(pl.multiple_of(base + 2 * BLOCK, BLOCK), BLOCK), :]
    result = []
    for g in range(2):
        rows = by_tile(following[g * PANEL : (g + 1) * PANEL])
        rows = minus(swept(rows, in_a), to_next_a[g], pa)
        rows = minus(swept(rows, in_b), to_next_b[g], pb)
        result.append(side_by_side(rows))
    return jnp.concatenate(result, axis=0)


def place_halves(place, pieces, first_row, flat):
    core = lax.axis_index(place.core)
    rows = flat.shape[0] // 2
    for r, piece in enumerate(pieces):
        start = pl.multiple_of(jnp.bitwise_xor(core, r) * rows, PANEL)
        flat[pl.ds(start, rows), :] = piece[first_row : first_row + rows]


def sweep_cost():
    return pl.CostEstimate(flops=1 << 30, bytes_accessed=1 << 20, transcendentals=0)


def clear(work):
    a_ref, left, right = work[:3]
    size = a_ref.shape[1]
    a_ref[:BLOCK] = jnp.zeros((BLOCK, size), jnp.float32)
    a_ref[BLOCK + size :] = jnp.zeros((BLOCK, size), jnp.float32)
    left[...] = jnp.zeros(left.shape, left.dtype)
    right[...] = jnp.zeros(right.shape, right.dtype)


def work_shapes(size):
    splits = 6 * BLOCK
    return [
        pltpu.VMEM((size + 2 * BLOCK, size), jnp.float32),
        pltpu.VMEM((splits, size), jnp.bfloat16),
        pltpu.VMEM((splits, size), jnp.bfloat16),
    ]


def row_shapes(size):
    return [
        pltpu.VMEM((PANEL, size), jnp.float32),
        pltpu.VMEM((PANEL * PANEL, LANES), jnp.float32),
    ] * 2


def aligned_rows(ref, index, count):
    if count % PANEL == 0:
        return ref[pl.ds(pl.multiple_of(index * count, count), count), :]
    per_slab = PANEL // count
    slab = ref[pl.ds(pl.multiple_of(index // per_slab * PANEL, PANEL), PANEL), :]
    value = slab[:count]
    for i in range(1, per_slab):
        value = jnp.where(index % per_slab == i, slab[i * count : (i + 1) * count], value)
    return value


def packs(cols, rows):
    return cols == 2 * PANEL and 2 * rows == LANES


def dot(a, b, last=False):
    return lax.dot_general(
        a,
        b,
        (((1,), (1 if last else 0,)), ((), ())),
        precision=HIGHEST,
        preferred_element_type=jnp.float32,
    )


STEPS = LANES // BLOCK
FIRST_STEPS = 5
SECOND_STEPS = 6


def sweep_both(wide_work, narrow_work, begin, end, blocks):
    def step(i, blocks):
        return (
            sweep_block(*wide_work, 0, i, blocks[0]),
            sweep_block(*narrow_work, 0, i, blocks[1]),
        )

    return lax.fori_loop(begin, end, step, blocks)


def sweep_wide(work, begin, end, block):
    return lax.fori_loop(begin, end, lambda i, block: sweep_block(*work, 1, i, block), block)


def unit_scale(block):
    row, col = iotas(block.shape)
    line = jnp.sum(jnp.where(row == col, block, 0.0), axis=0, keepdims=True)
    return jnp.broadcast_to(lax.rsqrt(line), (PANEL, block.shape[1]))


def on_rows(scale):
    n = scale.shape[1]
    return jnp.broadcast_to(scale[:1], (n, n))


def scaled(block, down, across):
    return (block * on_rows(down).T) * on_rows(across)


def first_kernel(
    place, total, mine, other, wa, wl, wr, wp, na, nl, nr, np_, ws_ref, ns_ref, *refs
):
    a_flat, b_flat = refs[:2]
    wide_work, narrow_work = (wa, wl, wr, *refs[2:6]), (na, nl, nr, *refs[6:])
    place_halves(place, (mine, other), 0, a_flat)
    place_halves(place, (mine, other), a_flat.shape[0] // 2, b_flat)
    n = LANES
    slab = a_flat[n : n + PANEL]
    first, square = unpack_pair(a_flat[:n], jnp.broadcast_to(slab[:1], (n, n)))
    corner = b_flat[:n] / total
    last = unfold(b_flat[n:], jnp.broadcast_to(slab[1:2], (n, n)))
    row, col = iotas((n, n))
    damp = jnp.where(row == col, DAMP, 0.0)
    clear(wide_work)
    clear(narrow_work)
    first, last, square = first / total + damp, last / total + damp, square / total + damp
    by_first, by_last, by_square = (unit_scale(block) for block in (first, last, square))
    ws_ref[:, :n] = by_first
    ws_ref[:, n:] = by_last
    ns_ref[...] = by_square
    first_across, last_across = on_rows(by_first), on_rows(by_last)
    first_down, last_down = first_across.T, last_across.T
    corner = (corner * first_down) * last_across
    wa[BLOCK : BLOCK + n, :n] = (first * first_down) * first_across
    wa[BLOCK : BLOCK + n, n:] = corner
    wa[BLOCK + n : BLOCK + 2 * n, :n] = corner.T
    wa[BLOCK + n : BLOCK + 2 * n, n:] = (last * last_down) * last_across
    na[BLOCK : BLOCK + n, :] = scaled(square, by_square, by_square)
    start = (wa[BLOCK : 2 * BLOCK, :], na[BLOCK : 2 * BLOCK, :])
    wp[...], np_[...] = sweep_both(wide_work, narrow_work, 0, FIRST_STEPS, start)


def second_kernel(*refs):
    given, scale, ninv_ref, state, narrow_state, wide_rows, narrow_rows = (
        refs[:8],
        refs[8],
        refs[9],
        refs[10:14],
        refs[14:17],
        refs[17:21],
        refs[21:],
    )
    for source, target in zip((*given[:3], *given[4:7]), (*state[:3], *narrow_state)):
        target[...] = source[...]
    wide_work, narrow_work = (*state[:3], *wide_rows), (*narrow_state, *narrow_rows)
    wp = state[3]
    panels = (given[3][...], given[7][...])
    panel, _ = sweep_both(wide_work, narrow_work, FIRST_STEPS, STEPS, panels)
    trailing_update(*narrow_work[:3], LANES)
    by_square = scale[...]
    ninv_ref[...] = scaled(-narrow_work[0][BLOCK : BLOCK + LANES, :], by_square, by_square)
    wp[...] = sweep_wide(wide_work, 0, SECOND_STEPS, panel)


def third_kernel(wa_in, wl_in, wr_in, panel_in, scale, winv, wa, wl, wr, *rows):
    wa[...] = wa_in[...]
    wl[...] = wl_in[...]
    wr[...] = wr_in[...]
    sweep_wide((wa, wl, wr, *rows), SECOND_STEPS, STEPS, panel_in[...])
    wide = wa.shape[1]
    trailing_update(wa, wl, wr, wide)
    parts = [slice(i, i + LANES) for i in range(0, wide, LANES)]
    across = [on_rows(scale[:, i]) for i in parts]
    down = [block.T for block in across]
    for i, rows_scale in zip(parts, down):
        for j, columns_scale in zip(parts, across):
            block = -wa[BLOCK + i.start : BLOCK + i.stop, j]
            winv[i, j] = (block * rows_scale) * columns_scale


def state_shapes(size):
    shapes = [jax.ShapeDtypeStruct(v.shape, v.dtype) for v in work_shapes(size)]
    return shapes + [jax.ShapeDtypeStruct((BLOCK, size), jnp.float32)]


def sweep_call(kernel, name, args, out_shapes, scratch):
    return pl.pallas_call(
        kernel,
        in_specs=[VMEM] * len(args),
        out_specs=[VMEM] * len(out_shapes),
        out_shape=out_shapes,
        scratch_shapes=scratch,
        cost_estimate=sweep_cost(),
        compiler_params=PARAMS,
        name=name,
    )(*args)


def first_panels(place, pieces, wide, narrow, total):
    return sweep_call(
        functools.partial(first_kernel, place, total),
        "first_panels",
        pieces,
        state_shapes(wide)
        + state_shapes(narrow)
        + [jax.ShapeDtypeStruct((PANEL, n), jnp.float32) for n in (wide, narrow)],
        [
            pltpu.VMEM((EARLY_ROWS, LANES), jnp.float32),
            pltpu.VMEM((LATE_ROWS, LANES), jnp.float32),
            *row_shapes(wide),
            *row_shapes(narrow),
        ],
    )


def second_panels(state, wide, narrow):
    ninv = jax.ShapeDtypeStruct((narrow, narrow), jnp.float32)
    return sweep_call(
        second_kernel,
        "second_panels",
        state,
        [ninv] + state_shapes(wide),
        [*work_shapes(narrow), *row_shapes(wide), *row_shapes(narrow)],
    )


def third_panels(state, wide):
    winv = jax.ShapeDtypeStruct((wide, wide), jnp.float32)
    scratch = [*work_shapes(wide), *row_shapes(wide)]
    return sweep_call(third_kernel, "third_panels", state, [winv], scratch)[0]


def product_kernel(place, total, rows, winv, ninv_ref, mine, other, out_ref, flat):
    place_halves(place, (mine, other), 0, flat)
    ninv = ninv_ref[...]
    n = LANES
    inner = jnp.concatenate(
        [
            transposed_dot(flat[c * n : (c + 1) * n] / total, ninv, HIGHEST)
            for c in range(2)
        ],
        axis=0,
    )
    wide = winv.shape[1]
    cols = wide // 2 ** len(place.dp)
    near, second = lax.axis_index(place.near), lax.axis_index(place.second)
    near_stride = 2 ** (len(place.dp) - 2)
    base = place.index(place.dp) - near * near_stride - second * 2
    _, lane = iotas((PANEL, LANES))
    picks = [
        aligned_rows(winv, base + (j // 2) * near_stride + (j % 2) * 2, cols) for j in range(4)
    ]
    if cols % PANEL == 0:
        whole = dot(jnp.concatenate(picks, axis=0), inner)
        updates = [whole[j * cols : (j + 1) * cols] for j in range(4)]
    else:
        updates = [dot(picked, inner) for picked in picks]
    for j, (picked, update) in enumerate(zip(picks, updates)):
        for x in range(2):
            block = 2 * j + x
            out_ref[block, :cols] = picked[:, :LANES]
            out_ref[block, cols : 2 * cols] = picked[:, LANES:]
            if packs(cols, rows):
                upper, lower = update[:PANEL], update[PANEL:]
                if x == 0:
                    lower = pltpu.roll(lower, rows, 1)
                else:
                    upper = pltpu.roll(upper, rows, 1)
                out_ref[block, 2 * cols :] = jnp.where(lane < rows, upper, lower)
            else:
                out_ref[block, 2 * cols :] = update


def products(place, winv, ninv, pieces, rows, total):
    wide, narrow = winv.shape[0], ninv.shape[0]
    cols = wide // 2 ** len(place.dp)
    height = 2 * cols + (PANEL if packs(cols, rows) else cols)
    return pl.pallas_call(
        functools.partial(product_kernel, place, total, rows),
        in_specs=[VMEM] * 4,
        out_specs=VMEM,
        out_shape=jax.ShapeDtypeStruct((8, height, LANES), jnp.float32),
        scratch_shapes=[pltpu.VMEM((2 * narrow, LANES), jnp.float32)],
        compiler_params=PARAMS,
        name="products",
    )(winv, ninv, *pieces)


def placing_kernel(place, slots_ref, got_ref, kept_ref, update_ref):
    layers = got_ref.shape[0]
    slots, cols, wide = kept_ref.shape
    rows = update_ref.shape[2]
    own, dp = place.index(place.own), place.index(place.dp)
    step = min(cols, PANEL)
    row, col = iotas((step, LANES))
    for h in range(wide // LANES):
        lanes = slice(h * LANES, (h + 1) * LANES)
        for r in range(0, cols, step):
            here = h * cols + r
            empty = jnp.where(col + h * LANES == row + dp * cols + r, 1.0 / DAMP, 0.0)
            for c in range(slots):
                value = empty
                for l in range(layers):
                    taken = slots_ref[l, :step] == c
                    value = jnp.where(taken, got_ref[l, here : here + step], value)
                kept_ref[c, r : r + step, lanes] = value
    for l in range(layers):
        value = got_ref[l, 2 * cols :]
        if packs(cols, rows):
            update_ref[l, :PANEL] = value[:, :rows]
            update_ref[l, PANEL:] = value[:, rows:]
        else:
            part = value[:, :rows]
            for p in range(1, LANES // rows):
                part = jnp.where(own == p, value[:, p * rows : (p + 1) * rows], part)
            update_ref[l] = part


def placing(place, slots_of, got, wide, cols, slots, rows):
    layers = got.shape[0]
    return pl.pallas_call(
        functools.partial(placing_kernel, place),
        in_specs=[VMEM, VMEM],
        out_specs=[VMEM, VMEM],
        out_shape=[
            jax.ShapeDtypeStruct((slots, cols, wide), jnp.float32),
            jax.ShapeDtypeStruct((layers, cols, rows), jnp.float32),
        ],
        compiler_params=PARAMS,
        name="placing",
    )(slots_of, got)


def swap(value, axis):
    return lax.ppermute(value, axis, [(0, 1), (1, 0)])


def swap_by_core(value, place, stage, orders):
    names = (place.near, place.second, place.core, place.first)
    flips = {"near": 8, "second": 4, "first": 1}
    pairs = [(i, i ^ flips[orders[(i >> 1) & 1][stage]]) for i in range(16)]
    return lax.ppermute(value, names, pairs)


def after(value, *others):
    return lax.optimization_barrier((value,) + others)[0]


def on_device(place, wide_rows, narrow_rows, owner_map):
    layers, rows, wide = wide_rows.shape
    narrow = narrow_rows.shape[2]
    n_dp, n_own = 2 ** len(place.dp), 2 ** len(place.own)
    total = float(rows * n_dp * n_own)

    h_keep, h_send, wides, narrows = hot_squares(place, wide_rows, narrow_rows)
    first_send = h_send[4:]
    h_got = swap(first_send, place.core)
    c_keep, c_send = cold_squares(place, after(wides, first_send), narrows)
    h_keep, c_send = lax.optimization_barrier((h_keep, c_send))

    hot = h_keep[4:] + h_got
    s_got = swap_by_core(hot, place, 0, ORDERS)
    m_keep, m_send, slots_of = mixed_sums(place, owner_map, after(wides, hot), narrows)
    c_got = swap(after(c_send + h_send[:4], m_send), place.core)
    m_got = swap(m_send, place.core)

    s = (c_keep + h_keep[:4]) + s_got
    s = s + after(c_got, s)
    s_got = swap_by_core(s[2:], place, 1, ORDERS)
    m = after(m_keep, s) + m_got
    m_got = swap_by_core(m[4:], place, 0, LATE_ORDERS)

    s = s[:2] + s_got
    s_got = swap_by_core(s[1], place, 2, ORDERS)
    m = after(m[:4], s) + m_got
    m_got = swap_by_core(m[2:], place, 1, LATE_ORDERS)

    s = s[0] + s_got
    if place.extra:
        s = lax.psum(s, place.extra)
    s_got = swap(s, place.far)
    m = after(m[:2], s) + m_got
    m_got = swap_by_core(m[1], place, 2, LATE_ORDERS)

    s = s + s_got
    state = first_panels(place, [s, swap(s, place.core)], wide, narrow, total)
    m = after(m[0], state[0]) + m_got
    if place.extra:
        m = lax.psum(m, place.extra)
    m_got = swap(m, place.far)
    *state, wide_scale, narrow_scale = state
    ninv, *state = second_panels([*state, narrow_scale], wide, narrow)
    m = after(m, ninv) + m_got
    m_got = swap(m, place.core)
    winv = third_panels([*state, wide_scale], wide)
    cols, own_rows = wide // n_dp, narrow // n_own
    sent = products(place, winv, ninv, [m, m_got], own_rows, total)
    got = lax.all_to_all(sent, (place.near, place.second, place.first), 0, 0)
    kept, update = placing(
        place, slots_of, got, wide, cols, layers // n_own + 1, own_rows
    )
    return (jnp.swapaxes(kept, 1, 2), jnp.swapaxes(update, 1, 2))


def solution(mesh):
    n_dp, n_own = mesh.shape["dp"], mesh.shape["own"]
    dp_names = tuple(f"dp{i}" for i in range(int(np.log2(n_dp))))
    own_names = tuple(f"own{i}" for i in range(int(np.log2(n_own))))
    names = dp_names + own_names
    bits = jax.sharding.Mesh(mesh.devices.reshape((2,) * len(names)), names)
    in_specs = (P(None, names, None), P(None, names, None), P())
    out_specs = (P(own_names, None, dp_names), P(None, own_names, dp_names))
    return jax.shard_map(
        functools.partial(on_device, Place(dp_names, own_names)),
        mesh=bits,
        in_specs=in_specs,
        out_specs=out_specs,
        check_vma=False,
    )
```

```python
import functools

import jax
import jax.numpy as jnp
import numpy as np
from jax import lax
from jax.experimental import pallas as pl
from jax.experimental.pallas import tpu as pltpu
from jax.sharding import PartitionSpec as P

DAMP = 0.5
LANES = 128
PANEL = 8
BLOCK = 2 * PANEL
VMEM_LIMIT = 48 * 1024 * 1024
HIGHEST = lax.Precision.HIGHEST
VMEM = pl.BlockSpec(memory_space=pltpu.VMEM)
SMEM = pl.BlockSpec(memory_space=pltpu.SMEM)
HBM = pl.BlockSpec(memory_space=pltpu.HBM)
PARAMS = pltpu.CompilerParams(vmem_limit_bytes=VMEM_LIMIT)


class Place:
    def __init__(self, dp_names, own_names):
        self.dp, self.own = dp_names, own_names
        self.core, self.second, self.near, self.far = (
            dp_names[-1],
            dp_names[-2],
            dp_names[1],
            dp_names[0],
        )
        self.first = own_names[-1]
        used = (self.core, self.second, self.near, self.far, self.first)
        self.extra = tuple(n for n in dp_names + own_names if n not in used)

    def index(self, names):
        value = jnp.int32(0)
        for name in names:
            value = value * 2 + lax.axis_index(name)
        return value

    def layer(self):
        return self.index((self.near, self.second, self.first))


def transposed_dot(a, b, precision=None):
    return lax.dot_general(
        a, b, (((0,), (0,)), ((), ())), precision=precision, preferred_element_type=jnp.float32
    )


def layer_copies(place, sources, buffers, sems):
    layer = place.layer()
    return [
        [
            pltpu.make_async_copy(
                source.at[jnp.bitwise_xor(layer, i)], buffer.at[i], sems.at[i, s]
            )
            for s, (source, buffer) in enumerate(zip(sources, buffers))
        ]
        for i in range(buffers[0].shape[0])
    ]


def both_halves(place, flat, i):
    rows = flat.shape[1] // 2
    core = lax.axis_index(place.core)
    kept = pl.multiple_of(core * rows, PANEL)
    sent = pl.multiple_of((1 - core) * rows, PANEL)
    return flat[i, pl.ds(kept, rows), :], flat[i, pl.ds(sent, rows), :]


ORDERS = (("first", "second", "near"), ("second", "near", "first"))
LATE_ORDERS = (("first", "second", "near"), ("near", "first", "second"))


def position(axes, i):
    bits = {"near": i // 4, "second": (i // 2) % 2, "first": i % 2}
    return bits[axes[0]] * 4 + bits[axes[1]] * 2 + bits[axes[2]]


def positions(place, i, orders):
    core = lax.axis_index(place.core)
    first, second = (position(axes, i) for axes in orders)
    return jnp.where(core == 0, first, second), jnp.where(core == 0, second, first)


def iotas(shape):
    return (
        lax.broadcasted_iota(jnp.int32, shape, 0),
        lax.broadcasted_iota(jnp.int32, shape, 1),
    )


def pack_pair(first, second):
    row, col = iotas(first.shape)
    return jnp.where(row >= col, first, second)


def unpack_pair(packed, second_diagonal):
    row, col = iotas(packed.shape)
    turned = packed.T
    first = jnp.where(row >= col, packed, turned)
    second = jnp.where(col > row, packed, turned)
    return first, jnp.where(row == col, second_diagonal, second)


def fold(block):
    h = block.shape[0] // 2
    row, col = iotas((h, 2 * h))
    last = pltpu.roll(block[h:], h, 1)
    return jnp.where((col >= h) | (row >= col), block[:h], last)


def unfold(folded, diagonal):
    h, n = folded.shape
    row, col = iotas((n, n))
    block = jnp.concatenate([folded, jnp.zeros((h, n), jnp.float32)], axis=0)
    turned = block.T
    top = jnp.where((col >= h) | (col <= row), block, turned)
    moved = pltpu.roll(pltpu.roll(block, h, 0), h, 1)
    moved_turned = pltpu.roll(pltpu.roll(turned, h, 0), h, 1)
    last = jnp.where(col > row, moved, moved_turned)
    last = jnp.where(row == col, diagonal, last)
    return jnp.where(row < h, top, jnp.where(col < h, turned, last))


def diagonals(blocks, rows):
    n = blocks[0].shape[0]
    row, col = iotas((n, n))
    slab_row, _ = iotas((rows, n))
    slab = jnp.zeros((rows, n), jnp.float32)
    for i, block in enumerate(blocks):
        line = jnp.sum(jnp.where(row == col, block, 0.0), axis=0, keepdims=True)
        slab = jnp.where(slab_row == i, jnp.broadcast_to(line, (rows, n)), slab)
    return slab


EARLY_ROWS = 144
LATE_ROWS = 192


HOT = (1, 2, 3, 5, 6, 7)
COLD = (0, 4)


def square_sums(wide, narrow):
    return transposed_dot(wide, wide), transposed_dot(narrow, narrow)


def pack_layer(place, i, wcov, ncov, a_flat, b_flat):
    n = LANES
    last = wcov[n:, n:]
    a_flat[i, :n] = pack_pair(wcov[:n, :n], ncov)
    a_flat[i, n:] = diagonals((ncov, last), EARLY_ROWS - n)
    b_flat[i, :n] = wcov[:n, n:]
    b_flat[i, n:] = fold(last)
    a_kept, a_sent = both_halves(place, a_flat, i)
    b_kept, b_sent = both_halves(place, b_flat, i)
    return (a_kept, b_kept), (a_sent, b_sent)


def put(ref, index, parts):
    rows = EARLY_ROWS // 2
    ref[index, :rows] = parts[0]
    ref[index, rows:] = parts[1]


def put_layer(place, i, sums, a_flat, b_flat, keep, send):
    kept, sent = pack_layer(place, i, *sums, a_flat, b_flat)
    mine, other = positions(place, i, ORDERS)
    put(keep, mine, kept)
    put(send, other, sent)


def clear_others(place, layers, keep, send):
    for i in layers:
        mine, other = positions(place, i, ORDERS)
        keep[mine] = jnp.zeros(keep.shape[1:], jnp.float32)
        send[other] = jnp.zeros(send.shape[1:], jnp.float32)


def hot_kernel(place, wide_hbm, narrow_hbm, keep, send, wides, narrows, a_flat, b_flat, sems):
    copies = layer_copies(place, (wide_hbm, narrow_hbm), (wides, narrows), sems)
    for i in HOT + COLD:
        for copy in copies[i]:
            copy.start()
    clear_others(place, COLD, keep, send)
    for group in (HOT[:3], HOT[3:], COLD):
        for i in group:
            for copy in copies[i]:
                copy.wait()
        if group is not COLD:
            for i in group:
                sums = square_sums(wides[i], narrows[i])
                put_layer(place, i, sums, a_flat, b_flat, keep, send)


def cold_kernel(place, wides, narrows, keep, send, a_flat, b_flat):
    for i in COLD:
        put_layer(
            place, i, square_sums(wides[i], narrows[i]), a_flat, b_flat, keep, send
        )
    core = lax.axis_index(place.core)
    stay = [[i for i in HOT if position(axes, i) < 4] for axes in ORDERS]
    for first, second in zip(*stay):
        here = [position(axes, i) for axes, i in zip(ORDERS, (first, second))]
        mine = jnp.where(core == 0, here[0], here[1])
        other = jnp.where(core == 0, here[1], here[0])
        keep[mine] = jnp.zeros(keep.shape[1:], jnp.float32)
        send[other] = jnp.zeros(send.shape[1:], jnp.float32)


def write_slots(place, owner_map, slots_ref):
    own = place.index(place.own)
    count = jnp.int32(0)
    for l in range(slots_ref.shape[0]):
        mine = owner_map[l] == own
        slot = jnp.where(mine, count, -1)
        slots_ref[l] = jnp.full(slots_ref.shape[1:], 0, jnp.int32) + slot
        count = count + mine.astype(jnp.int32)


def mixed_kernel(place, owner_map, wides, narrows, keep, send, slots_ref, flat):
    n = LANES
    write_slots(place, owner_map, slots_ref)
    for i in range(wides.shape[0]):
        mixed = transposed_dot(narrows[i], wides[i])
        flat[i, :n] = mixed[:, :n]
        flat[i, n:] = mixed[:, n:]
        kept, sent = both_halves(place, flat, i)
        mine, other = positions(place, i, LATE_ORDERS)
        keep[mine] = kept
        send[other] = sent


def gram_cost(wide_rows, columns):
    return pl.CostEstimate(
        flops=2 * wide_rows.size * columns, bytes_accessed=2 * wide_rows.size, transcendentals=0
    )


HALF_ROWS = (EARLY_ROWS + LATE_ROWS) // 2


def pack_shapes(layers):
    return [
        pltpu.VMEM((layers, EARLY_ROWS, LANES), jnp.float32),
        pltpu.VMEM((layers, LATE_ROWS, LANES), jnp.float32),
    ]


def hot_squares(place, wide_rows, narrow_rows):
    layers = wide_rows.shape[0]
    half = jax.ShapeDtypeStruct((layers, HALF_ROWS, LANES), jnp.float32)
    return pl.pallas_call(
        functools.partial(hot_kernel, place),
        in_specs=[HBM, HBM],
        out_specs=[VMEM] * 4,
        out_shape=[
            half,
            half,
            jax.ShapeDtypeStruct(wide_rows.shape, wide_rows.dtype),
            jax.ShapeDtypeStruct(narrow_rows.shape, narrow_rows.dtype),
        ],
        scratch_shapes=[*pack_shapes(layers), pltpu.SemaphoreType.DMA((layers, 2))],
        cost_estimate=gram_cost(wide_rows, 240),
        compiler_params=PARAMS,
        name="hot_squares",
    )(
        pltpu.with_memory_space_constraint(wide_rows, pltpu.HBM),
        pltpu.with_memory_space_constraint(narrow_rows, pltpu.HBM),
    )


def cold_squares(place, wides, narrows):
    half = jax.ShapeDtypeStruct((wides.shape[0] // 2, HALF_ROWS, LANES), jnp.float32)
    return pl.pallas_call(
        functools.partial(cold_kernel, place),
        in_specs=[VMEM, VMEM],
        out_specs=[VMEM, VMEM],
        out_shape=[half, half],
        scratch_shapes=pack_shapes(wides.shape[0]),
        cost_estimate=gram_cost(wides, 80),
        compiler_params=PARAMS,
        name="cold_squares",
    )(wides, narrows)


def mixed_sums(place, owner_map, wides, narrows):
    layers, _, narrow = narrows.shape
    half = jax.ShapeDtypeStruct((layers, narrow, LANES), jnp.float32)
    return pl.pallas_call(
        functools.partial(mixed_kernel, place),
        in_specs=[SMEM, VMEM, VMEM],
        out_specs=[VMEM] * 3,
        out_shape=[half, half, jax.ShapeDtypeStruct((layers, PANEL, LANES), jnp.int32)],
        scratch_shapes=[pltpu.VMEM((layers, 2 * narrow, LANES), jnp.float32)],
        cost_estimate=gram_cost(wides, 128),
        compiler_params=PARAMS,
        name="mixed",
    )(owner_map, wides, narrows)


def lane_gather(x, index):
    return jnp.take_along_axis(x, index, axis=1, mode="promise_in_bounds")


def trailing_update(a_ref, left_ref, right_ref, base):
    size = a_ref.shape[1]
    a_ref[pl.ds(pl.multiple_of(base, BLOCK), BLOCK), :] = jnp.zeros((BLOCK, size), jnp.float32)
    lane = lax.broadcasted_iota(jnp.int32, (1, size), 1)
    swept = (lane >= base - BLOCK) & (lane < base)
    update = transposed_dot(left_ref[...], right_ref[...])
    a_ref[BLOCK : BLOCK + size, :] = (
        jnp.where(swept, 0.0, a_ref[BLOCK : BLOCK + size, :]) - update
    )


def in_three(x):
    high = x.astype(jnp.bfloat16).astype(jnp.float32)
    rest = x - high
    middle = rest.astype(jnp.bfloat16).astype(jnp.float32)
    return high, middle, rest - middle


def factor_panel(rows_ref, cols_ref, tile, first, panel, targets):
    tiles = panel.shape[1] // LANES
    shape = (PANEL, LANES)
    _, lane = iotas(shape)

    def on_all(ref, k, lanes):
        return jnp.broadcast_to(ref[k : k + 1, lanes], shape)

    rows_ref[...] = panel
    lanes = [slice(LANES * t, LANES * (t + 1)) for t in range(tiles)]
    rows = [[on_all(rows_ref, k, part) for part in lanes] for k in range(PANEL)]
    here = panel[:, lanes[tile]]
    for j in range(PANEL):
        column = lane_gather(here, jnp.full(shape, 0, jnp.int32) + (first + j))
        cols_ref[PANEL * j : PANEL * (j + 1)] = column
    d = [[None] * PANEL for _ in range(PANEL)]
    for j in range(PANEL):
        for i in range(j, PANEL):
            d[i][j] = on_all(cols_ref, PANEL * j + i, slice(None))
    own = (lane >= first) & (lane < first + PANEL)
    q = [[None] * tiles for _ in range(PANEL)]
    p = [[None] * tiles for _ in range(PANEL)]
    weights = [[None] * PANEL for _ in targets]
    factor = [[None] * PANEL for _ in range(PANEL)]

    def substitute(k, scale):
        for t in range(tiles):
            value = rows[k][t]
            if t == tile:
                value = jnp.where(own, jnp.where(lane == first + k, -1.0, 0.0), value)
            for j in range(k):
                value = value - factor[k][j] * q[j][t]
            q[k][t] = value
            p[k][t] = value * scale
        for target, weight in zip(targets, weights):
            source, index = target(rows[k])
            value = lane_gather(source, index)
            for j in range(k):
                value = value - factor[k][j] * weight[j]
            weight[k] = value

    for k in range(0, PANEL, 2):
        m = k + 1
        a, b, c = d[k][k], d[m][k], d[m][m]
        first_scale = 1.0 / a
        second_scale = a * (1.0 / (a * c - b * b))
        factor[m][k] = b * first_scale
        left_over = {i: d[i][m] - d[i][k] * factor[m][k] for i in range(k + 2, PANEL)}
        for i in range(k + 2, PANEL):
            factor[i][k] = d[i][k] * first_scale
            factor[i][m] = left_over[i] * second_scale
        for i in range(k + 2, PANEL):
            for j in range(k + 2, i + 1):
                value = d[i][j] - d[i][k] * factor[j][k]
                d[i][j] = value - (left_over[i] * left_over[j]) * second_scale
        substitute(k, first_scale)
        substitute(m, second_scale)
    return q, p, weights


def packed_rows(values):
    sub, _ = iotas((PANEL, LANES))
    whole = []
    for t in range(len(values[0])):
        value = values[0][t]
        for k in range(1, PANEL):
            value = jnp.where(sub == k, values[k][t], value)
        whole.append(value)
    return whole


def side_by_side(tiles):
    return jnp.concatenate(tiles, axis=1) if len(tiles) > 1 else tiles[0]


def sweep_block(a_ref, left_ref, right_ref, a_rows, a_cols, b_rows, b_cols, tile, step, block):
    size = a_ref.shape[1]
    tiles = size // LANES
    first = step * BLOCK
    second = first + PANEL
    base = tile * LANES + first
    trailing_update(a_ref, left_ref, right_ref, base)

    sub, lane = iotas((PANEL, LANES))
    last = first == LANES - BLOCK
    next_first = jnp.where(last, 0, first + BLOCK)

    def in_block(row):
        return row[tile], second + sub

    def in_next(offset):
        def target(row):
            source = row[tile]
            if tile + 1 < tiles:
                source = jnp.where(last, row[tile + 1], source)
            return source, next_first + offset + sub

        return target

    nexts = [in_next(0), in_next(PANEL)]
    in_a = (lane >= first) & (lane < second)
    in_b = (lane >= second) & (lane < second + PANEL)

    def swept(tiles_of, mask):
        return [jnp.where(mask, 0.0, v) if t == tile else v for t, v in enumerate(tiles_of)]

    def minus(tiles_of, weight, p):
        result = []
        for t, value in enumerate(tiles_of):
            for k in range(PANEL):
                value = value - weight[k] * p[k][t]
            result.append(value)
        return result

    def by_tile(rows):
        return [rows[:, LANES * t : LANES * (t + 1)] for t in range(tiles)]

    qa, pa, (to_b, *to_next_a) = factor_panel(
        a_rows, a_cols, tile, first, block[:PANEL], [in_block, *nexts]
    )
    panel_b = side_by_side(minus(swept(by_tile(block[PANEL:]), in_a), to_b, pa))
    qb, pb, to_next_b = factor_panel(b_rows, b_cols, tile, second, panel_b, nexts)

    left, right = [], []
    for q, p, mask in ((qa, pa, in_b), (qb, pb, None)):
        q, p = packed_rows(q), packed_rows(p)
        if mask is not None:
            q, p = swept(q, mask), swept(p, mask)
        qs, ps = in_three(side_by_side(q)), in_three(side_by_side(p))
        left += [qs[i] for i in (0, 0, 1, 1, 0, 2)]
        right += [ps[i] for i in (0, 1, 0, 1, 2, 0)]
    left_ref[...] = jnp.concatenate(left, axis=0).astype(jnp.bfloat16)
    right_ref[...] = jnp.concatenate(right, axis=0).astype(jnp.bfloat16)

    following = a_ref[pl.ds(pl.multiple_of(base + 2 * BLOCK, BLOCK), BLOCK), :]
    result = []
    for g in range(2):
        rows = by_tile(following[g * PANEL : (g + 1) * PANEL])
        rows = minus(swept(rows, in_a), to_next_a[g], pa)
        rows = minus(swept(rows, in_b), to_next_b[g], pb)
        result.append(side_by_side(rows))
    return jnp.concatenate(result, axis=0)


def place_halves(place, pieces, first_row, flat):
    core = lax.axis_index(place.core)
    rows = flat.shape[0] // 2
    for r, piece in enumerate(pieces):
        start = pl.multiple_of(jnp.bitwise_xor(core, r) * rows, PANEL)
        flat[pl.ds(start, rows), :] = piece[first_row : first_row + rows]


def sweep_cost():
    return pl.CostEstimate(flops=1 << 30, bytes_accessed=1 << 20, transcendentals=0)


def clear(work):
    a_ref, left, right = work[:3]
    size = a_ref.shape[1]
    a_ref[:BLOCK] = jnp.zeros((BLOCK, size), jnp.float32)
    a_ref[BLOCK + size :] = jnp.zeros((BLOCK, size), jnp.float32)
    left[...] = jnp.zeros(left.shape, left.dtype)
    right[...] = jnp.zeros(right.shape, right.dtype)


def work_shapes(size):
    splits = 6 * BLOCK
    return [
        pltpu.VMEM((size + 2 * BLOCK, size), jnp.float32),
        pltpu.VMEM((splits, size), jnp.bfloat16),
        pltpu.VMEM((splits, size), jnp.bfloat16),
    ]


def row_shapes(size):
    return [
        pltpu.VMEM((PANEL, size), jnp.float32),
        pltpu.VMEM((PANEL * PANEL, LANES), jnp.float32),
    ] * 2


def aligned_rows(ref, index, count):
    if count % PANEL == 0:
        return ref[pl.ds(pl.multiple_of(index * count, count), count), :]
    per_slab = PANEL // count
    slab = ref[pl.ds(pl.multiple_of(index // per_slab * PANEL, PANEL), PANEL), :]
    value = slab[:count]
    for i in range(1, per_slab):
        value = jnp.where(index % per_slab == i, slab[i * count : (i + 1) * count], value)
    return value


def packs(cols, rows):
    return cols == 2 * PANEL and 2 * rows == LANES


def dot(a, b, last=False):
    return lax.dot_general(
        a,
        b,
        (((1,), (1 if last else 0,)), ((), ())),
        precision=HIGHEST,
        preferred_element_type=jnp.float32,
    )


STEPS = LANES // BLOCK
FIRST_STEPS = 6
SECOND_STEPS = 6


def sweep_both(wide_work, narrow_work, begin, end, blocks):
    def step(i, blocks):
        return (
            sweep_block(*wide_work, 0, i, blocks[0]),
            sweep_block(*narrow_work, 0, i, blocks[1]),
        )

    return lax.fori_loop(begin, end, step, blocks)


def sweep_wide(work, begin, end, block):
    return lax.fori_loop(begin, end, lambda i, block: sweep_block(*work, 1, i, block), block)


def unit_scale(block):
    row, col = iotas(block.shape)
    line = jnp.sum(jnp.where(row == col, block, 0.0), axis=0, keepdims=True)
    return jnp.broadcast_to(lax.rsqrt(line), (PANEL, block.shape[1]))


def on_rows(scale):
    n = scale.shape[1]
    return jnp.broadcast_to(scale[:1], (n, n))


def scaled(block, down, across):
    return (block * on_rows(down).T) * on_rows(across)


def first_kernel(
    place, total, mine, other, wa, wl, wr, wp, na, nl, nr, np_, ws_ref, ns_ref, *refs
):
    a_flat, b_flat = refs[:2]
    wide_work, narrow_work = (wa, wl, wr, *refs[2:6]), (na, nl, nr, *refs[6:])
    place_halves(place, (mine, other), 0, a_flat)
    place_halves(place, (mine, other), a_flat.shape[0] // 2, b_flat)
    n = LANES
    slab = a_flat[n : n + PANEL]
    first, square = unpack_pair(a_flat[:n], jnp.broadcast_to(slab[:1], (n, n)))
    corner = b_flat[:n] / total
    last = unfold(b_flat[n:], jnp.broadcast_to(slab[1:2], (n, n)))
    row, col = iotas((n, n))
    damp = jnp.where(row == col, DAMP, 0.0)
    clear(wide_work)
    clear(narrow_work)
    first, last, square = first / total + damp, last / total + damp, square / total + damp
    by_first, by_last, by_square = (unit_scale(block) for block in (first, last, square))
    ws_ref[:, :n] = by_first
    ws_ref[:, n:] = by_last
    ns_ref[...] = by_square
    first_across, last_across = on_rows(by_first), on_rows(by_last)
    first_down, last_down = first_across.T, last_across.T
    corner = (corner * first_down) * last_across
    wa[BLOCK : BLOCK + n, :n] = (first * first_down) * first_across
    wa[BLOCK : BLOCK + n, n:] = corner
    wa[BLOCK + n : BLOCK + 2 * n, :n] = corner.T
    wa[BLOCK + n : BLOCK + 2 * n, n:] = (last * last_down) * last_across
    na[BLOCK : BLOCK + n, :] = scaled(square, by_square, by_square)
    start = (wa[BLOCK : 2 * BLOCK, :], na[BLOCK : 2 * BLOCK, :])
    wp[...], np_[...] = sweep_both(wide_work, narrow_work, 0, FIRST_STEPS, start)


def second_kernel(*refs):
    given, scale, ninv_ref, state, narrow_state, wide_rows, narrow_rows = (
        refs[:8],
        refs[8],
        refs[9],
        refs[10:14],
        refs[14:17],
        refs[17:21],
        refs[21:],
    )
    for source, target in zip((*given[:3], *given[4:7]), (*state[:3], *narrow_state)):
        target[...] = source[...]
    wide_work, narrow_work = (*state[:3], *wide_rows), (*narrow_state, *narrow_rows)
    wp = state[3]
    panels = (given[3][...], given[7][...])
    panel, _ = sweep_both(wide_work, narrow_work, FIRST_STEPS, STEPS, panels)
    trailing_update(*narrow_work[:3], LANES)
    by_square = scale[...]
    ninv_ref[...] = scaled(-narrow_work[0][BLOCK : BLOCK + LANES, :], by_square, by_square)
    wp[...] = sweep_wide(wide_work, 0, SECOND_STEPS, panel)


def third_kernel(wa_in, wl_in, wr_in, panel_in, scale, winv, wa, wl, wr, *rows):
    wa[...] = wa_in[...]
    wl[...] = wl_in[...]
    wr[...] = wr_in[...]
    sweep_wide((wa, wl, wr, *rows), SECOND_STEPS, STEPS, panel_in[...])
    wide = wa.shape[1]
    trailing_update(wa, wl, wr, wide)
    parts = [slice(i, i + LANES) for i in range(0, wide, LANES)]
    across = [on_rows(scale[:, i]) for i in parts]
    down = [block.T for block in across]
    for i, rows_scale in zip(parts, down):
        for j, columns_scale in zip(parts, across):
            block = -wa[BLOCK + i.start : BLOCK + i.stop, j]
            winv[i, j] = (block * rows_scale) * columns_scale


def state_shapes(size):
    shapes = [jax.ShapeDtypeStruct(v.shape, v.dtype) for v in work_shapes(size)]
    return shapes + [jax.ShapeDtypeStruct((BLOCK, size), jnp.float32)]


def sweep_call(kernel, name, args, out_shapes, scratch):
    return pl.pallas_call(
        kernel,
        in_specs=[VMEM] * len(args),
        out_specs=[VMEM] * len(out_shapes),
        out_shape=out_shapes,
        scratch_shapes=scratch,
        cost_estimate=sweep_cost(),
        compiler_params=PARAMS,
        name=name,
    )(*args)


def first_panels(place, pieces, wide, narrow, total):
    return sweep_call(
        functools.partial(first_kernel, place, total),
        "first_panels",
        pieces,
        state_shapes(wide)
        + state_shapes(narrow)
        + [jax.ShapeDtypeStruct((PANEL, n), jnp.float32) for n in (wide, narrow)],
        [
            pltpu.VMEM((EARLY_ROWS, LANES), jnp.float32),
            pltpu.VMEM((LATE_ROWS, LANES), jnp.float32),
            *row_shapes(wide),
            *row_shapes(narrow),
        ],
    )


def second_panels(state, wide, narrow):
    ninv = jax.ShapeDtypeStruct((narrow, narrow), jnp.float32)
    return sweep_call(
        second_kernel,
        "second_panels",
        state,
        [ninv] + state_shapes(wide),
        [*work_shapes(narrow), *row_shapes(wide), *row_shapes(narrow)],
    )


def third_panels(state, wide):
    winv = jax.ShapeDtypeStruct((wide, wide), jnp.float32)
    scratch = [*work_shapes(wide), *row_shapes(wide)]
    return sweep_call(third_kernel, "third_panels", state, [winv], scratch)[0]


def product_kernel(place, total, rows, winv, ninv_ref, mine, other, out_ref, flat):
    place_halves(place, (mine, other), 0, flat)
    ninv = ninv_ref[...]
    n = LANES
    inner = jnp.concatenate(
        [
            transposed_dot(flat[c * n : (c + 1) * n] / total, ninv, HIGHEST)
            for c in range(2)
        ],
        axis=0,
    )
    wide = winv.shape[1]
    cols = wide // 2 ** len(place.dp)
    near, second = lax.axis_index(place.near), lax.axis_index(place.second)
    near_stride = 2 ** (len(place.dp) - 2)
    base = place.index(place.dp) - near * near_stride - second * 2
    _, lane = iotas((PANEL, LANES))
    picks = [
        aligned_rows(winv, base + (j // 2) * near_stride + (j % 2) * 2, cols) for j in range(4)
    ]
    if cols % PANEL == 0:
        whole = dot(jnp.concatenate(picks, axis=0), inner)
        updates = [whole[j * cols : (j + 1) * cols] for j in range(4)]
    else:
        updates = [dot(picked, inner) for picked in picks]
    for j, (picked, update) in enumerate(zip(picks, updates)):
        for x in range(2):
            block = 2 * j + x
            out_ref[block, :cols] = picked[:, :LANES]
            out_ref[block, cols : 2 * cols] = picked[:, LANES:]
            if packs(cols, rows):
                upper, lower = update[:PANEL], update[PANEL:]
                if x == 0:
                    lower = pltpu.roll(lower, rows, 1)
                else:
                    upper = pltpu.roll(upper, rows, 1)
                out_ref[block, 2 * cols :] = jnp.where(lane < rows, upper, lower)
            else:
                out_ref[block, 2 * cols :] = update


def products(place, winv, ninv, pieces, rows, total):
    wide, narrow = winv.shape[0], ninv.shape[0]
    cols = wide // 2 ** len(place.dp)
    height = 2 * cols + (PANEL if packs(cols, rows) else cols)
    return pl.pallas_call(
        functools.partial(product_kernel, place, total, rows),
        in_specs=[VMEM] * 4,
        out_specs=VMEM,
        out_shape=jax.ShapeDtypeStruct((8, height, LANES), jnp.float32),
        scratch_shapes=[pltpu.VMEM((2 * narrow, LANES), jnp.float32)],
        compiler_params=PARAMS,
        name="products",
    )(winv, ninv, *pieces)


def placing_kernel(place, slots_ref, got_ref, kept_ref, update_ref):
    layers = got_ref.shape[0]
    slots, cols, wide = kept_ref.shape
    rows = update_ref.shape[2]
    own, dp = place.index(place.own), place.index(place.dp)
    step = min(cols, PANEL)
    row, col = iotas((step, LANES))
    for h in range(wide // LANES):
        lanes = slice(h * LANES, (h + 1) * LANES)
        for r in range(0, cols, step):
            here = h * cols + r
            empty = jnp.where(col + h * LANES == row + dp * cols + r, 1.0 / DAMP, 0.0)
            for c in range(slots):
                value = empty
                for l in range(layers):
                    taken = slots_ref[l, :step] == c
                    value = jnp.where(taken, got_ref[l, here : here + step], value)
                kept_ref[c, r : r + step, lanes] = value
    for l in range(layers):
        value = got_ref[l, 2 * cols :]
        if packs(cols, rows):
            update_ref[l, :PANEL] = value[:, :rows]
            update_ref[l, PANEL:] = value[:, rows:]
        else:
            part = value[:, :rows]
            for p in range(1, LANES // rows):
                part = jnp.where(own == p, value[:, p * rows : (p + 1) * rows], part)
            update_ref[l] = part


def placing(place, slots_of, got, wide, cols, slots, rows):
    layers = got.shape[0]
    return pl.pallas_call(
        functools.partial(placing_kernel, place),
        in_specs=[VMEM, VMEM],
        out_specs=[VMEM, VMEM],
        out_shape=[
            jax.ShapeDtypeStruct((slots, cols, wide), jnp.float32),
            jax.ShapeDtypeStruct((layers, cols, rows), jnp.float32),
        ],
        compiler_params=PARAMS,
        name="placing",
    )(slots_of, got)


def swap(value, axis):
    return lax.ppermute(value, axis, [(0, 1), (1, 0)])


def swap_by_core(value, place, stage, orders):
    names = (place.near, place.second, place.core, place.first)
    flips = {"near": 8, "second": 4, "first": 1}
    pairs = [(i, i ^ flips[orders[(i >> 1) & 1][stage]]) for i in range(16)]
    return lax.ppermute(value, names, pairs)


def after(value, *others):
    return lax.optimization_barrier((value,) + others)[0]


def on_device(place, wide_rows, narrow_rows, owner_map):
    layers, rows, wide = wide_rows.shape
    narrow = narrow_rows.shape[2]
    n_dp, n_own = 2 ** len(place.dp), 2 ** len(place.own)
    total = float(rows * n_dp * n_own)

    h_keep, h_send, wides, narrows = hot_squares(place, wide_rows, narrow_rows)
    first_send = h_send[4:]
    h_got = swap(first_send, place.core)
    c_keep, c_send = cold_squares(place, after(wides, first_send), narrows)
    h_keep, c_send = lax.optimization_barrier((h_keep, c_send))

    hot = h_keep[4:] + h_got
    s_got = swap_by_core(hot, place, 0, ORDERS)
    m_keep, m_send, slots_of = mixed_sums(place, owner_map, after(wides, hot), narrows)
    c_got = swap(after(c_send + h_send[:4], m_send), place.core)
    m_got = swap(m_send, place.core)

    s = (c_keep + h_keep[:4]) + s_got
    s = s + after(c_got, s)
    s_got = swap_by_core(s[2:], place, 1, ORDERS)
    m = after(m_keep, s) + m_got
    m_got = swap_by_core(m[4:], place, 0, LATE_ORDERS)

    s = s[:2] + s_got
    s_got = swap_by_core(s[1], place, 2, ORDERS)
    m = after(m[:4], s) + m_got
    m_got = swap_by_core(m[2:], place, 1, LATE_ORDERS)

    s = s[0] + s_got
    if place.extra:
        s = lax.psum(s, place.extra)
    s_got = swap(s, place.far)
    m = after(m[:2], s) + m_got
    m_got = swap_by_core(m[1], place, 2, LATE_ORDERS)

    s = s + s_got
    state = first_panels(place, [s, swap(s, place.core)], wide, narrow, total)
    m = after(m[0], state[0]) + m_got
    if place.extra:
        m = lax.psum(m, place.extra)
    m_got = swap(m, place.far)
    *state, wide_scale, narrow_scale = state
    ninv, *state = second_panels([*state, narrow_scale], wide, narrow)
    m = after(m, ninv) + m_got
    m_got = swap(m, place.core)
    winv = third_panels([*state, wide_scale], wide)
    cols, own_rows = wide // n_dp, narrow // n_own
    sent = products(place, winv, ninv, [m, m_got], own_rows, total)
    got = lax.all_to_all(sent, (place.near, place.second, place.first), 0, 0)
    kept, update = placing(
        place, slots_of, got, wide, cols, layers // n_own + 1, own_rows
    )
    return (jnp.swapaxes(kept, 1, 2), jnp.swapaxes(update, 1, 2))


def solution(mesh):
    n_dp, n_own = mesh.shape["dp"], mesh.shape["own"]
    dp_names = tuple(f"dp{i}" for i in range(int(np.log2(n_dp))))
    own_names = tuple(f"own{i}" for i in range(int(np.log2(n_own))))
    names = dp_names + own_names
    bits = jax.sharding.Mesh(mesh.devices.reshape((2,) * len(names)), names)
    in_specs = (P(None, names, None), P(None, names, None), P())
    out_specs = (P(own_names, None, dp_names), P(None, own_names, dp_names))
    return jax.shard_map(
        functools.partial(on_device, Place(dp_names, own_names)),
        mesh=bits,
        in_specs=in_specs,
        out_specs=out_specs,
        check_vma=False,
    )
```

```python
import functools

import jax
import jax.numpy as jnp
import numpy as np
from jax import lax
from jax.experimental import pallas as pl
from jax.experimental.pallas import tpu as pltpu
from jax.sharding import PartitionSpec as P

DAMP = 0.5
LANES = 128
PANEL = 8
BLOCK = 2 * PANEL
VMEM_LIMIT = 48 * 1024 * 1024
HIGHEST = lax.Precision.HIGHEST
VMEM = pl.BlockSpec(memory_space=pltpu.VMEM)
SMEM = pl.BlockSpec(memory_space=pltpu.SMEM)
HBM = pl.BlockSpec(memory_space=pltpu.HBM)
PARAMS = pltpu.CompilerParams(vmem_limit_bytes=VMEM_LIMIT)


class Place:
    def __init__(self, dp_names, own_names):
        self.dp, self.own = dp_names, own_names
        self.core, self.second, self.near, self.far = (
            dp_names[-1],
            dp_names[-2],
            dp_names[1],
            dp_names[0],
        )
        self.first = own_names[-1]
        used = (self.core, self.second, self.near, self.far, self.first)
        self.extra = tuple(n for n in dp_names + own_names if n not in used)

    def index(self, names):
        value = jnp.int32(0)
        for name in names:
            value = value * 2 + lax.axis_index(name)
        return value

    def layer(self):
        return self.index((self.near, self.second, self.first))


def transposed_dot(a, b, precision=None):
    return lax.dot_general(
        a, b, (((0,), (0,)), ((), ())), precision=precision, preferred_element_type=jnp.float32
    )


def layer_copies(place, sources, buffers, sems):
    layer = place.layer()
    return [
        [
            pltpu.make_async_copy(
                source.at[jnp.bitwise_xor(layer, i)], buffer.at[i], sems.at[i, s]
            )
            for s, (source, buffer) in enumerate(zip(sources, buffers))
        ]
        for i in range(buffers[0].shape[0])
    ]


def both_halves(place, flat, i):
    rows = flat.shape[1] // 2
    core = lax.axis_index(place.core)
    kept = pl.multiple_of(core * rows, PANEL)
    sent = pl.multiple_of((1 - core) * rows, PANEL)
    return flat[i, pl.ds(kept, rows), :], flat[i, pl.ds(sent, rows), :]


ORDERS = (("first", "second", "near"), ("second", "near", "first"))
LATE_ORDERS = (("first", "second", "near"), ("near", "first", "second"))


def position(axes, i):
    bits = {"near": i // 4, "second": (i // 2) % 2, "first": i % 2}
    return bits[axes[0]] * 4 + bits[axes[1]] * 2 + bits[axes[2]]


def positions(place, i, orders):
    core = lax.axis_index(place.core)
    first, second = (position(axes, i) for axes in orders)
    return jnp.where(core == 0, first, second), jnp.where(core == 0, second, first)


def iotas(shape):
    return (
        lax.broadcasted_iota(jnp.int32, shape, 0),
        lax.broadcasted_iota(jnp.int32, shape, 1),
    )


def pack_pair(first, second):
    row, col = iotas(first.shape)
    return jnp.where(row >= col, first, second)


def unpack_pair(packed, second_diagonal):
    row, col = iotas(packed.shape)
    turned = packed.T
    first = jnp.where(row >= col, packed, turned)
    second = jnp.where(col > row, packed, turned)
    return first, jnp.where(row == col, second_diagonal, second)


def fold(block):
    h = block.shape[0] // 2
    row, col = iotas((h, 2 * h))
    last = pltpu.roll(block[h:], h, 1)
    return jnp.where((col >= h) | (row >= col), block[:h], last)


def unfold(folded, diagonal):
    h, n = folded.shape
    row, col = iotas((n, n))
    block = jnp.concatenate([folded, jnp.zeros((h, n), jnp.float32)], axis=0)
    turned = block.T
    top = jnp.where((col >= h) | (col <= row), block, turned)
    moved = pltpu.roll(pltpu.roll(block, h, 0), h, 1)
    moved_turned = pltpu.roll(pltpu.roll(turned, h, 0), h, 1)
    last = jnp.where(col > row, moved, moved_turned)
    last = jnp.where(row == col, diagonal, last)
    return jnp.where(row < h, top, jnp.where(col < h, turned, last))


def diagonals(blocks, rows):
    n = blocks[0].shape[0]
    row, col = iotas((n, n))
    slab_row, _ = iotas((rows, n))
    slab = jnp.zeros((rows, n), jnp.float32)
    for i, block in enumerate(blocks):
        line = jnp.sum(jnp.where(row == col, block, 0.0), axis=0, keepdims=True)
        slab = jnp.where(slab_row == i, jnp.broadcast_to(line, (rows, n)), slab)
    return slab


EARLY_ROWS = 144
LATE_ROWS = 192


HOT = (1, 2, 3, 5, 6, 7)
COLD = (0, 4)


def square_sums(wide, narrow):
    return transposed_dot(wide, wide), transposed_dot(narrow, narrow)


def pack_layer(place, i, wcov, ncov, a_flat, b_flat):
    n = LANES
    last = wcov[n:, n:]
    a_flat[i, :n] = pack_pair(wcov[:n, :n], ncov)
    a_flat[i, n:] = diagonals((ncov, last), EARLY_ROWS - n)
    b_flat[i, :n] = wcov[:n, n:]
    b_flat[i, n:] = fold(last)
    a_kept, a_sent = both_halves(place, a_flat, i)
    b_kept, b_sent = both_halves(place, b_flat, i)
    return (a_kept, b_kept), (a_sent, b_sent)


def put(ref, index, parts):
    rows = EARLY_ROWS // 2
    ref[index, :rows] = parts[0]
    ref[index, rows:] = parts[1]


def put_layer(place, i, sums, a_flat, b_flat, keep, send):
    kept, sent = pack_layer(place, i, *sums, a_flat, b_flat)
    mine, other = positions(place, i, ORDERS)
    put(keep, mine, kept)
    put(send, other, sent)


def clear_others(place, layers, keep, send):
    for i in layers:
        mine, other = positions(place, i, ORDERS)
        keep[mine] = jnp.zeros(keep.shape[1:], jnp.float32)
        send[other] = jnp.zeros(send.shape[1:], jnp.float32)


def hot_kernel(place, wide_hbm, narrow_hbm, keep, send, wides, narrows, a_flat, b_flat, sems):
    copies = layer_copies(place, (wide_hbm, narrow_hbm), (wides, narrows), sems)
    for i in HOT + COLD:
        for copy in copies[i]:
            copy.start()
    clear_others(place, COLD, keep, send)
    for group in (HOT[:2], HOT[2:], COLD):
        for i in group:
            for copy in copies[i]:
                copy.wait()
        if group is not COLD:
            for i in group:
                sums = square_sums(wides[i], narrows[i])
                put_layer(place, i, sums, a_flat, b_flat, keep, send)


def cold_kernel(place, wides, narrows, keep, send, a_flat, b_flat):
    for i in COLD:
        put_layer(
            place, i, square_sums(wides[i], narrows[i]), a_flat, b_flat, keep, send
        )
    core = lax.axis_index(place.core)
    stay = [[i for i in HOT if position(axes, i) < 4] for axes in ORDERS]
    for first, second in zip(*stay):
        here = [position(axes, i) for axes, i in zip(ORDERS, (first, second))]
        mine = jnp.where(core == 0, here[0], here[1])
        other = jnp.where(core == 0, here[1], here[0])
        keep[mine] = jnp.zeros(keep.shape[1:], jnp.float32)
        send[other] = jnp.zeros(send.shape[1:], jnp.float32)


def write_slots(place, owner_map, slots_ref):
    own = place.index(place.own)
    count = jnp.int32(0)
    for l in range(slots_ref.shape[0]):
        mine = owner_map[l] == own
        slot = jnp.where(mine, count, -1)
        slots_ref[l] = jnp.full(slots_ref.shape[1:], 0, jnp.int32) + slot
        count = count + mine.astype(jnp.int32)


def mixed_kernel(place, owner_map, wides, narrows, keep, send, slots_ref, flat):
    n = LANES
    write_slots(place, owner_map, slots_ref)
    for i in range(wides.shape[0]):
        mixed = transposed_dot(narrows[i], wides[i])
        flat[i, :n] = mixed[:, :n]
        flat[i, n:] = mixed[:, n:]
        kept, sent = both_halves(place, flat, i)
        mine, other = positions(place, i, LATE_ORDERS)
        keep[mine] = kept
        send[other] = sent


def gram_cost(wide_rows, columns):
    return pl.CostEstimate(
        flops=2 * wide_rows.size * columns, bytes_accessed=2 * wide_rows.size, transcendentals=0
    )


HALF_ROWS = (EARLY_ROWS + LATE_ROWS) // 2


def pack_shapes(layers):
    return [
        pltpu.VMEM((layers, EARLY_ROWS, LANES), jnp.float32),
        pltpu.VMEM((layers, LATE_ROWS, LANES), jnp.float32),
    ]


def hot_squares(place, wide_rows, narrow_rows):
    layers = wide_rows.shape[0]
    half = jax.ShapeDtypeStruct((layers, HALF_ROWS, LANES), jnp.float32)
    return pl.pallas_call(
        functools.partial(hot_kernel, place),
        in_specs=[HBM, HBM],
        out_specs=[VMEM] * 4,
        out_shape=[
            half,
            half,
            jax.ShapeDtypeStruct(wide_rows.shape, wide_rows.dtype),
            jax.ShapeDtypeStruct(narrow_rows.shape, narrow_rows.dtype),
        ],
        scratch_shapes=[*pack_shapes(layers), pltpu.SemaphoreType.DMA((layers, 2))],
        cost_estimate=gram_cost(wide_rows, 240),
        compiler_params=PARAMS,
        name="hot_squares",
    )(
        pltpu.with_memory_space_constraint(wide_rows, pltpu.HBM),
        pltpu.with_memory_space_constraint(narrow_rows, pltpu.HBM),
    )


def cold_squares(place, wides, narrows):
    half = jax.ShapeDtypeStruct((wides.shape[0] // 2, HALF_ROWS, LANES), jnp.float32)
    return pl.pallas_call(
        functools.partial(cold_kernel, place),
        in_specs=[VMEM, VMEM],
        out_specs=[VMEM, VMEM],
        out_shape=[half, half],
        scratch_shapes=pack_shapes(wides.shape[0]),
        cost_estimate=gram_cost(wides, 80),
        compiler_params=PARAMS,
        name="cold_squares",
    )(wides, narrows)


def mixed_sums(place, owner_map, wides, narrows):
    layers, _, narrow = narrows.shape
    half = jax.ShapeDtypeStruct((layers, narrow, LANES), jnp.float32)
    return pl.pallas_call(
        functools.partial(mixed_kernel, place),
        in_specs=[SMEM, VMEM, VMEM],
        out_specs=[VMEM] * 3,
        out_shape=[half, half, jax.ShapeDtypeStruct((layers, PANEL, LANES), jnp.int32)],
        scratch_shapes=[pltpu.VMEM((layers, 2 * narrow, LANES), jnp.float32)],
        cost_estimate=gram_cost(wides, 128),
        compiler_params=PARAMS,
        name="mixed",
    )(owner_map, wides, narrows)


def lane_gather(x, index):
    return jnp.take_along_axis(x, index, axis=1, mode="promise_in_bounds")


def trailing_update(a_ref, left_ref, right_ref, base):
    size = a_ref.shape[1]
    a_ref[pl.ds(pl.multiple_of(base, BLOCK), BLOCK), :] = jnp.zeros((BLOCK, size), jnp.float32)
    lane = lax.broadcasted_iota(jnp.int32, (1, size), 1)
    swept = (lane >= base - BLOCK) & (lane < base)
    update = transposed_dot(left_ref[...], right_ref[...])
    a_ref[BLOCK : BLOCK + size, :] = (
        jnp.where(swept, 0.0, a_ref[BLOCK : BLOCK + size, :]) - update
    )


def in_three(x):
    high = x.astype(jnp.bfloat16).astype(jnp.float32)
    rest = x - high
    middle = rest.astype(jnp.bfloat16).astype(jnp.float32)
    return high, middle, rest - middle


def factor_panel(rows_ref, cols_ref, tile, first, panel, targets):
    tiles = panel.shape[1] // LANES
    shape = (PANEL, LANES)
    _, lane = iotas(shape)

    def on_all(ref, k, lanes):
        return jnp.broadcast_to(ref[k : k + 1, lanes], shape)

    rows_ref[...] = panel
    lanes = [slice(LANES * t, LANES * (t + 1)) for t in range(tiles)]
    rows = [[on_all(rows_ref, k, part) for part in lanes] for k in range(PANEL)]
    here = panel[:, lanes[tile]]
    for j in range(PANEL):
        column = lane_gather(here, jnp.full(shape, 0, jnp.int32) + (first + j))
        cols_ref[PANEL * j : PANEL * (j + 1)] = column
    d = [[None] * PANEL for _ in range(PANEL)]
    for j in range(PANEL):
        for i in range(j, PANEL):
            d[i][j] = on_all(cols_ref, PANEL * j + i, slice(None))
    own = (lane >= first) & (lane < first + PANEL)
    q = [[None] * tiles for _ in range(PANEL)]
    p = [[None] * tiles for _ in range(PANEL)]
    weights = [[None] * PANEL for _ in targets]
    factor = [[None] * PANEL for _ in range(PANEL)]

    def substitute(k, scale):
        for t in range(tiles):
            value = rows[k][t]
            if t == tile:
                value = jnp.where(own, jnp.where(lane == first + k, -1.0, 0.0), value)
            for j in range(k):
                value = value - factor[k][j] * q[j][t]
            q[k][t] = value
            p[k][t] = value * scale
        for target, weight in zip(targets, weights):
            source, index = target(rows[k])
            value = lane_gather(source, index)
            for j in range(k):
                value = value - factor[k][j] * weight[j]
            weight[k] = value

    for k in range(0, PANEL, 2):
        m = k + 1
        a, b, c = d[k][k], d[m][k], d[m][m]
        first_scale = 1.0 / a
        second_scale = a * (1.0 / (a * c - b * b))
        factor[m][k] = b * first_scale
        left_over = {i: d[i][m] - d[i][k] * factor[m][k] for i in range(k + 2, PANEL)}
        for i in range(k + 2, PANEL):
            factor[i][k] = d[i][k] * first_scale
            factor[i][m] = left_over[i] * second_scale
        for i in range(k + 2, PANEL):
            for j in range(k + 2, i + 1):
                value = d[i][j] - d[i][k] * factor[j][k]
                d[i][j] = value - (left_over[i] * left_over[j]) * second_scale
        substitute(k, first_scale)
        substitute(m, second_scale)
    return q, p, weights


def packed_rows(values):
    sub, _ = iotas((PANEL, LANES))
    whole = []
    for t in range(len(values[0])):
        value = values[0][t]
        for k in range(1, PANEL):
            value = jnp.where(sub == k, values[k][t], value)
        whole.append(value)
    return whole


def side_by_side(tiles):
    return jnp.concatenate(tiles, axis=1) if len(tiles) > 1 else tiles[0]


def sweep_block(a_ref, left_ref, right_ref, a_rows, a_cols, b_rows, b_cols, tile, step, block):
    size = a_ref.shape[1]
    tiles = size // LANES
    first = step * BLOCK
    second = first + PANEL
    base = tile * LANES + first
    trailing_update(a_ref, left_ref, right_ref, base)

    sub, lane = iotas((PANEL, LANES))
    last = first == LANES - BLOCK
    next_first = jnp.where(last, 0, first + BLOCK)

    def in_block(row):
        return row[tile], second + sub

    def in_next(offset):
        def target(row):
            source = row[tile]
            if tile + 1 < tiles:
                source = jnp.where(last, row[tile + 1], source)
            return source, next_first + offset + sub

        return target

    nexts = [in_next(0), in_next(PANEL)]
    in_a = (lane >= first) & (lane < second)
    in_b = (lane >= second) & (lane < second + PANEL)

    def swept(tiles_of, mask):
        return [jnp.where(mask, 0.0, v) if t == tile else v for t, v in enumerate(tiles_of)]

    def minus(tiles_of, weight, p):
        result = []
        for t, value in enumerate(tiles_of):
            for k in range(PANEL):
                value = value - weight[k] * p[k][t]
            result.append(value)
        return result

    def by_tile(rows):
        return [rows[:, LANES * t : LANES * (t + 1)] for t in range(tiles)]

    qa, pa, (to_b, *to_next_a) = factor_panel(
        a_rows, a_cols, tile, first, block[:PANEL], [in_block, *nexts]
    )
    panel_b = side_by_side(minus(swept(by_tile(block[PANEL:]), in_a), to_b, pa))
    qb, pb, to_next_b = factor_panel(b_rows, b_cols, tile, second, panel_b, nexts)

    left, right = [], []
    for q, p, mask in ((qa, pa, in_b), (qb, pb, None)):
        q, p = packed_rows(q), packed_rows(p)
        if mask is not None:
            q, p = swept(q, mask), swept(p, mask)
        qs, ps = in_three(side_by_side(q)), in_three(side_by_side(p))
        left += [qs[i] for i in (0, 0, 1, 1, 0, 2)]
        right += [ps[i] for i in (0, 1, 0, 1, 2, 0)]
    left_ref[...] = jnp.concatenate(left, axis=0).astype(jnp.bfloat16)
    right_ref[...] = jnp.concatenate(right, axis=0).astype(jnp.bfloat16)

    following = a_ref[pl.ds(pl.multiple_of(base + 2 * BLOCK, BLOCK), BLOCK), :]
    result = []
    for g in range(2):
        rows = by_tile(following[g * PANEL : (g + 1) * PANEL])
        rows = minus(swept(rows, in_a), to_next_a[g], pa)
        rows = minus(swept(rows, in_b), to_next_b[g], pb)
        result.append(side_by_side(rows))
    return jnp.concatenate(result, axis=0)


def place_halves(place, pieces, first_row, flat):
    core = lax.axis_index(place.core)
    rows = flat.shape[0] // 2
    for r, piece in enumerate(pieces):
        start = pl.multiple_of(jnp.bitwise_xor(core, r) * rows, PANEL)
        flat[pl.ds(start, rows), :] = piece[first_row : first_row + rows]


def sweep_cost():
    return pl.CostEstimate(flops=1 << 30, bytes_accessed=1 << 20, transcendentals=0)


def clear(work):
    a_ref, left, right = work[:3]
    size = a_ref.shape[1]
    a_ref[:BLOCK] = jnp.zeros((BLOCK, size), jnp.float32)
    a_ref[BLOCK + size :] = jnp.zeros((BLOCK, size), jnp.float32)
    left[...] = jnp.zeros(left.shape, left.dtype)
    right[...] = jnp.zeros(right.shape, right.dtype)


def work_shapes(size):
    splits = 6 * BLOCK
    return [
        pltpu.VMEM((size + 2 * BLOCK, size), jnp.float32),
        pltpu.VMEM((splits, size), jnp.bfloat16),
        pltpu.VMEM((splits, size), jnp.bfloat16),
    ]


def row_shapes(size):
    return [
        pltpu.VMEM((PANEL, size), jnp.float32),
        pltpu.VMEM((PANEL * PANEL, LANES), jnp.float32),
    ] * 2


def aligned_rows(ref, index, count):
    if count % PANEL == 0:
        return ref[pl.ds(pl.multiple_of(index * count, count), count), :]
    per_slab = PANEL // count
    slab = ref[pl.ds(pl.multiple_of(index // per_slab * PANEL, PANEL), PANEL), :]
    value = slab[:count]
    for i in range(1, per_slab):
        value = jnp.where(index % per_slab == i, slab[i * count : (i + 1) * count], value)
    return value


def packs(cols, rows):
    return cols == 2 * PANEL and 2 * rows == LANES


def dot(a, b, last=False):
    return lax.dot_general(
        a,
        b,
        (((1,), (1 if last else 0,)), ((), ())),
        precision=HIGHEST,
        preferred_element_type=jnp.float32,
    )


STEPS = LANES // BLOCK
FIRST_STEPS = 6
SECOND_STEPS = 6


def sweep_both(wide_work, narrow_work, begin, end, blocks):
    def step(i, blocks):
        return (
            sweep_block(*wide_work, 0, i, blocks[0]),
            sweep_block(*narrow_work, 0, i, blocks[1]),
        )

    return lax.fori_loop(begin, end, step, blocks)


def sweep_wide(work, begin, end, block):
    return lax.fori_loop(begin, end, lambda i, block: sweep_block(*work, 1, i, block), block)


def unit_scale(block):
    row, col = iotas(block.shape)
    line = jnp.sum(jnp.where(row == col, block, 0.0), axis=0, keepdims=True)
    return jnp.broadcast_to(lax.rsqrt(line), (PANEL, block.shape[1]))


def on_rows(scale):
    n = scale.shape[1]
    return jnp.broadcast_to(scale[:1], (n, n))


def scaled(block, down, across):
    return (block * on_rows(down).T) * on_rows(across)


def first_kernel(
    place, total, mine, other, wa, wl, wr, wp, na, nl, nr, np_, ws_ref, ns_ref, *refs
):
    a_flat, b_flat = refs[:2]
    wide_work, narrow_work = (wa, wl, wr, *refs[2:6]), (na, nl, nr, *refs[6:])
    place_halves(place, (mine, other), 0, a_flat)
    place_halves(place, (mine, other), a_flat.shape[0] // 2, b_flat)
    n = LANES
    slab = a_flat[n : n + PANEL]
    first, square = unpack_pair(a_flat[:n], jnp.broadcast_to(slab[:1], (n, n)))
    corner = b_flat[:n] / total
    last = unfold(b_flat[n:], jnp.broadcast_to(slab[1:2], (n, n)))
    row, col = iotas((n, n))
    damp = jnp.where(row == col, DAMP, 0.0)
    clear(wide_work)
    clear(narrow_work)
    first, last, square = first / total + damp, last / total + damp, square / total + damp
    by_first, by_last, by_square = (unit_scale(block) for block in (first, last, square))
    ws_ref[:, :n] = by_first
    ws_ref[:, n:] = by_last
    ns_ref[...] = by_square
    first_across, last_across = on_rows(by_first), on_rows(by_last)
    first_down, last_down = first_across.T, last_across.T
    corner = (corner * first_down) * last_across
    wa[BLOCK : BLOCK + n, :n] = (first * first_down) * first_across
    wa[BLOCK : BLOCK + n, n:] = corner
    wa[BLOCK + n : BLOCK + 2 * n, :n] = corner.T
    wa[BLOCK + n : BLOCK + 2 * n, n:] = (last * last_down) * last_across
    na[BLOCK : BLOCK + n, :] = scaled(square, by_square, by_square)
    start = (wa[BLOCK : 2 * BLOCK, :], na[BLOCK : 2 * BLOCK, :])
    wp[...], np_[...] = sweep_both(wide_work, narrow_work, 0, FIRST_STEPS, start)


def second_kernel(*refs):
    given, scale, ninv_ref, state, narrow_state, wide_rows, narrow_rows = (
        refs[:8],
        refs[8],
        refs[9],
        refs[10:14],
        refs[14:17],
        refs[17:21],
        refs[21:],
    )
    for source, target in zip((*given[:3], *given[4:7]), (*state[:3], *narrow_state)):
        target[...] = source[...]
    wide_work, narrow_work = (*state[:3], *wide_rows), (*narrow_state, *narrow_rows)
    wp = state[3]
    panels = (given[3][...], given[7][...])
    panel, _ = sweep_both(wide_work, narrow_work, FIRST_STEPS, STEPS, panels)
    trailing_update(*narrow_work[:3], LANES)
    by_square = scale[...]
    ninv_ref[...] = scaled(-narrow_work[0][BLOCK : BLOCK + LANES, :], by_square, by_square)
    wp[...] = sweep_wide(wide_work, 0, SECOND_STEPS, panel)


def third_kernel(wa_in, wl_in, wr_in, panel_in, scale, winv, wa, wl, wr, *rows):
    wa[...] = wa_in[...]
    wl[...] = wl_in[...]
    wr[...] = wr_in[...]
    sweep_wide((wa, wl, wr, *rows), SECOND_STEPS, STEPS, panel_in[...])
    wide = wa.shape[1]
    trailing_update(wa, wl, wr, wide)
    parts = [slice(i, i + LANES) for i in range(0, wide, LANES)]
    across = [on_rows(scale[:, i]) for i in parts]
    down = [block.T for block in across]
    for i, rows_scale in zip(parts, down):
        for j, columns_scale in zip(parts, across):
            block = -wa[BLOCK + i.start : BLOCK + i.stop, j]
            winv[i, j] = (block * rows_scale) * columns_scale


def state_shapes(size):
    shapes = [jax.ShapeDtypeStruct(v.shape, v.dtype) for v in work_shapes(size)]
    return shapes + [jax.ShapeDtypeStruct((BLOCK, size), jnp.float32)]


def sweep_call(kernel, name, args, out_shapes, scratch):
    return pl.pallas_call(
        kernel,
        in_specs=[VMEM] * len(args),
        out_specs=[VMEM] * len(out_shapes),
        out_shape=out_shapes,
        scratch_shapes=scratch,
        cost_estimate=sweep_cost(),
        compiler_params=PARAMS,
        name=name,
    )(*args)


def first_panels(place, pieces, wide, narrow, total):
    return sweep_call(
        functools.partial(first_kernel, place, total),
        "first_panels",
        pieces,
        state_shapes(wide)
        + state_shapes(narrow)
        + [jax.ShapeDtypeStruct((PANEL, n), jnp.float32) for n in (wide, narrow)],
        [
            pltpu.VMEM((EARLY_ROWS, LANES), jnp.float32),
            pltpu.VMEM((LATE_ROWS, LANES), jnp.float32),
            *row_shapes(wide),
            *row_shapes(narrow),
        ],
    )


def second_panels(state, wide, narrow):
    ninv = jax.ShapeDtypeStruct((narrow, narrow), jnp.float32)
    return sweep_call(
        second_kernel,
        "second_panels",
        state,
        [ninv] + state_shapes(wide),
        [*work_shapes(narrow), *row_shapes(wide), *row_shapes(narrow)],
    )


def third_panels(state, wide):
    winv = jax.ShapeDtypeStruct((wide, wide), jnp.float32)
    scratch = [*work_shapes(wide), *row_shapes(wide)]
    return sweep_call(third_kernel, "third_panels", state, [winv], scratch)[0]


def product_kernel(place, total, rows, winv, ninv_ref, mine, other, out_ref, flat):
    place_halves(place, (mine, other), 0, flat)
    ninv = ninv_ref[...]
    n = LANES
    inner = jnp.concatenate(
        [
            transposed_dot(flat[c * n : (c + 1) * n] / total, ninv, HIGHEST)
            for c in range(2)
        ],
        axis=0,
    )
    wide = winv.shape[1]
    cols = wide // 2 ** len(place.dp)
    near, second = lax.axis_index(place.near), lax.axis_index(place.second)
    near_stride = 2 ** (len(place.dp) - 2)
    base = place.index(place.dp) - near * near_stride - second * 2
    _, lane = iotas((PANEL, LANES))
    picks = [
        aligned_rows(winv, base + (j // 2) * near_stride + (j % 2) * 2, cols) for j in range(4)
    ]
    if cols % PANEL == 0:
        whole = dot(jnp.concatenate(picks, axis=0), inner)
        updates = [whole[j * cols : (j + 1) * cols] for j in range(4)]
    else:
        updates = [dot(picked, inner) for picked in picks]
    for j, (picked, update) in enumerate(zip(picks, updates)):
        for x in range(2):
            block = 2 * j + x
            out_ref[block, :cols] = picked[:, :LANES]
            out_ref[block, cols : 2 * cols] = picked[:, LANES:]
            if packs(cols, rows):
                upper, lower = update[:PANEL], update[PANEL:]
                if x == 0:
                    lower = pltpu.roll(lower, rows, 1)
                else:
                    upper = pltpu.roll(upper, rows, 1)
                out_ref[block, 2 * cols :] = jnp.where(lane < rows, upper, lower)
            else:
                out_ref[block, 2 * cols :] = update


def products(place, winv, ninv, pieces, rows, total):
    wide, narrow = winv.shape[0], ninv.shape[0]
    cols = wide // 2 ** len(place.dp)
    height = 2 * cols + (PANEL if packs(cols, rows) else cols)
    return pl.pallas_call(
        functools.partial(product_kernel, place, total, rows),
        in_specs=[VMEM] * 4,
        out_specs=VMEM,
        out_shape=jax.ShapeDtypeStruct((8, height, LANES), jnp.float32),
        scratch_shapes=[pltpu.VMEM((2 * narrow, LANES), jnp.float32)],
        compiler_params=PARAMS,
        name="products",
    )(winv, ninv, *pieces)


def placing_kernel(place, slots_ref, got_ref, kept_ref, update_ref):
    layers = got_ref.shape[0]
    slots, cols, wide = kept_ref.shape
    rows = update_ref.shape[2]
    own, dp = place.index(place.own), place.index(place.dp)
    step = min(cols, PANEL)
    row, col = iotas((step, LANES))
    for h in range(wide // LANES):
        lanes = slice(h * LANES, (h + 1) * LANES)
        for r in range(0, cols, step):
            here = h * cols + r
            empty = jnp.where(col + h * LANES == row + dp * cols + r, 1.0 / DAMP, 0.0)
            for c in range(slots):
                value = empty
                for l in range(layers):
                    taken = slots_ref[l, :step] == c
                    value = jnp.where(taken, got_ref[l, here : here + step], value)
                kept_ref[c, r : r + step, lanes] = value
    for l in range(layers):
        value = got_ref[l, 2 * cols :]
        if packs(cols, rows):
            update_ref[l, :PANEL] = value[:, :rows]
            update_ref[l, PANEL:] = value[:, rows:]
        else:
            part = value[:, :rows]
            for p in range(1, LANES // rows):
                part = jnp.where(own == p, value[:, p * rows : (p + 1) * rows], part)
            update_ref[l] = part


def placing(place, slots_of, got, wide, cols, slots, rows):
    layers = got.shape[0]
    return pl.pallas_call(
        functools.partial(placing_kernel, place),
        in_specs=[VMEM, VMEM],
        out_specs=[VMEM, VMEM],
        out_shape=[
            jax.ShapeDtypeStruct((slots, cols, wide), jnp.float32),
            jax.ShapeDtypeStruct((layers, cols, rows), jnp.float32),
        ],
        compiler_params=PARAMS,
        name="placing",
    )(slots_of, got)


def swap(value, axis):
    return lax.ppermute(value, axis, [(0, 1), (1, 0)])


def swap_by_core(value, place, stage, orders):
    names = (place.near, place.second, place.core, place.first)
    flips = {"near": 8, "second": 4, "first": 1}
    pairs = [(i, i ^ flips[orders[(i >> 1) & 1][stage]]) for i in range(16)]
    return lax.ppermute(value, names, pairs)


def after(value, *others):
    return lax.optimization_barrier((value,) + others)[0]


def on_device(place, wide_rows, narrow_rows, owner_map):
    layers, rows, wide = wide_rows.shape
    narrow = narrow_rows.shape[2]
    n_dp, n_own = 2 ** len(place.dp), 2 ** len(place.own)
    total = float(rows * n_dp * n_own)

    h_keep, h_send, wides, narrows = hot_squares(place, wide_rows, narrow_rows)
    first_send = h_send[4:]
    h_got = swap(first_send, place.core)
    c_keep, c_send = cold_squares(place, after(wides, first_send), narrows)
    h_keep, c_send = lax.optimization_barrier((h_keep, c_send))

    hot = h_keep[4:] + h_got
    s_got = swap_by_core(hot, place, 0, ORDERS)
    m_keep, m_send, slots_of = mixed_sums(place, owner_map, after(wides, hot), narrows)
    c_got = swap(after(c_send + h_send[:4], m_send), place.core)
    m_got = swap(m_send, place.core)

    s = (c_keep + h_keep[:4]) + s_got
    s = s + after(c_got, s)
    s_got = swap_by_core(s[2:], place, 1, ORDERS)
    m = after(m_keep, s) + m_got
    m_got = swap_by_core(m[4:], place, 0, LATE_ORDERS)

    s = s[:2] + s_got
    s_got = swap_by_core(s[1], place, 2, ORDERS)
    m = after(m[:4], s) + m_got
    m_got = swap_by_core(m[2:], place, 1, LATE_ORDERS)

    s = s[0] + s_got
    if place.extra:
        s = lax.psum(s, place.extra)
    s_got = swap(s, place.far)
    m = after(m[:2], s) + m_got
    m_got = swap_by_core(m[1], place, 2, LATE_ORDERS)

    s = s + s_got
    state = first_panels(place, [s, swap(s, place.core)], wide, narrow, total)
    m = after(m[0], state[0]) + m_got
    if place.extra:
        m = lax.psum(m, place.extra)
    m_got = swap(m, place.far)
    *state, wide_scale, narrow_scale = state
    ninv, *state = second_panels([*state, narrow_scale], wide, narrow)
    m = after(m, ninv) + m_got
    m_got = swap(m, place.core)
    winv = third_panels([*state, wide_scale], wide)
    cols, own_rows = wide // n_dp, narrow // n_own
    sent = products(place, winv, ninv, [m, m_got], own_rows, total)
    got = lax.all_to_all(sent, (place.near, place.second, place.first), 0, 0)
    kept, update = placing(
        place, slots_of, got, wide, cols, layers // n_own + 1, own_rows
    )
    return (jnp.swapaxes(kept, 1, 2), jnp.swapaxes(update, 1, 2))


def solution(mesh):
    n_dp, n_own = mesh.shape["dp"], mesh.shape["own"]
    dp_names = tuple(f"dp{i}" for i in range(int(np.log2(n_dp))))
    own_names = tuple(f"own{i}" for i in range(int(np.log2(n_own))))
    names = dp_names + own_names
    bits = jax.sharding.Mesh(mesh.devices.reshape((2,) * len(names)), names)
    in_specs = (P(None, names, None), P(None, names, None), P())
    out_specs = (P(own_names, None, dp_names), P(None, own_names, dp_names))
    return jax.shard_map(
        functools.partial(on_device, Place(dp_names, own_names)),
        mesh=bits,
        in_specs=in_specs,
        out_specs=out_specs,
        check_vma=False,
    )
```
